32 devices in a mesh: seq: 16 (over z, y, x), tensor: 2 (over core).
Axes of the slice: x: 2, y: 2, z: 4, core: 2. Of those that a mesh axis runs over, the one named last changes fastest.
Arguments:
- inputs: bfloat16 [4096, 2560], P('seq'), may hold values from -6 to 6
- segment_ids: int32 [4096], P('seq'), may hold values from 0 to 20, as said below
- cotangent: bfloat16 [4096, 2560], P('seq'), may hold values from -6 to 6
- attn_gain: bfloat16 [2560], P(('seq', 'tensor')), may hold values from 0.5 to 1.5
- query_weight: bfloat16 [2560, 2560], P('seq', 'tensor'), may hold values from -0.125 to 0.125
- key_value_weight: bfloat16 [2560, 512], P(('seq', 'tensor')), may hold values from -0.125 to 0.125
- out_weight: bfloat16 [2560, 2560], P('tensor', 'seq'), may hold values from -2.5 to 2.5
- out_bias: bfloat16 [2560], P(('seq', 'tensor')), may hold values from -1.5 to 1.5
- mlp_gain: bfloat16 [2560], P(('seq', 'tensor')), may hold values from 0.5 to 1.5
- gate_up_weight: bfloat16 [2, 2560, 7680], P(None, 'seq', 'tensor'), may hold values from -0.125 to 0.125
- gate_up_bias: bfloat16 [2, 7680], P(None, ('seq', 'tensor')), may hold values from -1.5 to 1.5
- down_weight: bfloat16 [7680, 2560], P('tensor', 'seq'), may hold values from -0.0625 to 0.0625
- down_bias: bfloat16 [2560], P(('seq', 'tensor')), may hold values from -1.5 to 1.5
Outputs:
- output: bfloat16 [4096, 2560], P('seq')
- input_grad: float32 [4096, 2560], P('seq')
- attn_gain_grad: float32 [2560], P(('seq', 'tensor'))
- query_grad: float32 [2560, 2560], P('seq', 'tensor')
- key_value_grad: float32 [2560, 512], P(('seq', 'tensor'))
- out_grad: float32 [2560, 2560], P('tensor', 'seq')
- out_bias_grad: float32 [2560], P(('seq', 'tensor'))
- mlp_gain_grad: float32 [2560], P(('seq', 'tensor'))
- gate_up_grad: float32 [2, 2560, 7680], P(None, 'seq', 'tensor')
- gate_up_bias_grad: float32 [2, 7680], P(None, ('seq', 'tensor'))
- down_grad: float32 [7680, 2560], P('tensor', 'seq')
- down_bias_grad: float32 [2560], P(('seq', 'tensor'))
The draws below stay inside these ranges and needn't reach their ends.
Inputs may be any that keep to these rules, and one draw needn't show every extreme that they name: `segment_ids`: segment numbers never fall along the tokens, and a new segment begins at every multiple of 4096 tokens.
All inputs are finite; a program needn't handle non-finite values.
Results may differ from the reference program's by a relative error of at most 0.019.
Values may be sent and summed in bfloat16 or wider, within the bound.
A program may use at most 512 MiB of HBM per device.

```python
import jax
import jax.numpy as jnp
from jax import lax

D = 2560
H = 10
HD = 256
FF = 7680
W = 2048
SEQ_LEN = 4096
DOC_MIN = 200
DOC_MAX = 2000
TOKENS = 4096


def draw_segment_ids(key, part):
    key = jax.random.fold_in(key, 11)
    per_sequence = SEQ_LEN // DOC_MIN + 1
    sequences = TOKENS // SEQ_LEN
    lengths = jax.random.randint(key, (sequences, per_sequence), DOC_MIN, DOC_MAX + 1, dtype=jnp.int32)
    ends = jnp.cumsum(lengths, axis=1)
    local_places = jnp.arange(SEQ_LEN, dtype=jnp.int32)
    local_ids = jnp.sum((ends[:, None, :] <= local_places[None, :, None]).astype(jnp.int32), axis=2)
    last_ids = local_ids[:, SEQ_LEN - 1:SEQ_LEN]
    tops = (jnp.arange(sequences, dtype=jnp.int32)[:, None] + 1) * per_sequence - 1
    return (tops - (last_ids - local_ids)).reshape(TOKENS).astype(jnp.int32)


def shard_levels(rng, dims, split, least, top_value):
    def one(position, shards_of):
        draws = jax.random.uniform(jax.random.fold_in(jax.random.fold_in(rng, 6), position), (shards_of,), jnp.float32, least / len(split), top_value / len(split))
        return jnp.repeat(jnp.exp(draws), dims[position] // shards_of).reshape((-1,) + (1,) * (len(dims) - position - 1))

    gain = one(*split[0])
    for cut in split[1:]:
        gain = gain * one(*cut)
    return gain


def normal_values(stream_key, extent, spread, reach, cuts=(), held_as=jnp.bfloat16):
    array = spread * jax.random.normal(stream_key, extent, jnp.float32)
    if cuts:
        array = array * shard_levels(stream_key, extent, cuts, -0.22, 0.18)
    return jnp.clip(array, -reach, reach).astype(held_as)


def setup_inputs(seed: int = 0) -> dict:
    splits = jax.random.split(jax.random.key(seed), 14)
    return {
        "inputs": normal_values(splits[0], (TOKENS, D), 1.0, 6.0, ((0, 16),)),
        "segment_ids": draw_segment_ids(jax.random.fold_in(splits[13], 71), 0),
        "cotangent": normal_values(splits[2], (TOKENS, D), 1.0, 6.0, ((0, 16),)),
        "attn_gain": jnp.clip(1.0 + 0.1 * jax.random.normal(splits[3], (D,), jnp.float32), 0.5, 1.5).astype(jnp.bfloat16),
        "query_weight": normal_values(splits[4], (D, H * HD), D ** -0.5, 0.125, ((0, 16), (1, 2))),
        "key_value_weight": normal_values(splits[5], (D, 2 * HD), D ** -0.5, 0.125, ((0, 32),)),
        "out_weight": normal_values(splits[6], (H * HD, D), (H * HD * 4 // W) ** -0.5, 2.5, ((0, 2), (1, 16))),
        "out_bias": normal_values(splits[7], (D,), 0.3, 1.5, ((0, 32),)),
        "mlp_gain": jnp.clip(1.0 + 0.1 * jax.random.normal(splits[8], (D,), jnp.float32), 0.5, 1.5).astype(jnp.bfloat16),
        "gate_up_weight": normal_values(splits[9], (2, D, FF), D ** -0.5, 0.125, ((1, 16), (2, 2))),
        "gate_up_bias": normal_values(splits[10], (2, FF), 0.3, 1.5, ((1, 32),)),
        "down_weight": normal_values(splits[11], (FF, D), FF ** -0.5, 0.0625, ((0, 2), (1, 16))),
        "down_bias": normal_values(splits[12], (D,), 0.3, 1.5, ((0, 32),)),
    }


@jax.custom_vjp
def low(v):
    return lax.optimization_barrier(v.astype(jnp.bfloat16)).astype(jnp.float32)

@jax.custom_vjp
def low_back(v):
    return v

def low_keep(v):
    return (low(v), None)

def low_pass(kept, grad):
    return (grad,)

def back_keep(v):
    return (v, None)

def back_low(kept, grad):
    return (low(grad),)
low.defvjp(low_keep, low_pass)
low_back.defvjp(back_keep, back_low)
epsilon = 1e-06

def matmul(left, right):
    return jnp.dot(left, right, precision=lax.Precision.HIGHEST)

def normalize(stream, scale_vec):
    return stream * lax.rsqrt(lax.optimization_barrier(jnp.mean(stream * stream, axis=-1, keepdims=True)) + epsilon) * scale_vec

def rotate(values, places, head_count, direction):
    head_size = values.shape[1] // head_count
    shaped = values.reshape(values.shape[0], head_count, head_size)
    quarter = head_size // 4
    first_part = shaped[..., :quarter]
    second = shaped[..., quarter:2 * quarter]
    remainder = shaped[..., 2 * quarter:]
    frequency = 10000.0 ** (-jnp.arange(quarter, dtype=jnp.float32) / quarter)
    angles = places.astype(jnp.float32)[:, None] * frequency[None, :]
    cosine = jnp.cos(angles)[:, None, :]
    sine_part = direction * jnp.sin(angles)[:, None, :]
    turned = jnp.concatenate([first_part * cosine - second * sine_part, second * cosine + first_part * sine_part, remainder], axis=-1)
    return turned.reshape(values.shape)

def attend(queries, keys, values_in, segments):
    qblock = min(512, SEQ_LEN)
    blocks = SEQ_LEN // qblock
    key_pad = jnp.concatenate([jnp.zeros((W, HD), jnp.float32), keys], axis=0)
    value_pad = jnp.concatenate([jnp.zeros((W, HD), jnp.float32), values_in], axis=0)
    segment_pad = jnp.concatenate([jnp.full((W,), -1, jnp.int32), segments.astype(jnp.int32)], axis=0)
    query_blocks = queries.reshape(blocks, qblock, H, HD)
    segment_blocks = segments.reshape(blocks, qblock)
    starts = (jnp.arange(blocks, dtype=jnp.int32) * qblock).astype(jnp.int32)

    @jax.checkpoint
    def one_block(item):
        query_here, segment_here, start = item
        key_here = lax.dynamic_slice_in_dim(key_pad, start, qblock + W, 0)
        value_here = lax.dynamic_slice_in_dim(value_pad, start, qblock + W, 0)
        segment_keys = lax.dynamic_slice_in_dim(segment_pad, start, qblock + W, 0)
        key_places = start - W + jnp.arange(qblock + W, dtype=jnp.int32)
        query_places = start + jnp.arange(qblock, dtype=jnp.int32)
        key_gap = query_places[:, None] - key_places[None, :]
        visible = (key_gap >= 0) & (key_gap < W) & (segment_here[:, None] == segment_keys[None, :])
        scores = low_back(jnp.einsum('qhd,kd->hqk', query_here, key_here, precision=lax.Precision.HIGHEST))
        scores = jnp.where(visible[None], scores, -1e+30)
        row_top = lax.optimization_barrier(jnp.max(scores, axis=-1, keepdims=True))
        exponent = jnp.exp(scores - row_top)
        probs_low = low(exponent / lax.optimization_barrier(jnp.sum(exponent, axis=-1, keepdims=True)))
        blended = jnp.einsum('hqk,kd->qhd', probs_low, value_here, precision=lax.Precision.HIGHEST)
        return blended.reshape(qblock, H * HD)
    mixed_all = lax.map(one_block, (query_blocks, segment_blocks, starts)).reshape(SEQ_LEN, H * HD)
    return low_back(low(mixed_all))

def forward(stream, weights, segments, places):
    attn_gain, query_weight, key_value_weight, out_weight, out_bias, mlp_gain, gate_up_weight, gate_up_bias, down_weight, down_bias = weights
    normed = low(normalize(stream, attn_gain))
    query_lin = low_back(matmul(normed, query_weight))
    queries = low(rotate(query_lin, places, H, 1.0) * HD ** (-0.5))
    key_value = low_back(matmul(normed, key_value_weight))
    keys = low(rotate(key_value[:, :HD], places, 1, 1.0))
    values_kept = low(key_value[:, HD:])
    mixed_low = attend(queries, keys, values_kept, segments)
    branch = low_back(matmul(mixed_low, out_weight))
    middle = stream + branch + out_bias
    normed_two = low(normalize(middle, mlp_gain))
    gate_pre = low_back(matmul(normed_two, gate_up_weight[0]) + gate_up_bias[0])
    up_pre = low_back(matmul(normed_two, gate_up_weight[1]) + gate_up_bias[1])
    hidden = low(jax.nn.gelu(gate_pre, approximate=True) * up_pre)
    return middle + low_back(matmul(hidden, down_weight)) + down_bias

def reference(inputs, segment_ids, cotangent, attn_gain, query_weight, key_value_weight, out_weight, out_bias, mlp_gain, gate_up_weight, gate_up_bias, down_weight, down_bias):
    params = tuple((piece.astype(jnp.float32) for piece in (attn_gain, query_weight, key_value_weight, out_weight, out_bias, mlp_gain, gate_up_weight, gate_up_bias, down_weight, down_bias)))
    sequences = TOKENS // SEQ_LEN
    stream_rows = inputs.astype(jnp.float32).reshape(sequences, SEQ_LEN, D)
    segment_rows = segment_ids.astype(jnp.int32).reshape(sequences, SEQ_LEN)
    cot_rows = cotangent.astype(jnp.float32).reshape(sequences, SEQ_LEN, D)
    places = jnp.arange(SEQ_LEN, dtype=jnp.int32)

    def per_sequence(totals, item):
        stream, segments, cot_here = item

        def apply_block(stream_in, *weights):
            return forward(stream_in, weights, segments, places)
        result, pullback = jax.vjp(apply_block, stream, *params)
        gradients = pullback(cot_here)
        totals = tuple((earlier + latest for earlier, latest in zip(totals, gradients[1:])))
        return (totals, (result, gradients[0]))
    starting = tuple((jnp.zeros_like(piece) for piece in params))
    totals, (results, input_grads) = lax.scan(per_sequence, starting, (stream_rows, segment_rows, cot_rows))
    return (results.reshape(TOKENS, D).astype(jnp.bfloat16), input_grads.reshape(TOKENS, D), totals[0], totals[1], totals[2], totals[3], totals[4], totals[5], totals[6], totals[7], totals[8], totals[9])
```

```python
import functools

import jax
import jax.numpy as jnp
from jax import lax
from jax.experimental import pallas as pl
from jax.experimental.pallas import tpu as pltpu
from jax.sharding import PartitionSpec as P

HD = 256
W = 2048
SEQ_LEN = 4096
LINE = 4
RING = 16
LANES = 128

epsilon = 1e-06
bf16 = jnp.bfloat16
f32 = jnp.float32
MESH = pl.DeviceIdType.MESH
ANY = pl.BlockSpec(memory_space=pl.ANY)


class Place:
    def __init__(self):
        seq = lax.axis_index("seq")
        self.t = lax.axis_index("tensor")
        self.r = lax.rem(seq, RING)
        self.base = seq - self.r
        self.z = lax.div(self.r, 4)
        self.q = lax.rem(self.r, 4)
        self.xq = self.q + 1 - 2 * lax.rem(self.q, 2)
        self.yq = self.q + 2 - 4 * lax.div(self.q, 2)
        self.dq = 3 - self.q
        self.half = lax.div(self.z, 2)
        self.inner = self.z + self.half * (3 - 2 * self.z)

    def at(self, z, q):
        return (self.base + 4 * z + q, self.t)

    def other(self):
        return (self.base + self.r, 1 - self.t)

    def order(self, j):
        v = j + self.inner * (1 - 2 * j if j < 2 else 0)
        return v + self.half * (3 - 2 * v)

    def greet(self, whole=False):
        barrier = pltpu.get_barrier_semaphore()
        if whole:
            peers = [
                (self.base + lax.rem(self.r + k, RING), self.t) for k in range(1, RING)
            ]
        else:
            peers = [self.at(lax.rem(self.z + k, 4), self.q) for k in range(1, 4)]
            peers += [self.at(self.z, self.xq), self.at(self.z, self.yq)]
        peers.append(self.other())
        for peer in peers:
            pl.semaphore_signal(barrier, inc=1, device_id=peer, device_id_type=MESH)
        pl.semaphore_wait(barrier, len(peers))


def remote(src, dst, send, recv, device):
    return pltpu.make_async_remote_copy(
        src_ref=src, dst_ref=dst, send_sem=send, recv_sem=recv, device_id=device, device_id_type=MESH
    )


def run(steps):
    steps = list(steps)
    while steps:
        for step in list(steps):
            try:
                next(step)
            except StopIteration:
                steps.remove(step)


GATHER_SEMS = [
    pltpu.SemaphoreType.DMA((4, 6)),
    pltpu.SemaphoreType.DMA((4, 5)),
    pltpu.SemaphoreType.DMA,
]


def gather(me, own, slot, part, sems, pieces=None):
    snd, rcv, loc = sems
    local = pltpu.make_async_copy(own, slot(me.z, me.q), loc)
    local.start()

    def line(z, k, src, to):
        return remote(src, slot(z, me.q), snd.at[z, k], rcv.at[z, 0], me.at(to, me.q))

    def across(z, k, src):
        q = (me.xq, me.yq)[k]
        return remote(src, slot(z, me.q), snd.at[z, 2 + k], rcv.at[z, 1 + k], me.at(me.z, q))

    def corner(z, k):
        src = part(z, (me.xq, me.yq)[k], k)
        return remote(src, src, snd.at[z, 4 + k], rcv.at[z, 3 + k], me.at(me.z, (me.yq, me.xq)[k]))

    if pieces is None:

        @pl.when(me.z < 3)
        def _():
            line(me.z, 0, own, me.z + 1).start()

        @pl.when(me.z > 0)
        def _():
            line(me.z, 1, own, me.z - 1).start()

    else:
        for j in range(1, 4):
            z = me.order(j)
            remote(
                pieces(z), slot(me.z, me.q), snd.at[z, 0], rcv.at[me.z, 0], me.at(z, me.q)
            ).start()
    for k in range(2):
        across(me.z, k, own).start()
    yield
    for j in range(1, 5):
        if j < 4:
            z = me.order(j)
            remote(
                slot(z, me.q), slot(z, me.q), snd.at[z, 0], rcv.at[z, 0], me.at(me.z, me.q)
            ).wait_recv()
            if pieces is None:

                @pl.when(me.inner == 1)
                def _():
                    step = 3 - 2 * me.z if j == 1 else 2 * me.z - 3
                    line(z, 0, slot(z, me.q), me.z + step).start()

            for k in range(2):
                across(z, k, slot(z, me.q)).start()
        z = me.order(j - 1)
        for k in range(2):
            q = (me.xq, me.yq)[k]
            remote(
                slot(z, q), slot(z, q), snd.at[z, 2 + k], rcv.at[z, 1 + k], me.at(me.z, q)
            ).wait_recv()
            corner(z, k).start()
        yield
    for j in range(4):
        z = me.order(j)
        for k in range(2):
            src = part(z, me.dq, k)
            remote(src, src, snd.at[z, 4 + k], rcv.at[z, 3 + k], me.at(me.z, me.xq)).wait_recv()
    local.wait()
    for j in range(4):
        z = me.order(j)
        for k in range(2):
            across(z, k, slot(z, me.q)).wait_send()
            corner(z, k).wait_send()
    if pieces is None:

        @pl.when(me.z < 3)
        def _():
            line(me.z, 0, own, me.z + 1).wait_send()

        @pl.when(me.z > 0)
        def _():
            line(me.z, 1, own, me.z - 1).wait_send()

        @pl.when(me.inner == 1)
        def _():
            for j in range(1, 4):
                z = me.order(j)
                line(z, 0, slot(z, me.q), me.z).wait_send()

    else:
        for j in range(1, 4):
            z = me.order(j)
            remote(pieces(z), pieces(z), snd.at[z, 0], rcv.at[z, 0], me.at(z, me.q)).wait_send()


SPREAD_SEMS = [
    pltpu.SemaphoreType.DMA((4, 3)),
    pltpu.SemaphoreType.DMA((4, 2)),
    pltpu.SemaphoreType.DMA,
]


def spread(me, src, dst, sems):
    snd, rcv, loc = sems
    rows = src.shape[0] // 2
    mine = pl.ds(pl.multiple_of(me.t * rows, rows), rows)
    local = pltpu.make_async_copy(src, dst.at[me.z], loc)
    local.start()

    def slot(z):
        return dst.at[z, mine]

    def line(z, k, source, to):
        return remote(source, slot(z), snd.at[z, k], rcv.at[z, 0], me.at(to, me.q))

    def share(z):
        return remote(slot(z), slot(z), snd.at[z, 2], rcv.at[z, 1], me.other())

    @pl.when(me.z < 3)
    def _():
        line(me.z, 0, src.at[mine], me.z + 1).start()

    @pl.when(me.z > 0)
    def _():
        line(me.z, 1, src.at[mine], me.z - 1).start()

    yield
    for j in range(1, 4):
        z = me.order(j)
        line(z, 0, slot(z), me.z).wait_recv()

        @pl.when(me.inner == 1)
        def _():
            step = 3 - 2 * me.z if j == 1 else 2 * me.z - 3
            line(z, 0, slot(z), me.z + step).start()

        share(z).start()
        yield
    other = pl.ds(pl.multiple_of((1 - me.t) * rows, rows), rows)
    for j in range(1, 4):
        z = me.order(j)
        remote(
            dst.at[z, other], dst.at[z, other], snd.at[z, 2], rcv.at[z, 1], me.other()
        ).wait_recv()
        share(z).wait_send()
    local.wait()

    @pl.when(me.z < 3)
    def _():
        line(me.z, 0, src.at[mine], me.z + 1).wait_send()

    @pl.when(me.z > 0)
    def _():
        line(me.z, 1, src.at[mine], me.z - 1).wait_send()

    @pl.when(me.inner == 1)
    def _():
        for j in range(1, 4):
            z = me.order(j)
            line(z, 0, slot(z), me.z).wait_send()


def swap(me, src, dst, sems):
    copy = remote(src, dst, sems[0], sems[1], me.other())
    copy.start()
    yield
    copy.wait()


SWAP_SEMS = [pltpu.SemaphoreType.DMA, pltpu.SemaphoreType.DMA]


def add_rows(out, terms):
    rows = out.shape[0]
    step = 16

    @pl.loop(0, rows // step)
    def _(i):
        at = pl.ds(pl.multiple_of(i * step, step), step)
        total = terms[0][at].astype(f32)
        for term in terms[1:]:
            total += term[at].astype(f32)
        out[at] = total.astype(out.dtype)


def reduce_scratch(slots, rows, columns, dtype):
    return [
        pltpu.VMEM((slots, rows, columns), bf16),
        pltpu.VMEM((slots, rows, columns), bf16),
        pltpu.VMEM((slots, rows, columns), bf16),
        pltpu.VMEM((rows, columns), dtype),
        pltpu.SemaphoreType.DMA((slots, 3)),
        pltpu.SemaphoreType.DMA((slots, 2)),
        pltpu.SemaphoreType.DMA((3,)),
    ]


def reduce_line(me, src, out, scratch):
    here, there, landed, total, snd, rcv, end = scratch
    rows = here.shape[1]
    mine = pl.ds(pl.multiple_of(me.t * rows, rows), rows)
    theirs = pl.ds(pl.multiple_of((1 - me.t) * rows, rows), rows)

    def cross(z):
        return remote(src.at[z, theirs], there.at[z], snd.at[z, 0], rcv.at[z, 0], me.other())

    def local(z):
        return pltpu.make_async_copy(src.at[z, mine], here.at[z], snd.at[z, 1])

    def line(z):
        return remote(here.at[z], landed.at[me.z], snd.at[z, 2], rcv.at[me.z, 1], me.at(z, me.q))

    for j in (3, 2, 1, 0):
        z = me.order(j)
        cross(z).start()
        local(z).start()
    yield
    for j in (3, 2, 1, 0):
        z = me.order(j)
        local(z).wait()
        cross(z).wait_recv()
        add_rows(here.at[z], (here.at[z], there.at[z]))
        if j:
            line(z).start()
        yield
    for j in range(1, 4):
        z = me.order(j)
        remote(landed.at[z], landed.at[z], snd.at[z, 2], rcv.at[z, 1], me.at(z, me.q)).wait_recv()
    add_rows(total, [here.at[me.z]] + [landed.at[me.order(j)] for j in range(1, 4)])
    keep = pltpu.make_async_copy(total, out.at[mine], end.at[0])
    give = remote(total, out.at[mine], end.at[1], end.at[2], me.other())
    keep.start()
    give.start()
    yield
    for j in range(4):
        z = me.order(j)
        cross(z).wait_send()
        if j:
            line(z).wait_send()
    keep.wait()
    give.wait()


def reduce_window(me, reach, src, out, scratch):
    here, there, landed, total, snd, rcv, end = scratch
    rows = here.shape[1]
    slots = reach + 1
    mine = pl.ds(pl.multiple_of(me.t * rows, rows), rows)
    theirs = pl.ds(pl.multiple_of((1 - me.t) * rows, rows), rows)
    start = jnp.maximum(me.r - reach, 0)

    def cross(j):
        return remote(src.at[j, theirs], there.at[j], snd.at[j, 0], rcv.at[j, 0], me.other())

    def local(j):
        return pltpu.make_async_copy(src.at[j, mine], here.at[j], snd.at[j, 1])

    def back(k):
        j = me.r - k - start
        return remote(
            here.at[j], landed.at[k], snd.at[k, 2], rcv.at[k, 1], (me.base + me.r - k, me.t)
        )

    for j in range(slots):
        cross(j).start()
        local(j).start()
    yield
    for j in range(slots):
        local(j).wait()
        cross(j).wait_recv()
        add_rows(here.at[j], (here.at[j], there.at[j]))
    for k in range(reach, 0, -1):

        @pl.when(me.r >= k)
        def _():
            back(k).start()

    yield
    add_rows(total, [here.at[me.r - start]])
    for k in range(1, slots):

        @pl.when(me.r + k < RING)
        def _():
            remote(
                landed.at[k], landed.at[k], snd.at[k, 2], rcv.at[k, 1], me.at(me.z, me.q)
            ).wait_recv()
            add_rows(total, (total, landed.at[k]))

    keep = pltpu.make_async_copy(total, out.at[mine], end.at[0])
    give = remote(total, out.at[mine], end.at[1], end.at[2], me.other())
    keep.start()
    give.start()
    yield
    for j in range(slots):
        cross(j).wait_send()
    for k in range(1, slots):

        @pl.when(me.r >= k)
        def _():
            back(k).wait_send()

    keep.wait()
    give.wait()


PLANE_SEMS = [pltpu.SemaphoreType.DMA((4,)), pltpu.SemaphoreType.DMA((4,))]


def plane_first(me, src, got, sems):
    snd, rcv = sems
    rows = src.shape[-2] // 2
    copies = []
    lead = (slice(None),) * (len(src.shape) - 3)
    for h in range(2):
        q = (me.xq, me.yq)[h]
        for i in range(2):
            place = (q, me.dq)[i]
            n = 2 * h + i
            view = src.at[lead + (place, pl.ds(h * rows, rows))]
            copies.append(remote(view, got.at[h, i], snd.at[n], rcv.at[n], me.at(me.z, q)))
    for copy in copies:
        copy.start()
    yield
    for copy in copies:
        copy.wait()


def plane_second(me, src, got, sems):
    snd, rcv = sems
    copies = [
        remote(src.at[h], got.at[h], snd.at[h], rcv.at[h], me.at(me.z, (me.yq, me.xq)[h]))
        for h in range(2)
    ]
    for copy in copies:
        copy.start()
    yield
    for copy in copies:
        copy.wait()


LINE_SEMS = [pltpu.SemaphoreType.DMA((4,)), pltpu.SemaphoreType.DMA((4,)), pltpu.SemaphoreType.DMA]


def line_exchange(me, piece, got, sems):
    snd, rcv, loc = sems
    local = pltpu.make_async_copy(piece(me.z), got.at[me.z], loc)
    local.start()

    def send(j):
        z = me.order(j)
        return remote(piece(z), got.at[me.z], snd.at[z], rcv.at[me.z], me.at(z, me.q))

    for j in (3, 2, 1):
        send(j).start()
    yield
    for j in range(1, 4):
        z = me.order(j)
        remote(got.at[z], got.at[z], snd.at[z], rcv.at[z], me.at(z, me.q)).wait_recv()
    for j in range(1, 4):
        send(j).wait_send()
    local.wait()


def transfer(number, inputs, outputs, scratch, steps, whole=False):
    flat = [item for group in scratch for item in group]
    sizes = [len(group) for group in scratch]

    def kernel(*refs):
        ins = refs[: len(inputs)]
        outs = refs[len(inputs) : len(inputs) + len(outputs)]
        rest = refs[len(inputs) + len(outputs) :]
        groups = []
        for size in sizes:
            groups.append(rest[:size])
            rest = rest[size:]
        me = Place()
        me.greet(whole)
        run(steps(me, ins, outs, groups))

    return pl.pallas_call(
        kernel,
        out_shape=[jax.ShapeDtypeStruct(shape, dtype) for shape, dtype in outputs],
        in_specs=[ANY] * len(inputs),
        out_specs=[ANY] * len(outputs),
        scratch_shapes=flat,
        compiler_params=pltpu.CompilerParams(
            collective_id=number, has_side_effects=True, vmem_limit_bytes=48 * 2**20
        ),
    )(*inputs)


def gather_rows(me, src, dst, sems):
    half = src.shape[0] // 2
    return gather(
        me,
        src,
        lambda z, q: dst.at[4 * z + q],
        lambda z, q, h: dst.at[4 * z + q, pl.ds(h * half, half)],
        sems,
    )


def gather_pieces(me, src, dst, sems):
    half = src.shape[1] // 2
    width = dst.shape[-1]

    def piece(z):
        return src.at[:, :, pl.ds(pl.multiple_of(z * width, width), width)]

    return gather(
        me,
        piece(me.z),
        lambda z, q: dst.at[:, 4 * z + q],
        lambda z, q, h: dst.at[:, 4 * z + q, pl.ds(h * half, half)],
        sems,
        piece,
    )


def group_lists(groups):
    return [[r + RING * g for g in range(groups)] for r in range(RING)]


def grow(x, axis, groups):
    if groups == 1:
        return x
    return lax.all_gather(x, "seq", axis=axis, tiled=True, axis_index_groups=group_lists(groups))


def shrink(x, axis, groups):
    if groups == 1:
        return x
    return lax.psum_scatter(
        x, "seq", scatter_dimension=axis, tiled=True, axis_index_groups=group_lists(groups)
    )


def merge(blocks, axis, groups):
    shape = blocks.shape
    rows = shape[axis + 1]
    if groups > 1:
        blocks = blocks.reshape(shape[: axis + 1] + (groups, rows // groups) + shape[axis + 2 :])
        blocks = jnp.moveaxis(blocks, axis + 1, axis)
    return blocks.reshape(shape[:axis] + (shape[axis] * rows,) + shape[axis + 2 :])


def split(full, axis, places, groups):
    shape = full.shape
    rows = shape[axis] // (places * groups)
    blocks = full.reshape(shape[:axis] + (groups, places, rows) + shape[axis + 1 :])
    if groups > 1:
        blocks = jnp.moveaxis(blocks, axis, axis + 1)
    return blocks.reshape(shape[:axis] + (places, groups * rows) + shape[axis + 1 :])


def normalize(stream, scale_vec):
    return (
        stream * lax.rsqrt(jnp.mean(stream * stream, axis=-1, keepdims=True) + epsilon) * scale_vec
    )


def rotate(values, places, head_count, direction):
    head_size = values.shape[1] // head_count
    shaped = values.reshape(values.shape[0], head_count, head_size)
    quarter = head_size // 4
    first_part = shaped[..., :quarter]
    second = shaped[..., quarter : 2 * quarter]
    remainder = shaped[..., 2 * quarter :]
    frequency = 10000.0 ** (-jnp.arange(quarter, dtype=jnp.float32) / quarter)
    angles = places.astype(jnp.float32)[:, None] * frequency[None, :]
    cosine = jnp.cos(angles)[:, None, :]
    sine_part = direction * jnp.sin(angles)[:, None, :]
    turned = jnp.concatenate(
        [
            first_part * cosine - second * sine_part,
            second * cosine + first_part * sine_part,
            remainder,
        ],
        axis=-1,
    )
    return turned.reshape(values.shape)


def dot(a, b, ca=1, cb=0):
    return lax.dot_general(a, b, (((ca,), (cb,)), ((), ())), preferred_element_type=f32)


def body(
    inputs,
    segment_ids,
    cotangent,
    attn_gain,
    query_weight,
    key_value_weight,
    out_weight,
    out_bias,
    mlp_gain,
    gate_up_weight,
    gate_up_bias,
    down_weight,
    down_bias,
):
    seq_index = lax.axis_index("seq")
    t = lax.axis_index("tensor")
    r = seq_index % RING
    z = r // 4
    q = r % 4
    groups = lax.axis_size("seq") // RING
    tokens, width = inputs.shape
    heads = query_weight.shape[1] // HD
    hidden_half = gate_up_weight.shape[2]
    hidden_block = hidden_half // LINE
    hidden_pad = -(-hidden_block // LANES) * LANES
    reach = (W + tokens - 2) // tokens
    scale_factor = HD ** (-0.5)
    assert tokens * RING == SEQ_LEN and lax.axis_size("tensor") == 2

    kv_own = grow(key_value_weight, 0, groups)
    kv_rows = kv_own.shape[0]
    vectors = [grow(v, 0, groups) for v in (attn_gain, out_bias, mlp_gain, down_bias)]
    hidden_bias = grow(gate_up_bias, 1, groups)
    marks = jnp.stack([segment_ids // 256, segment_ids % 256]).astype(bf16)
    columns = kv_own.shape[1]

    def pad_to(x, n):
        return jnp.pad(x, ((0, 0), (0, n - x.shape[1])))

    small = jnp.concatenate(
        [
            pad_to(jnp.stack(vectors), columns),
            pad_to(hidden_bias, columns),
            pad_to(marks, columns),
            jnp.zeros((8, columns), bf16),
        ]
    )
    kv_block = jnp.concatenate([kv_own, small])
    query_own = grow(query_weight, 0, groups)
    out_own = grow(out_weight.T, 0, groups)
    ffn_own = grow(jnp.concatenate([gate_up_weight, down_weight.T[None]]), 1, groups)
    ffn_own = jnp.pad(
        ffn_own.reshape(3, -1, LINE, hidden_block),
        ((0, 0), (0, 0), (0, 0), (0, hidden_pad - hidden_block)),
    ).reshape(3, -1, LINE * hidden_pad)
    rows = query_own.shape[0]

    def first_steps(me, ins, outs, sems):
        def both():
            yield from gather_rows(me, ins[1], outs[1], sems[1])
            yield from swap(me, outs[1], outs[2], sems[2])

        return [gather_rows(me, ins[0], outs[0], sems[0]), both()]

    query_full, kv_mine, kv_theirs = transfer(
        0,
        [query_own, kv_block],
        [((RING,) + query_own.shape, bf16)] + [((RING,) + kv_block.shape, bf16)] * 2,
        [GATHER_SEMS, GATHER_SEMS, SWAP_SEMS],
        first_steps,
    )
    query_full = merge(query_full, 0, groups)
    kv_both = jnp.where(
        t == 0, jnp.stack([kv_mine, kv_theirs], 1), jnp.stack([kv_theirs, kv_mine], 1)
    )
    kv_full = merge(
        kv_both[:, :, :kv_rows]
        .reshape(RING, 2, groups, kv_rows // groups, columns)
        .swapaxes(1, 2)
        .reshape(RING, 2 * kv_rows, columns),
        0,
        groups,
    )

    def vector(row, count):
        piece = kv_both[:, :, kv_rows + row, :count].reshape(RING, 2, groups, count // groups)
        return jnp.transpose(piece, (2, 0, 1, 3)).reshape(-1).astype(f32)

    gain_one, bias_out, gain_two, bias_down = (vector(i, kv_rows) for i in range(4))
    bias_gate_up = jnp.stack([vector(4 + i, hidden_bias.shape[1]) for i in range(2)])
    bias_local = lax.dynamic_slice_in_dim(
        bias_gate_up, t * hidden_half + z * hidden_block, hidden_block, 1
    )
    bias_local = pad_to(bias_local, hidden_pad)
    all_marks = kv_both[:, 0, kv_rows + 6 : kv_rows + 8, :tokens].astype(f32)
    all_marks = (all_marks[:, 0] * 256.0 + all_marks[:, 1]).reshape(-1)

    stream = inputs.astype(f32)
    places = r * tokens + jnp.arange(tokens, dtype=jnp.int32)
    normed = normalize(stream, gain_one).astype(bf16)
    query_lin = dot(normed, query_full)
    queries = (rotate(query_lin, places, heads, 1.0) * scale_factor).astype(bf16)
    key_value = dot(normed, kv_full)
    keys_own = rotate(key_value[:, :HD], places, 1, 1.0).astype(bf16)
    values_own = key_value[:, HD:].astype(bf16)
    own_block = jnp.concatenate([keys_own, values_own], axis=1)

    def second_steps(me, ins, outs, sems):
        return [
            gather_rows(me, ins[0], outs[0], sems[0]),
            gather_rows(me, ins[1], outs[1], sems[1]),
            gather_pieces(me, ins[2], outs[2], sems[2]),
            spread(me, ins[3], outs[3], sems[3]),
        ]

    kv_all, out_full, ffn_full, cot_all = transfer(
        1,
        [own_block, out_own, ffn_own, cotangent],
        [
            ((RING,) + own_block.shape, bf16),
            ((RING,) + out_own.shape, bf16),
            ((3, RING, rows, hidden_pad), bf16),
            ((LINE,) + cotangent.shape, bf16),
        ],
        [GATHER_SEMS, GATHER_SEMS, GATHER_SEMS, SPREAD_SEMS],
        second_steps,
    )
    out_full = merge(out_full, 0, groups)
    ffn_full = merge(ffn_full, 1, groups)
    cot_all = cot_all.reshape(LINE * tokens, width)

    first_block = jnp.maximum(r - reach, 0)
    span = (reach + 1) * tokens
    window = lax.dynamic_slice_in_dim(
        kv_all.reshape(RING * tokens, 2 * HD), first_block * tokens, span, 0
    )
    window_marks = lax.dynamic_slice_in_dim(all_marks, first_block * tokens, span, 0)
    own_marks = lax.dynamic_slice_in_dim(all_marks, r * tokens, tokens, 0)
    key_places = first_block * tokens + jnp.arange(span, dtype=jnp.int32)
    key_gap = places[:, None] - key_places[None, :]
    visible = (key_gap >= 0) & (key_gap < W) & (own_marks[:, None] == window_marks[None, :])
    key_win = window[:, :HD]
    value_win = window[:, HD:]
    query_heads = queries.reshape(tokens, heads, HD)
    scores = jnp.einsum("qhd,kd->hqk", query_heads, key_win, preferred_element_type=f32)
    scores = jnp.where(visible[None], scores, -1e30)
    row_top = jnp.max(scores, axis=-1, keepdims=True)
    exponent = jnp.exp(scores - row_top)
    row_total = jnp.sum(exponent, axis=-1, keepdims=True)
    log_total = row_top + jnp.log(row_total)
    probs_low = (exponent / row_total).astype(bf16)
    mixed_low = (
        jnp.einsum("hqk,kd->qhd", probs_low, value_win, preferred_element_type=f32)
        .reshape(tokens, heads * HD)
        .astype(bf16)
    )

    def both_cores(number, part):
        (theirs,) = transfer(
            number,
            [part],
            [(part.shape, bf16)],
            [SWAP_SEMS],
            lambda me, ins, outs, sems: [swap(me, ins[0], outs[0], sems[0])],
        )
        return part.astype(f32) + theirs.astype(f32)

    branch = both_cores(2, dot(mixed_low, out_full, 1, 1).astype(bf16))
    middle = stream + branch + bias_out
    normed_two = normalize(middle, gain_two).astype(bf16)

    (normed_all,) = transfer(
        3,
        [normed_two],
        [((LINE,) + normed_two.shape, bf16)],
        [SPREAD_SEMS],
        lambda me, ins, outs, sems: [spread(me, ins[0], outs[0], sems[0])],
    )
    normed_all = normed_all.reshape(LINE * tokens, width)
    gate_pre = dot(normed_all, ffn_full[0]) + bias_local[0]
    up_pre = dot(normed_all, ffn_full[1]) + bias_local[1]
    hidden = (jax.nn.gelu(gate_pre, approximate=True) * up_pre).astype(bf16)
    mlp_part = dot(hidden, ffn_full[2], 1, 1).astype(bf16)
    hidden_grad = dot(cot_all, ffn_full[2])
    _, unit_pull = jax.vjp(
        lambda gate_in, up_in: jax.nn.gelu(gate_in, approximate=True) * up_in, gate_pre, up_pre
    )
    gate_grad, up_grad = unit_pull(hidden_grad)
    gate_low = gate_grad.astype(bf16)
    up_low = up_grad.astype(bf16)
    ffn_term = jnp.stack(
        [
            dot(normed_all, gate_low, 0, 0).astype(bf16),
            dot(normed_all, up_low, 0, 0).astype(bf16),
            dot(cot_all, hidden, 0, 0).astype(bf16),
        ]
    )
    ffn_term = split(ffn_term, 1, RING, groups).reshape(3, LINE, 4, rows, hidden_pad)
    normed_two_part = (dot(gate_low, ffn_full[0], 1, 1) + dot(up_low, ffn_full[1], 1, 1)).astype(
        bf16
    )
    hidden_bias_part = jnp.stack(
        [jnp.sum(gate_low.astype(f32), axis=0), jnp.sum(up_low.astype(f32), axis=0)]
    )
    hidden_bias_part = jnp.pad(hidden_bias_part, ((0, 14), (0, 0))).astype(bf16)

    def first_half(src, got):
        lead = src.ndim - 3
        half = rows_of(src)
        xq, yq = q + 1 - 2 * (q % 2), q + 2 - 4 * (q // 2)

        def own(place, h):
            piece = lax.dynamic_index_in_dim(src, place, lead, keepdims=False)
            return lax.slice_in_dim(piece, h * half, (h + 1) * half, axis=lead).astype(f32)

        kept = [own(q, h) + got[h, 0].astype(f32) for h in range(2)]
        passed = jnp.stack(
            [
                (own(yq, 0) + got[0, 1].astype(f32)).astype(bf16),
                (own(xq, 1) + got[1, 1].astype(f32)).astype(bf16),
            ]
        )
        return kept, passed

    def rows_of(src):
        return src.shape[-2] // 2

    def second_half(kept, got):
        return jnp.concatenate([kept[h] + got[h].astype(f32) for h in range(2)], axis=-2).astype(
            bf16
        )

    def first_shape(src):
        s = src.shape
        return (2, 2) + s[:-3] + (s[-2] // 2, s[-1])

    def third_steps(me, ins, outs, sems):
        return [
            plane_first(me, ins[1], outs[1], sems[1]),
            swap(me, ins[2], outs[2], sems[2]),
            reduce_line(me, ins[0], outs[0], sems[0]),
        ]

    normed_two_grad, ffn_got, bias_theirs = transfer(
        4,
        [normed_two_part.reshape(LINE, tokens, width), ffn_term, hidden_bias_part],
        [
            ((tokens, width), bf16),
            (first_shape(ffn_term), bf16),
            (hidden_bias_part.shape, bf16),
        ],
        [reduce_scratch(LINE, tokens // 2, width, bf16), PLANE_SEMS, SWAP_SEMS],
        third_steps,
    )
    ffn_kept, ffn_passed = first_half(ffn_term, ffn_got)
    cot_full = cotangent.astype(f32)
    _, norm_two_pull = jax.vjp(normalize, middle, gain_two)
    middle_part, gain_two_grad = norm_two_pull(normed_two_grad.astype(f32))
    middle_grad = cot_full + middle_part
    middle_low = middle_grad.astype(bf16)
    out_term = dot(middle_low, mixed_low, 0, 0).astype(bf16)
    out_term = split(out_term, 0, RING, groups).reshape(LINE, 4, rows, heads * HD)
    mixed_grad = dot(middle_low, out_full).astype(bf16).reshape(tokens, heads, HD)

    scores_again = jnp.einsum("qhd,kd->hqk", query_heads, key_win, preferred_element_type=f32)
    probs_again = jnp.where(visible[None], jnp.exp(scores_again - log_total), 0.0)
    probs_again_low = probs_again.astype(bf16)
    prob_grad = jnp.einsum("qhd,kd->hqk", mixed_grad, value_win, preferred_element_type=f32)
    value_grad = jnp.einsum("hqk,qhd->kd", probs_again_low, mixed_grad, preferred_element_type=f32)
    row_inner = jnp.sum(probs_again * prob_grad, axis=-1, keepdims=True)
    score_grad = (probs_again * (prob_grad - row_inner)).astype(bf16)
    query_grad_raw = jnp.einsum(
        "hqk,kd->qhd", score_grad, key_win, preferred_element_type=f32
    ).reshape(tokens, heads * HD)
    key_grad_raw = jnp.einsum("hqk,qhd->kd", score_grad, query_heads, preferred_element_type=f32)
    window_grad = (
        jnp.concatenate([key_grad_raw, value_grad], axis=1)
        .reshape(reach + 1, tokens, 2 * HD)
        .astype(bf16)
    )

    def fourth_steps(me, ins, outs, sems):
        return [
            reduce_window(me, reach, ins[0], outs[0], sems[0]),
            plane_second(me, ins[1], outs[1], sems[1]),
            plane_first(me, ins[2], outs[2], sems[2]),
            reduce_line(me, ins[3], outs[3], sems[3]),
        ]

    own_grad, ffn_got, out_got, mlp_out = transfer(
        5,
        [window_grad, ffn_passed, out_term, mlp_part.reshape(LINE, tokens, width)],
        [
            ((tokens, 2 * HD), f32),
            (ffn_passed.shape, bf16),
            (first_shape(out_term), bf16),
            ((tokens, width), bf16),
        ],
        [
            reduce_scratch(reach + 1, tokens // 2, 2 * HD, f32),
            PLANE_SEMS,
            PLANE_SEMS,
            reduce_scratch(LINE, tokens // 2, width, bf16),
        ],
        fourth_steps,
        whole=True,
    )
    output = (middle + mlp_out.astype(f32) + bias_down).astype(bf16)
    ffn_sum = second_half(ffn_kept, ffn_got)
    out_kept, out_passed = first_half(out_term, out_got)
    key_lin_grad = rotate(own_grad[:, :HD], places, 1, -1.0)
    kv_grad_low = jnp.concatenate([key_lin_grad, own_grad[:, HD:]], axis=1).astype(bf16)
    query_lin_grad = (rotate(query_grad_raw, places, heads, -1.0) * scale_factor).astype(bf16)
    normed_grad = both_cores(6, dot(query_lin_grad, query_full, 1, 1).astype(bf16)) + dot(
        kv_grad_low, kv_full, 1, 1
    )
    _, norm_one_pull = jax.vjp(normalize, stream, gain_one)
    stream_part, gain_one_grad = norm_one_pull(normed_grad)
    input_grad = middle_grad + stream_part
    query_term = dot(normed, query_lin_grad, 0, 0).astype(bf16)
    query_term = split(query_term, 0, RING, groups).reshape(LINE, 4, rows, heads * HD)

    def take_core(full):
        blocks = full.reshape(full.shape[0], groups, RING, 2, -1)
        mine = lax.dynamic_index_in_dim(blocks, t, 3, keepdims=False)
        return jnp.transpose(mine, (2, 0, 1, 3)).reshape(RING, full.shape[0], -1)

    kv_term = dot(normed, kv_grad_low, 0, 0)
    kv_term = jnp.moveaxis(take_core(kv_term.T), 1, 2)
    vector_terms = take_core(
        jnp.stack(
            [gain_one_grad, jnp.sum(middle_grad, axis=0), gain_two_grad, jnp.sum(cot_full, axis=0)]
        )
    )
    bias_pair = jnp.where(
        t == 0,
        jnp.stack([hidden_bias_part, bias_theirs]),
        jnp.stack([bias_theirs, hidden_bias_part]),
    )[:, :2, :hidden_block].astype(f32)
    bias_terms = lax.dynamic_update_slice_in_dim(
        jnp.zeros((2, 2, LINE, hidden_block), f32),
        jnp.swapaxes(bias_pair, 0, 1)[:, :, None],
        z,
        2,
    ).reshape(2, -1)
    bias_terms = take_core(bias_terms)

    def widen(x):
        return jnp.pad(x, ((0, 0), (0, 0), (0, columns - x.shape[2])))

    kv_term = jnp.concatenate(
        [kv_term, widen(vector_terms), widen(bias_terms), jnp.zeros((RING, 10, columns), f32)],
        axis=1,
    ).astype(bf16)
    kv_term = kv_term.reshape(LINE, 4, kv_rows + 16, columns)

    def fifth_steps(me, ins, outs, sems):
        return [
            line_exchange(me, lambda z: ins[0].at[:, z], outs[0], sems[0]),
            plane_second(me, ins[1], outs[1], sems[1]),
            plane_first(me, ins[2], outs[2], sems[2]),
            plane_first(me, ins[3], outs[3], sems[3]),
        ]

    ffn_done, out_got, query_got, kv_got = transfer(
        7,
        [ffn_sum, out_passed, query_term, kv_term],
        [
            ((LINE, 3, rows, hidden_pad), bf16),
            (out_passed.shape, bf16),
            (first_shape(query_term), bf16),
            (first_shape(kv_term), bf16),
        ],
        [LINE_SEMS, PLANE_SEMS, PLANE_SEMS, PLANE_SEMS],
        fifth_steps,
    )
    out_sum = second_half(out_kept, out_got)
    query_kept, query_passed = first_half(query_term, query_got)
    kv_kept, kv_passed = first_half(kv_term, kv_got)

    def sixth_steps(me, ins, outs, sems):
        return [
            line_exchange(me, lambda z: ins[0].at[z], outs[0], sems[0]),
            plane_second(me, ins[1], outs[1], sems[1]),
            plane_second(me, ins[2], outs[2], sems[2]),
        ]

    out_done, query_got, kv_got = transfer(
        8,
        [out_sum, query_passed, kv_passed],
        [(out_sum.shape, bf16), (query_passed.shape, bf16), (kv_passed.shape, bf16)],
        [LINE_SEMS, PLANE_SEMS, PLANE_SEMS],
        sixth_steps,
    )
    query_sum = second_half(query_kept, query_got)
    kv_sum = second_half(kv_kept, kv_got)

    def last_steps(me, ins, outs, sems):
        return [
            line_exchange(me, lambda z: ins[0].at[z], outs[0], sems[0]),
            line_exchange(me, lambda z: ins[1].at[z], outs[1], sems[1]),
        ]

    query_done, kv_done = transfer(
        9,
        [query_sum, kv_sum],
        [(query_sum.shape, bf16), (kv_sum.shape, bf16)],
        [LINE_SEMS, LINE_SEMS],
        last_steps,
    )

    ffn_grad = jnp.transpose(ffn_done[..., :hidden_block], (1, 2, 0, 3)).reshape(
        3, rows, hidden_half
    )
    ffn_grad = shrink(ffn_grad.astype(f32), 1, groups)
    out_grad = shrink(jnp.sum(out_done.astype(f32), axis=0), 0, groups).T
    query_grad = shrink(jnp.sum(query_done.astype(f32), axis=0), 0, groups)
    kv_sums = jnp.sum(kv_done.astype(f32), axis=0)
    key_value_grad = shrink(kv_sums[:kv_rows], 0, groups)
    small_grads = [shrink(kv_sums[kv_rows + i, :kv_rows], 0, groups) for i in range(4)]
    gate_up_bias_grad = shrink(
        kv_sums[kv_rows + 4 : kv_rows + 6, : hidden_bias.shape[1]], 1, groups
    )
    return (
        output,
        input_grad,
        small_grads[0],
        query_grad,
        key_value_grad,
        out_grad,
        small_grads[1],
        small_grads[2],
        ffn_grad[:2],
        gate_up_bias_grad,
        ffn_grad[2].T,
        small_grads[3],
    )


def solution(mesh):
    in_specs = (
        P("seq", None),
        P("seq"),
        P("seq", None),
        P(("seq", "tensor")),
        P("seq", "tensor"),
        P(("seq", "tensor"), None),
        P("tensor", "seq"),
        P(("seq", "tensor")),
        P(("seq", "tensor")),
        P(None, "seq", "tensor"),
        P(None, ("seq", "tensor")),
        P("tensor", "seq"),
        P(("seq", "tensor")),
    )
    out_specs = (
        P("seq", None),
        P("seq", None),
        P(("seq", "tensor")),
        P("seq", "tensor"),
        P(("seq", "tensor"), None),
        P("tensor", "seq"),
        P(("seq", "tensor")),
        P(("seq", "tensor")),
        P(None, "seq", "tensor"),
        P(None, ("seq", "tensor")),
        P("tensor", "seq"),
        P(("seq", "tensor")),
    )
    return jax.shard_map(body, mesh=mesh, in_specs=in_specs, out_specs=out_specs, check_vma=False)
```

```python
import functools

import jax
import jax.numpy as jnp
from jax import lax
from jax.experimental import pallas as pl
from jax.experimental.pallas import tpu as pltpu
from jax.sharding import PartitionSpec as P

HD = 256
W = 2048
SEQ_LEN = 4096
LINE = 4
RING = 16
LANES = 128

epsilon = 1e-06
bf16 = jnp.bfloat16
f32 = jnp.float32
MESH = pl.DeviceIdType.MESH
ANY = pl.BlockSpec(memory_space=pl.ANY)


class Place:
    def __init__(self):
        seq = lax.axis_index("seq")
        self.t = lax.axis_index("tensor")
        self.r = lax.rem(seq, RING)
        self.base = seq - self.r
        self.z = lax.div(self.r, 4)
        self.q = lax.rem(self.r, 4)
        self.xq = self.q + 1 - 2 * lax.rem(self.q, 2)
        self.yq = self.q + 2 - 4 * lax.div(self.q, 2)
        self.dq = 3 - self.q
        self.half = lax.div(self.z, 2)
        self.inner = self.z + self.half * (3 - 2 * self.z)

    def at(self, z, q):
        return (self.base + 4 * z + q, self.t)

    def other(self):
        return (self.base + self.r, 1 - self.t)

    def order(self, j):
        v = j + self.inner * (1 - 2 * j if j < 2 else 0)
        return v + self.half * (3 - 2 * v)

    def greet(self, whole=False):
        barrier = pltpu.get_barrier_semaphore()
        if whole:
            peers = [
                (self.base + lax.rem(self.r + k, RING), self.t) for k in range(1, RING)
            ]
        else:
            peers = [self.at(lax.rem(self.z + k, 4), self.q) for k in range(1, 4)]
            peers += [self.at(self.z, self.xq), self.at(self.z, self.yq)]
        peers.append(self.other())
        for peer in peers:
            pl.semaphore_signal(barrier, inc=1, device_id=peer, device_id_type=MESH)
        pl.semaphore_wait(barrier, len(peers))


def remote(src, dst, send, recv, device):
    return pltpu.make_async_remote_copy(
        src_ref=src, dst_ref=dst, send_sem=send, recv_sem=recv, device_id=device, device_id_type=MESH
    )


def run(steps):
    steps, ending = list(steps), []
    while steps:
        for step in list(steps):
            if next(step, True):
                steps.remove(step)
                ending.append(step)
    for step in ending:
        next(step, None)


GATHER_SEMS = [
    pltpu.SemaphoreType.DMA((4, 6)),
    pltpu.SemaphoreType.DMA((4, 5)),
    pltpu.SemaphoreType.DMA,
]


def gather(me, own, slot, part, sems, pieces=None):
    snd, rcv, loc = sems
    local = pltpu.make_async_copy(own, slot(me.z, me.q), loc)
    local.start()

    def line(z, k, src, to):
        return remote(src, slot(z, me.q), snd.at[z, k], rcv.at[z, 0], me.at(to, me.q))

    def across(z, k, src):
        q = (me.xq, me.yq)[k]
        return remote(src, slot(z, me.q), snd.at[z, 2 + k], rcv.at[z, 1 + k], me.at(me.z, q))

    def corner(z, k):
        src = part(z, (me.xq, me.yq)[k], k)
        return remote(src, src, snd.at[z, 4 + k], rcv.at[z, 3 + k], me.at(me.z, (me.yq, me.xq)[k]))

    if pieces is None:

        @pl.when(me.z < 3)
        def _():
            line(me.z, 0, own, me.z + 1).start()

        @pl.when(me.z > 0)
        def _():
            line(me.z, 1, own, me.z - 1).start()

    else:
        for j in range(1, 4):
            z = me.order(j)
            remote(
                pieces(z), slot(me.z, me.q), snd.at[z, 0], rcv.at[me.z, 0], me.at(z, me.q)
            ).start()
    for k in range(2):
        across(me.z, k, own).start()
    yield
    for j in range(1, 5):
        if j < 4:
            z = me.order(j)
            remote(
                slot(z, me.q), slot(z, me.q), snd.at[z, 0], rcv.at[z, 0], me.at(me.z, me.q)
            ).wait_recv()
            if pieces is None:

                @pl.when(me.inner == 1)
                def _():
                    step = 3 - 2 * me.z if j == 1 else 2 * me.z - 3
                    line(z, 0, slot(z, me.q), me.z + step).start()

            for k in range(2):
                across(z, k, slot(z, me.q)).start()
        z = me.order(j - 1)
        for k in range(2):
            q = (me.xq, me.yq)[k]
            remote(
                slot(z, q), slot(z, q), snd.at[z, 2 + k], rcv.at[z, 1 + k], me.at(me.z, q)
            ).wait_recv()
            corner(z, k).start()
        yield
    yield True
    for j in range(4):
        z = me.order(j)
        for k in range(2):
            src = part(z, me.dq, k)
            remote(src, src, snd.at[z, 4 + k], rcv.at[z, 3 + k], me.at(me.z, me.xq)).wait_recv()
    local.wait()
    for j in range(4):
        z = me.order(j)
        for k in range(2):
            across(z, k, slot(z, me.q)).wait_send()
            corner(z, k).wait_send()
    if pieces is None:

        @pl.when(me.z < 3)
        def _():
            line(me.z, 0, own, me.z + 1).wait_send()

        @pl.when(me.z > 0)
        def _():
            line(me.z, 1, own, me.z - 1).wait_send()

        @pl.when(me.inner == 1)
        def _():
            for j in range(1, 4):
                z = me.order(j)
                line(z, 0, slot(z, me.q), me.z).wait_send()

    else:
        for j in range(1, 4):
            z = me.order(j)
            remote(pieces(z), pieces(z), snd.at[z, 0], rcv.at[z, 0], me.at(z, me.q)).wait_send()


SPREAD_SEMS = [
    pltpu.SemaphoreType.DMA((4, 3)),
    pltpu.SemaphoreType.DMA((4, 2)),
    pltpu.SemaphoreType.DMA,
]


def spread(me, src, dst, sems):
    snd, rcv, loc = sems
    rows = src.shape[0] // 2
    mine = pl.ds(pl.multiple_of(me.t * rows, rows), rows)
    local = pltpu.make_async_copy(src, dst.at[me.z], loc)
    local.start()

    def slot(z):
        return dst.at[z, mine]

    def line(z, k, source, to):
        return remote(source, slot(z), snd.at[z, k], rcv.at[z, 0], me.at(to, me.q))

    def share(z):
        return remote(slot(z), slot(z), snd.at[z, 2], rcv.at[z, 1], me.other())

    @pl.when(me.z < 3)
    def _():
        line(me.z, 0, src.at[mine], me.z + 1).start()

    @pl.when(me.z > 0)
    def _():
        line(me.z, 1, src.at[mine], me.z - 1).start()

    yield
    for j in range(1, 4):
        z = me.order(j)
        line(z, 0, slot(z), me.z).wait_recv()

        @pl.when(me.inner == 1)
        def _():
            step = 3 - 2 * me.z if j == 1 else 2 * me.z - 3
            line(z, 0, slot(z), me.z + step).start()

        share(z).start()
        yield
    yield True
    other = pl.ds(pl.multiple_of((1 - me.t) * rows, rows), rows)
    for j in range(1, 4):
        z = me.order(j)
        remote(
            dst.at[z, other], dst.at[z, other], snd.at[z, 2], rcv.at[z, 1], me.other()
        ).wait_recv()
        share(z).wait_send()
    local.wait()

    @pl.when(me.z < 3)
    def _():
        line(me.z, 0, src.at[mine], me.z + 1).wait_send()

    @pl.when(me.z > 0)
    def _():
        line(me.z, 1, src.at[mine], me.z - 1).wait_send()

    @pl.when(me.inner == 1)
    def _():
        for j in range(1, 4):
            z = me.order(j)
            line(z, 0, slot(z), me.z).wait_send()


def swap(me, src, dst, sems):
    copy = remote(src, dst, sems[0], sems[1], me.other())
    copy.start()
    yield True
    copy.wait()


SWAP_SEMS = [pltpu.SemaphoreType.DMA, pltpu.SemaphoreType.DMA]


def add_rows(out, terms):
    rows = out.shape[0]
    step = 16

    @pl.loop(0, rows // step)
    def _(i):
        at = pl.ds(pl.multiple_of(i * step, step), step)
        total = terms[0][at].astype(f32)
        for term in terms[1:]:
            total += term[at].astype(f32)
        out[at] = total.astype(out.dtype)


def reduce_scratch(slots, rows, columns, dtype):
    return [
        pltpu.VMEM((slots, rows, columns), bf16),
        pltpu.VMEM((slots, rows, columns), bf16),
        pltpu.VMEM((slots, rows, columns), bf16),
        pltpu.VMEM((rows, columns), dtype),
        pltpu.SemaphoreType.DMA((slots, 3)),
        pltpu.SemaphoreType.DMA((slots, 2)),
        pltpu.SemaphoreType.DMA((3,)),
    ]


def chain_scratch(rows, columns):
    return [
        pltpu.VMEM((LINE, rows, columns), bf16),
        pltpu.VMEM((LINE, rows, columns), bf16),
        pltpu.VMEM((2, 3, rows, columns), bf16),
        pltpu.SemaphoreType.DMA((LINE, 2)),
        pltpu.SemaphoreType.DMA((LINE,)),
        pltpu.SemaphoreType.DMA((2, 3)),
        pltpu.SemaphoreType.DMA((2, 3)),
        pltpu.SemaphoreType.DMA((3,)),
    ]


def reduce_line(me, src, out, scratch):
    here, there, landed, snd, rcv, line_snd, line_rcv, end = scratch
    rows = here.shape[1]
    mine = pl.ds(pl.multiple_of(me.t * rows, rows), rows)
    theirs = pl.ds(pl.multiple_of((1 - me.t) * rows, rows), rows)
    order = (3, 0, 2, 1)

    def cross(z):
        return remote(src.at[z, theirs], there.at[z], snd.at[z, 0], rcv.at[z], me.other())

    def local(z):
        return pltpu.make_async_copy(src.at[z, mine], here.at[z], snd.at[z, 1])

    def send(way, k, source):
        to = me.z + 1 - 2 * way
        return remote(
            source, landed.at[way, k], line_snd.at[way, k], line_rcv.at[way, k], me.at(to, me.q)
        )

    for z in order:
        cross(z).start()
        local(z).start()
    yield
    for z in order:
        local(z).wait()
        cross(z).wait_recv()
        add_rows(here.at[z], (here.at[z], there.at[z]))
    for k in range(3):
        for way in range(2):
            w = me.z if way == 0 else 3 - me.z
            block = 3 + w - k if way == 0 else k - w

            @pl.when(w <= k)
            def _():
                if k:

                    @pl.when(w < k)
                    def _():
                        send(way, k - 1, here.at[0]).wait_send()

                @pl.when(w == 0)
                def _():
                    send(way, k, here.at[block]).start()

                if k:

                    @pl.when(w > 0)
                    def _():
                        partial = landed.at[way, k - 1]
                        send(way, k - 1, partial).wait_recv()
                        add_rows(partial, (partial, here.at[block]))
                        send(way, k, partial).start()

        yield
    for way in range(2):
        w = me.z if way == 0 else 3 - me.z

        @pl.when(w > 0)
        def _():
            send(way, 2, landed.at[way, 2]).wait_recv()
            add_rows(here.at[me.z], (here.at[me.z], landed.at[way, 2]))

        @pl.when(w < 3)
        def _():
            send(way, 2, here.at[0]).wait_send()

    keep = pltpu.make_async_copy(here.at[me.z], out.at[mine], end.at[0])
    give = remote(here.at[me.z], out.at[mine], end.at[1], end.at[2], me.other())
    keep.start()
    give.start()
    yield True
    for z in range(LINE):
        cross(z).wait_send()
    keep.wait()
    give.wait()


def reduce_window(me, reach, src, out, scratch):
    here, there, landed, total, snd, rcv, end = scratch
    rows = here.shape[1]
    slots = reach + 1
    mine = pl.ds(pl.multiple_of(me.t * rows, rows), rows)
    theirs = pl.ds(pl.multiple_of((1 - me.t) * rows, rows), rows)
    start = jnp.maximum(me.r - reach, 0)

    def cross(j):
        return remote(src.at[j, theirs], there.at[j], snd.at[j, 0], rcv.at[j, 0], me.other())

    def local(j):
        return pltpu.make_async_copy(src.at[j, mine], here.at[j], snd.at[j, 1])

    def back(k):
        j = me.r - k - start
        return remote(
            here.at[j], landed.at[k], snd.at[k, 2], rcv.at[k, 1], (me.base + me.r - k, me.t)
        )

    for j in range(slots):
        cross(j).start()
        local(j).start()
    yield
    for j in range(slots):
        local(j).wait()
        cross(j).wait_recv()
        add_rows(here.at[j], (here.at[j], there.at[j]))
    for k in range(reach, 0, -1):

        @pl.when(me.r >= k)
        def _():
            back(k).start()

    yield
    add_rows(total, [here.at[me.r - start]])
    for k in range(1, slots):

        @pl.when(me.r + k < RING)
        def _():
            remote(
                landed.at[k], landed.at[k], snd.at[k, 2], rcv.at[k, 1], me.at(me.z, me.q)
            ).wait_recv()
            add_rows(total, (total, landed.at[k]))

    keep = pltpu.make_async_copy(total, out.at[mine], end.at[0])
    give = remote(total, out.at[mine], end.at[1], end.at[2], me.other())
    keep.start()
    give.start()
    yield True
    for j in range(slots):
        cross(j).wait_send()
    for k in range(1, slots):

        @pl.when(me.r >= k)
        def _():
            back(k).wait_send()

    keep.wait()
    give.wait()


PLANE_SEMS = [pltpu.SemaphoreType.DMA((4,)), pltpu.SemaphoreType.DMA((4,))]


def plane_first(me, src, got, sems):
    snd, rcv = sems
    rows = src.shape[-2] // 2
    copies = []
    lead = (slice(None),) * (len(src.shape) - 3)
    for h in range(2):
        q = (me.xq, me.yq)[h]
        for i in range(2):
            place = (q, me.dq)[i]
            n = 2 * h + i
            view = src.at[lead + (place, pl.ds(h * rows, rows))]
            copies.append(remote(view, got.at[h, i], snd.at[n], rcv.at[n], me.at(me.z, q)))
    for copy in copies:
        copy.start()
    yield True
    for copy in copies:
        copy.wait()


def plane_sums_scratch(shape):
    parts, line, _, rows, columns = shape
    block = (parts, 2, 2, line, rows // 2, columns)
    return [
        pltpu.VMEM(block, bf16),
        pltpu.VMEM(block, bf16),
        pltpu.SemaphoreType.DMA((parts, 4)),
        pltpu.SemaphoreType.DMA((parts, 4)),
        pltpu.SemaphoreType.DMA((parts, 4)),
        pltpu.SemaphoreType.DMA((parts, 4)),
    ]


def plane_sums(me, order, src, kept, passed, scratch):
    here, there, loc, snd, rcv, end = scratch
    half = src.shape[3] // 2

    def view(part, place, h):
        return src.at[part, :, place, pl.ds(h * half, half)]

    def sends(part):
        for h in range(2):
            q = (me.xq, me.yq)[h]
            for i in range(2):
                n = 2 * h + i
                yield remote(
                    view(part, (q, me.dq)[i], h),
                    there.at[part, h, i],
                    snd.at[part, n],
                    rcv.at[part, n],
                    me.at(me.z, q),
                )

    def loads(part):
        for h in range(2):
            for i in range(2):
                place = (me.q, (me.yq, me.xq)[h])[i]
                yield pltpu.make_async_copy(
                    view(part, place, h), here.at[part, h, i], loc.at[part, 2 * h + i]
                )

    def stores(part):
        for h in range(2):
            for i in range(2):
                yield pltpu.make_async_copy(
                    here.at[part, h, i], (kept, passed)[i].at[h, part], end.at[part, 2 * h + i]
                )

    for part in order:
        for copy in sends(part):
            copy.start()
        for copy in loads(part):
            copy.start()
    yield
    for part in order:
        yield
        for copy in loads(part):
            copy.wait()
        for copy in sends(part):
            copy.wait_recv()
        for h in range(2):
            for i in range(2):
                for z in range(here.shape[3]):
                    block = here.at[part, h, i, z]
                    add_rows(block, (block, there.at[part, h, i, z]))
        for copy in stores(part):
            copy.start()
    yield True
    for part in order:
        for copy in sends(part):
            copy.wait_send()
        for copy in stores(part):
            copy.wait()


def plane_second(me, src, got, sems):
    snd, rcv = sems
    copies = [
        remote(src.at[h], got.at[h], snd.at[h], rcv.at[h], me.at(me.z, (me.yq, me.xq)[h]))
        for h in range(2)
    ]
    for copy in copies:
        copy.start()
    yield True
    for copy in copies:
        copy.wait()


LINE_SEMS = [pltpu.SemaphoreType.DMA((4,)), pltpu.SemaphoreType.DMA((4,)), pltpu.SemaphoreType.DMA]


def line_exchange(me, piece, got, sems):
    snd, rcv, loc = sems
    local = pltpu.make_async_copy(piece(me.z), got.at[me.z], loc)
    local.start()

    def send(j):
        z = me.order(j)
        return remote(piece(z), got.at[me.z], snd.at[z], rcv.at[me.z], me.at(z, me.q))

    for j in (3, 2, 1):
        send(j).start()
    yield True
    for j in range(1, 4):
        z = me.order(j)
        remote(got.at[z], got.at[z], snd.at[z], rcv.at[z], me.at(z, me.q)).wait_recv()
    for j in range(1, 4):
        send(j).wait_send()
    local.wait()


def transfer(number, inputs, outputs, scratch, steps, whole=False):
    flat = [item for group in scratch for item in group]
    sizes = [len(group) for group in scratch]

    def kernel(*refs):
        ins = refs[: len(inputs)]
        outs = refs[len(inputs) : len(inputs) + len(outputs)]
        rest = refs[len(inputs) + len(outputs) :]
        groups = []
        for size in sizes:
            groups.append(rest[:size])
            rest = rest[size:]
        me = Place()
        me.greet(whole)
        run(steps(me, ins, outs, groups))

    return pl.pallas_call(
        kernel,
        out_shape=[jax.ShapeDtypeStruct(shape, dtype) for shape, dtype in outputs],
        in_specs=[ANY] * len(inputs),
        out_specs=[ANY] * len(outputs),
        scratch_shapes=flat,
        compiler_params=pltpu.CompilerParams(
            collective_id=number, has_side_effects=True, vmem_limit_bytes=48 * 2**20
        ),
    )(*inputs)


def gather_rows(me, src, dst, sems):
    half = src.shape[0] // 2
    return gather(
        me,
        src,
        lambda z, q: dst.at[4 * z + q],
        lambda z, q, h: dst.at[4 * z + q, pl.ds(h * half, half)],
        sems,
    )


def gather_pieces(me, src, dst, sems):
    half = src.shape[1] // 2
    width = dst.shape[-1]

    def piece(z):
        return src.at[:, :, pl.ds(pl.multiple_of(z * width, width), width)]

    return gather(
        me,
        piece(me.z),
        lambda z, q: dst.at[:, 4 * z + q],
        lambda z, q, h: dst.at[:, 4 * z + q, pl.ds(h * half, half)],
        sems,
        piece,
    )


def group_lists(groups):
    return [[r + RING * g for g in range(groups)] for r in range(RING)]


def grow(x, axis, groups):
    if groups == 1:
        return x
    return lax.all_gather(x, "seq", axis=axis, tiled=True, axis_index_groups=group_lists(groups))


def shrink(x, axis, groups):
    if groups == 1:
        return x
    return lax.psum_scatter(
        x, "seq", scatter_dimension=axis, tiled=True, axis_index_groups=group_lists(groups)
    )


def merge(blocks, axis, groups):
    shape = blocks.shape
    rows = shape[axis + 1]
    if groups > 1:
        blocks = blocks.reshape(shape[: axis + 1] + (groups, rows // groups) + shape[axis + 2 :])
        blocks = jnp.moveaxis(blocks, axis + 1, axis)
    return blocks.reshape(shape[:axis] + (shape[axis] * rows,) + shape[axis + 2 :])


def split(full, axis, places, groups):
    shape = full.shape
    rows = shape[axis] // (places * groups)
    blocks = full.reshape(shape[:axis] + (groups, places, rows) + shape[axis + 1 :])
    if groups > 1:
        blocks = jnp.moveaxis(blocks, axis, axis + 1)
    return blocks.reshape(shape[:axis] + (places, groups * rows) + shape[axis + 1 :])


def normalize(stream, scale_vec):
    return (
        stream * lax.rsqrt(jnp.mean(stream * stream, axis=-1, keepdims=True) + epsilon) * scale_vec
    )


def rotate(values, places, head_count, direction):
    head_size = values.shape[1] // head_count
    shaped = values.reshape(values.shape[0], head_count, head_size)
    quarter = head_size // 4
    first_part = shaped[..., :quarter]
    second = shaped[..., quarter : 2 * quarter]
    remainder = shaped[..., 2 * quarter :]
    frequency = 10000.0 ** (-jnp.arange(quarter, dtype=jnp.float32) / quarter)
    angles = places.astype(jnp.float32)[:, None] * frequency[None, :]
    cosine = jnp.cos(angles)[:, None, :]
    sine_part = direction * jnp.sin(angles)[:, None, :]
    turned = jnp.concatenate(
        [
            first_part * cosine - second * sine_part,
            second * cosine + first_part * sine_part,
            remainder,
        ],
        axis=-1,
    )
    return turned.reshape(values.shape)


def dot(a, b, ca=1, cb=0):
    return lax.dot_general(a, b, (((ca,), (cb,)), ((), ())), preferred_element_type=f32)


def body(
    inputs,
    segment_ids,
    cotangent,
    attn_gain,
    query_weight,
    key_value_weight,
    out_weight,
    out_bias,
    mlp_gain,
    gate_up_weight,
    gate_up_bias,
    down_weight,
    down_bias,
):
    seq_index = lax.axis_index("seq")
    t = lax.axis_index("tensor")
    r = seq_index % RING
    z = r // 4
    q = r % 4
    groups = lax.axis_size("seq") // RING
    tokens, width = inputs.shape
    heads = query_weight.shape[1] // HD
    hidden_half = gate_up_weight.shape[2]
    hidden_block = hidden_half // LINE
    hidden_pad = -(-hidden_block // LANES) * LANES
    reach = (W + tokens - 2) // tokens
    scale_factor = HD ** (-0.5)
    assert tokens * RING == SEQ_LEN and lax.axis_size("tensor") == 2

    kv_own = grow(key_value_weight, 0, groups)
    kv_rows = kv_own.shape[0]
    vectors = [grow(v, 0, groups) for v in (attn_gain, out_bias, mlp_gain, down_bias)]
    hidden_bias = grow(gate_up_bias, 1, groups)
    marks = jnp.stack([segment_ids // 256, segment_ids % 256]).astype(bf16)
    columns = kv_own.shape[1]

    def pad_to(x, n):
        return jnp.pad(x, ((0, 0), (0, n - x.shape[1])))

    small = jnp.concatenate(
        [
            pad_to(jnp.stack(vectors), columns),
            pad_to(hidden_bias, columns),
            pad_to(marks, columns),
            jnp.zeros((8, columns), bf16),
        ]
    )
    kv_block = jnp.concatenate([kv_own, small])
    query_own = grow(query_weight, 0, groups)
    out_own = grow(out_weight.T, 0, groups)
    ffn_own = grow(jnp.concatenate([gate_up_weight, down_weight.T[None]]), 1, groups)
    ffn_own = jnp.pad(
        ffn_own.reshape(3, -1, LINE, hidden_block),
        ((0, 0), (0, 0), (0, 0), (0, hidden_pad - hidden_block)),
    ).reshape(3, -1, LINE * hidden_pad)
    rows = query_own.shape[0]

    def first_steps(me, ins, outs, sems):
        def both():
            for _ in gather_rows(me, ins[1], outs[1], sems[1]):
                yield
            yield from swap(me, outs[1], outs[2], sems[2])

        return [gather_rows(me, ins[0], outs[0], sems[0]), both()]

    query_full, kv_mine, kv_theirs = transfer(
        0,
        [query_own, kv_block],
        [((RING,) + query_own.shape, bf16)] + [((RING,) + kv_block.shape, bf16)] * 2,
        [GATHER_SEMS, GATHER_SEMS, SWAP_SEMS],
        first_steps,
    )
    query_full = merge(query_full, 0, groups)
    kv_both = jnp.where(
        t == 0, jnp.stack([kv_mine, kv_theirs], 1), jnp.stack([kv_theirs, kv_mine], 1)
    )
    kv_full = merge(
        kv_both[:, :, :kv_rows]
        .reshape(RING, 2, groups, kv_rows // groups, columns)
        .swapaxes(1, 2)
        .reshape(RING, 2 * kv_rows, columns),
        0,
        groups,
    )

    def vector(row, count):
        piece = kv_both[:, :, kv_rows + row, :count].reshape(RING, 2, groups, count // groups)
        return jnp.transpose(piece, (2, 0, 1, 3)).reshape(-1).astype(f32)

    gain_one, bias_out, gain_two, bias_down = (vector(i, kv_rows) for i in range(4))
    bias_gate_up = jnp.stack([vector(4 + i, hidden_bias.shape[1]) for i in range(2)])
    bias_local = lax.dynamic_slice_in_dim(
        bias_gate_up, t * hidden_half + z * hidden_block, hidden_block, 1
    )
    bias_local = pad_to(bias_local, hidden_pad)
    all_marks = kv_both[:, 0, kv_rows + 6 : kv_rows + 8, :tokens].astype(f32)
    all_marks = (all_marks[:, 0] * 256.0 + all_marks[:, 1]).reshape(-1)

    stream = inputs.astype(f32)
    places = r * tokens + jnp.arange(tokens, dtype=jnp.int32)
    normed = normalize(stream, gain_one).astype(bf16)
    query_lin = dot(normed, query_full)
    queries = (rotate(query_lin, places, heads, 1.0) * scale_factor).astype(bf16)
    key_value = dot(normed, kv_full)
    keys_own = rotate(key_value[:, :HD], places, 1, 1.0).astype(bf16)
    values_own = key_value[:, HD:].astype(bf16)
    own_block = jnp.concatenate([keys_own, values_own], axis=1)

    def second_steps(me, ins, outs, sems):
        return [
            gather_rows(me, ins[0], outs[0], sems[0]),
            gather_rows(me, ins[1], outs[1], sems[1]),
            gather_pieces(me, ins[2], outs[2], sems[2]),
            spread(me, ins[3], outs[3], sems[3]),
        ]

    kv_all, out_full, ffn_full, cot_all = transfer(
        1,
        [own_block, out_own, ffn_own, cotangent],
        [
            ((RING,) + own_block.shape, bf16),
            ((RING,) + out_own.shape, bf16),
            ((3, RING, rows, hidden_pad), bf16),
            ((LINE,) + cotangent.shape, bf16),
        ],
        [GATHER_SEMS, GATHER_SEMS, GATHER_SEMS, SPREAD_SEMS],
        second_steps,
    )
    out_full = merge(out_full, 0, groups)
    ffn_full = merge(ffn_full, 1, groups)
    cot_all = cot_all.reshape(LINE * tokens, width)

    first_block = jnp.maximum(r - reach, 0)
    span = (reach + 1) * tokens
    window = lax.dynamic_slice_in_dim(
        kv_all.reshape(RING * tokens, 2 * HD), first_block * tokens, span, 0
    )
    window_marks = lax.dynamic_slice_in_dim(all_marks, first_block * tokens, span, 0)
    own_marks = lax.dynamic_slice_in_dim(all_marks, r * tokens, tokens, 0)
    key_places = first_block * tokens + jnp.arange(span, dtype=jnp.int32)
    key_gap = places[:, None] - key_places[None, :]
    visible = (key_gap >= 0) & (key_gap < W) & (own_marks[:, None] == window_marks[None, :])
    key_win = window[:, :HD]
    value_win = window[:, HD:]
    query_heads = queries.reshape(tokens, heads, HD)
    scores = jnp.einsum("qhd,kd->hqk", query_heads, key_win, preferred_element_type=f32)
    scores = jnp.where(visible[None], scores, -1e30)
    row_top = jnp.max(scores, axis=-1, keepdims=True)
    exponent = jnp.exp(scores - row_top)
    row_total = jnp.sum(exponent, axis=-1, keepdims=True)
    log_total = row_top + jnp.log(row_total)
    probs_low = (exponent / row_total).astype(bf16)
    mixed_low = (
        jnp.einsum("hqk,kd->qhd", probs_low, value_win, preferred_element_type=f32)
        .reshape(tokens, heads * HD)
        .astype(bf16)
    )

    def both_cores(number, part):
        (theirs,) = transfer(
            number,
            [part],
            [(part.shape, bf16)],
            [SWAP_SEMS],
            lambda me, ins, outs, sems: [swap(me, ins[0], outs[0], sems[0])],
        )
        return part.astype(f32) + theirs.astype(f32)

    branch = both_cores(2, dot(mixed_low, out_full, 1, 1).astype(bf16))
    middle = stream + branch + bias_out
    normed_two = normalize(middle, gain_two).astype(bf16)

    (normed_all,) = transfer(
        3,
        [normed_two],
        [((LINE,) + normed_two.shape, bf16)],
        [SPREAD_SEMS],
        lambda me, ins, outs, sems: [spread(me, ins[0], outs[0], sems[0])],
    )
    normed_all = normed_all.reshape(LINE * tokens, width)
    gate_pre = dot(normed_all, ffn_full[0]) + bias_local[0]
    up_pre = dot(normed_all, ffn_full[1]) + bias_local[1]
    hidden = (jax.nn.gelu(gate_pre, approximate=True) * up_pre).astype(bf16)
    mlp_part = dot(hidden, ffn_full[2], 1, 1).astype(bf16)
    hidden_grad = dot(cot_all, ffn_full[2])
    _, unit_pull = jax.vjp(
        lambda gate_in, up_in: jax.nn.gelu(gate_in, approximate=True) * up_in, gate_pre, up_pre
    )
    gate_grad, up_grad = unit_pull(hidden_grad)
    gate_low = gate_grad.astype(bf16)
    up_low = up_grad.astype(bf16)
    ffn_term = jnp.stack(
        [
            dot(normed_all, gate_low, 0, 0).astype(bf16),
            dot(normed_all, up_low, 0, 0).astype(bf16),
            dot(cot_all, hidden, 0, 0).astype(bf16),
        ]
    )
    ffn_term = split(ffn_term, 1, RING, groups).reshape(3, LINE, 4, rows, hidden_pad)
    normed_two_part = (dot(gate_low, ffn_full[0], 1, 1) + dot(up_low, ffn_full[1], 1, 1)).astype(
        bf16
    )
    hidden_bias_part = jnp.stack(
        [jnp.sum(gate_low.astype(f32), axis=0), jnp.sum(up_low.astype(f32), axis=0)]
    )
    hidden_bias_part = jnp.pad(hidden_bias_part, ((0, 14), (0, 0))).astype(bf16)

    def first_half(src, got):
        lead = src.ndim - 3
        half = rows_of(src)
        xq, yq = q + 1 - 2 * (q % 2), q + 2 - 4 * (q // 2)

        def own(place, h):
            piece = lax.dynamic_index_in_dim(src, place, lead, keepdims=False)
            return lax.slice_in_dim(piece, h * half, (h + 1) * half, axis=lead).astype(f32)

        kept = [own(q, h) + got[h, 0].astype(f32) for h in range(2)]
        passed = jnp.stack(
            [
                (own(yq, 0) + got[0, 1].astype(f32)).astype(bf16),
                (own(xq, 1) + got[1, 1].astype(f32)).astype(bf16),
            ]
        )
        return kept, passed

    def rows_of(src):
        return src.shape[-2] // 2

    def second_half(kept, got):
        return jnp.concatenate(
            [kept[h].astype(f32) + got[h].astype(f32) for h in range(2)], axis=-2
        ).astype(bf16)

    def first_shape(src):
        s = src.shape
        return (2, 2) + s[:-3] + (s[-2] // 2, s[-1])

    def third_steps(me, ins, outs, sems):
        yield from ()
        one = reduce_line(me, ins[0], outs[0], sems[0])
        two = reduce_line(me, ins[1], outs[1], sems[1])
        three = plane_sums(me, (2, 0, 1), ins[2], outs[2], outs[3], sems[2])
        next(one)
        next(three)
        ends = [swap(me, ins[3], outs[4], sems[3])]
        next(ends[0])
        next(two)
        for _ in range(4):
            next(one)
        next(three)
        for _ in range(3):
            next(two)
            next(three)
        next(two)
        for step in [one, two, three] + ends:
            next(step, None)

    kept_shape = (2, 3, LINE, rows // 2, hidden_pad)
    normed_two_grad, mlp_out, ffn_kept, ffn_passed, bias_theirs = transfer(
        4,
        [
            normed_two_part.reshape(LINE, tokens, width),
            mlp_part.reshape(LINE, tokens, width),
            ffn_term,
            hidden_bias_part,
        ],
        [
            ((tokens, width), bf16),
            ((tokens, width), bf16),
            (kept_shape, bf16),
            (kept_shape, bf16),
            (hidden_bias_part.shape, bf16),
        ],
        [
            chain_scratch(tokens // 2, width),
            chain_scratch(tokens // 2, width),
            plane_sums_scratch(ffn_term.shape),
            SWAP_SEMS,
        ],
        third_steps,
    )
    cot_full = cotangent.astype(f32)
    _, norm_two_pull = jax.vjp(normalize, middle, gain_two)
    middle_part, gain_two_grad = norm_two_pull(normed_two_grad.astype(f32))
    middle_grad = cot_full + middle_part
    middle_low = middle_grad.astype(bf16)
    out_term = dot(middle_low, mixed_low, 0, 0).astype(bf16)
    out_term = split(out_term, 0, RING, groups).reshape(LINE, 4, rows, heads * HD)
    mixed_grad = dot(middle_low, out_full).astype(bf16).reshape(tokens, heads, HD)

    scores_again = jnp.einsum("qhd,kd->hqk", query_heads, key_win, preferred_element_type=f32)
    probs_again = jnp.where(visible[None], jnp.exp(scores_again - log_total), 0.0)
    probs_again_low = probs_again.astype(bf16)
    prob_grad = jnp.einsum("qhd,kd->hqk", mixed_grad, value_win, preferred_element_type=f32)
    value_grad = jnp.einsum("hqk,qhd->kd", probs_again_low, mixed_grad, preferred_element_type=f32)
    row_inner = jnp.sum(probs_again * prob_grad, axis=-1, keepdims=True)
    score_grad = (probs_again * (prob_grad - row_inner)).astype(bf16)
    query_grad_raw = jnp.einsum(
        "hqk,kd->qhd", score_grad, key_win, preferred_element_type=f32
    ).reshape(tokens, heads * HD)
    key_grad_raw = jnp.einsum("hqk,qhd->kd", score_grad, query_heads, preferred_element_type=f32)
    window_grad = (
        jnp.concatenate([key_grad_raw, value_grad], axis=1)
        .reshape(reach + 1, tokens, 2 * HD)
        .astype(bf16)
    )

    def fourth_steps(me, ins, outs, sems):
        return [
            reduce_window(me, reach, ins[0], outs[0], sems[0]),
            plane_second(me, ins[1], outs[1], sems[1]),
            plane_first(me, ins[2], outs[2], sems[2]),
        ]

    own_grad, ffn_got, out_got = transfer(
        5,
        [window_grad, ffn_passed, out_term],
        [
            ((tokens, 2 * HD), f32),
            (ffn_passed.shape, bf16),
            (first_shape(out_term), bf16),
        ],
        [
            reduce_scratch(reach + 1, tokens // 2, 2 * HD, f32),
            PLANE_SEMS,
            PLANE_SEMS,
        ],
        fourth_steps,
        whole=True,
    )
    output = (middle + mlp_out.astype(f32) + bias_down).astype(bf16)
    ffn_sum = second_half(ffn_kept, ffn_got)
    out_kept, out_passed = first_half(out_term, out_got)
    key_lin_grad = rotate(own_grad[:, :HD], places, 1, -1.0)
    kv_grad_low = jnp.concatenate([key_lin_grad, own_grad[:, HD:]], axis=1).astype(bf16)
    query_lin_grad = (rotate(query_grad_raw, places, heads, -1.0) * scale_factor).astype(bf16)
    normed_grad = both_cores(6, dot(query_lin_grad, query_full, 1, 1).astype(bf16)) + dot(
        kv_grad_low, kv_full, 1, 1
    )
    _, norm_one_pull = jax.vjp(normalize, stream, gain_one)
    stream_part, gain_one_grad = norm_one_pull(normed_grad)
    input_grad = middle_grad + stream_part
    query_term = dot(normed, query_lin_grad, 0, 0).astype(bf16)
    query_term = split(query_term, 0, RING, groups).reshape(LINE, 4, rows, heads * HD)

    def take_core(full):
        blocks = full.reshape(full.shape[0], groups, RING, 2, -1)
        mine = lax.dynamic_index_in_dim(blocks, t, 3, keepdims=False)
        return jnp.transpose(mine, (2, 0, 1, 3)).reshape(RING, full.shape[0], -1)

    kv_term = dot(normed, kv_grad_low, 0, 0)
    kv_term = jnp.moveaxis(take_core(kv_term.T), 1, 2)
    vector_terms = take_core(
        jnp.stack(
            [gain_one_grad, jnp.sum(middle_grad, axis=0), gain_two_grad, jnp.sum(cot_full, axis=0)]
        )
    )
    bias_pair = jnp.where(
        t == 0,
        jnp.stack([hidden_bias_part, bias_theirs]),
        jnp.stack([bias_theirs, hidden_bias_part]),
    )[:, :2, :hidden_block].astype(f32)
    bias_terms = lax.dynamic_update_slice_in_dim(
        jnp.zeros((2, 2, LINE, hidden_block), f32),
        jnp.swapaxes(bias_pair, 0, 1)[:, :, None],
        z,
        2,
    ).reshape(2, -1)
    bias_terms = take_core(bias_terms)

    def widen(x):
        return jnp.pad(x, ((0, 0), (0, 0), (0, columns - x.shape[2])))

    kv_term = jnp.concatenate(
        [kv_term, widen(vector_terms), widen(bias_terms), jnp.zeros((RING, 10, columns), f32)],
        axis=1,
    ).astype(bf16)
    kv_term = kv_term.reshape(LINE, 4, kv_rows + 16, columns)

    def fifth_steps(me, ins, outs, sems):
        return [
            line_exchange(me, lambda z: ins[0].at[:, z], outs[0], sems[0]),
            plane_second(me, ins[1], outs[1], sems[1]),
            plane_first(me, ins[2], outs[2], sems[2]),
            plane_first(me, ins[3], outs[3], sems[3]),
        ]

    ffn_done, out_got, query_got, kv_got = transfer(
        7,
        [ffn_sum, out_passed, query_term, kv_term],
        [
            ((LINE, 3, rows, hidden_pad), bf16),
            (out_passed.shape, bf16),
            (first_shape(query_term), bf16),
            (first_shape(kv_term), bf16),
        ],
        [LINE_SEMS, PLANE_SEMS, PLANE_SEMS, PLANE_SEMS],
        fifth_steps,
    )
    out_sum = second_half(out_kept, out_got)
    query_kept, query_passed = first_half(query_term, query_got)
    kv_kept, kv_passed = first_half(kv_term, kv_got)

    def sixth_steps(me, ins, outs, sems):
        return [
            line_exchange(me, lambda z: ins[0].at[z], outs[0], sems[0]),
            plane_second(me, ins[1], outs[1], sems[1]),
            plane_second(me, ins[2], outs[2], sems[2]),
        ]

    out_done, query_got, kv_got = transfer(
        8,
        [out_sum, query_passed, kv_passed],
        [(out_sum.shape, bf16), (query_passed.shape, bf16), (kv_passed.shape, bf16)],
        [LINE_SEMS, PLANE_SEMS, PLANE_SEMS],
        sixth_steps,
    )
    query_sum = second_half(query_kept, query_got)
    kv_sum = second_half(kv_kept, kv_got)

    def last_steps(me, ins, outs, sems):
        return [
            line_exchange(me, lambda z: ins[0].at[z], outs[0], sems[0]),
            line_exchange(me, lambda z: ins[1].at[z], outs[1], sems[1]),
        ]

    query_done, kv_done = transfer(
        9,
        [query_sum, kv_sum],
        [(query_sum.shape, bf16), (kv_sum.shape, bf16)],
        [LINE_SEMS, LINE_SEMS],
        last_steps,
    )

    ffn_grad = jnp.transpose(ffn_done[..., :hidden_block], (1, 2, 0, 3)).reshape(
        3, rows, hidden_half
    )
    ffn_grad = shrink(ffn_grad.astype(f32), 1, groups)
    out_grad = shrink(jnp.sum(out_done.astype(f32), axis=0), 0, groups).T
    query_grad = shrink(jnp.sum(query_done.astype(f32), axis=0), 0, groups)
    kv_sums = jnp.sum(kv_done.astype(f32), axis=0)
    key_value_grad = shrink(kv_sums[:kv_rows], 0, groups)
    small_grads = [shrink(kv_sums[kv_rows + i, :kv_rows], 0, groups) for i in range(4)]
    gate_up_bias_grad = shrink(
        kv_sums[kv_rows + 4 : kv_rows + 6, : hidden_bias.shape[1]], 1, groups
    )
    return (
        output,
        input_grad,
        small_grads[0],
        query_grad,
        key_value_grad,
        out_grad,
        small_grads[1],
        small_grads[2],
        ffn_grad[:2],
        gate_up_bias_grad,
        ffn_grad[2].T,
        small_grads[3],
    )


def solution(mesh):
    in_specs = (
        P("seq", None),
        P("seq"),
        P("seq", None),
        P(("seq", "tensor")),
        P("seq", "tensor"),
        P(("seq", "tensor"), None),
        P("tensor", "seq"),
        P(("seq", "tensor")),
        P(("seq", "tensor")),
        P(None, "seq", "tensor"),
        P(None, ("seq", "tensor")),
        P("tensor", "seq"),
        P(("seq", "tensor")),
    )
    out_specs = (
        P("seq", None),
        P("seq", None),
        P(("seq", "tensor")),
        P("seq", "tensor"),
        P(("seq", "tensor"), None),
        P("tensor", "seq"),
        P(("seq", "tensor")),
        P(("seq", "tensor")),
        P(None, "seq", "tensor"),
        P(None, ("seq", "tensor")),
        P("tensor", "seq"),
        P(("seq", "tensor")),
    )
    return jax.shard_map(body, mesh=mesh, in_specs=in_specs, out_specs=out_specs, check_vma=False)
```

```python
import functools

import jax
import jax.numpy as jnp
from jax import lax
from jax.experimental import pallas as pl
from jax.experimental.pallas import tpu as pltpu
from jax.sharding import PartitionSpec as P

HD = 256
W = 2048
SEQ_LEN = 4096
LINE = 4
RING = 16
LANES = 128

epsilon = 1e-06
bf16 = jnp.bfloat16
f32 = jnp.float32
MESH = pl.DeviceIdType.MESH
ANY = pl.BlockSpec(memory_space=pl.ANY)
VMEM = pl.BlockSpec(memory_space=pltpu.VMEM)


class Place:
    def __init__(self):
        seq = lax.axis_index("seq")
        self.t = lax.axis_index("tensor")
        self.r = lax.rem(seq, RING)
        self.base = seq - self.r
        self.z = lax.div(self.r, 4)
        self.q = lax.rem(self.r, 4)
        self.xq = self.q + 1 - 2 * lax.rem(self.q, 2)
        self.yq = self.q + 2 - 4 * lax.div(self.q, 2)
        self.dq = 3 - self.q
        self.half = lax.div(self.z, 2)
        self.inner = self.z + self.half * (3 - 2 * self.z)

    def at(self, z, q):
        return (self.base + 4 * z + q, self.t)

    def other(self):
        return (self.base + self.r, 1 - self.t)

    def order(self, j):
        v = j + self.inner * (1 - 2 * j if j < 2 else 0)
        return v + self.half * (3 - 2 * v)

    def greet(self, whole=False):
        barrier = pltpu.get_barrier_semaphore()
        if whole:
            peers = [
                (self.base + lax.rem(self.r + k, RING), self.t) for k in range(1, RING)
            ]
        else:
            peers = [self.at(lax.rem(self.z + k, 4), self.q) for k in range(1, 4)]
            peers += [self.at(self.z, self.xq), self.at(self.z, self.yq)]
        peers.append(self.other())
        for peer in peers:
            pl.semaphore_signal(barrier, inc=1, device_id=peer, device_id_type=MESH)
        pl.semaphore_wait(barrier, len(peers))


def remote(src, dst, send, recv, device):
    return pltpu.make_async_remote_copy(
        src_ref=src, dst_ref=dst, send_sem=send, recv_sem=recv, device_id=device, device_id_type=MESH
    )


def run(steps):
    steps, ending = list(steps), []
    while steps:
        for step in list(steps):
            if next(step, True):
                steps.remove(step)
                ending.append(step)
    for step in ending:
        next(step, None)


GATHER_SEMS = [
    pltpu.SemaphoreType.DMA((4, 6)),
    pltpu.SemaphoreType.DMA((4, 5)),
    pltpu.SemaphoreType.DMA,
]


def gather(me, own, slot, part, sems):
    snd, rcv, loc = sems
    local = pltpu.make_async_copy(own, slot(me.z, me.q), loc)
    local.start()

    def line(z, k, src, to):
        return remote(src, slot(z, me.q), snd.at[z, k], rcv.at[z, 0], me.at(to, me.q))

    @pl.when(me.z < 3)
    def _():
        line(me.z, 0, own, me.z + 1).start()

    @pl.when(me.z > 0)
    def _():
        line(me.z, 1, own, me.z - 1).start()

    def arrive(j):
        z = me.order(j)
        line(z, 0, slot(z, me.q), me.z).wait_recv()

        @pl.when(me.inner == 1)
        def _():
            step = 3 - 2 * me.z if j == 1 else 2 * me.z - 3
            line(z, 0, slot(z, me.q), me.z + step).start()

    yield from in_plane(me, own, slot, part, snd, rcv, arrive)
    local.wait()

    @pl.when(me.z < 3)
    def _():
        line(me.z, 0, own, me.z + 1).wait_send()

    @pl.when(me.z > 0)
    def _():
        line(me.z, 1, own, me.z - 1).wait_send()

    @pl.when(me.inner == 1)
    def _():
        for j in range(1, 4):
            z = me.order(j)
            line(z, 0, slot(z, me.q), me.z).wait_send()


def in_plane(me, own, slot, part, snd, rcv, arrive):
    def across(z, k, src):
        q = (me.xq, me.yq)[k]
        return remote(src, slot(z, me.q), snd.at[z, 2 + k], rcv.at[z, 1 + k], me.at(me.z, q))

    def corner(z, k):
        src = part(z, (me.xq, me.yq)[k], k)
        if src is None:
            return None
        return remote(src, src, snd.at[z, 4 + k], rcv.at[z, 3 + k], me.at(me.z, (me.yq, me.xq)[k]))

    for k in range(2):
        across(me.z, k, own).start()
    yield
    for j in range(1, 5):
        if j < 4:
            arrive(j)
            z = me.order(j)
            for k in range(2):
                across(z, k, slot(z, me.q)).start()
        z = me.order(j - 1)
        for k in range(2):
            q = (me.xq, me.yq)[k]
            remote(
                slot(z, q), slot(z, q), snd.at[z, 2 + k], rcv.at[z, 1 + k], me.at(me.z, q)
            ).wait_recv()
            copy = corner(z, k)
            if copy is not None:
                copy.start()
        yield
    yield True
    for j in range(4):
        z = me.order(j)
        for k in range(2):
            src = part(z, me.dq, k)
            if src is not None:
                remote(src, src, snd.at[z, 4 + k], rcv.at[z, 3 + k], me.at(me.z, me.xq)).wait_recv()
    for j in range(4):
        z = me.order(j)
        for k in range(2):
            across(z, k, slot(z, me.q)).wait_send()
            copy = corner(z, k)
            if copy is not None:
                copy.wait_send()


PIECE_SEMS = [
    pltpu.SemaphoreType.DMA((4, 6)),
    pltpu.SemaphoreType.DMA((4, 5)),
    pltpu.SemaphoreType.DMA((4, 2)),
    pltpu.SemaphoreType.DMA((4, 2)),
]


def gather_pieces(me, sources, dst, sems):
    snd, rcv, piece_snd, piece_rcv = sems
    half = dst.shape[2] // 2

    def slot(z, q):
        return dst.at[:, 4 * z + q]

    def part(z, q, h):
        return dst.at[:, 4 * z + q, pl.ds(h * half, half)]

    def local(n):
        parts, piece = sources[n]
        return pltpu.make_async_copy(piece(me.z), dst.at[parts, me.r], piece_snd.at[me.z, n])

    def send(z, n):
        parts, piece = sources[n]
        return remote(
            piece(z), dst.at[parts, me.r], piece_snd.at[z, n], piece_rcv.at[me.z, n], me.at(z, me.q)
        )

    for n in range(len(sources)):
        local(n).start()
    for j in range(1, 3):
        for n in range(len(sources)):
            send(me.order(j), n).start()
    yield
    for n in range(len(sources)):
        send(me.order(3), n).start()
    yield

    def arrive(j):
        z = me.order(j)
        for n in range(len(sources)):
            view = dst.at[sources[n][0], 4 * z + me.q]
            remote(view, view, piece_snd.at[z, n], piece_rcv.at[z, n], me.at(z, me.q)).wait_recv()

    for n in range(len(sources)):
        local(n).wait()
    yield from in_plane(me, slot(me.z, me.q), slot, part, snd, rcv, arrive)
    for j in range(1, 4):
        for n in range(len(sources)):
            send(me.order(j), n).wait_send()


SPREAD_SEMS = [
    pltpu.SemaphoreType.DMA((4, 3)),
    pltpu.SemaphoreType.DMA((4, 2)),
    pltpu.SemaphoreType.DMA,
]


def spread(me, src, dst, sems):
    snd, rcv, loc = sems
    rows = src.shape[0] // 2
    mine = pl.ds(pl.multiple_of(me.t * rows, rows), rows)
    local = pltpu.make_async_copy(src, dst.at[me.z], loc)
    local.start()

    def slot(z):
        return dst.at[z, mine]

    def line(z, k, source, to):
        return remote(source, slot(z), snd.at[z, k], rcv.at[z, 0], me.at(to, me.q))

    def share(z):
        return remote(slot(z), slot(z), snd.at[z, 2], rcv.at[z, 1], me.other())

    @pl.when(me.z < 3)
    def _():
        line(me.z, 0, src.at[mine], me.z + 1).start()

    @pl.when(me.z > 0)
    def _():
        line(me.z, 1, src.at[mine], me.z - 1).start()

    yield
    for j in range(1, 4):
        z = me.order(j)
        line(z, 0, slot(z), me.z).wait_recv()

        @pl.when(me.inner == 1)
        def _():
            step = 3 - 2 * me.z if j == 1 else 2 * me.z - 3
            line(z, 0, slot(z), me.z + step).start()

        share(z).start()
        yield
    yield True
    other = pl.ds(pl.multiple_of((1 - me.t) * rows, rows), rows)
    for j in range(1, 4):
        z = me.order(j)
        remote(
            dst.at[z, other], dst.at[z, other], snd.at[z, 2], rcv.at[z, 1], me.other()
        ).wait_recv()
        share(z).wait_send()
    local.wait()

    @pl.when(me.z < 3)
    def _():
        line(me.z, 0, src.at[mine], me.z + 1).wait_send()

    @pl.when(me.z > 0)
    def _():
        line(me.z, 1, src.at[mine], me.z - 1).wait_send()

    @pl.when(me.inner == 1)
    def _():
        for j in range(1, 4):
            z = me.order(j)
            line(z, 0, slot(z), me.z).wait_send()


def swap(me, src, dst, sems):
    copy = remote(src, dst, sems[0], sems[1], me.other())
    copy.start()
    yield True
    copy.wait()


SWAP_SEMS = [pltpu.SemaphoreType.DMA, pltpu.SemaphoreType.DMA]


def add_rows(out, terms):
    rows = out.shape[0]
    step = 16

    @pl.loop(0, rows // step)
    def _(i):
        at = pl.ds(pl.multiple_of(i * step, step), step)
        total = terms[0][at].astype(f32)
        for term in terms[1:]:
            total += term[at].astype(f32)
        out[at] = total.astype(out.dtype)


def reduce_scratch(slots, rows, columns, dtype):
    return [
        pltpu.VMEM((slots, rows, columns), bf16),
        pltpu.VMEM((slots, rows, columns), bf16),
        pltpu.VMEM((slots, rows, columns), bf16),
        pltpu.VMEM((rows, columns), dtype),
        pltpu.SemaphoreType.DMA((slots, 3)),
        pltpu.SemaphoreType.DMA((slots, 2)),
        pltpu.SemaphoreType.DMA((3,)),
    ]


def chain_scratch(rows, columns):
    return [
        pltpu.VMEM((LINE, rows, columns), bf16),
        pltpu.VMEM((LINE, rows, columns), bf16),
        pltpu.VMEM((2, 3, rows, columns), bf16),
        pltpu.SemaphoreType.DMA((LINE, 2)),
        pltpu.SemaphoreType.DMA((LINE,)),
        pltpu.SemaphoreType.DMA((2, 3)),
        pltpu.SemaphoreType.DMA((2, 3)),
        pltpu.SemaphoreType.DMA((3,)),
    ]


def reduce_line(me, src, out, scratch):
    here, there, landed, snd, rcv, line_snd, line_rcv, end = scratch
    rows = here.shape[1]
    mine = pl.ds(pl.multiple_of(me.t * rows, rows), rows)
    theirs = pl.ds(pl.multiple_of((1 - me.t) * rows, rows), rows)
    order = (3, 0, 2, 1)

    def cross(z):
        return remote(src.at[z, theirs], there.at[z], snd.at[z, 0], rcv.at[z], me.other())

    def local(z):
        return pltpu.make_async_copy(src.at[z, mine], here.at[z], snd.at[z, 1])

    def send(way, k, source):
        to = me.z + 1 - 2 * way
        return remote(
            source, landed.at[way, k], line_snd.at[way, k], line_rcv.at[way, k], me.at(to, me.q)
        )

    for z in order:
        cross(z).start()
        local(z).start()
    yield
    for z in order:
        local(z).wait()
        cross(z).wait_recv()
        add_rows(here.at[z], (here.at[z], there.at[z]))
    for k in range(3):
        for way in range(2):
            w = me.z if way == 0 else 3 - me.z
            block = 3 + w - k if way == 0 else k - w

            @pl.when(w <= k)
            def _():
                if k:

                    @pl.when(w < k)
                    def _():
                        send(way, k - 1, here.at[0]).wait_send()

                @pl.when(w == 0)
                def _():
                    send(way, k, here.at[block]).start()

                if k:

                    @pl.when(w > 0)
                    def _():
                        partial = landed.at[way, k - 1]
                        send(way, k - 1, partial).wait_recv()
                        add_rows(partial, (partial, here.at[block]))
                        send(way, k, partial).start()

        yield
    for way in range(2):
        w = me.z if way == 0 else 3 - me.z

        @pl.when(w > 0)
        def _():
            send(way, 2, landed.at[way, 2]).wait_recv()
            add_rows(here.at[me.z], (here.at[me.z], landed.at[way, 2]))

        @pl.when(w < 3)
        def _():
            send(way, 2, here.at[0]).wait_send()

    keep = pltpu.make_async_copy(here.at[me.z], out.at[mine], end.at[0])
    give = remote(here.at[me.z], out.at[mine], end.at[1], end.at[2], me.other())
    keep.start()
    give.start()
    yield True
    for z in range(LINE):
        cross(z).wait_send()
    keep.wait()
    give.wait()


def reduce_window(me, reach, src, out, scratch):
    here, there, landed, total, snd, rcv, end = scratch
    rows = here.shape[1]
    slots = reach + 1
    mine = pl.ds(pl.multiple_of(me.t * rows, rows), rows)
    theirs = pl.ds(pl.multiple_of((1 - me.t) * rows, rows), rows)
    start = jnp.maximum(me.r - reach, 0)

    def cross(j):
        return remote(src.at[j, theirs], there.at[j], snd.at[j, 0], rcv.at[j, 0], me.other())

    def local(j):
        return pltpu.make_async_copy(src.at[j, mine], here.at[j], snd.at[j, 1])

    def back(k):
        j = me.r - k - start
        return remote(
            here.at[j], landed.at[k], snd.at[k, 2], rcv.at[k, 1], (me.base + me.r - k, me.t)
        )

    for j in range(slots):
        cross(j).start()
        local(j).start()
    yield
    for j in range(slots):
        local(j).wait()
        cross(j).wait_recv()
        add_rows(here.at[j], (here.at[j], there.at[j]))
    for k in range(reach, 0, -1):

        @pl.when(me.r >= k)
        def _():
            back(k).start()

    yield
    add_rows(total, [here.at[me.r - start]])
    for k in range(1, slots):

        @pl.when(me.r + k < RING)
        def _():
            remote(
                landed.at[k], landed.at[k], snd.at[k, 2], rcv.at[k, 1], me.at(me.z, me.q)
            ).wait_recv()
            add_rows(total, (total, landed.at[k]))

    keep = pltpu.make_async_copy(total, out.at[mine], end.at[0])
    give = remote(total, out.at[mine], end.at[1], end.at[2], me.other())
    keep.start()
    give.start()
    yield True
    for j in range(slots):
        cross(j).wait_send()
    for k in range(1, slots):

        @pl.when(me.r >= k)
        def _():
            back(k).wait_send()

    keep.wait()
    give.wait()


PLANE_SEMS = [pltpu.SemaphoreType.DMA((4,)), pltpu.SemaphoreType.DMA((4,))]


def plane_first(me, src, got, sems):
    snd, rcv = sems
    rows = src.shape[-2] // 2
    copies = []
    lead = (slice(None),) * (len(src.shape) - 3)
    for h in range(2):
        q = (me.xq, me.yq)[h]
        for i in range(2):
            place = (q, me.dq)[i]
            n = 2 * h + i
            view = src.at[lead + (place, pl.ds(h * rows, rows))]
            copies.append(remote(view, got.at[h, i], snd.at[n], rcv.at[n], me.at(me.z, q)))
    for copy in copies:
        copy.start()
    yield True
    for copy in copies:
        copy.wait()


def plane_sums_scratch(shape):
    parts, line, _, rows, columns = shape
    block = (parts, 2, 2, line, rows // 2, columns)
    return [
        pltpu.VMEM(block, bf16),
        pltpu.VMEM(block, bf16),
        pltpu.SemaphoreType.DMA((parts, 4)),
        pltpu.SemaphoreType.DMA((parts, 4)),
        pltpu.SemaphoreType.DMA((parts, 4)),
        pltpu.SemaphoreType.DMA((parts, 4)),
    ]


def plane_sums(me, order, src, kept, passed, scratch):
    here, there, loc, snd, rcv, end = scratch
    half = src.shape[3] // 2

    def view(part, place, h):
        return src.at[part, :, place, pl.ds(h * half, half)]

    def sends(part):
        for h in range(2):
            q = (me.xq, me.yq)[h]
            for i in range(2):
                n = 2 * h + i
                yield remote(
                    view(part, (q, me.dq)[i], h),
                    there.at[part, h, i],
                    snd.at[part, n],
                    rcv.at[part, n],
                    me.at(me.z, q),
                )

    def loads(part):
        for h in range(2):
            for i in range(2):
                place = (me.q, (me.yq, me.xq)[h])[i]
                yield pltpu.make_async_copy(
                    view(part, place, h), here.at[part, h, i], loc.at[part, 2 * h + i]
                )

    def stores(part):
        for h in range(2):
            for i in range(2):
                yield pltpu.make_async_copy(
                    here.at[part, h, i], (kept, passed)[i].at[h, part], end.at[part, 2 * h + i]
                )

    for part in order:
        for copy in sends(part):
            copy.start()
        for copy in loads(part):
            copy.start()
    yield
    for part in order:
        yield
        for copy in loads(part):
            copy.wait()
        for copy in sends(part):
            copy.wait_recv()
        for h in range(2):
            for i in range(2):
                for z in range(here.shape[3]):
                    block = here.at[part, h, i, z]
                    add_rows(block, (block, there.at[part, h, i, z]))
        for copy in stores(part):
            copy.start()
    yield True
    for part in order:
        for copy in sends(part):
            copy.wait_send()
        for copy in stores(part):
            copy.wait()


def plane_second(me, src, got, sems):
    snd, rcv = sems
    copies = [
        remote(src.at[h], got.at[h], snd.at[h], rcv.at[h], me.at(me.z, (me.yq, me.xq)[h]))
        for h in range(2)
    ]
    for copy in copies:
        copy.start()
    yield True
    for copy in copies:
        copy.wait()


LINE_SEMS = [pltpu.SemaphoreType.DMA((4,)), pltpu.SemaphoreType.DMA((4,)), pltpu.SemaphoreType.DMA]


def line_exchange(me, piece, got, sems):
    snd, rcv, loc = sems
    local = pltpu.make_async_copy(piece(me.z), got.at[me.z], loc)
    local.start()

    def send(j):
        z = me.order(j)
        return remote(piece(z), got.at[me.z], snd.at[z], rcv.at[me.z], me.at(z, me.q))

    for j in (3, 2, 1):
        send(j).start()
    yield True
    for j in range(1, 4):
        z = me.order(j)
        remote(got.at[z], got.at[z], snd.at[z], rcv.at[z], me.at(z, me.q)).wait_recv()
    for j in range(1, 4):
        send(j).wait_send()
    local.wait()


def transfer(number, inputs, outputs, scratch, steps, whole=False, near=()):
    flat = [item for group in scratch for item in group]
    sizes = [len(group) for group in scratch]

    def kernel(*refs):
        ins = refs[: len(inputs)]
        outs = refs[len(inputs) : len(inputs) + len(outputs)]
        rest = refs[len(inputs) + len(outputs) :]
        groups = []
        for size in sizes:
            groups.append(rest[:size])
            rest = rest[size:]
        me = Place()
        me.greet(whole)
        run(steps(me, ins, outs, groups))

    return pl.pallas_call(
        kernel,
        out_shape=[jax.ShapeDtypeStruct(shape, dtype) for shape, dtype in outputs],
        in_specs=[VMEM if i in near else ANY for i in range(len(inputs))],
        out_specs=[ANY] * len(outputs),
        scratch_shapes=flat,
        compiler_params=pltpu.CompilerParams(
            collective_id=number, has_side_effects=True, vmem_limit_bytes=56 * 2**20
        ),
    )(*inputs)


def gather_rows(me, src, dst, sems):
    rows = src.shape[0]
    cut = -(-rows // 32) * 16

    def part(z, q, h):
        if cut == rows and h:
            return None
        return dst.at[4 * z + q, pl.ds(h * cut, (rows - cut) if h else cut)]

    return gather(me, src, lambda z, q: dst.at[4 * z + q], part, sems)


def group_lists(groups):
    return [[r + RING * g for g in range(groups)] for r in range(RING)]


def grow(x, axis, groups):
    if groups == 1:
        return x
    return lax.all_gather(x, "seq", axis=axis, tiled=True, axis_index_groups=group_lists(groups))


def shrink(x, axis, groups):
    if groups == 1:
        return x
    return lax.psum_scatter(
        x, "seq", scatter_dimension=axis, tiled=True, axis_index_groups=group_lists(groups)
    )


def to_places(x, groups):
    if groups == 1:
        return x
    return x.reshape(x.shape[0], groups, RING, -1).swapaxes(1, 2).reshape(x.shape)


def from_places(x, groups):
    if groups == 1:
        return x
    return x.reshape(x.shape[0], RING, groups, -1).swapaxes(1, 2).reshape(x.shape)


def normalize(stream, scale_vec):
    return (
        stream * lax.rsqrt(jnp.mean(stream * stream, axis=-1, keepdims=True) + epsilon) * scale_vec
    )


def rotate(values, places, head_count, direction):
    head_size = values.shape[1] // head_count
    shaped = values.reshape(values.shape[0], head_count, head_size)
    quarter = head_size // 4
    first_part = shaped[..., :quarter]
    second = shaped[..., quarter : 2 * quarter]
    remainder = shaped[..., 2 * quarter :]
    frequency = 10000.0 ** (-jnp.arange(quarter, dtype=jnp.float32) / quarter)
    angles = places.astype(jnp.float32)[:, None] * frequency[None, :]
    cosine = jnp.cos(angles)[:, None, :]
    sine_part = direction * jnp.sin(angles)[:, None, :]
    turned = jnp.concatenate(
        [
            first_part * cosine - second * sine_part,
            second * cosine + first_part * sine_part,
            remainder,
        ],
        axis=-1,
    )
    return turned.reshape(values.shape)


def dot(a, b, ca=1, cb=0):
    return lax.dot_general(a, b, (((ca,), (cb,)), ((), ())), preferred_element_type=f32)


def body(
    inputs,
    segment_ids,
    cotangent,
    attn_gain,
    query_weight,
    key_value_weight,
    out_weight,
    out_bias,
    mlp_gain,
    gate_up_weight,
    gate_up_bias,
    down_weight,
    down_bias,
):
    seq_index = lax.axis_index("seq")
    t = lax.axis_index("tensor")
    r = seq_index % RING
    z = r // 4
    q = r % 4
    groups = lax.axis_size("seq") // RING
    tokens, width = inputs.shape
    inputs = to_places(inputs, groups)
    cotangent = to_places(cotangent, groups)
    heads = query_weight.shape[1] // HD
    hidden_half = gate_up_weight.shape[2]
    block = -(-hidden_half // (LINE * LANES)) * LANES
    block_start = jnp.minimum(z * block, hidden_half - block)
    block_skip = z * block - block_start
    reach = (W + tokens - 2) // tokens
    span = (reach + 1) * tokens
    first_block = jnp.maximum(r - reach, 0)
    scale_factor = HD ** (-0.5)
    assert tokens * RING == SEQ_LEN and lax.axis_size("tensor") == 2

    kv_own = grow(key_value_weight, 0, groups)
    kv_rows, columns = kv_own.shape
    vectors = [grow(v, 0, groups) for v in (attn_gain, out_bias, mlp_gain, down_bias)]
    hidden_bias = grow(gate_up_bias, 1, groups)
    marks = jnp.stack([segment_ids // 256, segment_ids % 256]).astype(bf16)

    def pad_to(x, n):
        return jnp.pad(x, ((0, 0), (0, n - x.shape[1])))

    small = jnp.concatenate(
        [
            pad_to(jnp.stack(vectors), columns),
            pad_to(hidden_bias, columns),
            pad_to(marks, columns),
            jnp.zeros((8, columns), bf16),
        ]
    )
    query_own = grow(query_weight, 0, groups)
    out_own = grow(out_weight.T, 0, groups)
    gate_up_own = grow(gate_up_weight, 1, groups)
    down_own = grow(down_weight.T, 0, groups)
    rows = query_own.shape[0]

    def first_steps(me, ins, outs, sems):
        def both(n):
            mine = outs[n].at[:, me.t]
            for _ in gather_rows(me, ins[n], mine, sems[n]):
                yield
            copy = remote(mine, mine, sems[4][0].at[n], sems[4][1].at[n], me.other())
            copy.start()
            yield True
            copy.wait()

        return [
            both(2),
            both(1),
            gather_rows(me, ins[0], outs[0], sems[0]),
            spread(me, ins[3], outs[3], sems[3]),
        ]

    query_full, kv_full, smalls, cot_all = transfer(
        0,
        [query_own, kv_own, small, cotangent],
        [
            ((RING,) + query_own.shape, bf16),
            ((RING, 2) + kv_own.shape, bf16),
            ((RING, 2) + small.shape, bf16),
            ((LINE,) + cotangent.shape, bf16),
        ],
        [
            GATHER_SEMS,
            GATHER_SEMS,
            GATHER_SEMS,
            SPREAD_SEMS,
            [pltpu.SemaphoreType.DMA((3,)), pltpu.SemaphoreType.DMA((3,))],
        ],
        first_steps,
    )
    query_full = query_full.reshape(width, heads * HD)
    if groups > 1:
        kv_full = kv_full.reshape(RING, 2, groups, kv_rows // groups, columns).swapaxes(1, 2)
    kv_full = kv_full.reshape(width, columns)
    cot_all = cot_all.reshape(LINE * tokens, width)

    def vector(row, count, order):
        piece = smalls[:, :, row, :count].reshape(RING, 2, groups, count // groups)
        return jnp.transpose(piece, order).reshape(-1).astype(f32)

    gain_one, bias_out, gain_two, bias_down = (
        vector(i, kv_rows, (0, 2, 1, 3)) for i in range(4)
    )
    bias_gate_up = jnp.stack(
        [vector(4 + i, hidden_bias.shape[1], (2, 0, 1, 3)) for i in range(2)]
    )
    bias_local = lax.dynamic_slice_in_dim(bias_gate_up, t * hidden_half + block_start, block, 1)
    all_marks = smalls[:, 0, 6:8, :tokens].astype(f32)
    all_marks = (all_marks[:, 0] * 256.0 + all_marks[:, 1]).reshape(-1)
    window_marks = lax.dynamic_slice_in_dim(all_marks, first_block * tokens, span, 0)
    own_marks = lax.dynamic_slice_in_dim(all_marks, r * tokens, tokens, 0)

    stream = inputs.astype(f32)
    places = r * tokens + jnp.arange(tokens, dtype=jnp.int32)
    normed = normalize(stream, gain_one).astype(bf16)
    query_lin = dot(normed, query_full)
    queries = (rotate(query_lin, places, heads, 1.0) * scale_factor).astype(bf16)
    key_value = dot(normed, kv_full)
    keys_own = rotate(key_value[:, :HD], places, 1, 1.0).astype(bf16)
    values_own = key_value[:, HD:].astype(bf16)
    own_block = jnp.concatenate([keys_own, values_own], axis=1)

    def second_steps(me, ins, outs, groups_in):
        own_kv, own_out, own_gate_up, own_down, q_in, x_in, vec, marks_row, marks_column = ins
        kv_all, out_all, ffn_all, mixed_out, log_out, middle_out, normed_out = outs
        kv_sems, out_sems, ffn_sems, spread_sems, swap_sems, scratch = groups_in
        qs, win, weight, mask, mixed, part, theirs, x, middle, normed_two, logs, loads = scratch

        def load(n, src, dst):
            return pltpu.make_async_copy(src, dst, loads.at[n])

        def columns_of(source, lead):
            def piece(place):
                start = jnp.minimum(place * block, hidden_half - block)
                at = pl.ds(pl.multiple_of(start, LANES), block)
                return source.at[:, :, at] if lead else source.at[:, at]

            return piece

        keys = gather_rows(me, own_kv, kv_all, kv_sems)
        outw = gather_rows(me, own_out, out_all, out_sems)
        ffn = gather_pieces(
            me,
            [(pl.ds(0, 2), columns_of(own_gate_up, True)), (2, columns_of(own_down, False))],
            ffn_all,
            ffn_sems,
        )
        next(keys)
        load(0, q_in, qs).start()
        load(1, x_in, x).start()
        next(outw)
        start = jnp.maximum(me.r - reach, 0)
        row_places = me.r * tokens + lax.broadcasted_iota(jnp.int32, (tokens, 1), 0)

        @pl.loop(0, reach + 1)
        def _(i):
            at = pl.ds(pl.multiple_of(i * tokens, tokens), tokens)
            key_places = (start + i) * tokens + lax.broadcasted_iota(jnp.int32, (1, tokens), 1)
            gap = row_places - key_places
            seen = (gap >= 0) & (gap < W) & (marks_column[...] == marks_row[:, at])
            mask[:, at] = jnp.where(seen, 0.0, -1e30)

        next(keys)
        next(keys)
        next(ffn)
        for _ in range(3):
            next(keys)
        next(outw)
        next(keys, None)
        window = load(2, kv_all.at[pl.ds(start, reach + 1)], win)
        window.start()
        load(0, q_in, qs).wait()
        window.wait()

        @pl.loop(0, heads)
        def _(h):
            at = pl.ds(pl.multiple_of(h * HD, HD), HD)
            both = win[...].reshape(span, 2 * HD)
            scores = dot(qs[:, at], both[:, :HD], 1, 1) + mask[...]
            top = jnp.max(scores, axis=1, keepdims=True)
            exponent = jnp.exp(scores - top)
            total = jnp.sum(exponent, axis=1, keepdims=True)
            blend = dot(exponent.astype(bf16), both[:, HD:])
            mixed[:, at] = (blend / total).astype(bf16)
            logs[h] = top + jnp.log(total)
            for i in range(1, heads):

                @pl.when(h == i)
                def _():
                    next(outw if i < 4 else ffn)

        next(ffn)
        for _ in outw:
            pass
        load(3, mixed, mixed_out).start()
        load(4, logs, log_out).start()
        weights = load(2, out_all, weight)
        weights.start()
        weights.wait()

        @pl.loop(0, LINE)
        def _(i):
            at = pl.ds(pl.multiple_of(i * 4 * rows, LANES), 4 * rows)
            piece = weight[pl.ds(4 * i, 4)].reshape(4 * rows, heads * HD)
            part[:, at] = dot(mixed[...], piece, 1, 1).astype(bf16)

        swapped = remote(part, theirs, swap_sems[0], swap_sems[1], me.other())
        swapped.start()
        load(1, x_in, x).wait()
        swapped.wait()

        @pl.loop(0, tokens // 16)
        def _(i):
            at = pl.ds(pl.multiple_of(i * 16, 16), 16)
            total = x[at].astype(f32) + (part[at].astype(f32) + theirs[at].astype(f32)) + vec[0:1]
            middle[at] = total
            scale = lax.rsqrt(jnp.mean(total * total, axis=1, keepdims=True) + epsilon)
            normed_two[at] = (total * scale * vec[1:2]).astype(bf16)

        out = spread(me, normed_two, normed_out, spread_sems)
        next(out)
        load(0, middle, middle_out).start()
        next(ffn)
        next(out)
        next(ffn)
        next(out)
        next(out)
        next(out)
        for step in (ffn, out):
            for _ in step:
                pass
        load(3, mixed, mixed_out).wait()
        load(4, logs, log_out).wait()
        load(0, middle, middle_out).wait()
        return []

    kv_all, out_full, ffn_full, mixed_low, log_total, middle, normed_all = transfer(
        1,
        [
            own_block,
            out_own,
            gate_up_own,
            down_own,
            queries,
            inputs,
            jnp.stack([bias_out, gain_two]),
            window_marks[None],
            own_marks[:, None],
        ],
        [
            ((RING,) + own_block.shape, bf16),
            ((RING,) + out_own.shape, bf16),
            ((3, RING, rows, block), bf16),
            (queries.shape, bf16),
            ((heads, tokens, 1), f32),
            (inputs.shape, f32),
            ((LINE,) + inputs.shape, bf16),
        ],
        [
            GATHER_SEMS,
            GATHER_SEMS,
            PIECE_SEMS,
            SPREAD_SEMS,
            SWAP_SEMS,
            [
                pltpu.VMEM(queries.shape, bf16),
                pltpu.VMEM((reach + 1, tokens, 2 * HD), bf16),
                pltpu.VMEM((RING,) + out_own.shape, bf16),
                pltpu.VMEM((tokens, span), f32),
                pltpu.VMEM(queries.shape, bf16),
                pltpu.VMEM(inputs.shape, bf16),
                pltpu.VMEM(inputs.shape, bf16),
                pltpu.VMEM(inputs.shape, bf16),
                pltpu.VMEM(inputs.shape, f32),
                pltpu.VMEM(inputs.shape, bf16),
                pltpu.VMEM((heads, tokens, 1), f32),
                pltpu.SemaphoreType.DMA((5,)),
            ],
        ],
        second_steps,
        near=(6, 7, 8),
    )
    out_full = out_full.reshape(width, heads * HD)
    ffn_full = ffn_full.reshape(3, width, block)
    key_places = first_block * tokens + jnp.arange(span, dtype=jnp.int32)
    key_gap = places[:, None] - key_places[None, :]
    visible = (key_gap >= 0) & (key_gap < W) & (own_marks[:, None] == window_marks[None, :])
    window = lax.dynamic_slice_in_dim(
        kv_all.reshape(RING * tokens, 2 * HD), first_block * tokens, span, 0
    )
    key_win = window[:, :HD]
    value_win = window[:, HD:]
    query_heads = queries.reshape(tokens, heads, HD)

    def both_cores(number, part):
        (theirs,) = transfer(
            number,
            [part],
            [(part.shape, bf16)],
            [SWAP_SEMS],
            lambda me, ins, outs, sems: [swap(me, ins[0], outs[0], sems[0])],
        )
        return part.astype(f32) + theirs.astype(f32)

    normed_all = normed_all.reshape(LINE * tokens, width)
    ours = (jnp.arange(block) >= block_skip)[None, :]
    gate_pre = dot(normed_all, ffn_full[0]) + bias_local[0]
    up_pre = dot(normed_all, ffn_full[1]) + bias_local[1]
    hidden = jnp.where(ours, jax.nn.gelu(gate_pre, approximate=True) * up_pre, 0.0).astype(bf16)
    mlp_part = dot(hidden, ffn_full[2], 1, 1).astype(bf16)
    hidden_grad = dot(cot_all, ffn_full[2])
    _, unit_pull = jax.vjp(
        lambda gate_in, up_in: jax.nn.gelu(gate_in, approximate=True) * up_in, gate_pre, up_pre
    )
    gate_grad, up_grad = unit_pull(hidden_grad)
    gate_low = jnp.where(ours, gate_grad, 0.0).astype(bf16)
    up_low = jnp.where(ours, up_grad, 0.0).astype(bf16)
    ffn_term = jnp.stack(
        [
            dot(normed_all, gate_low, 0, 0).astype(bf16),
            dot(normed_all, up_low, 0, 0).astype(bf16),
            dot(cot_all, hidden, 0, 0).astype(bf16),
        ]
    )
    ffn_term = ffn_term.reshape(3, LINE, 4, rows, block)
    normed_two_part = (dot(gate_low, ffn_full[0], 1, 1) + dot(up_low, ffn_full[1], 1, 1)).astype(
        bf16
    )
    hidden_bias_part = jnp.stack(
        [jnp.sum(gate_low.astype(f32), axis=0), jnp.sum(up_low.astype(f32), axis=0)]
    )
    hidden_bias_part = jnp.pad(hidden_bias_part, ((0, 14), (0, 0))).astype(bf16)

    def first_half(src, got):
        lead = src.ndim - 3
        half = rows_of(src)
        xq, yq = q + 1 - 2 * (q % 2), q + 2 - 4 * (q // 2)

        def own(place, h):
            piece = lax.dynamic_index_in_dim(src, place, lead, keepdims=False)
            return lax.slice_in_dim(piece, h * half, (h + 1) * half, axis=lead).astype(f32)

        kept = [own(q, h) + got[h, 0].astype(f32) for h in range(2)]
        passed = jnp.stack(
            [
                (own(yq, 0) + got[0, 1].astype(f32)).astype(bf16),
                (own(xq, 1) + got[1, 1].astype(f32)).astype(bf16),
            ]
        )
        return kept, passed

    def rows_of(src):
        return src.shape[-2] // 2

    def second_half(kept, got):
        return jnp.concatenate(
            [kept[h].astype(f32) + got[h].astype(f32) for h in range(2)], axis=-2
        ).astype(bf16)

    def first_shape(src):
        s = src.shape
        return (2, 2) + s[:-3] + (s[-2] // 2, s[-1])

    def third_steps(me, ins, outs, sems):
        yield from ()
        one = reduce_line(me, ins[0], outs[0], sems[0])
        two = reduce_line(me, ins[1], outs[1], sems[1])
        three = plane_sums(me, (2, 0, 1), ins[2], outs[2], outs[3], sems[2])
        next(one)
        next(three)
        ends = [swap(me, ins[3], outs[4], sems[3])]
        next(ends[0])
        next(two)
        for _ in range(4):
            next(one)
        next(three)
        for _ in range(3):
            next(two)
            next(three)
        next(two)
        for step in [one, two, three] + ends:
            next(step, None)

    kept_shape = (2, 3, LINE, rows // 2, block)
    normed_two_grad, mlp_out, ffn_kept, ffn_passed, bias_theirs = transfer(
        4,
        [
            normed_two_part.reshape(LINE, tokens, width),
            mlp_part.reshape(LINE, tokens, width),
            ffn_term,
            hidden_bias_part,
        ],
        [
            ((tokens, width), bf16),
            ((tokens, width), bf16),
            (kept_shape, bf16),
            (kept_shape, bf16),
            (hidden_bias_part.shape, bf16),
        ],
        [
            chain_scratch(tokens // 2, width),
            chain_scratch(tokens // 2, width),
            plane_sums_scratch(ffn_term.shape),
            SWAP_SEMS,
        ],
        third_steps,
    )
    cot_full = cotangent.astype(f32)
    _, norm_two_pull = jax.vjp(normalize, middle, gain_two)
    middle_part, gain_two_grad = norm_two_pull(normed_two_grad.astype(f32))
    middle_grad = cot_full + middle_part
    middle_low = middle_grad.astype(bf16)
    out_term = dot(middle_low, mixed_low, 0, 0).astype(bf16)
    out_term = out_term.reshape(LINE, 4, rows, heads * HD)
    mixed_grad = dot(middle_low, out_full).astype(bf16).reshape(tokens, heads, HD)

    scores_again = jnp.einsum("qhd,kd->hqk", query_heads, key_win, preferred_element_type=f32)
    probs_again = jnp.where(visible[None], jnp.exp(scores_again - log_total), 0.0)
    probs_again_low = probs_again.astype(bf16)
    prob_grad = jnp.einsum("qhd,kd->hqk", mixed_grad, value_win, preferred_element_type=f32)
    value_grad = jnp.einsum("hqk,qhd->kd", probs_again_low, mixed_grad, preferred_element_type=f32)
    row_inner = jnp.sum(probs_again * prob_grad, axis=-1, keepdims=True)
    score_grad = (probs_again * (prob_grad - row_inner)).astype(bf16)
    query_grad_raw = jnp.einsum(
        "hqk,kd->qhd", score_grad, key_win, preferred_element_type=f32
    ).reshape(tokens, heads * HD)
    key_grad_raw = jnp.einsum("hqk,qhd->kd", score_grad, query_heads, preferred_element_type=f32)
    window_grad = (
        jnp.concatenate([key_grad_raw, value_grad], axis=1)
        .reshape(reach + 1, tokens, 2 * HD)
        .astype(bf16)
    )

    def fourth_steps(me, ins, outs, sems):
        return [
            reduce_window(me, reach, ins[0], outs[0], sems[0]),
            plane_second(me, ins[1], outs[1], sems[1]),
            plane_first(me, ins[2], outs[2], sems[2]),
        ]

    own_grad, ffn_got, out_got = transfer(
        5,
        [window_grad, ffn_passed, out_term],
        [
            ((tokens, 2 * HD), f32),
            (ffn_passed.shape, bf16),
            (first_shape(out_term), bf16),
        ],
        [
            reduce_scratch(reach + 1, tokens // 2, 2 * HD, f32),
            PLANE_SEMS,
            PLANE_SEMS,
        ],
        fourth_steps,
        whole=True,
    )
    output = (middle + mlp_out.astype(f32) + bias_down).astype(bf16)
    ffn_sum = second_half(ffn_kept, ffn_got)
    out_kept, out_passed = first_half(out_term, out_got)
    key_lin_grad = rotate(own_grad[:, :HD], places, 1, -1.0)
    kv_grad_low = jnp.concatenate([key_lin_grad, own_grad[:, HD:]], axis=1).astype(bf16)
    query_lin_grad = (rotate(query_grad_raw, places, heads, -1.0) * scale_factor).astype(bf16)
    normed_grad = both_cores(6, dot(query_lin_grad, query_full, 1, 1).astype(bf16)) + dot(
        kv_grad_low, kv_full, 1, 1
    )
    _, norm_one_pull = jax.vjp(normalize, stream, gain_one)
    stream_part, gain_one_grad = norm_one_pull(normed_grad)
    input_grad = middle_grad + stream_part
    query_term = dot(normed, query_lin_grad, 0, 0).astype(bf16)
    query_term = query_term.reshape(LINE, 4, rows, heads * HD)

    def take_core(full, axis):
        blocks = lax.dynamic_index_in_dim(full, t, axis, keepdims=False)
        return jnp.moveaxis(blocks, 1, 0).reshape(RING, full.shape[0], -1)

    def core_features(full):
        return take_core(full.reshape(full.shape[0], RING, groups, 2, -1), 3)

    def core_hidden(full):
        blocks = full.reshape(full.shape[0], groups, RING, 2, -1)
        return take_core(jnp.swapaxes(blocks, 1, 2), 3)

    kv_term = dot(normed, kv_grad_low, 0, 0)
    kv_term = lax.dynamic_index_in_dim(
        kv_term.reshape(RING, groups, 2, -1, columns), t, 2, keepdims=False
    ).reshape(RING, kv_rows, columns)
    vector_terms = core_features(
        jnp.stack(
            [gain_one_grad, jnp.sum(middle_grad, axis=0), gain_two_grad, jnp.sum(cot_full, axis=0)]
        )
    )
    bias_pair = jnp.where(
        t == 0,
        jnp.stack([hidden_bias_part, bias_theirs]),
        jnp.stack([bias_theirs, hidden_bias_part]),
    )[:, :2].astype(f32)
    bias_terms = jnp.zeros((2, 2, hidden_half), f32)
    start = jnp.minimum(z * block, hidden_half - block)
    bias_terms = lax.dynamic_update_slice_in_dim(bias_terms, bias_pair, start, 2)
    bias_terms = core_hidden(jnp.swapaxes(bias_terms, 0, 1).reshape(2, -1))

    def widen(x):
        return jnp.pad(x, ((0, 0), (0, 0), (0, columns - x.shape[2])))

    kv_term = jnp.concatenate(
        [kv_term, widen(vector_terms), widen(bias_terms), jnp.zeros((RING, 10, columns), f32)],
        axis=1,
    ).astype(bf16)
    kv_term = kv_term.reshape(LINE, 4, kv_rows + 16, columns)

    def fifth_steps(me, ins, outs, sems):
        return [
            line_exchange(me, lambda z: ins[0].at[:, z], outs[0], sems[0]),
            plane_second(me, ins[1], outs[1], sems[1]),
            plane_first(me, ins[2], outs[2], sems[2]),
            plane_first(me, ins[3], outs[3], sems[3]),
        ]

    ffn_done, out_got, query_got, kv_got = transfer(
        7,
        [ffn_sum, out_passed, query_term, kv_term],
        [
            ((LINE, 3, rows, block), bf16),
            (out_passed.shape, bf16),
            (first_shape(query_term), bf16),
            (first_shape(kv_term), bf16),
        ],
        [LINE_SEMS, PLANE_SEMS, PLANE_SEMS, PLANE_SEMS],
        fifth_steps,
    )
    out_sum = second_half(out_kept, out_got)
    query_kept, query_passed = first_half(query_term, query_got)
    kv_kept, kv_passed = first_half(kv_term, kv_got)

    def sixth_steps(me, ins, outs, sems):
        return [
            line_exchange(me, lambda z: ins[0].at[z], outs[0], sems[0]),
            plane_second(me, ins[1], outs[1], sems[1]),
            plane_second(me, ins[2], outs[2], sems[2]),
        ]

    out_done, query_got, kv_got = transfer(
        8,
        [out_sum, query_passed, kv_passed],
        [(out_sum.shape, bf16), (query_passed.shape, bf16), (kv_passed.shape, bf16)],
        [LINE_SEMS, PLANE_SEMS, PLANE_SEMS],
        sixth_steps,
    )
    query_sum = second_half(query_kept, query_got)
    kv_sum = second_half(kv_kept, kv_got)

    def last_steps(me, ins, outs, sems):
        return [
            line_exchange(me, lambda z: ins[0].at[z], outs[0], sems[0]),
            line_exchange(me, lambda z: ins[1].at[z], outs[1], sems[1]),
        ]

    query_done, kv_done = transfer(
        9,
        [query_sum, kv_sum],
        [(query_sum.shape, bf16), (kv_sum.shape, bf16)],
        [LINE_SEMS, LINE_SEMS],
        last_steps,
    )

    last_skip = LINE * block - hidden_half
    ffn_grad = jnp.concatenate(
        [ffn_done[i] for i in range(LINE - 1)] + [ffn_done[LINE - 1, :, :, last_skip:]], axis=2
    )
    ffn_grad = shrink(ffn_grad.astype(f32), 1, groups)
    out_grad = shrink(jnp.sum(out_done.astype(f32), axis=0), 0, groups).T
    query_grad = shrink(jnp.sum(query_done.astype(f32), axis=0), 0, groups)
    kv_sums = jnp.sum(kv_done.astype(f32), axis=0)
    key_value_grad = shrink(kv_sums[:kv_rows], 0, groups)
    small_grads = [shrink(kv_sums[kv_rows + i, :kv_rows], 0, groups) for i in range(4)]
    gate_up_bias_grad = shrink(
        kv_sums[kv_rows + 4 : kv_rows + 6, : hidden_bias.shape[1]], 1, groups
    )
    return (
        from_places(output, groups),
        from_places(input_grad, groups),
        small_grads[0],
        query_grad,
        key_value_grad,
        out_grad,
        small_grads[1],
        small_grads[2],
        ffn_grad[:2],
        gate_up_bias_grad,
        ffn_grad[2].T,
        small_grads[3],
    )


def solution(mesh):
    in_specs = (
        P("seq", None),
        P("seq"),
        P("seq", None),
        P(("seq", "tensor")),
        P("seq", "tensor"),
        P(("seq", "tensor"), None),
        P("tensor", "seq"),
        P(("seq", "tensor")),
        P(("seq", "tensor")),
        P(None, "seq", "tensor"),
        P(None, ("seq", "tensor")),
        P("tensor", "seq"),
        P(("seq", "tensor")),
    )
    out_specs = (
        P("seq", None),
        P("seq", None),
        P(("seq", "tensor")),
        P("seq", "tensor"),
        P(("seq", "tensor"), None),
        P("tensor", "seq"),
        P(("seq", "tensor")),
        P(("seq", "tensor")),
        P(None, "seq", "tensor"),
        P(None, ("seq", "tensor")),
        P("tensor", "seq"),
        P(("seq", "tensor")),
    )
    return jax.shard_map(body, mesh=mesh, in_specs=in_specs, out_specs=out_specs, check_vma=False)
```

```python
import functools

import jax
import jax.numpy as jnp
from jax import lax
from jax.experimental import pallas as pl
from jax.experimental.pallas import tpu as pltpu
from jax.sharding import PartitionSpec as P

HD = 256
W = 2048
SEQ_LEN = 4096
LINE = 4
RING = 16
LANES = 128

epsilon = 1e-06
bf16 = jnp.bfloat16
f32 = jnp.float32
MESH = pl.DeviceIdType.MESH
ANY = pl.BlockSpec(memory_space=pl.ANY)
VMEM = pl.BlockSpec(memory_space=pltpu.VMEM)


class Place:
    def __init__(self):
        seq = lax.axis_index("seq")
        self.t = lax.axis_index("tensor")
        self.r = lax.rem(seq, RING)
        self.base = seq - self.r
        self.z = lax.div(self.r, 4)
        self.q = lax.rem(self.r, 4)
        self.xq = self.q + 1 - 2 * lax.rem(self.q, 2)
        self.yq = self.q + 2 - 4 * lax.div(self.q, 2)
        self.dq = 3 - self.q
        self.half = lax.div(self.z, 2)
        self.inner = self.z + self.half * (3 - 2 * self.z)

    def at(self, z, q):
        return (self.base + 4 * z + q, self.t)

    def other(self):
        return (self.base + self.r, 1 - self.t)

    def order(self, j):
        v = j + self.inner * (1 - 2 * j if j < 2 else 0)
        return v + self.half * (3 - 2 * v)

    def greet(self, whole=False):
        barrier = pltpu.get_barrier_semaphore()
        if whole:
            peers = [
                (self.base + lax.rem(self.r + k, RING), self.t) for k in range(1, RING)
            ]
        else:
            peers = [self.at(lax.rem(self.z + k, 4), self.q) for k in range(1, 4)]
            peers += [self.at(self.z, self.xq), self.at(self.z, self.yq)]
        peers.append(self.other())
        for peer in peers:
            pl.semaphore_signal(barrier, inc=1, device_id=peer, device_id_type=MESH)
        pl.semaphore_wait(barrier, len(peers))


def remote(src, dst, send, recv, device):
    return pltpu.make_async_remote_copy(
        src_ref=src, dst_ref=dst, send_sem=send, recv_sem=recv, device_id=device, device_id_type=MESH
    )


def run(steps):
    steps, ending = list(steps), []
    while steps:
        for step in list(steps):
            if next(step, True):
                steps.remove(step)
                ending.append(step)
    for step in ending:
        next(step, None)


GATHER_SEMS = [
    pltpu.SemaphoreType.DMA((4, 6)),
    pltpu.SemaphoreType.DMA((4, 5)),
    pltpu.SemaphoreType.DMA,
]


def gather(me, own, slot, part, sems):
    snd, rcv, loc = sems
    local = pltpu.make_async_copy(own, slot(me.z, me.q), loc)
    local.start()

    def line(z, k, src, to):
        return remote(src, slot(z, me.q), snd.at[z, k], rcv.at[z, 0], me.at(to, me.q))

    @pl.when(me.z < 3)
    def _():
        line(me.z, 0, own, me.z + 1).start()

    @pl.when(me.z > 0)
    def _():
        line(me.z, 1, own, me.z - 1).start()

    def arrive(j):
        z = me.order(j)
        line(z, 0, slot(z, me.q), me.z).wait_recv()

        @pl.when(me.inner == 1)
        def _():
            step = 3 - 2 * me.z if j == 1 else 2 * me.z - 3
            line(z, 0, slot(z, me.q), me.z + step).start()

    yield from in_plane(me, own, slot, part, snd, rcv, arrive)
    local.wait()

    @pl.when(me.z < 3)
    def _():
        line(me.z, 0, own, me.z + 1).wait_send()

    @pl.when(me.z > 0)
    def _():
        line(me.z, 1, own, me.z - 1).wait_send()

    @pl.when(me.inner == 1)
    def _():
        for j in range(1, 4):
            z = me.order(j)
            line(z, 0, slot(z, me.q), me.z).wait_send()


def in_plane(me, own, slot, part, snd, rcv, arrive):
    def across(z, k, src):
        q = (me.xq, me.yq)[k]
        return remote(src, slot(z, me.q), snd.at[z, 2 + k], rcv.at[z, 1 + k], me.at(me.z, q))

    def corner(z, k):
        src = part(z, (me.xq, me.yq)[k], k)
        if src is None:
            return None
        return remote(src, src, snd.at[z, 4 + k], rcv.at[z, 3 + k], me.at(me.z, (me.yq, me.xq)[k]))

    for k in range(2):
        across(me.z, k, own).start()
    yield
    for j in range(1, 5):
        if j < 4:
            arrive(j)
            z = me.order(j)
            for k in range(2):
                across(z, k, slot(z, me.q)).start()
        z = me.order(j - 1)
        for k in range(2):
            q = (me.xq, me.yq)[k]
            remote(
                slot(z, q), slot(z, q), snd.at[z, 2 + k], rcv.at[z, 1 + k], me.at(me.z, q)
            ).wait_recv()
            copy = corner(z, k)
            if copy is not None:
                copy.start()
        yield
    yield True
    for j in range(4):
        z = me.order(j)
        for k in range(2):
            src = part(z, me.dq, k)
            if src is not None:
                remote(src, src, snd.at[z, 4 + k], rcv.at[z, 3 + k], me.at(me.z, me.xq)).wait_recv()
    for j in range(4):
        z = me.order(j)
        for k in range(2):
            across(z, k, slot(z, me.q)).wait_send()
            copy = corner(z, k)
            if copy is not None:
                copy.wait_send()


PIECE_SEMS = [
    pltpu.SemaphoreType.DMA((4, 6)),
    pltpu.SemaphoreType.DMA((4, 5)),
    pltpu.SemaphoreType.DMA((4, 2)),
    pltpu.SemaphoreType.DMA((4, 2)),
]


def gather_pieces(me, sources, dst, sems):
    snd, rcv, piece_snd, piece_rcv = sems
    half = dst.shape[2] // 2

    def slot(z, q):
        return dst.at[:, 4 * z + q]

    def part(z, q, h):
        return dst.at[:, 4 * z + q, pl.ds(h * half, half)]

    def local(n):
        parts, piece = sources[n]
        return pltpu.make_async_copy(piece(me.z), dst.at[parts, me.r], piece_snd.at[me.z, n])

    def send(z, n):
        parts, piece = sources[n]
        return remote(
            piece(z), dst.at[parts, me.r], piece_snd.at[z, n], piece_rcv.at[me.z, n], me.at(z, me.q)
        )

    for n in range(len(sources)):
        local(n).start()
    for j in range(1, 3):
        for n in range(len(sources)):
            send(me.order(j), n).start()
    yield
    for n in range(len(sources)):
        send(me.order(3), n).start()
    yield

    def arrive(j):
        z = me.order(j)
        for n in range(len(sources)):
            view = dst.at[sources[n][0], 4 * z + me.q]
            remote(view, view, piece_snd.at[z, n], piece_rcv.at[z, n], me.at(z, me.q)).wait_recv()

    for n in range(len(sources)):
        local(n).wait()
    yield from in_plane(me, slot(me.z, me.q), slot, part, snd, rcv, arrive)
    for j in range(1, 4):
        for n in range(len(sources)):
            send(me.order(j), n).wait_send()


SPREAD_SEMS = [
    pltpu.SemaphoreType.DMA((4, 3)),
    pltpu.SemaphoreType.DMA((4, 2)),
    pltpu.SemaphoreType.DMA,
]


def spread(me, src, dst, sems):
    snd, rcv, loc = sems
    rows = src.shape[0] // 2
    mine = pl.ds(pl.multiple_of(me.t * rows, rows), rows)
    local = pltpu.make_async_copy(src, dst.at[me.z], loc)
    local.start()

    def slot(z):
        return dst.at[z, mine]

    def line(z, k, source, to):
        return remote(source, slot(z), snd.at[z, k], rcv.at[z, 0], me.at(to, me.q))

    def share(z):
        return remote(slot(z), slot(z), snd.at[z, 2], rcv.at[z, 1], me.other())

    @pl.when(me.z < 3)
    def _():
        line(me.z, 0, src.at[mine], me.z + 1).start()

    @pl.when(me.z > 0)
    def _():
        line(me.z, 1, src.at[mine], me.z - 1).start()

    yield
    for j in range(1, 4):
        z = me.order(j)
        line(z, 0, slot(z), me.z).wait_recv()

        @pl.when(me.inner == 1)
        def _():
            step = 3 - 2 * me.z if j == 1 else 2 * me.z - 3
            line(z, 0, slot(z), me.z + step).start()

        share(z).start()
        yield
    yield True
    other = pl.ds(pl.multiple_of((1 - me.t) * rows, rows), rows)
    for j in range(1, 4):
        z = me.order(j)
        remote(
            dst.at[z, other], dst.at[z, other], snd.at[z, 2], rcv.at[z, 1], me.other()
        ).wait_recv()
        share(z).wait_send()
    local.wait()

    @pl.when(me.z < 3)
    def _():
        line(me.z, 0, src.at[mine], me.z + 1).wait_send()

    @pl.when(me.z > 0)
    def _():
        line(me.z, 1, src.at[mine], me.z - 1).wait_send()

    @pl.when(me.inner == 1)
    def _():
        for j in range(1, 4):
            z = me.order(j)
            line(z, 0, slot(z), me.z).wait_send()


def swap(me, src, dst, sems):
    copy = remote(src, dst, sems[0], sems[1], me.other())
    copy.start()
    yield True
    copy.wait()


SWAP_SEMS = [pltpu.SemaphoreType.DMA, pltpu.SemaphoreType.DMA]


def add_rows(out, terms):
    rows = out.shape[0]
    step = 16

    @pl.loop(0, rows // step)
    def _(i):
        at = pl.ds(pl.multiple_of(i * step, step), step)
        total = terms[0][at].astype(f32)
        for term in terms[1:]:
            total += term[at].astype(f32)
        out[at] = total.astype(out.dtype)


def reduce_scratch(slots, rows, columns, dtype):
    return [
        pltpu.VMEM((slots, rows, columns), bf16),
        pltpu.VMEM((slots, rows, columns), bf16),
        pltpu.VMEM((slots, rows, columns), bf16),
        pltpu.VMEM((rows, columns), dtype),
        pltpu.SemaphoreType.DMA((slots, 3)),
        pltpu.SemaphoreType.DMA((slots, 2)),
        pltpu.SemaphoreType.DMA((3,)),
    ]


def chain_scratch(rows, columns):
    return [
        pltpu.VMEM((LINE, rows, columns), bf16),
        pltpu.VMEM((LINE, rows, columns), bf16),
        pltpu.VMEM((2, 3, rows, columns), bf16),
        pltpu.SemaphoreType.DMA((LINE, 2)),
        pltpu.SemaphoreType.DMA((LINE,)),
        pltpu.SemaphoreType.DMA((2, 3)),
        pltpu.SemaphoreType.DMA((2, 3)),
        pltpu.SemaphoreType.DMA((3,)),
    ]


def reduce_line(me, src, out, scratch):
    here, there, landed, snd, rcv, line_snd, line_rcv, end = scratch
    rows = here.shape[1]
    mine = pl.ds(pl.multiple_of(me.t * rows, rows), rows)
    theirs = pl.ds(pl.multiple_of((1 - me.t) * rows, rows), rows)
    order = (3, 0, 2, 1)

    def cross(z):
        return remote(src.at[z, theirs], there.at[z], snd.at[z, 0], rcv.at[z], me.other())

    def local(z):
        return pltpu.make_async_copy(src.at[z, mine], here.at[z], snd.at[z, 1])

    def send(way, k, source):
        to = me.z + 1 - 2 * way
        return remote(
            source, landed.at[way, k], line_snd.at[way, k], line_rcv.at[way, k], me.at(to, me.q)
        )

    for z in order:
        cross(z).start()
        local(z).start()
    yield
    for z in order:
        local(z).wait()
        cross(z).wait_recv()
        add_rows(here.at[z], (here.at[z], there.at[z]))
    for k in range(3):
        for way in range(2):
            w = me.z if way == 0 else 3 - me.z
            block = 3 + w - k if way == 0 else k - w

            @pl.when(w <= k)
            def _():
                if k:

                    @pl.when(w < k)
                    def _():
                        send(way, k - 1, here.at[0]).wait_send()

                @pl.when(w == 0)
                def _():
                    send(way, k, here.at[block]).start()

                if k:

                    @pl.when(w > 0)
                    def _():
                        partial = landed.at[way, k - 1]
                        send(way, k - 1, partial).wait_recv()
                        add_rows(partial, (partial, here.at[block]))
                        send(way, k, partial).start()

        yield
    for way in range(2):
        w = me.z if way == 0 else 3 - me.z

        @pl.when(w > 0)
        def _():
            send(way, 2, landed.at[way, 2]).wait_recv()
            add_rows(here.at[me.z], (here.at[me.z], landed.at[way, 2]))

        @pl.when(w < 3)
        def _():
            send(way, 2, here.at[0]).wait_send()

    keep = pltpu.make_async_copy(here.at[me.z], out.at[mine], end.at[0])
    give = remote(here.at[me.z], out.at[mine], end.at[1], end.at[2], me.other())
    keep.start()
    give.start()
    yield True
    for z in range(LINE):
        cross(z).wait_send()
    keep.wait()
    give.wait()


def reduce_window(me, reach, src, out, scratch):
    here, there, landed, total, snd, rcv, end = scratch
    rows = here.shape[1]
    slots = reach + 1
    mine = pl.ds(pl.multiple_of(me.t * rows, rows), rows)
    theirs = pl.ds(pl.multiple_of((1 - me.t) * rows, rows), rows)
    start = jnp.maximum(me.r - reach, 0)

    def cross(j):
        return remote(src.at[j, theirs], there.at[j], snd.at[j, 0], rcv.at[j, 0], me.other())

    def local(j):
        return pltpu.make_async_copy(src.at[j, mine], here.at[j], snd.at[j, 1])

    def back(k):
        j = me.r - k - start
        return remote(
            here.at[j], landed.at[k], snd.at[k, 2], rcv.at[k, 1], (me.base + me.r - k, me.t)
        )

    for j in range(slots):
        cross(j).start()
        local(j).start()
    yield
    for j in range(slots):
        local(j).wait()
        cross(j).wait_recv()
        add_rows(here.at[j], (here.at[j], there.at[j]))
    for k in range(reach, 0, -1):

        @pl.when(me.r >= k)
        def _():
            back(k).start()

    yield
    add_rows(total, [here.at[me.r - start]])
    for k in range(1, slots):

        @pl.when(me.r + k < RING)
        def _():
            remote(
                landed.at[k], landed.at[k], snd.at[k, 2], rcv.at[k, 1], me.at(me.z, me.q)
            ).wait_recv()
            add_rows(total, (total, landed.at[k]))

    keep = pltpu.make_async_copy(total, out.at[mine], end.at[0])
    give = remote(total, out.at[mine], end.at[1], end.at[2], me.other())
    keep.start()
    give.start()
    yield True
    for j in range(slots):
        cross(j).wait_send()
    for k in range(1, slots):

        @pl.when(me.r >= k)
        def _():
            back(k).wait_send()

    keep.wait()
    give.wait()


PLANE_SEMS = [pltpu.SemaphoreType.DMA((4,)), pltpu.SemaphoreType.DMA((4,))]


def plane_first(me, src, got, sems):
    snd, rcv = sems
    rows = src.shape[-2] // 2
    copies = []
    lead = (slice(None),) * (len(src.shape) - 3)
    for h in range(2):
        q = (me.xq, me.yq)[h]
        for i in range(2):
            place = (q, me.dq)[i]
            n = 2 * h + i
            view = src.at[lead + (place, pl.ds(h * rows, rows))]
            copies.append(remote(view, got.at[h, i], snd.at[n], rcv.at[n], me.at(me.z, q)))
    for copy in copies:
        copy.start()
    yield True
    for copy in copies:
        copy.wait()


def add_blocks(out, more):
    blocks, rows, _ = out.shape
    steps = rows // 16

    @pl.loop(0, blocks * steps)
    def _(i):
        n = lax.div(i, steps)
        at = pl.ds(pl.multiple_of(lax.rem(i, steps) * 16, 16), 16)
        out[n, at] = (out[n, at].astype(f32) + more[n, at].astype(f32)).astype(out.dtype)


def scatter_buffers(rows, columns):
    half = (2, LINE, rows // 2, columns)
    return [((2,) + half, bf16)] + [(half, bf16)] * 3 + [((LINE, rows, columns), bf16)]


SCATTER_SEMS = [
    pltpu.SemaphoreType.DMA((6,)),
    pltpu.SemaphoreType.DMA((6,)),
    pltpu.SemaphoreType.DMA((8,)),
    pltpu.SemaphoreType.DMA((4,)),
    pltpu.SemaphoreType.DMA((4,)),
]


def scatter(me, src, done, buffers, here, there, sems):
    got, kept, passed, got_two, total = buffers
    snd, rcv, loc, line_snd, line_rcv = sems
    half = src.shape[2] // 2
    first, second = [], []
    for h in range(2):
        q = (me.xq, me.yq)[h]
        rows = pl.ds(h * half, half)
        for i in range(2):
            n = 2 * h + i
            view = src.at[:, (q, me.dq)[i], rows]
            first.append(remote(view, got.at[h, i], snd.at[n], rcv.at[n], me.at(me.z, q)))
        q = (me.yq, me.xq)[h]
        second.append(
            remote(passed.at[h], got_two.at[h], snd.at[4 + h], rcv.at[4 + h], me.at(me.z, q))
        )
    for copy in first:
        copy.start()
    yield
    for copy in first:
        copy.wait_recv()
    loads, stores = [], []
    for h in range(2):
        for i in range(2):
            n = 2 * h + i
            view = src.at[:, (me.q, (me.yq, me.xq)[h])[i], pl.ds(h * half, half)]
            loads.append(pltpu.make_async_copy(view, here.at[h, i], loc.at[n]))
            loads.append(pltpu.make_async_copy(got.at[h, i], there.at[h, i], loc.at[4 + n]))
            stores.append(
                pltpu.make_async_copy(here.at[h, i], (kept, passed)[i].at[h], loc.at[n])
            )
    for copy in loads:
        copy.start()
    for copy in loads:
        copy.wait()
    for h in range(2):
        for i in range(2):
            add_blocks(here.at[h, i], there.at[h, i])
    for copy in stores:
        copy.start()
    for copy in stores:
        copy.wait()
    for copy in second:
        copy.start()
    yield
    for copy in second:
        copy.wait_recv()
    loads, stores = [], []
    for h in range(2):
        loads.append(pltpu.make_async_copy(kept.at[h], here.at[h, 0], loc.at[h]))
        loads.append(pltpu.make_async_copy(got_two.at[h], there.at[h, 0], loc.at[4 + h]))
        stores.append(
            pltpu.make_async_copy(here.at[h, 0], total.at[:, pl.ds(h * half, half)], loc.at[h])
        )
    for copy in loads:
        copy.start()
    for copy in loads:
        copy.wait()
    for h in range(2):
        add_blocks(here.at[h, 0], there.at[h, 0])
    for copy in stores:
        copy.start()
    for copy in stores:
        copy.wait()

    def send(j):
        z = me.order(j)
        return remote(total.at[z], done.at[me.z], line_snd.at[z], line_rcv.at[me.z], me.at(z, me.q))

    local = pltpu.make_async_copy(total.at[me.z], done.at[me.z], loc.at[7])
    local.start()
    for j in (3, 2, 1):
        send(j).start()
    yield True
    for j in range(1, 4):
        z = me.order(j)
        remote(done.at[z], done.at[z], line_snd.at[z], line_rcv.at[z], me.at(z, me.q)).wait_recv()
    local.wait()
    for copy in first + second:
        copy.wait_send()
    for j in range(1, 4):
        send(j).wait_send()


FFN_SEMS = [
    pltpu.SemaphoreType.DMA((3, 2)),
    pltpu.SemaphoreType.DMA((3, 2)),
    pltpu.SemaphoreType.DMA((3, 4)),
    pltpu.SemaphoreType.DMA((3, 4)),
    pltpu.SemaphoreType.DMA((3, 4)),
]


def ffn_scatter(me, order, kept, passed, got, total, done, here, there, sems):
    snd, rcv, loc, line_snd, line_rcv = sems
    half, columns = kept.shape[3:]

    def cross(part):
        return [
            remote(
                passed.at[h, part],
                got.at[h, part],
                snd.at[part, h],
                rcv.at[part, h],
                me.at(me.z, (me.yq, me.xq)[h]),
            )
            for h in range(2)
        ]

    def send(part, j):
        z = me.order(j)
        return remote(
            total.at[part, z],
            done.at[part, me.z],
            line_snd.at[part, z],
            line_rcv.at[part, me.z],
            me.at(z, me.q),
        )

    def local(part):
        return pltpu.make_async_copy(
            total.at[part, me.z], done.at[part, me.z], line_snd.at[part, me.z]
        )

    for part in order:
        for copy in cross(part):
            copy.start()
    yield
    at = pl.ds(0, columns)
    for part in order:
        for copy in cross(part):
            copy.wait_recv()
        loads, stores = [], []
        for h in range(2):
            a, b = here.at[h, 0, :, :, at], there.at[h, 0, :, :, at]
            loads.append(pltpu.make_async_copy(kept.at[h, part], a, loc.at[part, h]))
            loads.append(pltpu.make_async_copy(got.at[h, part], b, loc.at[part, 2 + h]))
            stores.append(
                pltpu.make_async_copy(
                    a, total.at[part, :, pl.ds(h * half, half)], loc.at[part, h]
                )
            )
        for copy in loads:
            copy.start()
        for copy in loads:
            copy.wait()
        for h in range(2):
            add_blocks(here.at[h, 0, :, :, at], there.at[h, 0, :, :, at])
        for copy in stores:
            copy.start()
        for copy in stores:
            copy.wait()
        local(part).start()
        for j in (3, 2, 1):
            send(part, j).start()
        yield
    yield True
    for part in order:
        for j in range(1, 4):
            z = me.order(j)
            view = done.at[part, z]
            remote(
                view, view, line_snd.at[part, z], line_rcv.at[part, z], me.at(z, me.q)
            ).wait_recv()
        local(part).wait()
        for copy in cross(part):
            copy.wait_send()
        for j in range(1, 4):
            send(part, j).wait_send()


def plane_sums_scratch(shape):
    parts, line, _, rows, columns = shape
    block = (parts, 2, 2, line, rows // 2, columns)
    return [
        pltpu.VMEM(block, bf16),
        pltpu.VMEM(block, bf16),
        pltpu.SemaphoreType.DMA((parts, 4)),
        pltpu.SemaphoreType.DMA((parts, 4)),
        pltpu.SemaphoreType.DMA((parts, 4)),
        pltpu.SemaphoreType.DMA((parts, 4)),
    ]


def plane_sums(me, order, src, kept, passed, scratch):
    here, there, loc, snd, rcv, end = scratch
    half = src.shape[3] // 2

    def view(part, place, h):
        return src.at[part, :, place, pl.ds(h * half, half)]

    def sends(part):
        for h in range(2):
            q = (me.xq, me.yq)[h]
            for i in range(2):
                n = 2 * h + i
                yield remote(
                    view(part, (q, me.dq)[i], h),
                    there.at[part, h, i],
                    snd.at[part, n],
                    rcv.at[part, n],
                    me.at(me.z, q),
                )

    def loads(part):
        for h in range(2):
            for i in range(2):
                place = (me.q, (me.yq, me.xq)[h])[i]
                yield pltpu.make_async_copy(
                    view(part, place, h), here.at[part, h, i], loc.at[part, 2 * h + i]
                )

    def stores(part):
        for h in range(2):
            for i in range(2):
                yield pltpu.make_async_copy(
                    here.at[part, h, i], (kept, passed)[i].at[h, part], end.at[part, 2 * h + i]
                )

    for part in order:
        for copy in sends(part):
            copy.start()
        for copy in loads(part):
            copy.start()
    yield
    for part in order:
        yield
        for copy in loads(part):
            copy.wait()
        for copy in sends(part):
            copy.wait_recv()
        for h in range(2):
            for i in range(2):
                for z in range(here.shape[3]):
                    block = here.at[part, h, i, z]
                    add_rows(block, (block, there.at[part, h, i, z]))
        for copy in stores(part):
            copy.start()
    yield True
    for part in order:
        for copy in sends(part):
            copy.wait_send()
        for copy in stores(part):
            copy.wait()


def plane_second(me, src, got, sems):
    snd, rcv = sems
    copies = [
        remote(src.at[h], got.at[h], snd.at[h], rcv.at[h], me.at(me.z, (me.yq, me.xq)[h]))
        for h in range(2)
    ]
    for copy in copies:
        copy.start()
    yield True
    for copy in copies:
        copy.wait()


LINE_SEMS = [pltpu.SemaphoreType.DMA((4,)), pltpu.SemaphoreType.DMA((4,)), pltpu.SemaphoreType.DMA]


def line_exchange(me, piece, got, sems):
    snd, rcv, loc = sems
    local = pltpu.make_async_copy(piece(me.z), got.at[me.z], loc)
    local.start()

    def send(j):
        z = me.order(j)
        return remote(piece(z), got.at[me.z], snd.at[z], rcv.at[me.z], me.at(z, me.q))

    for j in (3, 2, 1):
        send(j).start()
    yield True
    for j in range(1, 4):
        z = me.order(j)
        remote(got.at[z], got.at[z], snd.at[z], rcv.at[z], me.at(z, me.q)).wait_recv()
    for j in range(1, 4):
        send(j).wait_send()
    local.wait()


def transfer(number, inputs, outputs, scratch, steps, whole=False, near=()):
    flat = [item for group in scratch for item in group]
    sizes = [len(group) for group in scratch]

    def kernel(*refs):
        ins = refs[: len(inputs)]
        outs = refs[len(inputs) : len(inputs) + len(outputs)]
        rest = refs[len(inputs) + len(outputs) :]
        groups = []
        for size in sizes:
            groups.append(rest[:size])
            rest = rest[size:]
        me = Place()
        me.greet(whole)
        run(steps(me, ins, outs, groups))

    return pl.pallas_call(
        kernel,
        out_shape=[jax.ShapeDtypeStruct(shape, dtype) for shape, dtype in outputs],
        in_specs=[VMEM if i in near else ANY for i in range(len(inputs))],
        out_specs=[ANY] * len(outputs),
        scratch_shapes=flat,
        compiler_params=pltpu.CompilerParams(
            collective_id=number, has_side_effects=True, vmem_limit_bytes=56 * 2**20
        ),
    )(*inputs)


def gather_rows(me, src, dst, sems):
    rows = src.shape[0]
    cut = -(-rows // 32) * 16

    def part(z, q, h):
        if cut == rows and h:
            return None
        return dst.at[4 * z + q, pl.ds(h * cut, (rows - cut) if h else cut)]

    return gather(me, src, lambda z, q: dst.at[4 * z + q], part, sems)


def group_lists(groups):
    return [[r + RING * g for g in range(groups)] for r in range(RING)]


def grow(x, axis, groups):
    if groups == 1:
        return x
    return lax.all_gather(x, "seq", axis=axis, tiled=True, axis_index_groups=group_lists(groups))


def shrink(x, axis, groups):
    if groups == 1:
        return x
    return lax.psum_scatter(
        x, "seq", scatter_dimension=axis, tiled=True, axis_index_groups=group_lists(groups)
    )


def to_places(x, groups):
    if groups == 1:
        return x
    return x.reshape(x.shape[0], groups, RING, -1).swapaxes(1, 2).reshape(x.shape)


def from_places(x, groups):
    if groups == 1:
        return x
    return x.reshape(x.shape[0], RING, groups, -1).swapaxes(1, 2).reshape(x.shape)


def normalize(stream, scale_vec):
    return (
        stream * lax.rsqrt(jnp.mean(stream * stream, axis=-1, keepdims=True) + epsilon) * scale_vec
    )


def rotate(values, places, head_count, direction):
    head_size = values.shape[1] // head_count
    shaped = values.reshape(values.shape[0], head_count, head_size)
    quarter = head_size // 4
    first_part = shaped[..., :quarter]
    second = shaped[..., quarter : 2 * quarter]
    remainder = shaped[..., 2 * quarter :]
    frequency = 10000.0 ** (-jnp.arange(quarter, dtype=jnp.float32) / quarter)
    angles = places.astype(jnp.float32)[:, None] * frequency[None, :]
    cosine = jnp.cos(angles)[:, None, :]
    sine_part = direction * jnp.sin(angles)[:, None, :]
    turned = jnp.concatenate(
        [
            first_part * cosine - second * sine_part,
            second * cosine + first_part * sine_part,
            remainder,
        ],
        axis=-1,
    )
    return turned.reshape(values.shape)


def dot(a, b, ca=1, cb=0):
    return lax.dot_general(a, b, (((ca,), (cb,)), ((), ())), preferred_element_type=f32)


def body(
    inputs,
    segment_ids,
    cotangent,
    attn_gain,
    query_weight,
    key_value_weight,
    out_weight,
    out_bias,
    mlp_gain,
    gate_up_weight,
    gate_up_bias,
    down_weight,
    down_bias,
):
    seq_index = lax.axis_index("seq")
    t = lax.axis_index("tensor")
    r = seq_index % RING
    z = r // 4
    q = r % 4
    groups = lax.axis_size("seq") // RING
    tokens, width = inputs.shape
    inputs = to_places(inputs, groups)
    cotangent = to_places(cotangent, groups)
    heads = query_weight.shape[1] // HD
    hidden_half = gate_up_weight.shape[2]
    block = -(-hidden_half // (LINE * LANES)) * LANES
    block_start = jnp.minimum(z * block, hidden_half - block)
    block_skip = z * block - block_start
    reach = (W + tokens - 2) // tokens
    span = (reach + 1) * tokens
    first_block = jnp.maximum(r - reach, 0)
    scale_factor = HD ** (-0.5)
    assert tokens * RING == SEQ_LEN and lax.axis_size("tensor") == 2

    kv_own = grow(key_value_weight, 0, groups)
    kv_rows, columns = kv_own.shape
    vectors = [grow(v, 0, groups) for v in (attn_gain, out_bias, mlp_gain, down_bias)]
    hidden_bias = grow(gate_up_bias, 1, groups)
    marks = jnp.stack([segment_ids // 256, segment_ids % 256]).astype(bf16)

    def pad_to(x, n):
        return jnp.pad(x, ((0, 0), (0, n - x.shape[1])))

    small = jnp.concatenate(
        [
            pad_to(jnp.stack(vectors), columns),
            pad_to(hidden_bias, columns),
            pad_to(marks, columns),
            jnp.zeros((8, columns), bf16),
        ]
    )
    query_own = grow(query_weight, 0, groups)
    out_own = grow(out_weight.T, 0, groups)
    gate_up_own = grow(gate_up_weight, 1, groups)
    down_own = grow(down_weight.T, 0, groups)
    rows = query_own.shape[0]

    def first_steps(me, ins, outs, sems):
        def both(n):
            mine = outs[n].at[:, me.t]
            for _ in gather_rows(me, ins[n], mine, sems[n]):
                yield
            copy = remote(mine, mine, sems[4][0].at[n], sems[4][1].at[n], me.other())
            copy.start()
            yield True
            copy.wait()

        return [
            both(2),
            both(1),
            gather_rows(me, ins[0], outs[0], sems[0]),
            spread(me, ins[3], outs[3], sems[3]),
        ]

    query_full, kv_full, smalls, cot_all = transfer(
        0,
        [query_own, kv_own, small, cotangent],
        [
            ((RING,) + query_own.shape, bf16),
            ((RING, 2) + kv_own.shape, bf16),
            ((RING, 2) + small.shape, bf16),
            ((LINE,) + cotangent.shape, bf16),
        ],
        [
            GATHER_SEMS,
            GATHER_SEMS,
            GATHER_SEMS,
            SPREAD_SEMS,
            [pltpu.SemaphoreType.DMA((3,)), pltpu.SemaphoreType.DMA((3,))],
        ],
        first_steps,
    )
    query_full = query_full.reshape(width, heads * HD)
    if groups > 1:
        kv_full = kv_full.reshape(RING, 2, groups, kv_rows // groups, columns).swapaxes(1, 2)
    kv_full = kv_full.reshape(width, columns)
    cot_all = cot_all.reshape(LINE * tokens, width)

    def vector(row, count, order):
        piece = smalls[:, :, row, :count].reshape(RING, 2, groups, count // groups)
        return jnp.transpose(piece, order).reshape(-1).astype(f32)

    gain_one, bias_out, gain_two, bias_down = (
        vector(i, kv_rows, (0, 2, 1, 3)) for i in range(4)
    )
    bias_gate_up = jnp.stack(
        [vector(4 + i, hidden_bias.shape[1], (2, 0, 1, 3)) for i in range(2)]
    )
    bias_local = lax.dynamic_slice_in_dim(bias_gate_up, t * hidden_half + block_start, block, 1)
    all_marks = smalls[:, 0, 6:8, :tokens].astype(f32)
    all_marks = (all_marks[:, 0] * 256.0 + all_marks[:, 1]).reshape(-1)
    window_marks = lax.dynamic_slice_in_dim(all_marks, first_block * tokens, span, 0)
    own_marks = lax.dynamic_slice_in_dim(all_marks, r * tokens, tokens, 0)

    stream = inputs.astype(f32)
    places = r * tokens + jnp.arange(tokens, dtype=jnp.int32)
    normed = normalize(stream, gain_one).astype(bf16)
    query_lin = dot(normed, query_full)
    queries = (rotate(query_lin, places, heads, 1.0) * scale_factor).astype(bf16)
    key_value = dot(normed, kv_full)
    keys_own = rotate(key_value[:, :HD], places, 1, 1.0).astype(bf16)
    values_own = key_value[:, HD:].astype(bf16)
    own_block = jnp.concatenate([keys_own, values_own], axis=1)

    def second_steps(me, ins, outs, groups_in):
        own_kv, own_out, own_gate_up, own_down, q_in, x_in, vec, marks_row, marks_column = ins
        kv_all, out_all, ffn_all, mixed_out, log_out, middle_out, normed_out = outs
        kv_sems, out_sems, ffn_sems, spread_sems, swap_sems, scratch = groups_in
        qs, win, weight, mask, mixed, part, theirs, x, middle, normed_two, logs, loads = scratch

        def load(n, src, dst):
            return pltpu.make_async_copy(src, dst, loads.at[n])

        def columns_of(source, lead):
            def piece(place):
                start = jnp.minimum(place * block, hidden_half - block)
                at = pl.ds(pl.multiple_of(start, LANES), block)
                return source.at[:, :, at] if lead else source.at[:, at]

            return piece

        keys = gather_rows(me, own_kv, kv_all, kv_sems)
        outw = gather_rows(me, own_out, out_all, out_sems)
        ffn = gather_pieces(
            me,
            [(pl.ds(0, 2), columns_of(own_gate_up, True)), (2, columns_of(own_down, False))],
            ffn_all,
            ffn_sems,
        )
        next(keys)
        load(0, q_in, qs).start()
        load(1, x_in, x).start()
        next(outw)
        start = jnp.maximum(me.r - reach, 0)
        row_places = me.r * tokens + lax.broadcasted_iota(jnp.int32, (tokens, 1), 0)

        @pl.loop(0, reach + 1)
        def _(i):
            at = pl.ds(pl.multiple_of(i * tokens, tokens), tokens)
            key_places = (start + i) * tokens + lax.broadcasted_iota(jnp.int32, (1, tokens), 1)
            gap = row_places - key_places
            seen = (gap >= 0) & (gap < W) & (marks_column[...] == marks_row[:, at])
            mask[:, at] = jnp.where(seen, 0.0, -1e30)

        next(keys)
        next(keys)
        next(ffn)
        for _ in range(3):
            next(keys)
        next(outw)
        next(keys, None)
        window = load(2, kv_all.at[pl.ds(start, reach + 1)], win)
        window.start()
        load(0, q_in, qs).wait()
        window.wait()

        @pl.loop(0, heads)
        def _(h):
            at = pl.ds(pl.multiple_of(h * HD, HD), HD)
            both = win[...].reshape(span, 2 * HD)
            scores = dot(qs[:, at], both[:, :HD], 1, 1) + mask[...]
            top = jnp.max(scores, axis=1, keepdims=True)
            exponent = jnp.exp(scores - top)
            total = jnp.sum(exponent, axis=1, keepdims=True)
            blend = dot(exponent.astype(bf16), both[:, HD:])
            mixed[:, at] = (blend / total).astype(bf16)
            logs[h] = top + jnp.log(total)
            for i in range(1, heads):

                @pl.when(h == i)
                def _():
                    next(outw if i < 4 else ffn)

        next(ffn)
        for _ in outw:
            pass
        load(3, mixed, mixed_out).start()
        load(4, logs, log_out).start()
        weights = load(2, out_all, weight)
        weights.start()
        weights.wait()

        @pl.loop(0, LINE)
        def _(i):
            at = pl.ds(pl.multiple_of(i * 4 * rows, LANES), 4 * rows)
            piece = weight[pl.ds(4 * i, 4)].reshape(4 * rows, heads * HD)
            part[:, at] = dot(mixed[...], piece, 1, 1).astype(bf16)

        swapped = remote(part, theirs, swap_sems[0], swap_sems[1], me.other())
        swapped.start()
        load(1, x_in, x).wait()
        swapped.wait()

        @pl.loop(0, tokens // 16)
        def _(i):
            at = pl.ds(pl.multiple_of(i * 16, 16), 16)
            total = x[at].astype(f32) + (part[at].astype(f32) + theirs[at].astype(f32)) + vec[0:1]
            middle[at] = total
            scale = lax.rsqrt(jnp.mean(total * total, axis=1, keepdims=True) + epsilon)
            normed_two[at] = (total * scale * vec[1:2]).astype(bf16)

        out = spread(me, normed_two, normed_out, spread_sems)
        next(out)
        load(0, middle, middle_out).start()
        next(ffn)
        next(out)
        next(ffn)
        next(out)
        next(out)
        next(out)
        for step in (ffn, out):
            for _ in step:
                pass
        load(3, mixed, mixed_out).wait()
        load(4, logs, log_out).wait()
        load(0, middle, middle_out).wait()
        return []

    kv_all, out_full, ffn_full, mixed_low, log_total, middle, normed_all = transfer(
        1,
        [
            own_block,
            out_own,
            gate_up_own,
            down_own,
            queries,
            inputs,
            jnp.stack([bias_out, gain_two]),
            window_marks[None],
            own_marks[:, None],
        ],
        [
            ((RING,) + own_block.shape, bf16),
            ((RING,) + out_own.shape, bf16),
            ((3, RING, rows, block), bf16),
            (queries.shape, bf16),
            ((heads, tokens, 1), f32),
            (inputs.shape, f32),
            ((LINE,) + inputs.shape, bf16),
        ],
        [
            GATHER_SEMS,
            GATHER_SEMS,
            PIECE_SEMS,
            SPREAD_SEMS,
            SWAP_SEMS,
            [
                pltpu.VMEM(queries.shape, bf16),
                pltpu.VMEM((reach + 1, tokens, 2 * HD), bf16),
                pltpu.VMEM((RING,) + out_own.shape, bf16),
                pltpu.VMEM((tokens, span), f32),
                pltpu.VMEM(queries.shape, bf16),
                pltpu.VMEM(inputs.shape, bf16),
                pltpu.VMEM(inputs.shape, bf16),
                pltpu.VMEM(inputs.shape, bf16),
                pltpu.VMEM(inputs.shape, f32),
                pltpu.VMEM(inputs.shape, bf16),
                pltpu.VMEM((heads, tokens, 1), f32),
                pltpu.SemaphoreType.DMA((5,)),
            ],
        ],
        second_steps,
        near=(6, 7, 8),
    )
    out_full = out_full.reshape(width, heads * HD)
    ffn_full = ffn_full.reshape(3, width, block)
    key_places = first_block * tokens + jnp.arange(span, dtype=jnp.int32)
    key_gap = places[:, None] - key_places[None, :]
    visible = (key_gap >= 0) & (key_gap < W) & (own_marks[:, None] == window_marks[None, :])
    window = lax.dynamic_slice_in_dim(
        kv_all.reshape(RING * tokens, 2 * HD), first_block * tokens, span, 0
    )
    key_win = window[:, :HD]
    value_win = window[:, HD:]
    query_heads = queries.reshape(tokens, heads, HD)

    def both_cores(number, part):
        (theirs,) = transfer(
            number,
            [part],
            [(part.shape, bf16)],
            [SWAP_SEMS],
            lambda me, ins, outs, sems: [swap(me, ins[0], outs[0], sems[0])],
        )
        return part.astype(f32) + theirs.astype(f32)

    normed_all = normed_all.reshape(LINE * tokens, width)
    ours = (jnp.arange(block) >= block_skip)[None, :]
    gate_pre = dot(normed_all, ffn_full[0]) + bias_local[0]
    up_pre = dot(normed_all, ffn_full[1]) + bias_local[1]
    hidden = jnp.where(ours, jax.nn.gelu(gate_pre, approximate=True) * up_pre, 0.0).astype(bf16)
    mlp_part = dot(hidden, ffn_full[2], 1, 1).astype(bf16)
    hidden_grad = dot(cot_all, ffn_full[2])
    _, unit_pull = jax.vjp(
        lambda gate_in, up_in: jax.nn.gelu(gate_in, approximate=True) * up_in, gate_pre, up_pre
    )
    gate_grad, up_grad = unit_pull(hidden_grad)
    gate_low = jnp.where(ours, gate_grad, 0.0).astype(bf16)
    up_low = jnp.where(ours, up_grad, 0.0).astype(bf16)
    ffn_term = jnp.stack(
        [
            dot(normed_all, gate_low, 0, 0).astype(bf16),
            dot(normed_all, up_low, 0, 0).astype(bf16),
            dot(cot_all, hidden, 0, 0).astype(bf16),
        ]
    )
    ffn_term = ffn_term.reshape(3, LINE, 4, rows, block)
    normed_two_part = (dot(gate_low, ffn_full[0], 1, 1) + dot(up_low, ffn_full[1], 1, 1)).astype(
        bf16
    )
    hidden_bias_part = jnp.stack(
        [jnp.sum(gate_low.astype(f32), axis=0), jnp.sum(up_low.astype(f32), axis=0)]
    )
    hidden_bias_part = jnp.pad(hidden_bias_part, ((0, 14), (0, 0))).astype(bf16)

    def third_steps(me, ins, outs, sems):
        yield from ()
        one = reduce_line(me, ins[0], outs[0], sems[0])
        two = reduce_line(me, ins[1], outs[1], sems[1])
        three = plane_sums(me, (2, 0, 1), ins[2], outs[2], outs[3], sems[2])
        next(one)
        next(three)
        ends = [swap(me, ins[3], outs[4], sems[3])]
        next(ends[0])
        next(two)
        for _ in range(4):
            next(one)
        next(three)
        for _ in range(3):
            next(two)
            next(three)
        next(two)
        for step in [one, two, three] + ends:
            next(step, None)

    kept_shape = (2, 3, LINE, rows // 2, block)
    normed_two_grad, mlp_out, ffn_kept, ffn_passed, bias_theirs = transfer(
        4,
        [
            normed_two_part.reshape(LINE, tokens, width),
            mlp_part.reshape(LINE, tokens, width),
            ffn_term,
            hidden_bias_part,
        ],
        [
            ((tokens, width), bf16),
            ((tokens, width), bf16),
            (kept_shape, bf16),
            (kept_shape, bf16),
            (hidden_bias_part.shape, bf16),
        ],
        [
            chain_scratch(tokens // 2, width),
            chain_scratch(tokens // 2, width),
            plane_sums_scratch(ffn_term.shape),
            SWAP_SEMS,
        ],
        third_steps,
    )
    cot_full = cotangent.astype(f32)
    _, norm_two_pull = jax.vjp(normalize, middle, gain_two)
    middle_part, gain_two_grad = norm_two_pull(normed_two_grad.astype(f32))
    middle_grad = cot_full + middle_part
    middle_low = middle_grad.astype(bf16)

    def core_features(full):
        blocks = full.reshape(full.shape[0], RING, groups, 2, -1)
        blocks = lax.dynamic_index_in_dim(blocks, t, 3, keepdims=False)
        return jnp.moveaxis(blocks, 1, 0).reshape(RING, full.shape[0], -1)

    def core_hidden(full):
        blocks = full.reshape(full.shape[0], groups, RING, 2, -1)
        blocks = lax.dynamic_index_in_dim(blocks, t, 3, keepdims=False)
        return jnp.transpose(blocks, (2, 0, 1, 3)).reshape(RING, full.shape[0], -1)

    vector_terms = core_features(
        jnp.stack([jnp.sum(middle_grad, axis=0), gain_two_grad, jnp.sum(cot_full, axis=0)])
    )
    bias_pair = jnp.where(
        t == 0,
        jnp.stack([hidden_bias_part, bias_theirs]),
        jnp.stack([bias_theirs, hidden_bias_part]),
    )[:, :2].astype(f32)
    bias_terms = jnp.zeros((2, 2, hidden_half), f32)
    bias_terms = lax.dynamic_update_slice_in_dim(bias_terms, bias_pair, block_start, 2)
    bias_terms = core_hidden(jnp.swapaxes(bias_terms, 0, 1).reshape(2, -1))

    def widen(x):
        return jnp.pad(x, ((0, 0), (0, 0), (0, HD - x.shape[2])))

    small_terms = jnp.concatenate(
        [widen(vector_terms), widen(bias_terms), jnp.zeros((RING, 27, HD), f32)], axis=1
    ).astype(bf16)

    frequency = 10000.0 ** (-jnp.arange(HD // 4, dtype=f32) / (HD // 4))
    angles = places.astype(f32)[:, None] * frequency[None, :]
    turn_cos = jnp.concatenate([jnp.cos(angles), jnp.cos(angles)], axis=1)
    turn_sin = jnp.concatenate([-jnp.sin(angles), jnp.sin(angles)], axis=1)
    chunk = 3 if (reach + 1) % 3 == 0 else 1
    pieces = (reach + 1) // chunk
    kv_size = rows + small_terms.shape[1]
    vector_rows = -(-width // (LANES * 32)) * 32

    def fourth_steps(me, ins, outs, groups_in):
        (
            low_in, out_in, mixed_in, q_in, kv_in, logs_in, normed_in, query_in, kvw_in,
            kept_in, passed_in, small_in, grad_in, x_in,
            marks_row, marks_column, cos2, sin2, gain,
        ) = ins
        ffn_done, out_done, query_done, kv_done, input_out, gain_all = outs[:6]
        out_term, query_term, kv_term, ffn_got, ffn_total = outs[6:11]
        out_buffers, query_buffers, kv_buffers = outs[11:16], outs[16:21], outs[21:26]
        (
            ffn_sems, out_sems, query_sems, kv_sems, window_scratch, swap_sems, last_sems,
            vector_sems, scratch,
        ) = groups_in
        (
            low, weight, mixed, qs, win, normed_v, logs, mixed_grad, q_grad, window_sum, mask,
            kv_total, kv_low, kvw, stage, kv_stage, here, there, kv_here, kv_there, part, theirs,
            gain_sum, gain_rows, gain_low, loads,
        ) = scratch

        def load(n, src, dst):
            return pltpu.make_async_copy(src, dst, loads.at[n])

        def turn(v, direction):
            first = v[:, : HD // 2]
            turned = first * cos2[...] + direction * (pltpu.roll(first, HD // 4, 1) * sin2[...])
            return jnp.concatenate([turned, v[:, HD // 2 :]], axis=1)

        part_rows = 4 * rows

        def part_columns(i):
            return pl.ds(pl.multiple_of(i * part_rows, LANES), part_rows)

        ffn = ffn_scatter(
            me, (2, 0, 1), kept_in, passed_in, ffn_got, ffn_total, ffn_done, here, there, ffn_sems
        )
        outw = scatter(me, out_term, out_done, out_buffers, here, there, out_sems)
        query = scatter(me, query_term, query_done, query_buffers, here, there, query_sems)
        kvw_steps = scatter(
            me, kv_term, kv_done.at[me.t], kv_buffers, kv_here, kv_there, kv_sems
        )
        next(ffn)
        start = jnp.maximum(me.r - reach, 0)
        first_loads = [
            load(0, low_in, low),
            load(1, mixed_in, mixed),
            load(2, out_in, weight),
            load(3, q_in, qs),
            load(4, kv_in.at[pl.ds(start, reach + 1)], win),
            load(5, logs_in, logs),
            load(6, normed_in, normed_v),
            load(7, kvw_in, kvw),
        ]
        for copy in first_loads:
            copy.start()
        first_loads[0].wait()
        first_loads[1].wait()

        def weight_term(left, right, term):
            @pl.loop(0, LINE)
            def _(i):
                value = dot(left[:, part_columns(i)], right[...], 0, 0).astype(bf16)
                stage[...] = value.reshape(stage.shape)
                copy = load(8, stage, term.at[i])
                copy.start()
                copy.wait()

        weight_term(low, mixed, out_term)
        next(outw)
        first_loads[2].wait()

        @pl.loop(0, heads)
        def _(h):
            at = pl.ds(pl.multiple_of(h * HD, HD), HD)
            mixed_grad[:, at] = dot(low[...], weight[:, at]).astype(bf16)

        load(2, query_in, weight).start()
        load(0, x_in, low).start()
        row_places = me.r * tokens + lax.broadcasted_iota(jnp.int32, (tokens, 1), 0)

        @pl.loop(0, reach + 1)
        def _(i):
            at = pl.ds(pl.multiple_of(i * tokens, tokens), tokens)
            key_places = (start + i) * tokens + lax.broadcasted_iota(jnp.int32, (1, tokens), 1)
            gap = row_places - key_places
            seen = (gap >= 0) & (gap < W) & (marks_column[...] == marks_row[:, at])
            mask[:, at] = jnp.where(seen, 0.0, -1e30)
            window_sum[i] = jnp.zeros((tokens, 2 * HD), f32)

        for copy in first_loads[3:]:
            copy.wait()

        @pl.loop(0, heads)
        def _(h):
            at = pl.ds(pl.multiple_of(h * HD, HD), HD)
            q_head = qs[:, at]
            grad = mixed_grad[:, at]
            inner = jnp.sum(grad.astype(f32) * mixed[:, at].astype(f32), axis=1, keepdims=True)
            log = logs[h]
            q_sum = jnp.zeros((tokens, HD), f32)
            for c in range(pieces):
                blocks = pl.ds(c * chunk, chunk)
                both = win[blocks].reshape(chunk * tokens, 2 * HD)
                k, v = both[:, :HD], both[:, HD:]
                span_at = pl.ds(c * chunk * tokens, chunk * tokens)
                probs = jnp.exp(dot(q_head, k, 1, 1) + mask[:, span_at] - log)
                value_sum = dot(probs.astype(bf16), grad, 0, 0)
                score_grad = (probs * (dot(grad, v, 1, 1) - inner)).astype(bf16)
                q_sum += dot(score_grad, k)
                key_sum = dot(score_grad, q_head, 0, 0)
                window_sum[blocks, :, :HD] += key_sum.reshape(chunk, tokens, HD)
                window_sum[blocks, :, HD:] += value_sum.reshape(chunk, tokens, HD)
            q_grad[:, at] = (turn(q_sum, -1.0) * scale_factor).astype(bf16)
            for i in (2, 4):

                @pl.when(h == i)
                def _():
                    next(ffn)

        @pl.loop(0, reach + 1)
        def _(i):
            win[i] = window_sum[i].astype(bf16)

        window_steps = reduce_window(me, reach, win, kv_total, window_scratch)
        next(window_steps)
        load(5, grad_in, mask).start()
        weight_term(normed_v, q_grad, query_term)
        next(query)
        load(2, query_in, weight).wait()

        @pl.loop(0, LINE)
        def _(i):
            piece = weight[pl.ds(pl.multiple_of(i * part_rows, LANES), part_rows)]
            part[:, part_columns(i)] = dot(q_grad[...], piece, 1, 1).astype(bf16)

        swapped = remote(part, theirs, swap_sems[0], swap_sems[1], me.other())
        swapped.start()
        next(window_steps)
        next(outw)
        next(ffn)
        next(window_steps)
        next(window_steps, None)

        kv_low[:, :HD] = turn(kv_total[:, :HD], -1.0).astype(bf16)
        kv_low[:, HD:] = kv_total[:, HD:].astype(bf16)
        ours_at = pl.ds(pl.multiple_of(me.t * HD, HD), HD)
        small_copy = load(0, x_in, low)
        small_copy.wait()

        @pl.loop(0, LINE)
        def _(i):
            value = dot(normed_v[:, part_columns(i)], kv_low[:, ours_at], 0, 0).astype(bf16)
            kv_stage[:, pl.ds(0, rows)] = value.reshape(4, rows, HD)
            copy = load(9, small_in.at[pl.ds(4 * i, 4)], kv_stage.at[:, pl.ds(rows, kv_size - rows)])
            copy.start()
            copy.wait()
            copy = load(9, kv_stage, kv_term.at[i])
            copy.start()
            copy.wait()

        next(kvw_steps)
        next(outw)
        next(query)

        swapped.wait()

        @pl.loop(0, width // (2 * HD))
        def _(i):
            at = pl.ds(pl.multiple_of(i * 2 * HD, 2 * HD), 2 * HD)
            more = dot(kv_low[...], kvw[at], 1, 1)
            window_sum[i] = part[:, at].astype(f32) + theirs[:, at].astype(f32) + more

        gain_sum[...] = jnp.zeros(gain_sum.shape, f32)
        load(5, grad_in, mask).wait()

        @pl.loop(0, tokens // 16)
        def _(i):
            at = pl.ds(pl.multiple_of(i * 16, 16), 16)
            grad = jnp.concatenate([window_sum[n, at] for n in range(width // (2 * HD))], axis=1)
            stream_rows = low[at].astype(f32)
            scale = lax.rsqrt(
                jnp.mean(stream_rows * stream_rows, axis=1, keepdims=True) + epsilon
            )
            unit = stream_rows * scale
            gain_sum[...] += grad * unit
            scaled = grad * gain[...]
            inner = jnp.mean(scaled * unit, axis=1, keepdims=True)
            mask[at] = mask[at] + scale * (scaled - unit * inner)

        load(5, mask, input_out).start()
        gain_rows[...] = jnp.zeros(gain_rows.shape, f32)
        gain_total = jnp.sum(gain_sum[...], axis=0, keepdims=True)
        for i in range(width // LANES):
            gain_rows[pl.ds(i, 1)] = gain_total[:, i * LANES : (i + 1) * LANES]
        gain_low[...] = gain_rows[...].astype(bf16)

        def gain_send(k):
            to = (me.base + lax.rem(me.r + k, RING), me.t)
            return remote(
                gain_low, gain_all.at[me.r], vector_sems[0].at[k], vector_sems[1].at[me.r], to
            )

        keep_gain = load(9, gain_low, gain_all.at[me.r])
        keep_gain.start()

        @pl.loop(1, RING)
        def _(k):
            gain_send(k).start()

        next(kvw_steps)
        next(query)
        next(kvw_steps)
        for step in (ffn, outw, query, kvw_steps):
            for _ in step:
                pass
        mine = kv_done.at[me.t]
        last = remote(mine, mine, last_sems[0], last_sems[1], me.other())
        last.start()

        @pl.loop(1, RING)
        def _(k):
            gain_send(k).wait_send()
            source = lax.rem(me.r + k, RING)
            landed = gain_all.at[source]
            remote(
                landed, landed, vector_sems[0].at[k], vector_sems[1].at[source], me.at(me.z, me.q)
            ).wait_recv()

        keep_gain.wait()
        load(5, mask, input_out).wait()
        last.wait()
        return []

    term_shape = (LINE, 4, rows, heads * HD)
    ffn_shape = (3, LINE, rows, block)
    half = (2, 2, LINE, rows // 2, heads * HD)
    kv_half = (2, 2, LINE, kv_size // 2, HD)
    ffn_done, out_done, query_done, kv_done, input_grad, gain_all = transfer(
        5,
        [
            middle_low, out_full, mixed_low, queries, kv_all, log_total, normed, query_full, kv_full,
            ffn_kept, ffn_passed, small_terms, middle_grad, inputs,
            window_marks[None], own_marks[:, None], turn_cos, turn_sin, gain_one[None],
        ],
        [
            (ffn_shape, bf16),
            ((LINE, rows, heads * HD), bf16),
            ((LINE, rows, heads * HD), bf16),
            ((2, LINE, kv_size, HD), bf16),
            (inputs.shape, f32),
            ((RING, vector_rows, LANES), bf16),
            (term_shape, bf16),
            (term_shape, bf16),
            ((LINE, 4, kv_size, HD), bf16),
            (kept_shape, bf16),
            (ffn_shape, bf16),
        ]
        + scatter_buffers(rows, heads * HD) * 2
        + scatter_buffers(kv_size, HD),
        [
            FFN_SEMS,
            SCATTER_SEMS,
            SCATTER_SEMS,
            SCATTER_SEMS,
            reduce_scratch(reach + 1, tokens // 2, 2 * HD, f32),
            SWAP_SEMS,
            SWAP_SEMS,
            [pltpu.SemaphoreType.DMA((RING,)), pltpu.SemaphoreType.DMA((RING,))],
            [
                pltpu.VMEM(inputs.shape, bf16),
                pltpu.VMEM(out_full.shape, bf16),
                pltpu.VMEM(queries.shape, bf16),
                pltpu.VMEM(queries.shape, bf16),
                pltpu.VMEM((reach + 1, tokens, 2 * HD), bf16),
                pltpu.VMEM(inputs.shape, bf16),
                pltpu.VMEM((heads, tokens, 1), f32),
                pltpu.VMEM(queries.shape, bf16),
                pltpu.VMEM(queries.shape, bf16),
                pltpu.VMEM((reach + 1, tokens, 2 * HD), f32),
                pltpu.VMEM(inputs.shape, f32),
                pltpu.VMEM((tokens, 2 * HD), f32),
                pltpu.VMEM((tokens, 2 * HD), bf16),
                pltpu.VMEM(kv_full.shape, bf16),
                pltpu.VMEM((4, rows, heads * HD), bf16),
                pltpu.VMEM((4, kv_size, HD), bf16),
                pltpu.VMEM(half, bf16),
                pltpu.VMEM(half, bf16),
                pltpu.VMEM(kv_half, bf16),
                pltpu.VMEM(kv_half, bf16),
                pltpu.VMEM(inputs.shape, bf16),
                pltpu.VMEM(inputs.shape, bf16),
                pltpu.VMEM((16, width), f32),
                pltpu.VMEM((vector_rows, LANES), f32),
                pltpu.VMEM((vector_rows, LANES), bf16),
                pltpu.SemaphoreType.DMA((10,)),
            ],
        ],
        fourth_steps,
        whole=True,
        near=(14, 15, 16, 17, 18),
    )[:6]
    output = (middle + mlp_out.astype(f32) + bias_down).astype(bf16)

    last_skip = LINE * block - hidden_half
    ffn_grad = jnp.concatenate(
        [ffn_done[:, i] for i in range(LINE - 1)] + [ffn_done[:, LINE - 1, :, last_skip:]], axis=2
    )
    ffn_grad = shrink(ffn_grad.astype(f32), 1, groups)
    out_grad = shrink(jnp.sum(out_done.astype(f32), axis=0), 0, groups).T
    query_grad = shrink(jnp.sum(query_done.astype(f32), axis=0), 0, groups)
    kv_sums = jnp.sum(kv_done.astype(f32), axis=1)
    small_sums = lax.dynamic_index_in_dim(kv_sums[:, rows:], t, 0, keepdims=False)
    kv_grad = jnp.concatenate([kv_sums[0, :rows], kv_sums[1, :rows]], axis=1)
    kv_grad = lax.dynamic_index_in_dim(kv_grad.reshape(groups, 2, -1, columns), t, 1, keepdims=False)
    key_value_grad = shrink(kv_grad.reshape(kv_rows, columns), 0, groups)
    gain_sum = jnp.sum(gain_all[:, : width // LANES].astype(f32), axis=0).reshape(
        RING, groups, 2, kv_rows // groups
    )
    gain_sum = lax.dynamic_index_in_dim(gain_sum, r, 0, keepdims=False)
    gain_sum = lax.dynamic_index_in_dim(gain_sum, t, 1, keepdims=False).reshape(kv_rows)
    small_grads = [shrink(v, 0, groups) for v in [gain_sum] + [small_sums[i, :kv_rows] for i in range(3)]]
    gate_up_bias_grad = shrink(small_sums[3:5, : hidden_bias.shape[1]], 1, groups)
    return (
        from_places(output, groups),
        from_places(input_grad, groups),
        small_grads[0],
        query_grad,
        key_value_grad,
        out_grad,
        small_grads[1],
        small_grads[2],
        ffn_grad[:2],
        gate_up_bias_grad,
        ffn_grad[2].T,
        small_grads[3],
    )


def solution(mesh):
    in_specs = (
        P("seq", None),
        P("seq"),
        P("seq", None),
        P(("seq", "tensor")),
        P("seq", "tensor"),
        P(("seq", "tensor"), None),
        P("tensor", "seq"),
        P(("seq", "tensor")),
        P(("seq", "tensor")),
        P(None, "seq", "tensor"),
        P(None, ("seq", "tensor")),
        P("tensor", "seq"),
        P(("seq", "tensor")),
    )
    out_specs = (
        P("seq", None),
        P("seq", None),
        P(("seq", "tensor")),
        P("seq", "tensor"),
        P(("seq", "tensor"), None),
        P("tensor", "seq"),
        P(("seq", "tensor")),
        P(("seq", "tensor")),
        P(None, "seq", "tensor"),
        P(None, ("seq", "tensor")),
        P("tensor", "seq"),
        P(("seq", "tensor")),
    )
    return jax.shard_map(body, mesh=mesh, in_specs=in_specs, out_specs=out_specs, check_vma=False)
```

```python
import functools

import jax
import jax.numpy as jnp
from jax import lax
from jax.experimental import pallas as pl
from jax.experimental.pallas import tpu as pltpu
from jax.sharding import PartitionSpec as P

HD = 256
W = 2048
SEQ_LEN = 4096
LINE = 4
RING = 16
LANES = 128

epsilon = 1e-06
bf16 = jnp.bfloat16
f32 = jnp.float32
MESH = pl.DeviceIdType.MESH
ANY = pl.BlockSpec(memory_space=pl.ANY)
VMEM = pl.BlockSpec(memory_space=pltpu.VMEM)


class Place:
    def __init__(self):
        seq = lax.axis_index("seq")
        self.t = lax.axis_index("tensor")
        self.r = lax.rem(seq, RING)
        self.base = seq - self.r
        self.z = lax.div(self.r, 4)
        self.q = lax.rem(self.r, 4)
        self.xq = self.q + 1 - 2 * lax.rem(self.q, 2)
        self.yq = self.q + 2 - 4 * lax.div(self.q, 2)
        self.dq = 3 - self.q
        self.half = lax.div(self.z, 2)
        self.inner = self.z + self.half * (3 - 2 * self.z)

    def at(self, z, q):
        return (self.base + 4 * z + q, self.t)

    def other(self):
        return (self.base + self.r, 1 - self.t)

    def order(self, j):
        v = j + self.inner * (1 - 2 * j if j < 2 else 0)
        return v + self.half * (3 - 2 * v)

    def greet(self, whole=False):
        barrier = pltpu.get_barrier_semaphore()
        if whole:
            peers = [
                (self.base + lax.rem(self.r + k, RING), self.t) for k in range(1, RING)
            ]
        else:
            peers = [self.at(lax.rem(self.z + k, 4), self.q) for k in range(1, 4)]
            peers += [self.at(self.z, self.xq), self.at(self.z, self.yq)]
        peers.append(self.other())
        for peer in peers:
            pl.semaphore_signal(barrier, inc=1, device_id=peer, device_id_type=MESH)
        pl.semaphore_wait(barrier, len(peers))


def remote(src, dst, send, recv, device):
    return pltpu.make_async_remote_copy(
        src_ref=src, dst_ref=dst, send_sem=send, recv_sem=recv, device_id=device, device_id_type=MESH
    )


def run(steps):
    steps, ending = list(steps), []
    while steps:
        for step in list(steps):
            if next(step, True):
                steps.remove(step)
                ending.append(step)
    for step in ending:
        next(step, None)


GATHER_SEMS = [
    pltpu.SemaphoreType.DMA((4, 6)),
    pltpu.SemaphoreType.DMA((4, 5)),
    pltpu.SemaphoreType.DMA,
]


def gather(me, own, slot, part, sems):
    snd, rcv, loc = sems
    local = pltpu.make_async_copy(own, slot(me.z, me.q), loc)
    local.start()

    def line(z, k, src, to):
        return remote(src, slot(z, me.q), snd.at[z, k], rcv.at[z, 0], me.at(to, me.q))

    @pl.when(me.z < 3)
    def _():
        line(me.z, 0, own, me.z + 1).start()

    @pl.when(me.z > 0)
    def _():
        line(me.z, 1, own, me.z - 1).start()

    def arrive(j):
        z = me.order(j)
        line(z, 0, slot(z, me.q), me.z).wait_recv()

        @pl.when(me.inner == 1)
        def _():
            step = 3 - 2 * me.z if j == 1 else 2 * me.z - 3
            line(z, 0, slot(z, me.q), me.z + step).start()

    yield from in_plane(me, own, slot, part, snd, rcv, arrive)
    local.wait()

    @pl.when(me.z < 3)
    def _():
        line(me.z, 0, own, me.z + 1).wait_send()

    @pl.when(me.z > 0)
    def _():
        line(me.z, 1, own, me.z - 1).wait_send()

    @pl.when(me.inner == 1)
    def _():
        for j in range(1, 4):
            z = me.order(j)
            line(z, 0, slot(z, me.q), me.z).wait_send()


def in_plane(me, own, slot, part, snd, rcv, arrive):
    def across(z, k, src):
        q = (me.xq, me.yq)[k]
        return remote(src, slot(z, me.q), snd.at[z, 2 + k], rcv.at[z, 1 + k], me.at(me.z, q))

    def corner(z, k):
        src = part(z, (me.xq, me.yq)[k], k)
        if src is None:
            return None
        return remote(src, src, snd.at[z, 4 + k], rcv.at[z, 3 + k], me.at(me.z, (me.yq, me.xq)[k]))

    for k in range(2):
        across(me.z, k, own).start()
    yield
    for j in range(1, 5):
        if j < 4:
            arrive(j)
            z = me.order(j)
            for k in range(2):
                across(z, k, slot(z, me.q)).start()
        z = me.order(j - 1)
        for k in range(2):
            q = (me.xq, me.yq)[k]
            remote(
                slot(z, q), slot(z, q), snd.at[z, 2 + k], rcv.at[z, 1 + k], me.at(me.z, q)
            ).wait_recv()
            copy = corner(z, k)
            if copy is not None:
                copy.start()
        yield
    yield True
    for j in range(4):
        z = me.order(j)
        for k in range(2):
            src = part(z, me.dq, k)
            if src is not None:
                remote(src, src, snd.at[z, 4 + k], rcv.at[z, 3 + k], me.at(me.z, me.xq)).wait_recv()
    for j in range(4):
        z = me.order(j)
        for k in range(2):
            across(z, k, slot(z, me.q)).wait_send()
            copy = corner(z, k)
            if copy is not None:
                copy.wait_send()


PIECE_SEMS = [
    pltpu.SemaphoreType.DMA((4, 6)),
    pltpu.SemaphoreType.DMA((4, 5)),
    pltpu.SemaphoreType.DMA((4, 2)),
    pltpu.SemaphoreType.DMA((4, 2)),
]


def gather_pieces(me, sources, dst, sems):
    snd, rcv, piece_snd, piece_rcv = sems
    half = dst.shape[2] // 2

    def slot(z, q):
        return dst.at[:, 4 * z + q]

    def part(z, q, h):
        return dst.at[:, 4 * z + q, pl.ds(h * half, half)]

    def local(n):
        parts, piece = sources[n]
        return pltpu.make_async_copy(piece(me.z), dst.at[parts, me.r], piece_snd.at[me.z, n])

    def send(z, n):
        parts, piece = sources[n]
        return remote(
            piece(z), dst.at[parts, me.r], piece_snd.at[z, n], piece_rcv.at[me.z, n], me.at(z, me.q)
        )

    for n in range(len(sources)):
        local(n).start()
    for j in range(1, 3):
        for n in range(len(sources)):
            send(me.order(j), n).start()
    yield
    for n in range(len(sources)):
        send(me.order(3), n).start()
    yield

    def arrive(j):
        z = me.order(j)
        for n in range(len(sources)):
            view = dst.at[sources[n][0], 4 * z + me.q]
            remote(view, view, piece_snd.at[z, n], piece_rcv.at[z, n], me.at(z, me.q)).wait_recv()

    for n in range(len(sources)):
        local(n).wait()
    yield from in_plane(me, slot(me.z, me.q), slot, part, snd, rcv, arrive)
    for j in range(1, 4):
        for n in range(len(sources)):
            send(me.order(j), n).wait_send()


SPREAD_SEMS = [
    pltpu.SemaphoreType.DMA((4, 3)),
    pltpu.SemaphoreType.DMA((4, 2)),
    pltpu.SemaphoreType.DMA,
]


def spread(me, src, dst, sems):
    snd, rcv, loc = sems
    rows = src.shape[0] // 2
    mine = pl.ds(pl.multiple_of(me.t * rows, rows), rows)
    local = pltpu.make_async_copy(src, dst.at[me.z], loc)
    local.start()

    def slot(z):
        return dst.at[z, mine]

    def line(z, k, source, to):
        return remote(source, slot(z), snd.at[z, k], rcv.at[z, 0], me.at(to, me.q))

    def share(z):
        return remote(slot(z), slot(z), snd.at[z, 2], rcv.at[z, 1], me.other())

    @pl.when(me.z < 3)
    def _():
        line(me.z, 0, src.at[mine], me.z + 1).start()

    @pl.when(me.z > 0)
    def _():
        line(me.z, 1, src.at[mine], me.z - 1).start()

    yield
    for j in range(1, 4):
        z = me.order(j)
        line(z, 0, slot(z), me.z).wait_recv()

        @pl.when(me.inner == 1)
        def _():
            step = 3 - 2 * me.z if j == 1 else 2 * me.z - 3
            line(z, 0, slot(z), me.z + step).start()

        share(z).start()
        yield
    yield True
    other = pl.ds(pl.multiple_of((1 - me.t) * rows, rows), rows)
    for j in range(1, 4):
        z = me.order(j)
        remote(
            dst.at[z, other], dst.at[z, other], snd.at[z, 2], rcv.at[z, 1], me.other()
        ).wait_recv()
        share(z).wait_send()
    local.wait()

    @pl.when(me.z < 3)
    def _():
        line(me.z, 0, src.at[mine], me.z + 1).wait_send()

    @pl.when(me.z > 0)
    def _():
        line(me.z, 1, src.at[mine], me.z - 1).wait_send()

    @pl.when(me.inner == 1)
    def _():
        for j in range(1, 4):
            z = me.order(j)
            line(z, 0, slot(z), me.z).wait_send()


def swap(me, src, dst, sems):
    copy = remote(src, dst, sems[0], sems[1], me.other())
    copy.start()
    yield True
    copy.wait()


SWAP_SEMS = [pltpu.SemaphoreType.DMA, pltpu.SemaphoreType.DMA]


def add_rows(out, terms):
    rows = out.shape[0]
    step = 16

    @pl.loop(0, rows // step)
    def _(i):
        at = pl.ds(pl.multiple_of(i * step, step), step)
        total = terms[0][at].astype(f32)
        for term in terms[1:]:
            total += term[at].astype(f32)
        out[at] = total.astype(out.dtype)


def reduce_scratch(slots, rows, columns, dtype):
    return [
        pltpu.VMEM((slots, rows, columns), bf16),
        pltpu.VMEM((slots, rows, columns), bf16),
        pltpu.VMEM((slots, rows, columns), bf16),
        pltpu.VMEM((rows, columns), dtype),
        pltpu.SemaphoreType.DMA((slots, 3)),
        pltpu.SemaphoreType.DMA((slots, 2)),
        pltpu.SemaphoreType.DMA((3,)),
    ]


def line_sum_scratch(rows, columns):
    return [
        pltpu.VMEM((LINE, 2 * rows, columns), bf16),
        pltpu.VMEM((LINE, rows, columns), bf16),
        pltpu.VMEM((2, 3, rows, columns), bf16),
        pltpu.SemaphoreType.DMA((LINE,)),
        pltpu.SemaphoreType.DMA((LINE,)),
        pltpu.SemaphoreType.DMA((2, 3)),
        pltpu.SemaphoreType.DMA((2, 3)),
        pltpu.SemaphoreType.DMA((3,)),
    ]


class LineSum:
    def __init__(self, me, out, scratch):
        self.me = me
        self.src, self.there, self.landed, *self.sems = scratch
        rows = self.there.shape[1]
        self.mine = pl.ds(pl.multiple_of(me.t * rows, rows), rows)
        self.theirs = pl.ds(pl.multiple_of((1 - me.t) * rows, rows), rows)
        self.out = out

    def here(self, z):
        return self.src.at[z, self.mine]

    def cross(self, z):
        snd, rcv = self.sems[:2]
        source = self.src.at[z, self.theirs]
        return remote(source, self.there.at[z], snd.at[z], rcv.at[z], self.me.other())

    def send(self, way, k, source):
        me = self.me
        snd, rcv = self.sems[2:4]
        to = me.at(me.z + 1 - 2 * way, me.q)
        return remote(source, self.landed.at[way, k], snd.at[way, k], rcv.at[way, k], to)

    def ends(self):
        me = self.me
        end = self.sems[4]
        done = self.here(me.z)
        keep = pltpu.make_async_copy(done, self.out.at[self.mine], end.at[0])
        return keep, remote(done, self.out.at[self.mine], end.at[1], end.at[2], me.other())

    def fold(self, z):
        self.cross(z).wait_recv()
        add_rows(self.here(z), (self.here(z), self.there.at[z]))

    def step(self, k):
        for way in range(2):
            w = self.me.z if way == 0 else 3 - self.me.z
            block = 3 + w - k if way == 0 else k - w

            @pl.when(w <= k)
            def _():
                if k:

                    @pl.when(w < k)
                    def _():
                        self.send(way, k - 1, self.here(0)).wait_send()

                @pl.when(w == 0)
                def _():
                    self.send(way, k, self.here(block)).start()

                if k:

                    @pl.when(w > 0)
                    def _():
                        partial = self.landed.at[way, k - 1]
                        self.send(way, k - 1, partial).wait_recv()
                        add_rows(partial, (partial, self.here(block)))
                        self.send(way, k, partial).start()

    def finish(self):
        for way in range(2):
            w = self.me.z if way == 0 else 3 - self.me.z

            @pl.when(w > 0)
            def _():
                last = self.landed.at[way, 2]
                self.send(way, 2, last).wait_recv()
                here = self.here(self.me.z)
                add_rows(here, (here, last))

            @pl.when(w < 3)
            def _():
                self.send(way, 2, self.here(0)).wait_send()

        for copy in self.ends():
            copy.start()

    def close(self):
        for z in range(LINE):
            self.cross(z).wait_send()
        for copy in self.ends():
            copy.wait()


def reduce_window(me, reach, src, out, scratch):
    here, there, landed, total, snd, rcv, end = scratch
    rows = here.shape[1]
    slots = reach + 1
    mine = pl.ds(pl.multiple_of(me.t * rows, rows), rows)
    theirs = pl.ds(pl.multiple_of((1 - me.t) * rows, rows), rows)
    start = jnp.maximum(me.r - reach, 0)

    def cross(j):
        return remote(src.at[j, theirs], there.at[j], snd.at[j, 0], rcv.at[j, 0], me.other())

    def local(j):
        return pltpu.make_async_copy(src.at[j, mine], here.at[j], snd.at[j, 1])

    def back(k):
        j = me.r - k - start
        return remote(
            here.at[j], landed.at[k], snd.at[k, 2], rcv.at[k, 1], (me.base + me.r - k, me.t)
        )

    for j in range(slots):
        cross(j).start()
        local(j).start()
    yield
    for j in range(slots):
        local(j).wait()
        cross(j).wait_recv()
        add_rows(here.at[j], (here.at[j], there.at[j]))
    for k in range(reach, 0, -1):

        @pl.when(me.r >= k)
        def _():
            back(k).start()

    yield
    add_rows(total, [here.at[me.r - start]])
    for k in range(1, slots):

        @pl.when(me.r + k < RING)
        def _():
            remote(
                landed.at[k], landed.at[k], snd.at[k, 2], rcv.at[k, 1], me.at(me.z, me.q)
            ).wait_recv()
            add_rows(total, (total, landed.at[k]))

    keep = pltpu.make_async_copy(total, out.at[mine], end.at[0])
    give = remote(total, out.at[mine], end.at[1], end.at[2], me.other())
    keep.start()
    give.start()
    yield True
    for j in range(slots):
        cross(j).wait_send()
    for k in range(1, slots):

        @pl.when(me.r >= k)
        def _():
            back(k).wait_send()

    keep.wait()
    give.wait()


PLANE_SEMS = [pltpu.SemaphoreType.DMA((4,)), pltpu.SemaphoreType.DMA((4,))]


def add_blocks(out, more):
    blocks, rows, _ = out.shape
    steps = rows // 16

    @pl.loop(0, blocks * steps)
    def _(i):
        n = lax.div(i, steps)
        at = pl.ds(pl.multiple_of(lax.rem(i, steps) * 16, 16), 16)
        out[n, at] = (out[n, at].astype(f32) + more[n, at].astype(f32)).astype(out.dtype)


def scatter_buffers(rows, columns):
    half = (2, LINE, rows // 2, columns)
    return [((2,) + half, bf16)] + [(half, bf16)] * 3 + [((LINE, rows, columns), bf16)]


SCATTER_SEMS = [
    pltpu.SemaphoreType.DMA((6,)),
    pltpu.SemaphoreType.DMA((6,)),
    pltpu.SemaphoreType.DMA((8,)),
    pltpu.SemaphoreType.DMA((4,)),
    pltpu.SemaphoreType.DMA((4,)),
]


def scatter(me, src, done, buffers, here, there, sems):
    got, kept, passed, got_two, total = buffers
    snd, rcv, loc, line_snd, line_rcv = sems
    half = src.shape[2] // 2
    across = pl.ds(0, src.shape[3])
    first, second = [], []

    def held(ref, h, i):
        return ref.at[h, i, :, :, across]

    for h in range(2):
        q = (me.xq, me.yq)[h]
        rows = pl.ds(h * half, half)
        for i in range(2):
            n = 2 * h + i
            view = src.at[:, (q, me.dq)[i], rows]
            first.append(remote(view, got.at[h, i], snd.at[n], rcv.at[n], me.at(me.z, q)))
        q = (me.yq, me.xq)[h]
        second.append(
            remote(passed.at[h], got_two.at[h], snd.at[4 + h], rcv.at[4 + h], me.at(me.z, q))
        )
    yield
    for copy in first:
        copy.start()
    yield
    for copy in first:
        copy.wait_recv()
    loads, stores = [], []
    for h in range(2):
        for i in range(2):
            n = 2 * h + i
            view = src.at[:, (me.q, (me.yq, me.xq)[h])[i], pl.ds(h * half, half)]
            loads.append(pltpu.make_async_copy(view, held(here, h, i), loc.at[n]))
            loads.append(pltpu.make_async_copy(got.at[h, i], held(there, h, i), loc.at[4 + n]))
            stores.append(
                pltpu.make_async_copy(held(here, h, i), (kept, passed)[i].at[h], loc.at[n])
            )
    for copy in loads:
        copy.start()
    for copy in loads:
        copy.wait()
    for h in range(2):
        for i in range(2):
            add_blocks(held(here, h, i), held(there, h, i))
    for copy in stores:
        copy.start()
    for copy in stores:
        copy.wait()
    for copy in second:
        copy.start()
    yield
    for copy in second:
        copy.wait_recv()
    loads, stores = [], []
    for h in range(2):
        loads.append(pltpu.make_async_copy(kept.at[h], held(here, h, 0), loc.at[h]))
        loads.append(pltpu.make_async_copy(got_two.at[h], held(there, h, 0), loc.at[4 + h]))
        stores.append(
            pltpu.make_async_copy(held(here, h, 0), total.at[:, pl.ds(h * half, half)], loc.at[h])
        )
    for copy in loads:
        copy.start()
    for copy in loads:
        copy.wait()
    for h in range(2):
        add_blocks(held(here, h, 0), held(there, h, 0))
    for copy in stores:
        copy.start()
    for copy in stores:
        copy.wait()

    def send(j):
        z = me.order(j)
        return remote(total.at[z], done.at[me.z], line_snd.at[z], line_rcv.at[me.z], me.at(z, me.q))

    def local():
        return pltpu.make_async_copy(total.at[me.z], done.at[me.z], loc.at[7])

    local().start()
    for j in (3, 2, 1):
        send(j).start()
    yield True
    for j in range(1, 4):
        z = me.order(j)
        remote(done.at[z], done.at[z], line_snd.at[z], line_rcv.at[z], me.at(z, me.q)).wait_recv()
    local().wait()
    for copy in first + second:
        copy.wait_send()
    for j in range(1, 4):
        send(j).wait_send()


PLANE_SUM_SEMS = [
    pltpu.SemaphoreType.DMA((3, 6)),
    pltpu.SemaphoreType.DMA((3, 6)),
    pltpu.SemaphoreType.DMA((4,)),
]


class PlaneSum:
    def __init__(self, me, src, buffers, total, here, there, sems):
        self.me, self.src, self.total = me, src, total
        self.got, self.kept, self.passed, self.got_two = buffers
        self.here, self.there = here, there
        self.snd, self.rcv, self.loc = sems
        self.half = src.shape[3] // 2

    def view(self, part, place, h):
        return self.src.at[part, :, place, pl.ds(h * self.half, self.half)]

    def sends(self, part):
        me = self.me
        copies = []
        for h in range(2):
            q = (me.xq, me.yq)[h]
            for i in range(2):
                n = 2 * h + i
                copies.append(
                    remote(
                        self.view(part, (q, me.dq)[i], h),
                        self.got.at[part, h, i],
                        self.snd.at[part, n],
                        self.rcv.at[part, n],
                        me.at(me.z, q),
                    )
                )
        return copies

    def start(self, part):
        for copy in self.sends(part):
            copy.start()

    def fold(self, part):
        me = self.me
        for copy in self.sends(part):
            copy.wait_recv()
        for h in range(2):
            places = (me.q, (me.yq, me.xq)[h])
            loads, stores = [], []
            for i in range(2):
                a, b = self.here.at[i], self.there.at[i]
                loads.append(pltpu.make_async_copy(self.view(part, places[i], h), a, self.loc.at[i]))
                loads.append(
                    pltpu.make_async_copy(self.got.at[part, h, i], b, self.loc.at[2 + i])
                )
                stores.append(
                    pltpu.make_async_copy(
                        a, (self.kept, self.passed)[i].at[h, part], self.loc.at[i]
                    )
                )
            for copy in loads:
                copy.start()
            for copy in loads:
                copy.wait()
            for i in range(2):
                add_blocks(self.here.at[i], self.there.at[i])
            for copy in stores:
                copy.start()
            for copy in stores:
                copy.wait()

    def second(self, part):
        me = self.me
        return [
            remote(
                self.passed.at[h, part],
                self.got_two.at[h, part],
                self.snd.at[part, 4 + h],
                self.rcv.at[part, 4 + h],
                me.at(me.z, (me.yq, me.xq)[h]),
            )
            for h in range(2)
        ]

    def pass_on(self, part):
        for copy in self.second(part):
            copy.start()

    def fold_again(self, part):
        for copy in self.second(part):
            copy.wait_recv()
        loads, stores = [], []
        for h in range(2):
            a, b = self.here.at[h], self.there.at[h]
            target = self.total.at[part, :, pl.ds(h * self.half, self.half)]
            loads.append(pltpu.make_async_copy(self.kept.at[h, part], a, self.loc.at[h]))
            loads.append(pltpu.make_async_copy(self.got_two.at[h, part], b, self.loc.at[2 + h]))
            stores.append(pltpu.make_async_copy(a, target, self.loc.at[h]))
        for copy in loads:
            copy.start()
        for copy in loads:
            copy.wait()
        for h in range(2):
            add_blocks(self.here.at[h], self.there.at[h])
        for copy in stores:
            copy.start()
        for copy in stores:
            copy.wait()

    def close(self, part):
        for copy in self.sends(part) + self.second(part):
            copy.wait_send()


LINE_SEMS = [pltpu.SemaphoreType.DMA((4,)), pltpu.SemaphoreType.DMA((4,)), pltpu.SemaphoreType.DMA]


def line_exchange(me, src, done, sems):
    snd, rcv, loc = sems
    local = pltpu.make_async_copy(src.at[me.z], done.at[me.z], loc)
    local.start()

    def send(j):
        z = me.order(j)
        return remote(src.at[z], done.at[me.z], snd.at[z], rcv.at[me.z], me.at(z, me.q))

    for j in (3, 2, 1):
        send(j).start()
    yield True
    for j in range(1, 4):
        z = me.order(j)
        remote(done.at[z], done.at[z], snd.at[z], rcv.at[z], me.at(z, me.q)).wait_recv()
    for j in range(1, 4):
        send(j).wait_send()
    local.wait()


def transfer(number, inputs, outputs, scratch, steps, whole=False, near=()):
    flat = [item for group in scratch for item in group]
    sizes = [len(group) for group in scratch]

    def kernel(*refs):
        ins = refs[: len(inputs)]
        outs = refs[len(inputs) : len(inputs) + len(outputs)]
        rest = refs[len(inputs) + len(outputs) :]
        groups = []
        for size in sizes:
            groups.append(rest[:size])
            rest = rest[size:]
        me = Place()
        me.greet(whole)
        run(steps(me, ins, outs, groups))

    return pl.pallas_call(
        kernel,
        out_shape=[jax.ShapeDtypeStruct(shape, dtype) for shape, dtype in outputs],
        in_specs=[VMEM if i in near else ANY for i in range(len(inputs))],
        out_specs=[ANY] * len(outputs),
        scratch_shapes=flat,
        compiler_params=pltpu.CompilerParams(
            collective_id=number, has_side_effects=True, vmem_limit_bytes=62 * 2**20
        ),
    )(*inputs)


def gather_rows(me, src, dst, sems):
    rows = src.shape[0]
    cut = -(-rows // 32) * 16

    def part(z, q, h):
        if cut == rows and h:
            return None
        return dst.at[4 * z + q, pl.ds(h * cut, (rows - cut) if h else cut)]

    return gather(me, src, lambda z, q: dst.at[4 * z + q], part, sems)


def group_lists(groups):
    return [[r + RING * g for g in range(groups)] for r in range(RING)]


def grow(x, axis, groups):
    if groups == 1:
        return x
    return lax.all_gather(x, "seq", axis=axis, tiled=True, axis_index_groups=group_lists(groups))


def shrink(x, axis, groups):
    if groups == 1:
        return x
    return lax.psum_scatter(
        x, "seq", scatter_dimension=axis, tiled=True, axis_index_groups=group_lists(groups)
    )


def to_places(x, groups):
    if groups == 1:
        return x
    return x.reshape(x.shape[0], groups, RING, -1).swapaxes(1, 2).reshape(x.shape)


def from_places(x, groups):
    if groups == 1:
        return x
    return x.reshape(x.shape[0], RING, groups, -1).swapaxes(1, 2).reshape(x.shape)


def normalize(stream, scale_vec):
    return (
        stream * lax.rsqrt(jnp.mean(stream * stream, axis=-1, keepdims=True) + epsilon) * scale_vec
    )


def rotate(values, places, head_count, direction):
    head_size = values.shape[1] // head_count
    shaped = values.reshape(values.shape[0], head_count, head_size)
    quarter = head_size // 4
    first_part = shaped[..., :quarter]
    second = shaped[..., quarter : 2 * quarter]
    remainder = shaped[..., 2 * quarter :]
    frequency = 10000.0 ** (-jnp.arange(quarter, dtype=jnp.float32) / quarter)
    angles = places.astype(jnp.float32)[:, None] * frequency[None, :]
    cosine = jnp.cos(angles)[:, None, :]
    sine_part = direction * jnp.sin(angles)[:, None, :]
    turned = jnp.concatenate(
        [
            first_part * cosine - second * sine_part,
            second * cosine + first_part * sine_part,
            remainder,
        ],
        axis=-1,
    )
    return turned.reshape(values.shape)


def dot(a, b, ca=1, cb=0):
    return lax.dot_general(a, b, (((ca,), (cb,)), ((), ())), preferred_element_type=f32)


def body(
    inputs,
    segment_ids,
    cotangent,
    attn_gain,
    query_weight,
    key_value_weight,
    out_weight,
    out_bias,
    mlp_gain,
    gate_up_weight,
    gate_up_bias,
    down_weight,
    down_bias,
):
    seq_index = lax.axis_index("seq")
    t = lax.axis_index("tensor")
    r = seq_index % RING
    z = r // 4
    q = r % 4
    groups = lax.axis_size("seq") // RING
    tokens, width = inputs.shape
    inputs = to_places(inputs, groups)
    cotangent = to_places(cotangent, groups)
    heads = query_weight.shape[1] // HD
    hidden_half = gate_up_weight.shape[2]
    block = -(-hidden_half // (LINE * LANES)) * LANES
    block_start = jnp.minimum(z * block, hidden_half - block)
    block_skip = z * block - block_start
    reach = (W + tokens - 2) // tokens
    span = (reach + 1) * tokens
    first_block = jnp.maximum(r - reach, 0)
    scale_factor = HD ** (-0.5)
    assert tokens * RING == SEQ_LEN and lax.axis_size("tensor") == 2

    kv_own = grow(key_value_weight, 0, groups)
    kv_rows, columns = kv_own.shape
    vectors = [grow(v, 0, groups) for v in (attn_gain, out_bias, mlp_gain, down_bias)]
    hidden_bias = grow(gate_up_bias, 1, groups)
    marks = jnp.stack([segment_ids // 256, segment_ids % 256]).astype(bf16)

    def pad_to(x, n):
        return jnp.pad(x, ((0, 0), (0, n - x.shape[1])))

    small = jnp.concatenate(
        [
            pad_to(jnp.stack(vectors), columns),
            pad_to(hidden_bias, columns),
            pad_to(marks, columns),
            jnp.zeros((8, columns), bf16),
        ]
    )
    query_own = grow(query_weight, 0, groups)
    out_own = grow(out_weight.T, 0, groups)
    gate_up_own = grow(gate_up_weight, 1, groups)
    down_own = grow(down_weight.T, 0, groups)
    rows = query_own.shape[0]

    def first_steps(me, ins, outs, sems):
        def both(n):
            mine = outs[n].at[:, me.t]
            for _ in gather_rows(me, ins[n], mine, sems[n]):
                yield
            copy = remote(mine, mine, sems[4][0].at[n], sems[4][1].at[n], me.other())
            copy.start()
            yield True
            copy.wait()

        return [
            both(2),
            both(1),
            gather_rows(me, ins[0], outs[0], sems[0]),
            spread(me, ins[3], outs[3], sems[3]),
        ]

    query_full, kv_full, smalls, cot_all = transfer(
        0,
        [query_own, kv_own, small, cotangent],
        [
            ((RING,) + query_own.shape, bf16),
            ((RING, 2) + kv_own.shape, bf16),
            ((RING, 2) + small.shape, bf16),
            ((LINE,) + cotangent.shape, bf16),
        ],
        [
            GATHER_SEMS,
            GATHER_SEMS,
            GATHER_SEMS,
            SPREAD_SEMS,
            [pltpu.SemaphoreType.DMA((3,)), pltpu.SemaphoreType.DMA((3,))],
        ],
        first_steps,
    )
    query_full = query_full.reshape(width, heads * HD)
    if groups > 1:
        kv_full = kv_full.reshape(RING, 2, groups, kv_rows // groups, columns).swapaxes(1, 2)
    kv_full = kv_full.reshape(width, columns)

    def vector(row, count, order):
        piece = smalls[:, :, row, :count].reshape(RING, 2, groups, count // groups)
        return jnp.transpose(piece, order).reshape(-1).astype(f32)

    gain_one, bias_out, gain_two, bias_down = (
        vector(i, kv_rows, (0, 2, 1, 3)) for i in range(4)
    )
    bias_gate_up = jnp.stack(
        [vector(4 + i, hidden_bias.shape[1], (2, 0, 1, 3)) for i in range(2)]
    )
    bias_local = lax.dynamic_slice_in_dim(bias_gate_up, t * hidden_half + block_start, block, 1)
    all_marks = smalls[:, 0, 6:8, :tokens].astype(f32)
    all_marks = (all_marks[:, 0] * 256.0 + all_marks[:, 1]).reshape(-1)
    window_marks = lax.dynamic_slice_in_dim(all_marks, first_block * tokens, span, 0)
    own_marks = lax.dynamic_slice_in_dim(all_marks, r * tokens, tokens, 0)

    stream = inputs.astype(f32)
    places = r * tokens + jnp.arange(tokens, dtype=jnp.int32)
    normed = normalize(stream, gain_one).astype(bf16)
    query_lin = dot(normed, query_full)
    queries = (rotate(query_lin, places, heads, 1.0) * scale_factor).astype(bf16)
    key_value = dot(normed, kv_full)
    keys_own = rotate(key_value[:, :HD], places, 1, 1.0).astype(bf16)
    values_own = key_value[:, HD:].astype(bf16)
    own_block = jnp.concatenate([keys_own, values_own], axis=1)

    def second_steps(me, ins, outs, groups_in):
        own_kv, own_out, own_gate_up, own_down, q_in, x_in, vec, marks_row, marks_column = ins
        kv_all, out_all, ffn_all, mixed_out, log_out, middle_out, normed_out = outs
        kv_sems, out_sems, ffn_sems, spread_sems, swap_sems, scratch = groups_in
        qs, win, weight, mask, mixed, part, theirs, x, middle, normed_two, logs, loads = scratch

        def load(n, src, dst):
            return pltpu.make_async_copy(src, dst, loads.at[n])

        def columns_of(source, lead):
            def piece(place):
                start = jnp.minimum(place * block, hidden_half - block)
                at = pl.ds(pl.multiple_of(start, LANES), block)
                return source.at[:, :, at] if lead else source.at[:, at]

            return piece

        keys = gather_rows(me, own_kv, kv_all, kv_sems)
        outw = gather_rows(me, own_out, out_all, out_sems)
        ffn = gather_pieces(
            me,
            [(pl.ds(0, 2), columns_of(own_gate_up, True)), (2, columns_of(own_down, False))],
            ffn_all,
            ffn_sems,
        )
        next(keys)
        load(0, q_in, qs).start()
        load(1, x_in, x).start()
        next(outw)
        start = jnp.maximum(me.r - reach, 0)
        row_places = me.r * tokens + lax.broadcasted_iota(jnp.int32, (tokens, 1), 0)

        @pl.loop(0, reach + 1)
        def _(i):
            at = pl.ds(pl.multiple_of(i * tokens, tokens), tokens)
            key_places = (start + i) * tokens + lax.broadcasted_iota(jnp.int32, (1, tokens), 1)
            gap = row_places - key_places
            seen = (gap >= 0) & (gap < W) & (marks_column[...] == marks_row[:, at])
            mask[:, at] = jnp.where(seen, 0.0, -1e30)

        next(keys)
        next(keys)
        next(ffn)
        for _ in range(3):
            next(keys)
        next(outw)
        next(keys, None)
        window = load(2, kv_all.at[pl.ds(start, reach + 1)], win)
        window.start()
        load(0, q_in, qs).wait()
        window.wait()

        @pl.loop(0, heads)
        def _(h):
            at = pl.ds(pl.multiple_of(h * HD, HD), HD)
            both = win[...].reshape(span, 2 * HD)
            scores = dot(qs[:, at], both[:, :HD], 1, 1) + mask[...]
            top = jnp.max(scores, axis=1, keepdims=True)
            exponent = jnp.exp(scores - top)
            total = jnp.sum(exponent, axis=1, keepdims=True)
            blend = dot(exponent.astype(bf16), both[:, HD:])
            mixed[:, at] = (blend / total).astype(bf16)
            logs[h] = top + jnp.log(total)
            for i in range(1, heads):

                @pl.when(h == i)
                def _():
                    next(outw if i < 4 else ffn)

        next(ffn)
        for _ in outw:
            pass
        load(3, mixed, mixed_out).start()
        load(4, logs, log_out).start()
        weights = load(2, out_all, weight)
        weights.start()
        weights.wait()

        @pl.loop(0, LINE)
        def _(i):
            at = pl.ds(pl.multiple_of(i * 4 * rows, LANES), 4 * rows)
            piece = weight[pl.ds(4 * i, 4)].reshape(4 * rows, heads * HD)
            part[:, at] = dot(mixed[...], piece, 1, 1).astype(bf16)

        swapped = remote(part, theirs, swap_sems[0], swap_sems[1], me.other())
        swapped.start()
        load(1, x_in, x).wait()
        swapped.wait()

        @pl.loop(0, tokens // 16)
        def _(i):
            at = pl.ds(pl.multiple_of(i * 16, 16), 16)
            total = x[at].astype(f32) + (part[at].astype(f32) + theirs[at].astype(f32)) + vec[0:1]
            middle[at] = total
            scale = lax.rsqrt(jnp.mean(total * total, axis=1, keepdims=True) + epsilon)
            normed_two[at] = (total * scale * vec[1:2]).astype(bf16)

        out = spread(me, normed_two, normed_out, spread_sems)
        next(out)
        load(0, middle, middle_out).start()
        next(ffn)
        next(out)
        next(ffn)
        next(out)
        next(out)
        next(out)
        for step in (ffn, out):
            for _ in step:
                pass
        load(3, mixed, mixed_out).wait()
        load(4, logs, log_out).wait()
        load(0, middle, middle_out).wait()
        return []

    kv_all, out_full, ffn_full, mixed_low, log_total, middle, normed_all = transfer(
        1,
        [
            own_block,
            out_own,
            gate_up_own,
            down_own,
            queries,
            inputs,
            jnp.stack([bias_out, gain_two]),
            window_marks[None],
            own_marks[:, None],
        ],
        [
            ((RING,) + own_block.shape, bf16),
            ((RING,) + out_own.shape, bf16),
            ((3, RING, rows, block), bf16),
            (queries.shape, bf16),
            ((heads, tokens, 1), f32),
            (inputs.shape, f32),
            ((LINE,) + inputs.shape, bf16),
        ],
        [
            GATHER_SEMS,
            GATHER_SEMS,
            PIECE_SEMS,
            SPREAD_SEMS,
            SWAP_SEMS,
            [
                pltpu.VMEM(queries.shape, bf16),
                pltpu.VMEM((reach + 1, tokens, 2 * HD), bf16),
                pltpu.VMEM((RING,) + out_own.shape, bf16),
                pltpu.VMEM((tokens, span), f32),
                pltpu.VMEM(queries.shape, bf16),
                pltpu.VMEM(inputs.shape, bf16),
                pltpu.VMEM(inputs.shape, bf16),
                pltpu.VMEM(inputs.shape, bf16),
                pltpu.VMEM(inputs.shape, f32),
                pltpu.VMEM(inputs.shape, bf16),
                pltpu.VMEM((heads, tokens, 1), f32),
                pltpu.SemaphoreType.DMA((5,)),
            ],
        ],
        second_steps,
        near=(6, 7, 8),
    )
    out_full = out_full.reshape(width, heads * HD)
    ffn_full = ffn_full.reshape(3, width, block)
    key_places = first_block * tokens + jnp.arange(span, dtype=jnp.int32)
    key_gap = places[:, None] - key_places[None, :]
    visible = (key_gap >= 0) & (key_gap < W) & (own_marks[:, None] == window_marks[None, :])
    window = lax.dynamic_slice_in_dim(
        kv_all.reshape(RING * tokens, 2 * HD), first_block * tokens, span, 0
    )
    key_win = window[:, :HD]
    value_win = window[:, HD:]
    query_heads = queries.reshape(tokens, heads, HD)

    def both_cores(number, part):
        (theirs,) = transfer(
            number,
            [part],
            [(part.shape, bf16)],
            [SWAP_SEMS],
            lambda me, ins, outs, sems: [swap(me, ins[0], outs[0], sems[0])],
        )
        return part.astype(f32) + theirs.astype(f32)

    ours = (jnp.arange(block) >= block_skip).astype(f32)[None, :]
    part_rows = 4 * rows
    pace = block // 2

    def third_steps(me, ins, outs, groups_in):
        normed_in, cot_in, weights_in, bias, valid = ins
        normed_grad_out, mlp_out, total, bias_own, bias_theirs, term, *buffers = outs
        one_scratch, two_scratch, plane_sems, swap_sems, scratch = groups_in
        (
            weights, normed_v, cot_v, chunks, hidden, gate_low, up_low, bias_sum, bias_low,
            stage, here, there, loads,
        ) = scratch
        one = LineSum(me, normed_grad_out, one_scratch)
        two = LineSum(me, mlp_out, two_scratch)
        plane = PlaneSum(me, term, buffers, total, here, there, plane_sems)

        def load(n, src, dst):
            return pltpu.make_async_copy(src, dst, loads.at[n])

        def part_columns(i):
            return pl.ds(pl.multiple_of(i * part_rows, LANES), part_rows)

        def rows_of(i):
            return pl.ds(pl.multiple_of(i * tokens, tokens), tokens)

        for n in range(3):
            load(n, weights_in.at[n], weights.at[n]).start()
        load(3, normed_in.at[0], normed_v).start()
        load(4, cot_in.at[0], cot_v).start()
        bias_sum[...] = jnp.zeros(bias_sum.shape, f32)
        for n in range(3):
            load(n, weights_in.at[n], weights.at[n]).wait()

        def both_ways(place):
            load(3, normed_in.at[place], normed_v).wait()
            load(4, cot_in.at[place], cot_v).wait()
            at = rows_of(place)

            @pl.loop(0, 2)
            def _(n):
                part = pl.ds(pl.multiple_of(n * pace, LANES), pace)
                gate = dot(normed_v[...], weights[0, :, part]) + bias[0:1, part]
                up = dot(normed_v[...], weights[1, :, part]) + bias[1:2, part]
                grad = dot(cot_v[...], weights[2, :, part]) * valid[:, part]
                square = gate * gate
                slope = 0.7978845608028654 * (1.0 + 3.0 * 0.044715 * square)
                turn = jnp.tanh(0.7978845608028654 * gate * (1.0 + 0.044715 * square))
                side = 0.5 * (1.0 + turn)
                unit = gate * side
                hidden[at, part] = (unit * up * valid[:, part]).astype(bf16)
                gate_grad = grad * up * (side + 0.5 * gate * (1.0 - turn * turn) * slope)
                gate_low[at, part] = gate_grad.astype(bf16)
                up_low[at, part] = (grad * unit).astype(bf16)
                for i, low in enumerate((gate_low, up_low)):
                    bias_sum[i : i + 1, part] += jnp.sum(
                        low[at, part].astype(f32), axis=0, keepdims=True
                    )

            @pl.when(place < LINE - 1)
            def _():
                load(3, normed_in.at[place + 1], normed_v).start()
                load(4, cot_in.at[place + 1], cot_v).start()

        pl.loop(0, LINE)(both_ways)

        def back(place):
            at = rows_of(place)

            @pl.loop(0, LINE)
            def _(i):
                lines = part_columns(i)
                value = dot(gate_low[at], weights[0, lines], 1, 1)
                value += dot(up_low[at], weights[1, lines], 1, 1)
                one.src[place, :, lines] = value.astype(bf16)

            one.cross(place).start()

        bias_low[...] = bias_sum[...].astype(bf16)
        bias_swap = remote(bias_low, bias_theirs, swap_sems[0], swap_sems[1], me.other())
        bias_swap.start()
        bias_keep = load(0, bias_low, bias_own)
        bias_keep.start()

        def chunk(source, i, slot):
            return load(3 + slot, source.at[:, :, part_columns(i)], chunks.at[slot])

        def stored(n, target):
            return load(1 + n, stage.at[n], target)

        def weight_term(slot, factor, n, target):
            left = chunks[slot].reshape(LINE * tokens, part_rows)
            stage[n] = dot(left, factor[...], 0, 0).astype(bf16).reshape(stage.shape[1:])
            stored(n, target).start()

        def outputs_of(place):
            @pl.loop(0, LINE)
            def _(i):
                lines = part_columns(i)
                value = dot(hidden[rows_of(place)], weights[2, lines], 1, 1)
                two.src[place, :, lines] = value.astype(bf16)

            two.cross(place).start()

        def down_terms(i):
            slot = lax.rem(i, 2)
            chunk(cot_in, i, slot).wait()

            @pl.when(i < LINE - 1)
            def _():
                chunk(cot_in, i + 1, 1 - slot).start()

            @pl.when(i > 1)
            def _():
                stored(slot, term.at[2, i]).wait()

            weight_term(slot, hidden, slot, term.at[2, i])

        def gate_up_terms(i):
            slot = lax.rem(i, 2)
            chunk(normed_in, i, slot).wait()

            @pl.when(i < LINE - 1)
            def _():
                chunk(normed_in, i + 1, 1 - slot).start()

            for n, factor in enumerate((gate_low, up_low)):

                @pl.when(i > 0)
                def _():
                    stored(n, term.at[n, i]).wait()

                weight_term(slot, factor, n, term.at[n, i])

        chunk(cot_in, 0, 0).start()

        @pl.loop(0, 2)
        def _(i):
            outputs_of(3 - 3 * i)

        two.fold(3)
        two.fold(0)
        two.step(0)
        pl.loop(0, LINE)(down_terms)
        chunk(normed_in, 0, 0).start()
        for n in range(2):
            stored(n, term.at[2, 0]).wait()
        plane.start(2)

        @pl.loop(0, 2)
        def _(i):
            outputs_of(2 - i)

        two.fold(2)
        two.fold(1)
        two.step(1)
        pl.loop(0, LINE)(gate_up_terms)
        for n in range(2):
            stored(n, term.at[n, 0]).wait()
        plane.start(0)
        two.step(2)

        @pl.loop(0, 2)
        def _(i):
            back(3 - 3 * i)

        one.fold(3)
        one.fold(0)
        one.step(0)

        @pl.loop(0, 2)
        def _(i):
            back(2 - i)

        one.fold(2)
        one.fold(1)
        two.finish()
        one.step(1)
        plane.fold(2)
        plane.pass_on(2)
        one.step(2)
        plane.fold(0)
        plane.pass_on(0)
        plane.fold_again(2)
        one.finish()
        plane.fold_again(0)
        one.close()
        two.close()
        for part in (0, 2):
            plane.close(part)
        bias_swap.wait()
        bias_keep.wait()
        return []

    half_shape = (2, 3, LINE, rows // 2, block)
    normed_two_grad, mlp_out, ffn_total, hidden_bias_part, bias_theirs, ffn_term = transfer(
        4,
        [normed_all, cot_all, ffn_full, bias_local, ours],
        [
            ((tokens, width), bf16),
            ((tokens, width), bf16),
            ((3, LINE, rows, block), bf16),
            ((16, block), bf16),
            ((16, block), bf16),
            ((3, LINE, 4, rows, block), bf16),
            ((3, 2, 2, LINE, rows // 2, block), bf16),
            (half_shape, bf16),
            (half_shape, bf16),
            (half_shape, bf16),
        ],
        [
            line_sum_scratch(tokens // 2, width),
            line_sum_scratch(tokens // 2, width),
            PLANE_SUM_SEMS,
            SWAP_SEMS,
            [
                pltpu.VMEM((3, width, block), bf16),
                pltpu.VMEM((tokens, width), bf16),
                pltpu.VMEM((tokens, width), bf16),
                pltpu.VMEM((2, LINE, tokens, part_rows), bf16),
                pltpu.VMEM((LINE * tokens, block), bf16),
                pltpu.VMEM((LINE * tokens, block), bf16),
                pltpu.VMEM((LINE * tokens, block), bf16),
                pltpu.VMEM((16, block), f32),
                pltpu.VMEM((16, block), bf16),
                pltpu.VMEM((2, 4, rows, block), bf16),
                pltpu.VMEM((2, LINE, rows // 2, block), bf16),
                pltpu.VMEM((2, LINE, rows // 2, block), bf16),
                pltpu.SemaphoreType.DMA((5,)),
            ],
        ],
        third_steps,
        near=(3, 4),
    )[:6]
    cot_full = cotangent.astype(f32)
    _, norm_two_pull = jax.vjp(normalize, middle, gain_two)
    middle_part, gain_two_grad = norm_two_pull(normed_two_grad.astype(f32))
    middle_grad = cot_full + middle_part
    middle_low = middle_grad.astype(bf16)

    def core_features(full):
        blocks = full.reshape(full.shape[0], RING, groups, 2, -1)
        blocks = lax.dynamic_index_in_dim(blocks, t, 3, keepdims=False)
        return jnp.moveaxis(blocks, 1, 0).reshape(RING, full.shape[0], -1)

    def core_hidden(full):
        blocks = full.reshape(full.shape[0], groups, RING, 2, -1)
        blocks = lax.dynamic_index_in_dim(blocks, t, 3, keepdims=False)
        return jnp.transpose(blocks, (2, 0, 1, 3)).reshape(RING, full.shape[0], -1)

    vector_terms = core_features(
        jnp.stack([jnp.sum(middle_grad, axis=0), gain_two_grad, jnp.sum(cot_full, axis=0)])
    )
    bias_pair = jnp.where(
        t == 0,
        jnp.stack([hidden_bias_part, bias_theirs]),
        jnp.stack([bias_theirs, hidden_bias_part]),
    )[:, :2].astype(f32)
    bias_terms = jnp.zeros((2, 2, hidden_half), f32)
    bias_terms = lax.dynamic_update_slice_in_dim(bias_terms, bias_pair, block_start, 2)
    bias_terms = core_hidden(jnp.swapaxes(bias_terms, 0, 1).reshape(2, -1))

    def widen(x):
        return jnp.pad(x, ((0, 0), (0, 0), (0, HD - x.shape[2])))

    small_terms = jnp.concatenate(
        [widen(vector_terms), widen(bias_terms), jnp.zeros((RING, 27, HD), f32)], axis=1
    ).astype(bf16)

    frequency = 10000.0 ** (-jnp.arange(HD // 4, dtype=f32) / (HD // 4))
    angles = places.astype(f32)[:, None] * frequency[None, :]
    turn_cos = jnp.concatenate([jnp.cos(angles), jnp.cos(angles)], axis=1)
    turn_sin = jnp.concatenate([-jnp.sin(angles), jnp.sin(angles)], axis=1)
    chunk = 3 if (reach + 1) % 3 == 0 else 1
    pieces = (reach + 1) // chunk
    kv_size = rows + small_terms.shape[1]
    vector_rows = -(-width // (LANES * 32)) * 32

    def fourth_steps(me, ins, outs, groups_in):
        (
            low_in, out_in, mixed_in, q_in, kv_in, logs_in, normed_in, query_in, kvw_in,
            ffn_in, total_in, small_in, grad_in, x_in,
            marks_row, marks_column, cos2, sin2, gain,
        ) = ins
        ffn_done, out_done, query_done, kv_done, input_out, gain_all = outs[:6]
        out_term, query_term, kv_term = outs[6:9]
        out_buffers, kv_buffers, ffn_buffers = outs[9:14], outs[14:19], outs[19:24]
        query_buffers = (outs[24:29], outs[29:34])
        (
            line_sems, line_sems_two, ffn_sems, out_sems, query_sems, more_sems, kv_sems, window_scratch, swap_sems, last_sems,
            vector_sems, scratch,
        ) = groups_in
        (
            low, weight, mixed, qs, win, normed_v, logs, mixed_grad, q_grad, window_sum, mask,
            kv_total, kv_low, kvw, stage, kv_stage, here, there, kv_here, kv_there, part, theirs,
            gain_sum, gain_rows, gain_low, loads,
        ) = scratch

        def load(n, src, dst):
            return pltpu.make_async_copy(src, dst, loads.at[n])

        def turn(v, direction):
            first = v[:, : HD // 2]
            turned = first * cos2[...] + direction * (pltpu.roll(first, HD // 4, 1) * sin2[...])
            return jnp.concatenate([turned, v[:, HD // 2 :]], axis=1)

        part_rows = 4 * rows

        def part_columns(i):
            return pl.ds(pl.multiple_of(i * part_rows, LANES), part_rows)

        lines = [
            line_exchange(me, total_in.at[2], ffn_done.at[2], line_sems),
            line_exchange(me, total_in.at[0], ffn_done.at[0], line_sems_two),
        ]
        ffn = scatter(me, ffn_in.at[1], ffn_done.at[1], ffn_buffers, here, there, ffn_sems)
        outw = scatter(me, out_term, out_done, out_buffers, here, there, out_sems)
        query, more = (
            scatter(me, query_term.at[n], query_done.at[n], query_buffers[n], here, there, sems)
            for n, sems in enumerate((query_sems, more_sems))
        )
        kvw_steps = scatter(
            me, kv_term, kv_done.at[me.t], kv_buffers, kv_here, kv_there, kv_sems
        )
        for step in [ffn, outw, query, more, kvw_steps] + lines + [ffn]:
            next(step)
        start = jnp.maximum(me.r - reach, 0)
        first_loads = [
            load(0, low_in, low),
            load(1, mixed_in, mixed),
            load(2, out_in, weight),
            load(3, q_in, qs),
            load(4, kv_in.at[pl.ds(start, reach + 1)], win),
            load(5, logs_in, logs),
            load(6, normed_in, normed_v),
            load(7, kvw_in, kvw),
        ]
        for copy in first_loads:
            copy.start()
        first_loads[0].wait()
        first_loads[1].wait()

        def weight_term(left, right, targets):
            width_of = heads * HD // len(targets)

            @pl.loop(0, LINE)
            def _(i):
                value = dot(left[:, part_columns(i)], right[...], 0, 0).astype(bf16)
                stage[...] = value.reshape(stage.shape)
                copies = [
                    load(8 + n, stage.at[:, :, pl.ds(n * width_of, width_of)], term.at[i])
                    for n, term in enumerate(targets)
                ]
                for copy in copies:
                    copy.start()
                for copy in copies:
                    copy.wait()

        weight_term(low, mixed, [out_term])
        first_loads[2].wait()

        @pl.loop(0, heads)
        def _(h):
            at = pl.ds(pl.multiple_of(h * HD, HD), HD)
            mixed_grad[:, at] = dot(low[...], weight[:, at]).astype(bf16)

        load(2, query_in, weight).start()
        load(0, x_in, low).start()
        row_places = me.r * tokens + lax.broadcasted_iota(jnp.int32, (tokens, 1), 0)

        @pl.loop(0, reach + 1)
        def _(i):
            at = pl.ds(pl.multiple_of(i * tokens, tokens), tokens)
            key_places = (start + i) * tokens + lax.broadcasted_iota(jnp.int32, (1, tokens), 1)
            gap = row_places - key_places
            seen = (gap >= 0) & (gap < W) & (marks_column[...] == marks_row[:, at])
            mask[:, at] = jnp.where(seen, 0.0, -1e30)
            window_sum[i] = jnp.zeros((tokens, 2 * HD), f32)

        for copy in first_loads[3:]:
            copy.wait()

        @pl.loop(0, heads)
        def _(h):
            at = pl.ds(pl.multiple_of(h * HD, HD), HD)
            q_head = qs[:, at]
            grad = mixed_grad[:, at]
            inner = jnp.sum(grad.astype(f32) * mixed[:, at].astype(f32), axis=1, keepdims=True)
            log = logs[h]
            q_sum = jnp.zeros((tokens, HD), f32)
            for c in range(pieces):
                blocks = pl.ds(c * chunk, chunk)
                both = win[blocks].reshape(chunk * tokens, 2 * HD)
                k, v = both[:, :HD], both[:, HD:]
                span_at = pl.ds(c * chunk * tokens, chunk * tokens)
                probs = jnp.exp(dot(q_head, k, 1, 1) + mask[:, span_at] - log)
                value_sum = dot(probs.astype(bf16), grad, 0, 0)
                score_grad = (probs * (dot(grad, v, 1, 1) - inner)).astype(bf16)
                q_sum += dot(score_grad, k)
                key_sum = dot(score_grad, q_head, 0, 0)
                window_sum[blocks, :, :HD] += key_sum.reshape(chunk, tokens, HD)
                window_sum[blocks, :, HD:] += value_sum.reshape(chunk, tokens, HD)
            q_grad[:, at] = (turn(q_sum, -1.0) * scale_factor).astype(bf16)

            @pl.when(h == heads - 1)
            def _():
                next(outw)


        @pl.loop(0, reach + 1)
        def _(i):
            win[i] = window_sum[i].astype(bf16)

        window_steps = reduce_window(me, reach, win, kv_total, window_scratch)
        next(window_steps)
        load(5, grad_in, mask).start()
        next(window_steps)
        weight_term(normed_v, q_grad, [query_term.at[0], query_term.at[1]])
        load(2, query_in, weight).wait()

        @pl.loop(0, LINE)
        def _(i):
            piece = weight[pl.ds(pl.multiple_of(i * part_rows, LANES), part_rows)]
            part[:, part_columns(i)] = dot(q_grad[...], piece, 1, 1).astype(bf16)

        swapped = remote(part, theirs, swap_sems[0], swap_sems[1], me.other())
        swapped.start()
        next(ffn)
        next(window_steps)
        next(window_steps, None)

        kv_low[:, :HD] = turn(kv_total[:, :HD], -1.0).astype(bf16)
        kv_low[:, HD:] = kv_total[:, HD:].astype(bf16)
        ours_at = pl.ds(pl.multiple_of(me.t * HD, HD), HD)
        small_copy = load(0, x_in, low)
        small_copy.wait()

        @pl.loop(0, LINE)
        def _(i):
            value = dot(normed_v[:, part_columns(i)], kv_low[:, ours_at], 0, 0).astype(bf16)
            kv_stage[:, pl.ds(0, rows)] = value.reshape(4, rows, HD)
            copy = load(9, small_in.at[pl.ds(4 * i, 4)], kv_stage.at[:, pl.ds(rows, kv_size - rows)])
            copy.start()
            copy.wait()
            copy = load(9, kv_stage, kv_term.at[i])
            copy.start()
            copy.wait()

        next(outw)
        next(query)
        next(ffn)
        next(more)
        next(kvw_steps)
        next(query)
        next(outw)

        swapped.wait()

        @pl.loop(0, width // (2 * HD))
        def _(i):
            at = pl.ds(pl.multiple_of(i * 2 * HD, 2 * HD), 2 * HD)
            more = dot(kv_low[...], kvw[at], 1, 1)
            window_sum[i] = part[:, at].astype(f32) + theirs[:, at].astype(f32) + more

        gain_sum[...] = jnp.zeros(gain_sum.shape, f32)
        load(5, grad_in, mask).wait()

        @pl.loop(0, tokens // 16)
        def _(i):
            at = pl.ds(pl.multiple_of(i * 16, 16), 16)
            grad = jnp.concatenate([window_sum[n, at] for n in range(width // (2 * HD))], axis=1)
            stream_rows = low[at].astype(f32)
            scale = lax.rsqrt(
                jnp.mean(stream_rows * stream_rows, axis=1, keepdims=True) + epsilon
            )
            unit = stream_rows * scale
            gain_sum[...] += grad * unit
            scaled = grad * gain[...]
            inner = jnp.mean(scaled * unit, axis=1, keepdims=True)
            mask[at] = mask[at] + scale * (scaled - unit * inner)

        load(5, mask, input_out).start()
        gain_rows[...] = jnp.zeros(gain_rows.shape, f32)
        gain_total = jnp.sum(gain_sum[...], axis=0, keepdims=True)
        for i in range(width // LANES):
            gain_rows[pl.ds(i, 1)] = gain_total[:, i * LANES : (i + 1) * LANES]
        gain_low[...] = gain_rows[...].astype(bf16)

        def gain_send(k):
            to = (me.base + lax.rem(me.r + k, RING), me.t)
            return remote(
                gain_low, gain_all.at[me.r], vector_sems[0].at[k], vector_sems[1].at[me.r], to
            )

        keep_gain = load(9, gain_low, gain_all.at[me.r])
        keep_gain.start()

        @pl.loop(1, RING)
        def _(k):
            gain_send(k).start()

        next(more)
        next(kvw_steps)
        next(query)
        next(more)
        next(kvw_steps)
        for step in lines + [ffn, outw, query, more, kvw_steps]:
            for _ in step:
                pass
        mine = kv_done.at[me.t]
        last = remote(mine, mine, last_sems[0], last_sems[1], me.other())
        last.start()

        @pl.loop(1, RING)
        def _(k):
            gain_send(k).wait_send()
            source = lax.rem(me.r + k, RING)
            landed = gain_all.at[source]
            remote(
                landed, landed, vector_sems[0].at[k], vector_sems[1].at[source], me.at(me.z, me.q)
            ).wait_recv()

        keep_gain.wait()
        load(5, mask, input_out).wait()
        last.wait()
        return []

    term_shape = (LINE, 4, rows, heads * HD)
    ffn_shape = (3, LINE, rows, block)
    half = (2, 2, LINE, rows // 2, heads * HD)
    kv_half = (2, 2, LINE, kv_size // 2, HD)
    ffn_done, out_done, query_done, kv_done, input_grad, gain_all = transfer(
        5,
        [
            middle_low, out_full, mixed_low, queries, kv_all, log_total, normed, query_full, kv_full,
            ffn_term, ffn_total, small_terms, middle_grad, inputs,
            window_marks[None], own_marks[:, None], turn_cos, turn_sin, gain_one[None],
        ],
        [
            (ffn_shape, bf16),
            ((LINE, rows, heads * HD), bf16),
            ((2, LINE, rows, heads * HD // 2), bf16),
            ((2, LINE, kv_size, HD), bf16),
            (inputs.shape, f32),
            ((RING, vector_rows, LANES), bf16),
            (term_shape, bf16),
            ((2,) + term_shape[:-1] + (heads * HD // 2,), bf16),
            ((LINE, 4, kv_size, HD), bf16),
        ]
        + scatter_buffers(rows, heads * HD)
        + scatter_buffers(kv_size, HD)
        + scatter_buffers(rows, block)
        + scatter_buffers(rows, heads * HD // 2) * 2,
        [
            LINE_SEMS,
            LINE_SEMS,
            SCATTER_SEMS,
            SCATTER_SEMS,
            SCATTER_SEMS,
            SCATTER_SEMS,
            SCATTER_SEMS,
            reduce_scratch(reach + 1, tokens // 2, 2 * HD, f32),
            SWAP_SEMS,
            SWAP_SEMS,
            [pltpu.SemaphoreType.DMA((RING,)), pltpu.SemaphoreType.DMA((RING,))],
            [
                pltpu.VMEM(inputs.shape, bf16),
                pltpu.VMEM(out_full.shape, bf16),
                pltpu.VMEM(queries.shape, bf16),
                pltpu.VMEM(queries.shape, bf16),
                pltpu.VMEM((reach + 1, tokens, 2 * HD), bf16),
                pltpu.VMEM(inputs.shape, bf16),
                pltpu.VMEM((heads, tokens, 1), f32),
                pltpu.VMEM(queries.shape, bf16),
                pltpu.VMEM(queries.shape, bf16),
                pltpu.VMEM((reach + 1, tokens, 2 * HD), f32),
                pltpu.VMEM(inputs.shape, f32),
                pltpu.VMEM((tokens, 2 * HD), f32),
                pltpu.VMEM((tokens, 2 * HD), bf16),
                pltpu.VMEM(kv_full.shape, bf16),
                pltpu.VMEM((4, rows, heads * HD), bf16),
                pltpu.VMEM((4, kv_size, HD), bf16),
                pltpu.VMEM(half, bf16),
                pltpu.VMEM(half, bf16),
                pltpu.VMEM(kv_half, bf16),
                pltpu.VMEM(kv_half, bf16),
                pltpu.VMEM(inputs.shape, bf16),
                pltpu.VMEM(inputs.shape, bf16),
                pltpu.VMEM((16, width), f32),
                pltpu.VMEM((vector_rows, LANES), f32),
                pltpu.VMEM((vector_rows, LANES), bf16),
                pltpu.SemaphoreType.DMA((10,)),
            ],
        ],
        fourth_steps,
        whole=True,
        near=(14, 15, 16, 17, 18),
    )[:6]
    output = (middle + mlp_out.astype(f32) + bias_down).astype(bf16)

    last_skip = LINE * block - hidden_half
    ffn_grad = jnp.concatenate(
        [ffn_done[:, i] for i in range(LINE - 1)] + [ffn_done[:, LINE - 1, :, last_skip:]], axis=2
    )
    ffn_grad = shrink(ffn_grad.astype(f32), 1, groups)
    out_grad = shrink(jnp.sum(out_done.astype(f32), axis=0), 0, groups).T
    query_sum = jnp.sum(query_done.astype(f32), axis=1)
    query_grad = shrink(jnp.concatenate([query_sum[0], query_sum[1]], axis=1), 0, groups)
    kv_sums = jnp.sum(kv_done.astype(f32), axis=1)
    small_sums = lax.dynamic_index_in_dim(kv_sums[:, rows:], t, 0, keepdims=False)
    kv_grad = jnp.concatenate([kv_sums[0, :rows], kv_sums[1, :rows]], axis=1)
    kv_grad = lax.dynamic_index_in_dim(kv_grad.reshape(groups, 2, -1, columns), t, 1, keepdims=False)
    key_value_grad = shrink(kv_grad.reshape(kv_rows, columns), 0, groups)
    gain_sum = jnp.sum(gain_all[:, : width // LANES].astype(f32), axis=0).reshape(
        RING, groups, 2, kv_rows // groups
    )
    gain_sum = lax.dynamic_index_in_dim(gain_sum, r, 0, keepdims=False)
    gain_sum = lax.dynamic_index_in_dim(gain_sum, t, 1, keepdims=False).reshape(kv_rows)
    small_grads = [shrink(v, 0, groups) for v in [gain_sum] + [small_sums[i, :kv_rows] for i in range(3)]]
    gate_up_bias_grad = shrink(small_sums[3:5, : hidden_bias.shape[1]], 1, groups)
    return (
        from_places(output, groups),
        from_places(input_grad, groups),
        small_grads[0],
        query_grad,
        key_value_grad,
        out_grad,
        small_grads[1],
        small_grads[2],
        ffn_grad[:2],
        gate_up_bias_grad,
        ffn_grad[2].T,
        small_grads[3],
    )


def solution(mesh):
    in_specs = (
        P("seq", None),
        P("seq"),
        P("seq", None),
        P(("seq", "tensor")),
        P("seq", "tensor"),
        P(("seq", "tensor"), None),
        P("tensor", "seq"),
        P(("seq", "tensor")),
        P(("seq", "tensor")),
        P(None, "seq", "tensor"),
        P(None, ("seq", "tensor")),
        P("tensor", "seq"),
        P(("seq", "tensor")),
    )
    out_specs = (
        P("seq", None),
        P("seq", None),
        P(("seq", "tensor")),
        P("seq", "tensor"),
        P(("seq", "tensor"), None),
        P("tensor", "seq"),
        P(("seq", "tensor")),
        P(("seq", "tensor")),
        P(None, "seq", "tensor"),
        P(None, ("seq", "tensor")),
        P("tensor", "seq"),
        P(("seq", "tensor")),
    )
    return jax.shard_map(body, mesh=mesh, in_specs=in_specs, out_specs=out_specs, check_vma=False)
```

```python
import functools

import jax
import jax.numpy as jnp
from jax import lax
from jax.experimental import pallas as pl
from jax.experimental.pallas import tpu as pltpu
from jax.sharding import PartitionSpec as P

HD = 256
W = 2048
SEQ_LEN = 4096
LINE = 4
RING = 16
LANES = 128

epsilon = 1e-06
bf16 = jnp.bfloat16
f32 = jnp.float32
MESH = pl.DeviceIdType.MESH
ANY = pl.BlockSpec(memory_space=pl.ANY)
VMEM = pl.BlockSpec(memory_space=pltpu.VMEM)


class Place:
    def __init__(self):
        seq = lax.axis_index("seq")
        self.t = lax.axis_index("tensor")
        self.r = lax.rem(seq, RING)
        self.base = seq - self.r
        self.z = lax.div(self.r, 4)
        self.q = lax.rem(self.r, 4)
        self.xq = self.q + 1 - 2 * lax.rem(self.q, 2)
        self.yq = self.q + 2 - 4 * lax.div(self.q, 2)
        self.dq = 3 - self.q
        self.half = lax.div(self.z, 2)
        self.inner = self.z + self.half * (3 - 2 * self.z)

    def at(self, z, q):
        return (self.base + 4 * z + q, self.t)

    def other(self):
        return (self.base + self.r, 1 - self.t)

    def order(self, j):
        v = j + self.inner * (1 - 2 * j if j < 2 else 0)
        return v + self.half * (3 - 2 * v)

    def greet(self, whole=False):
        barrier = pltpu.get_barrier_semaphore()
        if whole:
            peers = [
                (self.base + lax.rem(self.r + k, RING), self.t) for k in range(1, RING)
            ]
        else:
            peers = [self.at(lax.rem(self.z + k, 4), self.q) for k in range(1, 4)]
            peers += [self.at(self.z, self.xq), self.at(self.z, self.yq)]
        peers.append(self.other())
        for peer in peers:
            pl.semaphore_signal(barrier, inc=1, device_id=peer, device_id_type=MESH)
        pl.semaphore_wait(barrier, len(peers))


def remote(src, dst, send, recv, device):
    return pltpu.make_async_remote_copy(
        src_ref=src, dst_ref=dst, send_sem=send, recv_sem=recv, device_id=device, device_id_type=MESH
    )


def run(steps):
    steps, ending = list(steps), []
    while steps:
        for step in list(steps):
            if next(step, True):
                steps.remove(step)
                ending.append(step)
    for step in ending:
        next(step, None)


GATHER_SEMS = [
    pltpu.SemaphoreType.DMA((4, 6)),
    pltpu.SemaphoreType.DMA((4, 5)),
    pltpu.SemaphoreType.DMA,
]


def gather(me, own, slot, part, sems):
    snd, rcv, loc = sems
    local = pltpu.make_async_copy(own, slot(me.z, me.q), loc)
    local.start()

    def line(z, k, src, to):
        return remote(src, slot(z, me.q), snd.at[z, k], rcv.at[z, 0], me.at(to, me.q))

    @pl.when(me.z < 3)
    def _():
        line(me.z, 0, own, me.z + 1).start()

    @pl.when(me.z > 0)
    def _():
        line(me.z, 1, own, me.z - 1).start()

    def arrive(j):
        z = me.order(j)
        line(z, 0, slot(z, me.q), me.z).wait_recv()

        @pl.when(me.inner == 1)
        def _():
            step = 3 - 2 * me.z if j == 1 else 2 * me.z - 3
            line(z, 0, slot(z, me.q), me.z + step).start()

    yield from in_plane(me, own, slot, part, snd, rcv, arrive)
    local.wait()

    @pl.when(me.z < 3)
    def _():
        line(me.z, 0, own, me.z + 1).wait_send()

    @pl.when(me.z > 0)
    def _():
        line(me.z, 1, own, me.z - 1).wait_send()

    @pl.when(me.inner == 1)
    def _():
        for j in range(1, 4):
            z = me.order(j)
            line(z, 0, slot(z, me.q), me.z).wait_send()


def in_plane(me, own, slot, part, snd, rcv, arrive):
    def across(z, k, src):
        q = (me.xq, me.yq)[k]
        return remote(src, slot(z, me.q), snd.at[z, 2 + k], rcv.at[z, 1 + k], me.at(me.z, q))

    def corner(z, k):
        src = part(z, (me.xq, me.yq)[k], k)
        if src is None:
            return None
        return remote(src, src, snd.at[z, 4 + k], rcv.at[z, 3 + k], me.at(me.z, (me.yq, me.xq)[k]))

    for k in range(2):
        across(me.z, k, own).start()
    yield
    for j in range(1, 5):
        if j < 4:
            arrive(j)
            z = me.order(j)
            for k in range(2):
                across(z, k, slot(z, me.q)).start()
        z = me.order(j - 1)
        for k in range(2):
            q = (me.xq, me.yq)[k]
            remote(
                slot(z, q), slot(z, q), snd.at[z, 2 + k], rcv.at[z, 1 + k], me.at(me.z, q)
            ).wait_recv()
            copy = corner(z, k)
            if copy is not None:
                copy.start()
        yield
    yield True
    for j in range(4):
        z = me.order(j)
        for k in range(2):
            src = part(z, me.dq, k)
            if src is not None:
                remote(src, src, snd.at[z, 4 + k], rcv.at[z, 3 + k], me.at(me.z, me.xq)).wait_recv()
    for j in range(4):
        z = me.order(j)
        for k in range(2):
            across(z, k, slot(z, me.q)).wait_send()
            copy = corner(z, k)
            if copy is not None:
                copy.wait_send()


PIECE_SEMS = [
    pltpu.SemaphoreType.DMA((4, 6)),
    pltpu.SemaphoreType.DMA((4, 5)),
    pltpu.SemaphoreType.DMA((4, 2)),
    pltpu.SemaphoreType.DMA((4, 2)),
]


def gather_pieces(me, sources, dst, sems):
    snd, rcv, piece_snd, piece_rcv = sems
    half = dst.shape[2] // 2

    def slot(z, q):
        return dst.at[:, 4 * z + q]

    def part(z, q, h):
        return dst.at[:, 4 * z + q, pl.ds(h * half, half)]

    def local(n):
        parts, piece = sources[n]
        return pltpu.make_async_copy(piece(me.z), dst.at[parts, me.r], piece_snd.at[me.z, n])

    def send(z, n):
        parts, piece = sources[n]
        return remote(
            piece(z), dst.at[parts, me.r], piece_snd.at[z, n], piece_rcv.at[me.z, n], me.at(z, me.q)
        )

    for n in range(len(sources)):
        local(n).start()
    for j in range(1, 3):
        for n in range(len(sources)):
            send(me.order(j), n).start()
    yield
    for n in range(len(sources)):
        send(me.order(3), n).start()
    yield

    def arrive(j):
        z = me.order(j)
        for n in range(len(sources)):
            view = dst.at[sources[n][0], 4 * z + me.q]
            remote(view, view, piece_snd.at[z, n], piece_rcv.at[z, n], me.at(z, me.q)).wait_recv()

    for n in range(len(sources)):
        local(n).wait()
    yield from in_plane(me, slot(me.z, me.q), slot, part, snd, rcv, arrive)
    for j in range(1, 4):
        for n in range(len(sources)):
            send(me.order(j), n).wait_send()


SPREAD_SEMS = [
    pltpu.SemaphoreType.DMA((4, 3)),
    pltpu.SemaphoreType.DMA((4, 2)),
    pltpu.SemaphoreType.DMA,
]


def spread(me, src, dst, sems):
    snd, rcv, loc = sems
    rows = src.shape[0] // 2
    mine = pl.ds(pl.multiple_of(me.t * rows, rows), rows)
    local = pltpu.make_async_copy(src, dst.at[me.z], loc)
    local.start()

    def slot(z):
        return dst.at[z, mine]

    def line(z, k, source, to):
        return remote(source, slot(z), snd.at[z, k], rcv.at[z, 0], me.at(to, me.q))

    def share(z):
        return remote(slot(z), slot(z), snd.at[z, 2], rcv.at[z, 1], me.other())

    @pl.when(me.z < 3)
    def _():
        line(me.z, 0, src.at[mine], me.z + 1).start()

    @pl.when(me.z > 0)
    def _():
        line(me.z, 1, src.at[mine], me.z - 1).start()

    yield
    for j in range(1, 4):
        z = me.order(j)
        line(z, 0, slot(z), me.z).wait_recv()

        @pl.when(me.inner == 1)
        def _():
            step = 3 - 2 * me.z if j == 1 else 2 * me.z - 3
            line(z, 0, slot(z), me.z + step).start()

        share(z).start()
        yield
    yield True
    other = pl.ds(pl.multiple_of((1 - me.t) * rows, rows), rows)
    for j in range(1, 4):
        z = me.order(j)
        remote(
            dst.at[z, other], dst.at[z, other], snd.at[z, 2], rcv.at[z, 1], me.other()
        ).wait_recv()
        share(z).wait_send()
    local.wait()

    @pl.when(me.z < 3)
    def _():
        line(me.z, 0, src.at[mine], me.z + 1).wait_send()

    @pl.when(me.z > 0)
    def _():
        line(me.z, 1, src.at[mine], me.z - 1).wait_send()

    @pl.when(me.inner == 1)
    def _():
        for j in range(1, 4):
            z = me.order(j)
            line(z, 0, slot(z), me.z).wait_send()


def swap(me, src, dst, sems):
    copy = remote(src, dst, sems[0], sems[1], me.other())
    copy.start()
    yield True
    copy.wait()


SWAP_SEMS = [pltpu.SemaphoreType.DMA, pltpu.SemaphoreType.DMA]


def add_rows(out, terms):
    rows = out.shape[0]
    step = 16

    @pl.loop(0, rows // step)
    def _(i):
        at = pl.ds(pl.multiple_of(i * step, step), step)
        total = terms[0][at].astype(f32)
        for term in terms[1:]:
            total += term[at].astype(f32)
        out[at] = total.astype(out.dtype)


def reduce_scratch(slots, rows, columns, dtype):
    return [
        pltpu.VMEM((slots, rows, columns), bf16),
        pltpu.VMEM((slots, rows, columns), bf16),
        pltpu.VMEM((slots, rows, columns), bf16),
        pltpu.VMEM((rows, columns), dtype),
        pltpu.SemaphoreType.DMA((slots, 3)),
        pltpu.SemaphoreType.DMA((slots, 2)),
        pltpu.SemaphoreType.DMA((3,)),
    ]


def line_sum_scratch(rows, columns):
    return [
        pltpu.VMEM((LINE, 2 * rows, columns), bf16),
        pltpu.VMEM((LINE, rows, columns), bf16),
        pltpu.VMEM((2, 3, rows, columns), bf16),
        pltpu.SemaphoreType.DMA((LINE,)),
        pltpu.SemaphoreType.DMA((LINE,)),
        pltpu.SemaphoreType.DMA((2, 3)),
        pltpu.SemaphoreType.DMA((2, 3)),
        pltpu.SemaphoreType.DMA((3,)),
    ]


class LineSum:
    def __init__(self, me, out, scratch):
        self.me = me
        self.src, self.there, self.landed, *self.sems = scratch
        rows = self.there.shape[1]
        self.mine = pl.ds(pl.multiple_of(me.t * rows, rows), rows)
        self.theirs = pl.ds(pl.multiple_of((1 - me.t) * rows, rows), rows)
        self.out = out

    def here(self, z):
        return self.src.at[z, self.mine]

    def cross(self, z):
        snd, rcv = self.sems[:2]
        source = self.src.at[z, self.theirs]
        return remote(source, self.there.at[z], snd.at[z], rcv.at[z], self.me.other())

    def send(self, way, k, source):
        me = self.me
        snd, rcv = self.sems[2:4]
        to = me.at(me.z + 1 - 2 * way, me.q)
        return remote(source, self.landed.at[way, k], snd.at[way, k], rcv.at[way, k], to)

    def ends(self):
        me = self.me
        end = self.sems[4]
        done = self.here(me.z)
        keep = pltpu.make_async_copy(done, self.out.at[self.mine], end.at[0])
        return keep, remote(done, self.out.at[self.mine], end.at[1], end.at[2], me.other())

    def fold(self, z):
        self.cross(z).wait_recv()
        add_rows(self.here(z), (self.here(z), self.there.at[z]))

    def step(self, k):
        for way in range(2):
            w = self.me.z if way == 0 else 3 - self.me.z
            block = 3 + w - k if way == 0 else k - w

            @pl.when(w <= k)
            def _():
                if k:

                    @pl.when(w < k)
                    def _():
                        self.send(way, k - 1, self.here(0)).wait_send()

                @pl.when(w == 0)
                def _():
                    self.send(way, k, self.here(block)).start()

                if k:

                    @pl.when(w > 0)
                    def _():
                        partial = self.landed.at[way, k - 1]
                        self.send(way, k - 1, partial).wait_recv()
                        add_rows(partial, (partial, self.here(block)))
                        self.send(way, k, partial).start()

    def finish(self):
        for way in range(2):
            w = self.me.z if way == 0 else 3 - self.me.z

            @pl.when(w > 0)
            def _():
                last = self.landed.at[way, 2]
                self.send(way, 2, last).wait_recv()
                here = self.here(self.me.z)
                add_rows(here, (here, last))

            @pl.when(w < 3)
            def _():
                self.send(way, 2, self.here(0)).wait_send()

        for copy in self.ends():
            copy.start()

    def close(self):
        for z in range(LINE):
            self.cross(z).wait_send()
        for copy in self.ends():
            copy.wait()


def reduce_window(me, reach, src, out, scratch):
    here, there, landed, total, snd, rcv, end = scratch
    rows = here.shape[1]
    slots = reach + 1
    mine = pl.ds(pl.multiple_of(me.t * rows, rows), rows)
    theirs = pl.ds(pl.multiple_of((1 - me.t) * rows, rows), rows)
    start = jnp.maximum(me.r - reach, 0)

    def cross(j):
        return remote(src.at[j, theirs], there.at[j], snd.at[j, 0], rcv.at[j, 0], me.other())

    def local(j):
        return pltpu.make_async_copy(src.at[j, mine], here.at[j], snd.at[j, 1])

    def back(k):
        j = me.r - k - start
        return remote(
            here.at[j], landed.at[k], snd.at[k, 2], rcv.at[k, 1], (me.base + me.r - k, me.t)
        )

    for j in range(slots):
        cross(j).start()
        local(j).start()
    yield
    for j in range(slots):
        local(j).wait()
        cross(j).wait_recv()
        add_rows(here.at[j], (here.at[j], there.at[j]))
    for k in range(reach, 0, -1):

        @pl.when(me.r >= k)
        def _():
            back(k).start()

    yield
    add_rows(total, [here.at[me.r - start]])
    for k in range(1, slots):

        @pl.when(me.r + k < RING)
        def _():
            remote(
                landed.at[k], landed.at[k], snd.at[k, 2], rcv.at[k, 1], me.at(me.z, me.q)
            ).wait_recv()
            add_rows(total, (total, landed.at[k]))

    keep = pltpu.make_async_copy(total, out.at[mine], end.at[0])
    give = remote(total, out.at[mine], end.at[1], end.at[2], me.other())
    keep.start()
    give.start()
    yield True
    for j in range(slots):
        cross(j).wait_send()
    for k in range(1, slots):

        @pl.when(me.r >= k)
        def _():
            back(k).wait_send()

    keep.wait()
    give.wait()


PLANE_SEMS = [pltpu.SemaphoreType.DMA((4,)), pltpu.SemaphoreType.DMA((4,))]


def add_blocks(out, more):
    blocks, rows, _ = out.shape
    steps = rows // 16

    @pl.loop(0, blocks * steps)
    def _(i):
        n = lax.div(i, steps)
        at = pl.ds(pl.multiple_of(lax.rem(i, steps) * 16, 16), 16)
        out[n, at] = (out[n, at].astype(f32) + more[n, at].astype(f32)).astype(out.dtype)


def scatter_buffers(rows, columns):
    half = (2, LINE, rows // 2, columns)
    return [((2,) + half, bf16)] + [(half, bf16)] * 3 + [((LINE, rows, columns), bf16)]


SCATTER_SEMS = [
    pltpu.SemaphoreType.DMA((6,)),
    pltpu.SemaphoreType.DMA((6,)),
    pltpu.SemaphoreType.DMA((8,)),
    pltpu.SemaphoreType.DMA((4,)),
    pltpu.SemaphoreType.DMA((4,)),
]


def scatter(me, src, done, buffers, here, there, sems):
    got, kept, passed, got_two, total = buffers
    snd, rcv, loc, line_snd, line_rcv = sems
    half = src.shape[2] // 2
    across = pl.ds(0, src.shape[3])
    first, second = [], []

    def held(ref, h, i):
        return ref.at[h, i, :, :, across]

    for h in range(2):
        q = (me.xq, me.yq)[h]
        rows = pl.ds(h * half, half)
        for i in range(2):
            n = 2 * h + i
            view = src.at[:, (q, me.dq)[i], rows]
            first.append(remote(view, got.at[h, i], snd.at[n], rcv.at[n], me.at(me.z, q)))
        q = (me.yq, me.xq)[h]
        second.append(
            remote(passed.at[h], got_two.at[h], snd.at[4 + h], rcv.at[4 + h], me.at(me.z, q))
        )
    yield
    for copy in first:
        copy.start()
    yield
    for copy in first:
        copy.wait_recv()
    loads, stores = [], []
    for h in range(2):
        for i in range(2):
            n = 2 * h + i
            view = src.at[:, (me.q, (me.yq, me.xq)[h])[i], pl.ds(h * half, half)]
            loads.append(pltpu.make_async_copy(view, held(here, h, i), loc.at[n]))
            loads.append(pltpu.make_async_copy(got.at[h, i], held(there, h, i), loc.at[4 + n]))
            stores.append(
                pltpu.make_async_copy(held(here, h, i), (kept, passed)[i].at[h], loc.at[n])
            )
    for copy in loads:
        copy.start()
    for copy in loads:
        copy.wait()
    for h in range(2):
        for i in range(2):
            add_blocks(held(here, h, i), held(there, h, i))
    for copy in stores:
        copy.start()
    for copy in stores:
        copy.wait()
    for copy in second:
        copy.start()
    yield
    for copy in second:
        copy.wait_recv()
    loads, stores = [], []
    for h in range(2):
        loads.append(pltpu.make_async_copy(kept.at[h], held(here, h, 0), loc.at[h]))
        loads.append(pltpu.make_async_copy(got_two.at[h], held(there, h, 0), loc.at[4 + h]))
        stores.append(
            pltpu.make_async_copy(held(here, h, 0), total.at[:, pl.ds(h * half, half)], loc.at[h])
        )
    for copy in loads:
        copy.start()
    for copy in loads:
        copy.wait()
    for h in range(2):
        add_blocks(held(here, h, 0), held(there, h, 0))
    for copy in stores:
        copy.start()
    for copy in stores:
        copy.wait()

    def send(j):
        z = me.order(j)
        return remote(total.at[z], done.at[me.z], line_snd.at[z], line_rcv.at[me.z], me.at(z, me.q))

    def local():
        return pltpu.make_async_copy(total.at[me.z], done.at[me.z], loc.at[7])

    local().start()
    for j in (3, 2, 1):
        send(j).start()
    yield True
    for j in range(1, 4):
        z = me.order(j)
        remote(done.at[z], done.at[z], line_snd.at[z], line_rcv.at[z], me.at(z, me.q)).wait_recv()
    local().wait()
    for copy in first + second:
        copy.wait_send()
    for j in range(1, 4):
        send(j).wait_send()


PLANE_SUM_SEMS = [
    pltpu.SemaphoreType.DMA((3, 6)),
    pltpu.SemaphoreType.DMA((3, 6)),
    pltpu.SemaphoreType.DMA((4,)),
]


class PlaneSum:
    def __init__(self, me, src, buffers, total, here, there, sems):
        self.me, self.src, self.total = me, src, total
        self.got, self.kept, self.passed, self.got_two = buffers
        self.here, self.there = here, there
        self.snd, self.rcv, self.loc = sems
        self.half = src.shape[3] // 2

    def view(self, part, place, h):
        return self.src.at[part, :, place, pl.ds(h * self.half, self.half)]

    def sends(self, part):
        me = self.me
        copies = []
        for h in range(2):
            q = (me.xq, me.yq)[h]
            for i in range(2):
                n = 2 * h + i
                copies.append(
                    remote(
                        self.view(part, (q, me.dq)[i], h),
                        self.got.at[part, h, i],
                        self.snd.at[part, n],
                        self.rcv.at[part, n],
                        me.at(me.z, q),
                    )
                )
        return copies

    def start(self, part):
        for copy in self.sends(part):
            copy.start()

    def fold(self, part):
        me = self.me
        for copy in self.sends(part):
            copy.wait_recv()
        for h in range(2):
            places = (me.q, (me.yq, me.xq)[h])
            loads, stores = [], []
            for i in range(2):
                a, b = self.here.at[i], self.there.at[i]
                loads.append(pltpu.make_async_copy(self.view(part, places[i], h), a, self.loc.at[i]))
                loads.append(
                    pltpu.make_async_copy(self.got.at[part, h, i], b, self.loc.at[2 + i])
                )
                stores.append(
                    pltpu.make_async_copy(
                        a, (self.kept, self.passed)[i].at[h, part], self.loc.at[i]
                    )
                )
            for copy in loads:
                copy.start()
            for copy in loads:
                copy.wait()
            for i in range(2):
                add_blocks(self.here.at[i], self.there.at[i])
            for copy in stores:
                copy.start()
            for copy in stores:
                copy.wait()

    def second(self, part):
        me = self.me
        return [
            remote(
                self.passed.at[h, part],
                self.got_two.at[h, part],
                self.snd.at[part, 4 + h],
                self.rcv.at[part, 4 + h],
                me.at(me.z, (me.yq, me.xq)[h]),
            )
            for h in range(2)
        ]

    def pass_on(self, part):
        for copy in self.second(part):
            copy.start()

    def fold_again(self, part):
        for copy in self.second(part):
            copy.wait_recv()
        loads, stores = [], []
        for h in range(2):
            a, b = self.here.at[h], self.there.at[h]
            target = self.total.at[part, :, pl.ds(h * self.half, self.half)]
            loads.append(pltpu.make_async_copy(self.kept.at[h, part], a, self.loc.at[h]))
            loads.append(pltpu.make_async_copy(self.got_two.at[h, part], b, self.loc.at[2 + h]))
            stores.append(pltpu.make_async_copy(a, target, self.loc.at[h]))
        for copy in loads:
            copy.start()
        for copy in loads:
            copy.wait()
        for h in range(2):
            add_blocks(self.here.at[h], self.there.at[h])
        for copy in stores:
            copy.start()
        for copy in stores:
            copy.wait()

    def close(self, part):
        for copy in self.sends(part) + self.second(part):
            copy.wait_send()


LINE_SEMS = [pltpu.SemaphoreType.DMA((4,)), pltpu.SemaphoreType.DMA((4,)), pltpu.SemaphoreType.DMA]


def line_exchange(me, src, done, sems):
    snd, rcv, loc = sems
    local = pltpu.make_async_copy(src.at[me.z], done.at[me.z], loc)
    local.start()

    def send(j):
        z = me.order(j)
        return remote(src.at[z], done.at[me.z], snd.at[z], rcv.at[me.z], me.at(z, me.q))

    for j in (3, 2, 1):
        send(j).start()
    yield True
    for j in range(1, 4):
        z = me.order(j)
        remote(done.at[z], done.at[z], snd.at[z], rcv.at[z], me.at(z, me.q)).wait_recv()
    for j in range(1, 4):
        send(j).wait_send()
    local.wait()


def transfer(number, inputs, outputs, scratch, steps, whole=False, near=()):
    flat = [item for group in scratch for item in group]
    sizes = [len(group) for group in scratch]

    def kernel(*refs):
        ins = refs[: len(inputs)]
        outs = refs[len(inputs) : len(inputs) + len(outputs)]
        rest = refs[len(inputs) + len(outputs) :]
        groups = []
        for size in sizes:
            groups.append(rest[:size])
            rest = rest[size:]
        me = Place()
        me.greet(whole)
        run(steps(me, ins, outs, groups))

    return pl.pallas_call(
        kernel,
        out_shape=[jax.ShapeDtypeStruct(shape, dtype) for shape, dtype in outputs],
        in_specs=[VMEM if i in near else ANY for i in range(len(inputs))],
        out_specs=[ANY] * len(outputs),
        scratch_shapes=flat,
        compiler_params=pltpu.CompilerParams(
            collective_id=number, has_side_effects=True, vmem_limit_bytes=62 * 2**20
        ),
    )(*inputs)


def gather_rows(me, src, dst, sems):
    rows = src.shape[0]
    cut = -(-rows // 32) * 16

    def part(z, q, h):
        if cut == rows and h:
            return None
        return dst.at[4 * z + q, pl.ds(h * cut, (rows - cut) if h else cut)]

    return gather(me, src, lambda z, q: dst.at[4 * z + q], part, sems)


def group_lists(groups):
    return [[r + RING * g for g in range(groups)] for r in range(RING)]


def grow(x, axis, groups):
    if groups == 1:
        return x
    return lax.all_gather(x, "seq", axis=axis, tiled=True, axis_index_groups=group_lists(groups))


def shrink(x, axis, groups):
    if groups == 1:
        return x
    return lax.psum_scatter(
        x, "seq", scatter_dimension=axis, tiled=True, axis_index_groups=group_lists(groups)
    )


def to_places(x, groups):
    if groups == 1:
        return x
    return x.reshape(x.shape[0], groups, RING, -1).swapaxes(1, 2).reshape(x.shape)


def from_places(x, groups):
    if groups == 1:
        return x
    return x.reshape(x.shape[0], RING, groups, -1).swapaxes(1, 2).reshape(x.shape)


def normalize(stream, scale_vec):
    return (
        stream * lax.rsqrt(jnp.mean(stream * stream, axis=-1, keepdims=True) + epsilon) * scale_vec
    )


def rotate(values, places, head_count, direction):
    head_size = values.shape[1] // head_count
    shaped = values.reshape(values.shape[0], head_count, head_size)
    quarter = head_size // 4
    first_part = shaped[..., :quarter]
    second = shaped[..., quarter : 2 * quarter]
    remainder = shaped[..., 2 * quarter :]
    frequency = 10000.0 ** (-jnp.arange(quarter, dtype=jnp.float32) / quarter)
    angles = places.astype(jnp.float32)[:, None] * frequency[None, :]
    cosine = jnp.cos(angles)[:, None, :]
    sine_part = direction * jnp.sin(angles)[:, None, :]
    turned = jnp.concatenate(
        [
            first_part * cosine - second * sine_part,
            second * cosine + first_part * sine_part,
            remainder,
        ],
        axis=-1,
    )
    return turned.reshape(values.shape)


def dot(a, b, ca=1, cb=0):
    return lax.dot_general(a, b, (((ca,), (cb,)), ((), ())), preferred_element_type=f32)


def body(
    inputs,
    segment_ids,
    cotangent,
    attn_gain,
    query_weight,
    key_value_weight,
    out_weight,
    out_bias,
    mlp_gain,
    gate_up_weight,
    gate_up_bias,
    down_weight,
    down_bias,
):
    seq_index = lax.axis_index("seq")
    t = lax.axis_index("tensor")
    r = seq_index % RING
    z = r // 4
    q = r % 4
    groups = lax.axis_size("seq") // RING
    tokens, width = inputs.shape
    inputs = to_places(inputs, groups)
    cotangent = to_places(cotangent, groups)
    heads = query_weight.shape[1] // HD
    hidden_half = gate_up_weight.shape[2]
    block = -(-hidden_half // (LINE * LANES)) * LANES
    block_start = jnp.minimum(z * block, hidden_half - block)
    block_skip = z * block - block_start
    reach = (W + tokens - 2) // tokens
    span = (reach + 1) * tokens
    first_block = jnp.maximum(r - reach, 0)
    scale_factor = HD ** (-0.5)
    assert tokens * RING == SEQ_LEN and lax.axis_size("tensor") == 2

    def own_features(x):
        if groups == 1:
            return x
        both = lax.all_gather(x, "tensor", axis=0)
        both = lax.all_gather(both, "seq", axis=0, axis_index_groups=group_lists(groups))
        both = both.reshape((2, -1) + x.shape[1:])
        return lax.dynamic_index_in_dim(both, t, 0, keepdims=False)

    kv_own = own_features(key_value_weight)
    kv_rows, columns = kv_own.shape
    vectors = [own_features(v) for v in (attn_gain, out_bias, mlp_gain, down_bias)]
    hidden_bias = grow(gate_up_bias, 1, groups)
    marks = jnp.stack([segment_ids // 256, segment_ids % 256]).astype(bf16)

    def pad_to(x, n):
        return jnp.pad(x, ((0, 0), (0, n - x.shape[1])))

    small = jnp.concatenate(
        [
            pad_to(jnp.stack(vectors), columns),
            pad_to(hidden_bias, columns),
            pad_to(marks, columns),
            jnp.zeros((8, columns), bf16),
        ]
    )
    query_own = grow(query_weight, 0, groups)
    out_own = grow(out_weight.T, 0, groups)
    gate_up_own = grow(gate_up_weight, 1, groups)
    down_own = grow(down_weight.T, 0, groups)
    rows = query_own.shape[0]
    places = r * tokens + jnp.arange(tokens, dtype=jnp.int32)
    frequency = 10000.0 ** (-jnp.arange(HD // 4, dtype=f32) / (HD // 4))
    angles = places.astype(f32)[:, None] * frequency[None, :]
    turn_cos = jnp.concatenate([jnp.cos(angles), jnp.cos(angles)], axis=1)
    turn_sin = jnp.concatenate([-jnp.sin(angles), jnp.sin(angles)], axis=1)
    own_marks = segment_ids.astype(f32)[:, None]
    feature = jnp.arange(width)[None, :]
    pick_device = (feature // kv_rows == jnp.arange(2 * RING)[:, None]).astype(bf16)
    pick_entry = (feature % kv_rows == jnp.arange(LANES)[:, None]).astype(bf16)

    def first_steps(me, ins, outs, groups_in):
        (
            own_query, own_kvw, own_small, own_out, own_gate_up, own_down, x_in, cot_in,
            marks_column, cos2, sin2, device_of, entry_of,
        ) = ins
        (
            query_all, kvw_all, small_all, kv_all, out_all, ffn_all, cot_out, mixed_out, log_out,
            middle_out, normed_two_out, queries_out, normed_out, vec_out, marks_out,
        ) = outs
        (
            query_sems, kvw_sems, small_sems, kv_sems, out_sems, ffn_sems, cot_sems, spread_sems,
            swap_sems, scratch,
        ) = groups_in
        (
            qs, win, weight, kvw, mask, mixed, part, theirs, x, middle, normed, normed_two, logs,
            small, small_wide, vec, marks_row, kv_low, loads,
        ) = scratch

        def load(n, src, dst):
            return pltpu.make_async_copy(src, dst, loads.at[n])

        def turn(v):
            first = v[:, : HD // 2]
            turned = first * cos2[...] + pltpu.roll(first, HD // 4, 1) * sin2[...]
            return jnp.concatenate([turned, v[:, HD // 2 :]], axis=1)

        def columns_of(source, lead):
            def piece(place):
                at = jnp.minimum(place * block, hidden_half - block)
                at = pl.ds(pl.multiple_of(at, LANES), block)
                return source.at[:, :, at] if lead else source.at[:, at]

            return piece

        def share(n, ref):
            mine = ref.at[:, me.t]
            return remote(mine, mine, swap_sems[0].at[n], swap_sems[1].at[n], me.other())

        smalls = gather_rows(me, own_small, small_all.at[:, me.t], small_sems)
        kvws = gather_rows(me, own_kvw, kvw_all.at[:, me.t], kvw_sems)
        queries = gather_rows(me, own_query, query_all, query_sems)
        keys = gather_rows(me, kv_low, kv_all, kv_sems)
        outw = gather_rows(me, own_out, out_all, out_sems)
        ffn = gather_pieces(
            me,
            [(pl.ds(0, 2), columns_of(own_gate_up, True)), (2, columns_of(own_down, False))],
            ffn_all,
            ffn_sems,
        )
        cot = spread(me, cot_in, cot_out, cot_sems)
        load(0, x_in, x).start()
        for n in range(5):
            next(smalls)
            next(kvws)
            next(queries)
            if n == 3:
                next(outw)
        next(ffn)
        for _ in smalls:
            pass
        share(0, small_all).start()
        for _ in kvws:
            pass
        share(1, kvw_all).start()
        share(0, small_all).wait()
        load(1, small_all, small).start()
        load(1, small_all, small).wait()
        small_wide[...] = small[...].reshape(small_wide.shape).astype(f32)
        vec[...] = jnp.zeros(vec.shape, f32)
        for i in range(4):
            piece = small_wide[:, i, :LANES].astype(bf16)
            spread_out = dot(piece, device_of[...], 0, 0) * entry_of[...].astype(f32)
            vec[i : i + 1] = jnp.sum(spread_out, axis=0, keepdims=True)
        start = jnp.maximum(me.r - reach, 0)
        row_places = me.r * tokens + lax.broadcasted_iota(jnp.int32, (tokens, 1), 0)

        @pl.loop(0, reach + 1)
        def _(i):
            at = pl.ds(pl.multiple_of(i * tokens, tokens), tokens)
            high = small_wide[2 * (start + i), 6:7, :tokens]
            low = small_wide[2 * (start + i), 7:8, :tokens]
            key_marks = high * 256.0 + low
            marks_row[:, at] = key_marks
            key_places = (start + i) * tokens + lax.broadcasted_iota(jnp.int32, (1, tokens), 1)
            gap = row_places - key_places
            seen = (gap >= 0) & (gap < W) & (marks_column[...] == key_marks)
            mask[:, at] = jnp.where(seen, 0.0, -1e30)

        load(1, vec, vec_out).start()
        load(2, marks_row, marks_out).start()
        load(0, x_in, x).wait()

        @pl.loop(0, tokens // 16)
        def _(i):
            at = pl.ds(pl.multiple_of(i * 16, 16), 16)
            value = x[at].astype(f32)
            scale = lax.rsqrt(jnp.mean(value * value, axis=1, keepdims=True) + epsilon)
            normed[at] = (value * scale * vec[0:1]).astype(bf16)

        load(0, normed, normed_out).start()
        share(1, kvw_all).wait()
        load(3, kvw_all, kvw).start()
        load(3, kvw_all, kvw).wait()
        both = dot(normed[...], kvw[...].reshape(width, 2 * HD))
        kv_low[:, :HD] = turn(both[:, :HD]).astype(bf16)
        kv_low[:, HD:] = both[:, HD:].astype(bf16)
        next(keys)
        for _ in queries:
            pass
        load(3, query_all, weight).start()
        load(3, query_all, weight).wait()

        @pl.loop(0, heads)
        def _(h):
            at = pl.ds(pl.multiple_of(h * HD, HD), HD)
            value = dot(normed[...], weight[:, :, at].reshape(width, HD))
            qs[:, at] = (turn(value) * scale_factor).astype(bf16)

        load(4, qs, queries_out).start()
        for _ in range(3):
            next(outw)
            next(keys)
        for _ in keys:
            pass
        load(3, kv_all.at[pl.ds(start, reach + 1)], win).start()
        load(3, kv_all.at[pl.ds(start, reach + 1)], win).wait()

        @pl.loop(0, heads)
        def _(h):
            at = pl.ds(pl.multiple_of(h * HD, HD), HD)
            window = win[...].reshape(span, 2 * HD)
            scores = dot(qs[:, at], window[:, :HD], 1, 1) + mask[...]
            top = jnp.max(scores, axis=1, keepdims=True)
            exponent = jnp.exp(scores - top)
            total = jnp.sum(exponent, axis=1, keepdims=True)
            blend = dot(exponent.astype(bf16), window[:, HD:])
            mixed[:, at] = (blend / total).astype(bf16)
            logs[h] = top + jnp.log(total)

        load(5, mixed, mixed_out).start()
        load(6, logs, log_out).start()
        next(ffn)
        next(outw)
        next(ffn)
        for _ in outw:
            pass
        load(3, out_all, weight).start()
        load(3, out_all, weight).wait()

        @pl.loop(0, LINE)
        def _(i):
            at = pl.ds(pl.multiple_of(i * 4 * rows, LANES), 4 * rows)
            piece = weight[pl.ds(4 * i, 4)].reshape(4 * rows, heads * HD)
            part[:, at] = dot(mixed[...], piece, 1, 1).astype(bf16)

        swapped = remote(part, theirs, swap_sems[0].at[2], swap_sems[1].at[2], me.other())
        swapped.start()
        swapped.wait()

        @pl.loop(0, tokens // 16)
        def _(i):
            at = pl.ds(pl.multiple_of(i * 16, 16), 16)
            total = x[at].astype(f32) + (part[at].astype(f32) + theirs[at].astype(f32)) + vec[1:2]
            middle[at] = total
            scale = lax.rsqrt(jnp.mean(total * total, axis=1, keepdims=True) + epsilon)
            normed_two[at] = (total * scale * vec[2:3]).astype(bf16)

        out = spread(me, normed_two, normed_two_out, spread_sems)
        next(out)
        load(7, middle, middle_out).start()
        next(ffn)
        next(out)
        next(ffn)
        next(out)
        next(out)
        next(cot)
        next(ffn)
        for _ in range(3):
            next(cot)
        for step in (ffn, out, cot):
            for _ in step:
                pass
        for n, src, dst in (
            (0, normed, normed_out),
            (1, vec, vec_out),
            (2, marks_row, marks_out),
            (4, qs, queries_out),
            (5, mixed, mixed_out),
            (6, logs, log_out),
            (7, middle, middle_out),
        ):
            load(n, src, dst).wait()
        return []

    query_shape = (tokens, heads * HD)
    (
        query_full, kv_full, smalls, kv_all, out_full, ffn_full, cot_all, mixed_low, log_total,
        middle, normed_all, queries, normed, vec, window_marks,
    ) = transfer(
        0,
        [
            query_own, kv_own, small, out_own, gate_up_own, down_own, inputs, cotangent,
            own_marks, turn_cos, turn_sin, pick_device, pick_entry,
        ],
        [
            ((RING,) + query_own.shape, bf16),
            ((RING, 2) + kv_own.shape, bf16),
            ((RING, 2) + small.shape, bf16),
            ((RING, tokens, 2 * HD), bf16),
            ((RING,) + out_own.shape, bf16),
            ((3, RING, rows, block), bf16),
            ((LINE,) + inputs.shape, bf16),
            (query_shape, bf16),
            ((heads, tokens, 1), f32),
            (inputs.shape, f32),
            ((LINE,) + inputs.shape, bf16),
            (query_shape, bf16),
            (inputs.shape, bf16),
            ((8, width), f32),
            ((1, span), f32),
        ],
        [
            GATHER_SEMS,
            GATHER_SEMS,
            GATHER_SEMS,
            GATHER_SEMS,
            GATHER_SEMS,
            PIECE_SEMS,
            SPREAD_SEMS,
            SPREAD_SEMS,
            [pltpu.SemaphoreType.DMA((3,)), pltpu.SemaphoreType.DMA((3,))],
            [
                pltpu.VMEM(query_shape, bf16),
                pltpu.VMEM((reach + 1, tokens, 2 * HD), bf16),
                pltpu.VMEM((RING,) + out_own.shape, bf16),
                pltpu.VMEM((RING, 2) + kv_own.shape, bf16),
                pltpu.VMEM((tokens, span), f32),
                pltpu.VMEM(query_shape, bf16),
                pltpu.VMEM(inputs.shape, bf16),
                pltpu.VMEM(inputs.shape, bf16),
                pltpu.VMEM(inputs.shape, bf16),
                pltpu.VMEM(inputs.shape, f32),
                pltpu.VMEM(inputs.shape, bf16),
                pltpu.VMEM(inputs.shape, bf16),
                pltpu.VMEM((heads, tokens, 1), f32),
                pltpu.VMEM((RING, 2) + small.shape, bf16),
                pltpu.VMEM((2 * RING,) + small.shape, f32),
                pltpu.VMEM((8, width), f32),
                pltpu.VMEM((1, span), f32),
                pltpu.VMEM((tokens, 2 * HD), bf16),
                pltpu.SemaphoreType.DMA((8,)),
            ],
        ],
        first_steps,
        near=(8, 9, 10, 11, 12),
    )
    query_full = query_full.reshape(width, heads * HD)
    kv_full = kv_full.reshape(width, columns)
    out_full = out_full.reshape(width, heads * HD)
    ffn_full = ffn_full.reshape(3, width, block)
    gain_one, _, gain_two, bias_down = (vec[i] for i in range(4))
    stream = inputs.astype(f32)

    def hidden_vector(row):
        piece = smalls[:, :, row, : hidden_bias.shape[1]].reshape(RING, 2, groups, -1)
        return jnp.transpose(piece, (2, 0, 1, 3)).reshape(-1).astype(f32)

    bias_gate_up = jnp.stack([hidden_vector(4 + i) for i in range(2)])
    bias_local = lax.dynamic_slice_in_dim(bias_gate_up, t * hidden_half + block_start, block, 1)

    ours = (jnp.arange(block) >= block_skip).astype(f32)[None, :]
    part_rows = 4 * rows
    pace = block // 2

    def third_steps(me, ins, outs, groups_in):
        normed_in, cot_in, weights_in, bias, valid = ins
        normed_grad_out, mlp_out, total, bias_own, bias_theirs, term, *buffers = outs
        one_scratch, two_scratch, plane_sems, swap_sems, scratch = groups_in
        (
            weights, normed_v, cot_v, chunks, hidden, gate_low, up_low, bias_sum, bias_low,
            stage, here, there, loads,
        ) = scratch
        one = LineSum(me, normed_grad_out, one_scratch)
        two = LineSum(me, mlp_out, two_scratch)
        plane = PlaneSum(me, term, buffers, total, here, there, plane_sems)

        def load(n, src, dst):
            return pltpu.make_async_copy(src, dst, loads.at[n])

        def part_columns(i):
            return pl.ds(pl.multiple_of(i * part_rows, LANES), part_rows)

        def rows_of(i):
            return pl.ds(pl.multiple_of(i * tokens, tokens), tokens)

        for n in range(3):
            load(n, weights_in.at[n], weights.at[n]).start()
        load(3, normed_in.at[0], normed_v).start()
        load(4, cot_in.at[0], cot_v).start()
        bias_sum[...] = jnp.zeros(bias_sum.shape, f32)
        for n in range(3):
            load(n, weights_in.at[n], weights.at[n]).wait()

        def both_ways(place):
            load(3, normed_in.at[place], normed_v).wait()
            load(4, cot_in.at[place], cot_v).wait()
            at = rows_of(place)

            @pl.loop(0, 2)
            def _(n):
                part = pl.ds(pl.multiple_of(n * pace, LANES), pace)
                gate = dot(normed_v[...], weights[0, :, part]) + bias[0:1, part]
                up = dot(normed_v[...], weights[1, :, part]) + bias[1:2, part]
                grad = dot(cot_v[...], weights[2, :, part]) * valid[:, part]
                square = gate * gate
                slope = 0.7978845608028654 * (1.0 + 3.0 * 0.044715 * square)
                turn = jnp.tanh(0.7978845608028654 * gate * (1.0 + 0.044715 * square))
                side = 0.5 * (1.0 + turn)
                unit = gate * side
                hidden[at, part] = (unit * up * valid[:, part]).astype(bf16)
                gate_grad = grad * up * (side + 0.5 * gate * (1.0 - turn * turn) * slope)
                gate_low[at, part] = gate_grad.astype(bf16)
                up_low[at, part] = (grad * unit).astype(bf16)
                for i, low in enumerate((gate_low, up_low)):
                    bias_sum[i : i + 1, part] += jnp.sum(
                        low[at, part].astype(f32), axis=0, keepdims=True
                    )

            @pl.when(place < LINE - 1)
            def _():
                load(3, normed_in.at[place + 1], normed_v).start()
                load(4, cot_in.at[place + 1], cot_v).start()

        pl.loop(0, LINE)(both_ways)

        def back(place):
            at = rows_of(place)

            @pl.loop(0, LINE)
            def _(i):
                lines = part_columns(i)
                value = dot(gate_low[at], weights[0, lines], 1, 1)
                value += dot(up_low[at], weights[1, lines], 1, 1)
                one.src[place, :, lines] = value.astype(bf16)

            one.cross(place).start()

        bias_low[...] = bias_sum[...].astype(bf16)
        bias_swap = remote(bias_low, bias_theirs, swap_sems[0], swap_sems[1], me.other())
        bias_swap.start()
        bias_keep = load(0, bias_low, bias_own)
        bias_keep.start()

        def chunk(source, i, slot):
            return load(3 + slot, source.at[:, :, part_columns(i)], chunks.at[slot])

        def stored(n, target):
            return load(1 + n, stage.at[n], target)

        def weight_term(slot, factor, n, target):
            left = chunks[slot].reshape(LINE * tokens, part_rows)
            stage[n] = dot(left, factor[...], 0, 0).astype(bf16).reshape(stage.shape[1:])
            stored(n, target).start()

        def outputs_of(place):
            @pl.loop(0, LINE)
            def _(i):
                lines = part_columns(i)
                value = dot(hidden[rows_of(place)], weights[2, lines], 1, 1)
                two.src[place, :, lines] = value.astype(bf16)

            two.cross(place).start()

        def down_terms(i):
            slot = lax.rem(i, 2)
            chunk(cot_in, i, slot).wait()

            @pl.when(i < LINE - 1)
            def _():
                chunk(cot_in, i + 1, 1 - slot).start()

            @pl.when(i > 1)
            def _():
                stored(slot, term.at[2, i]).wait()

            weight_term(slot, hidden, slot, term.at[2, i])

        def gate_up_terms(i):
            slot = lax.rem(i, 2)
            chunk(normed_in, i, slot).wait()

            @pl.when(i < LINE - 1)
            def _():
                chunk(normed_in, i + 1, 1 - slot).start()

            for n, factor in enumerate((gate_low, up_low)):

                @pl.when(i > 0)
                def _():
                    stored(n, term.at[n, i]).wait()

                weight_term(slot, factor, n, term.at[n, i])

        chunk(cot_in, 0, 0).start()

        @pl.loop(0, 2)
        def _(i):
            outputs_of(3 - 3 * i)

        two.fold(3)
        two.fold(0)
        two.step(0)
        pl.loop(0, LINE)(down_terms)
        chunk(normed_in, 0, 0).start()
        for n in range(2):
            stored(n, term.at[2, 0]).wait()
        plane.start(2)

        @pl.loop(0, 2)
        def _(i):
            outputs_of(2 - i)

        two.fold(2)
        two.fold(1)
        two.step(1)
        pl.loop(0, LINE)(gate_up_terms)
        for n in range(2):
            stored(n, term.at[n, 0]).wait()
        plane.start(0)
        two.step(2)

        @pl.loop(0, 2)
        def _(i):
            back(3 - 3 * i)

        one.fold(3)
        one.fold(0)
        one.step(0)

        @pl.loop(0, 2)
        def _(i):
            back(2 - i)

        one.fold(2)
        one.fold(1)
        two.finish()
        one.step(1)
        plane.fold(2)
        plane.pass_on(2)
        one.step(2)
        plane.fold(0)
        plane.pass_on(0)
        plane.fold_again(2)
        one.finish()
        plane.fold_again(0)
        one.close()
        two.close()
        for part in (0, 2):
            plane.close(part)
        bias_swap.wait()
        bias_keep.wait()
        return []

    half_shape = (2, 3, LINE, rows // 2, block)
    normed_two_grad, mlp_out, ffn_total, hidden_bias_part, bias_theirs, ffn_term = transfer(
        1,
        [normed_all, cot_all, ffn_full, bias_local, ours],
        [
            ((tokens, width), bf16),
            ((tokens, width), bf16),
            ((3, LINE, rows, block), bf16),
            ((16, block), bf16),
            ((16, block), bf16),
            ((3, LINE, 4, rows, block), bf16),
            ((3, 2, 2, LINE, rows // 2, block), bf16),
            (half_shape, bf16),
            (half_shape, bf16),
            (half_shape, bf16),
        ],
        [
            line_sum_scratch(tokens // 2, width),
            line_sum_scratch(tokens // 2, width),
            PLANE_SUM_SEMS,
            SWAP_SEMS,
            [
                pltpu.VMEM((3, width, block), bf16),
                pltpu.VMEM((tokens, width), bf16),
                pltpu.VMEM((tokens, width), bf16),
                pltpu.VMEM((2, LINE, tokens, part_rows), bf16),
                pltpu.VMEM((LINE * tokens, block), bf16),
                pltpu.VMEM((LINE * tokens, block), bf16),
                pltpu.VMEM((LINE * tokens, block), bf16),
                pltpu.VMEM((16, block), f32),
                pltpu.VMEM((16, block), bf16),
                pltpu.VMEM((2, 4, rows, block), bf16),
                pltpu.VMEM((2, LINE, rows // 2, block), bf16),
                pltpu.VMEM((2, LINE, rows // 2, block), bf16),
                pltpu.SemaphoreType.DMA((5,)),
            ],
        ],
        third_steps,
        near=(3, 4),
    )[:6]
    cot_full = cotangent.astype(f32)
    _, norm_two_pull = jax.vjp(normalize, middle, gain_two)
    middle_part, gain_two_grad = norm_two_pull(normed_two_grad.astype(f32))
    middle_grad = cot_full + middle_part
    middle_low = middle_grad.astype(bf16)

    def core_features(full):
        blocks = full.reshape(full.shape[0], RING, groups, 2, -1)
        blocks = lax.dynamic_index_in_dim(blocks, t, 3, keepdims=False)
        return jnp.moveaxis(blocks, 1, 0).reshape(RING, full.shape[0], -1)

    def core_hidden(full):
        blocks = full.reshape(full.shape[0], groups, RING, 2, -1)
        blocks = lax.dynamic_index_in_dim(blocks, t, 3, keepdims=False)
        return jnp.transpose(blocks, (2, 0, 1, 3)).reshape(RING, full.shape[0], -1)

    vector_terms = core_features(
        jnp.stack([jnp.sum(middle_grad, axis=0), gain_two_grad, jnp.sum(cot_full, axis=0)])
    )
    bias_pair = jnp.where(
        t == 0,
        jnp.stack([hidden_bias_part, bias_theirs]),
        jnp.stack([bias_theirs, hidden_bias_part]),
    )[:, :2].astype(f32)
    bias_terms = jnp.zeros((2, 2, hidden_half), f32)
    bias_terms = lax.dynamic_update_slice_in_dim(bias_terms, bias_pair, block_start, 2)
    bias_terms = core_hidden(jnp.swapaxes(bias_terms, 0, 1).reshape(2, -1))

    def widen(x):
        return jnp.pad(x, ((0, 0), (0, 0), (0, HD - x.shape[2])))

    small_terms = jnp.concatenate(
        [widen(vector_terms), widen(bias_terms), jnp.zeros((RING, 27, HD), f32)], axis=1
    ).astype(bf16)

    chunk = 3 if (reach + 1) % 3 == 0 else 1
    pieces = (reach + 1) // chunk
    kv_size = rows + small_terms.shape[1]
    vector_rows = -(-width // (LANES * 32)) * 32

    def fourth_steps(me, ins, outs, groups_in):
        (
            low_in, out_in, mixed_in, q_in, kv_in, logs_in, normed_in, query_in, kvw_in,
            ffn_in, total_in, small_in, grad_in, x_in,
            marks_row, marks_column, cos2, sin2, gain,
        ) = ins
        ffn_done, out_done, query_done, kv_done, input_out, gain_all = outs[:6]
        out_term, query_term, kv_term = outs[6:9]
        out_buffers, kv_buffers, ffn_buffers = outs[9:14], outs[14:19], outs[19:24]
        query_buffers = (outs[24:29], outs[29:34])
        (
            line_sems, line_sems_two, ffn_sems, out_sems, query_sems, more_sems, kv_sems, window_scratch, swap_sems, last_sems,
            vector_sems, scratch,
        ) = groups_in
        (
            low, weight, mixed, qs, win, normed_v, logs, mixed_grad, q_grad, window_sum, mask,
            kv_total, kv_low, kvw, stage, kv_stage, here, there, kv_here, kv_there, part, theirs,
            gain_sum, gain_rows, gain_low, loads,
        ) = scratch

        def load(n, src, dst):
            return pltpu.make_async_copy(src, dst, loads.at[n])

        def turn(v, direction):
            first = v[:, : HD // 2]
            turned = first * cos2[...] + direction * (pltpu.roll(first, HD // 4, 1) * sin2[...])
            return jnp.concatenate([turned, v[:, HD // 2 :]], axis=1)

        part_rows = 4 * rows

        def part_columns(i):
            return pl.ds(pl.multiple_of(i * part_rows, LANES), part_rows)

        lines = [
            line_exchange(me, total_in.at[2], ffn_done.at[2], line_sems),
            line_exchange(me, total_in.at[0], ffn_done.at[0], line_sems_two),
        ]
        ffn = scatter(me, ffn_in.at[1], ffn_done.at[1], ffn_buffers, here, there, ffn_sems)
        outw = scatter(me, out_term, out_done, out_buffers, here, there, out_sems)
        query, more = (
            scatter(me, query_term.at[n], query_done.at[n], query_buffers[n], here, there, sems)
            for n, sems in enumerate((query_sems, more_sems))
        )
        kvw_steps = scatter(
            me, kv_term, kv_done.at[me.t], kv_buffers, kv_here, kv_there, kv_sems
        )
        for step in [ffn, outw, query, more, kvw_steps] + lines + [ffn]:
            next(step)
        start = jnp.maximum(me.r - reach, 0)
        first_loads = [
            load(0, low_in, low),
            load(1, mixed_in, mixed),
            load(2, out_in, weight),
            load(3, q_in, qs),
            load(4, kv_in.at[pl.ds(start, reach + 1)], win),
            load(5, logs_in, logs),
            load(6, normed_in, normed_v),
            load(7, kvw_in, kvw),
        ]
        for copy in first_loads:
            copy.start()
        first_loads[0].wait()
        first_loads[1].wait()

        def weight_term(left, right, targets):
            width_of = heads * HD // len(targets)

            @pl.loop(0, LINE)
            def _(i):
                value = dot(left[:, part_columns(i)], right[...], 0, 0).astype(bf16)
                stage[...] = value.reshape(stage.shape)
                copies = [
                    load(8 + n, stage.at[:, :, pl.ds(n * width_of, width_of)], term.at[i])
                    for n, term in enumerate(targets)
                ]
                for copy in copies:
                    copy.start()
                for copy in copies:
                    copy.wait()

        weight_term(low, mixed, [out_term])
        first_loads[2].wait()

        @pl.loop(0, heads)
        def _(h):
            at = pl.ds(pl.multiple_of(h * HD, HD), HD)
            mixed_grad[:, at] = dot(low[...], weight[:, at]).astype(bf16)

        load(2, query_in, weight).start()
        load(0, x_in, low).start()
        row_places = me.r * tokens + lax.broadcasted_iota(jnp.int32, (tokens, 1), 0)

        @pl.loop(0, reach + 1)
        def _(i):
            at = pl.ds(pl.multiple_of(i * tokens, tokens), tokens)
            key_places = (start + i) * tokens + lax.broadcasted_iota(jnp.int32, (1, tokens), 1)
            gap = row_places - key_places
            seen = (gap >= 0) & (gap < W) & (marks_column[...] == marks_row[:, at])
            mask[:, at] = jnp.where(seen, 0.0, -1e30)
            window_sum[i] = jnp.zeros((tokens, 2 * HD), f32)

        for copy in first_loads[3:]:
            copy.wait()

        @pl.loop(0, heads)
        def _(h):
            at = pl.ds(pl.multiple_of(h * HD, HD), HD)
            q_head = qs[:, at]
            grad = mixed_grad[:, at]
            inner = jnp.sum(grad.astype(f32) * mixed[:, at].astype(f32), axis=1, keepdims=True)
            log = logs[h]
            q_sum = jnp.zeros((tokens, HD), f32)
            for c in range(pieces):
                blocks = pl.ds(c * chunk, chunk)
                both = win[blocks].reshape(chunk * tokens, 2 * HD)
                k, v = both[:, :HD], both[:, HD:]
                span_at = pl.ds(c * chunk * tokens, chunk * tokens)
                probs = jnp.exp(dot(q_head, k, 1, 1) + mask[:, span_at] - log)
                value_sum = dot(probs.astype(bf16), grad, 0, 0)
                score_grad = (probs * (dot(grad, v, 1, 1) - inner)).astype(bf16)
                q_sum += dot(score_grad, k)
                key_sum = dot(score_grad, q_head, 0, 0)
                window_sum[blocks, :, :HD] += key_sum.reshape(chunk, tokens, HD)
                window_sum[blocks, :, HD:] += value_sum.reshape(chunk, tokens, HD)
            q_grad[:, at] = (turn(q_sum, -1.0) * scale_factor).astype(bf16)

            @pl.when(h == heads - 1)
            def _():
                next(outw)


        @pl.loop(0, reach + 1)
        def _(i):
            win[i] = window_sum[i].astype(bf16)

        window_steps = reduce_window(me, reach, win, kv_total, window_scratch)
        next(window_steps)
        load(5, grad_in, mask).start()
        next(window_steps)
        weight_term(normed_v, q_grad, [query_term.at[0], query_term.at[1]])
        load(2, query_in, weight).wait()

        @pl.loop(0, LINE)
        def _(i):
            piece = weight[pl.ds(pl.multiple_of(i * part_rows, LANES), part_rows)]
            part[:, part_columns(i)] = dot(q_grad[...], piece, 1, 1).astype(bf16)

        swapped = remote(part, theirs, swap_sems[0], swap_sems[1], me.other())
        swapped.start()
        next(ffn)
        next(window_steps)
        next(window_steps, None)

        kv_low[:, :HD] = turn(kv_total[:, :HD], -1.0).astype(bf16)
        kv_low[:, HD:] = kv_total[:, HD:].astype(bf16)
        ours_at = pl.ds(pl.multiple_of(me.t * HD, HD), HD)
        small_copy = load(0, x_in, low)
        small_copy.wait()

        @pl.loop(0, LINE)
        def _(i):
            value = dot(normed_v[:, part_columns(i)], kv_low[:, ours_at], 0, 0).astype(bf16)
            kv_stage[:, pl.ds(0, rows)] = value.reshape(4, rows, HD)
            copy = load(9, small_in.at[pl.ds(4 * i, 4)], kv_stage.at[:, pl.ds(rows, kv_size - rows)])
            copy.start()
            copy.wait()
            copy = load(9, kv_stage, kv_term.at[i])
            copy.start()
            copy.wait()

        next(outw)
        next(query)
        next(ffn)
        next(more)
        next(kvw_steps)
        next(query)
        next(outw)

        swapped.wait()

        @pl.loop(0, width // (2 * HD))
        def _(i):
            at = pl.ds(pl.multiple_of(i * 2 * HD, 2 * HD), 2 * HD)
            more = dot(kv_low[...], kvw[at], 1, 1)
            window_sum[i] = part[:, at].astype(f32) + theirs[:, at].astype(f32) + more

        gain_sum[...] = jnp.zeros(gain_sum.shape, f32)
        load(5, grad_in, mask).wait()

        @pl.loop(0, tokens // 16)
        def _(i):
            at = pl.ds(pl.multiple_of(i * 16, 16), 16)
            grad = jnp.concatenate([window_sum[n, at] for n in range(width // (2 * HD))], axis=1)
            stream_rows = low[at].astype(f32)
            scale = lax.rsqrt(
                jnp.mean(stream_rows * stream_rows, axis=1, keepdims=True) + epsilon
            )
            unit = stream_rows * scale
            gain_sum[...] += grad * unit
            scaled = grad * gain[...]
            inner = jnp.mean(scaled * unit, axis=1, keepdims=True)
            mask[at] = mask[at] + scale * (scaled - unit * inner)

        load(5, mask, input_out).start()
        gain_rows[...] = jnp.zeros(gain_rows.shape, f32)
        gain_total = jnp.sum(gain_sum[...], axis=0, keepdims=True)
        for i in range(width // LANES):
            gain_rows[pl.ds(i, 1)] = gain_total[:, i * LANES : (i + 1) * LANES]
        gain_low[...] = gain_rows[...].astype(bf16)

        def gain_send(k):
            to = (me.base + lax.rem(me.r + k, RING), me.t)
            return remote(
                gain_low, gain_all.at[me.r], vector_sems[0].at[k], vector_sems[1].at[me.r], to
            )

        keep_gain = load(9, gain_low, gain_all.at[me.r])
        keep_gain.start()

        @pl.loop(1, RING)
        def _(k):
            gain_send(k).start()

        next(more)
        next(kvw_steps)
        next(query)
        next(more)
        next(kvw_steps)
        for step in lines + [ffn, outw, query, more, kvw_steps]:
            for _ in step:
                pass
        mine = kv_done.at[me.t]
        last = remote(mine, mine, last_sems[0], last_sems[1], me.other())
        last.start()

        @pl.loop(1, RING)
        def _(k):
            gain_send(k).wait_send()
            source = lax.rem(me.r + k, RING)
            landed = gain_all.at[source]
            remote(
                landed, landed, vector_sems[0].at[k], vector_sems[1].at[source], me.at(me.z, me.q)
            ).wait_recv()

        keep_gain.wait()
        load(5, mask, input_out).wait()
        last.wait()
        return []

    term_shape = (LINE, 4, rows, heads * HD)
    ffn_shape = (3, LINE, rows, block)
    half = (2, 2, LINE, rows // 2, heads * HD)
    kv_half = (2, 2, LINE, kv_size // 2, HD)
    ffn_done, out_done, query_done, kv_done, input_grad, gain_all = transfer(
        2,
        [
            middle_low, out_full, mixed_low, queries, kv_all, log_total, normed, query_full, kv_full,
            ffn_term, ffn_total, small_terms, middle_grad, inputs,
            window_marks, own_marks, turn_cos, turn_sin, gain_one[None],
        ],
        [
            (ffn_shape, bf16),
            ((LINE, rows, heads * HD), bf16),
            ((2, LINE, rows, heads * HD // 2), bf16),
            ((2, LINE, kv_size, HD), bf16),
            (inputs.shape, f32),
            ((RING, vector_rows, LANES), bf16),
            (term_shape, bf16),
            ((2,) + term_shape[:-1] + (heads * HD // 2,), bf16),
            ((LINE, 4, kv_size, HD), bf16),
        ]
        + scatter_buffers(rows, heads * HD)
        + scatter_buffers(kv_size, HD)
        + scatter_buffers(rows, block)
        + scatter_buffers(rows, heads * HD // 2) * 2,
        [
            LINE_SEMS,
            LINE_SEMS,
            SCATTER_SEMS,
            SCATTER_SEMS,
            SCATTER_SEMS,
            SCATTER_SEMS,
            SCATTER_SEMS,
            reduce_scratch(reach + 1, tokens // 2, 2 * HD, f32),
            SWAP_SEMS,
            SWAP_SEMS,
            [pltpu.SemaphoreType.DMA((RING,)), pltpu.SemaphoreType.DMA((RING,))],
            [
                pltpu.VMEM(inputs.shape, bf16),
                pltpu.VMEM(out_full.shape, bf16),
                pltpu.VMEM(queries.shape, bf16),
                pltpu.VMEM(queries.shape, bf16),
                pltpu.VMEM((reach + 1, tokens, 2 * HD), bf16),
                pltpu.VMEM(inputs.shape, bf16),
                pltpu.VMEM((heads, tokens, 1), f32),
                pltpu.VMEM(queries.shape, bf16),
                pltpu.VMEM(queries.shape, bf16),
                pltpu.VMEM((reach + 1, tokens, 2 * HD), f32),
                pltpu.VMEM(inputs.shape, f32),
                pltpu.VMEM((tokens, 2 * HD), f32),
                pltpu.VMEM((tokens, 2 * HD), bf16),
                pltpu.VMEM(kv_full.shape, bf16),
                pltpu.VMEM((4, rows, heads * HD), bf16),
                pltpu.VMEM((4, kv_size, HD), bf16),
                pltpu.VMEM(half, bf16),
                pltpu.VMEM(half, bf16),
                pltpu.VMEM(kv_half, bf16),
                pltpu.VMEM(kv_half, bf16),
                pltpu.VMEM(inputs.shape, bf16),
                pltpu.VMEM(inputs.shape, bf16),
                pltpu.VMEM((16, width), f32),
                pltpu.VMEM((vector_rows, LANES), f32),
                pltpu.VMEM((vector_rows, LANES), bf16),
                pltpu.SemaphoreType.DMA((10,)),
            ],
        ],
        fourth_steps,
        whole=True,
        near=(14, 15, 16, 17, 18),
    )[:6]
    output = (middle + mlp_out.astype(f32) + bias_down).astype(bf16)

    last_skip = LINE * block - hidden_half
    ffn_grad = jnp.concatenate(
        [ffn_done[:, i] for i in range(LINE - 1)] + [ffn_done[:, LINE - 1, :, last_skip:]], axis=2
    )
    ffn_grad = shrink(ffn_grad.astype(f32), 1, groups)
    out_grad = shrink(jnp.sum(out_done.astype(f32), axis=0), 0, groups).T
    query_sum = jnp.sum(query_done.astype(f32), axis=1)
    query_grad = shrink(jnp.concatenate([query_sum[0], query_sum[1]], axis=1), 0, groups)
    kv_sums = jnp.sum(kv_done.astype(f32), axis=1)
    small_sums = lax.dynamic_index_in_dim(kv_sums[:, rows:], t, 0, keepdims=False)
    kv_grad = jnp.concatenate([kv_sums[0, :rows], kv_sums[1, :rows]], axis=1)
    kv_grad = lax.dynamic_index_in_dim(kv_grad.reshape(groups, 2, -1, columns), t, 1, keepdims=False)
    key_value_grad = shrink(kv_grad.reshape(kv_rows, columns), 0, groups)
    gain_sum = jnp.sum(gain_all[:, : width // LANES].astype(f32), axis=0).reshape(
        RING, groups, 2, kv_rows // groups
    )
    gain_sum = lax.dynamic_index_in_dim(gain_sum, r, 0, keepdims=False)
    gain_sum = lax.dynamic_index_in_dim(gain_sum, t, 1, keepdims=False).reshape(kv_rows)
    small_grads = [shrink(v, 0, groups) for v in [gain_sum] + [small_sums[i, :kv_rows] for i in range(3)]]
    gate_up_bias_grad = shrink(small_sums[3:5, : hidden_bias.shape[1]], 1, groups)
    return (
        from_places(output, groups),
        from_places(input_grad, groups),
        small_grads[0],
        query_grad,
        key_value_grad,
        out_grad,
        small_grads[1],
        small_grads[2],
        ffn_grad[:2],
        gate_up_bias_grad,
        ffn_grad[2].T,
        small_grads[3],
    )


def solution(mesh):
    in_specs = (
        P("seq", None),
        P("seq"),
        P("seq", None),
        P(("seq", "tensor")),
        P("seq", "tensor"),
        P(("seq", "tensor"), None),
        P("tensor", "seq"),
        P(("seq", "tensor")),
        P(("seq", "tensor")),
        P(None, "seq", "tensor"),
        P(None, ("seq", "tensor")),
        P("tensor", "seq"),
        P(("seq", "tensor")),
    )
    out_specs = (
        P("seq", None),
        P("seq", None),
        P(("seq", "tensor")),
        P("seq", "tensor"),
        P(("seq", "tensor"), None),
        P("tensor", "seq"),
        P(("seq", "tensor")),
        P(("seq", "tensor")),
        P(None, "seq", "tensor"),
        P(None, ("seq", "tensor")),
        P("tensor", "seq"),
        P(("seq", "tensor")),
    )
    return jax.shard_map(body, mesh=mesh, in_specs=in_specs, out_specs=out_specs, check_vma=False)
```

```python
import functools

import jax
import jax.numpy as jnp
from jax import lax
from jax.experimental import pallas as pl
from jax.experimental.pallas import tpu as pltpu
from jax.sharding import PartitionSpec as P

HD = 256
W = 2048
SEQ_LEN = 4096
LINE = 4
RING = 16
LANES = 128

epsilon = 1e-06
bf16 = jnp.bfloat16
f32 = jnp.float32
MESH = pl.DeviceIdType.MESH
ANY = pl.BlockSpec(memory_space=pl.ANY)
VMEM = pl.BlockSpec(memory_space=pltpu.VMEM)


class Place:
    def __init__(self):
        seq = lax.axis_index("seq")
        self.t = lax.axis_index("tensor")
        self.r = lax.rem(seq, RING)
        self.base = seq - self.r
        self.z = lax.div(self.r, 4)
        self.q = lax.rem(self.r, 4)
        self.xq = self.q + 1 - 2 * lax.rem(self.q, 2)
        self.yq = self.q + 2 - 4 * lax.div(self.q, 2)
        self.dq = 3 - self.q
        self.half = lax.div(self.z, 2)
        self.inner = self.z + self.half * (3 - 2 * self.z)

    def at(self, z, q):
        return (self.base + 4 * z + q, self.t)

    def other(self):
        return (self.base + self.r, 1 - self.t)

    def order(self, j):
        v = j + self.inner * (1 - 2 * j if j < 2 else 0)
        return v + self.half * (3 - 2 * v)

    def greet(self, whole=False):
        barrier = pltpu.get_barrier_semaphore()
        if whole:
            peers = [
                (self.base + lax.rem(self.r + k, RING), self.t) for k in range(1, RING)
            ]
        else:
            peers = [self.at(lax.rem(self.z + k, 4), self.q) for k in range(1, 4)]
            peers += [self.at(self.z, self.xq), self.at(self.z, self.yq)]
        peers.append(self.other())
        for peer in peers:
            pl.semaphore_signal(barrier, inc=1, device_id=peer, device_id_type=MESH)
        pl.semaphore_wait(barrier, len(peers))


def remote(src, dst, send, recv, device):
    return pltpu.make_async_remote_copy(
        src_ref=src, dst_ref=dst, send_sem=send, recv_sem=recv, device_id=device, device_id_type=MESH
    )


def run(steps):
    steps, ending = list(steps), []
    while steps:
        for step in list(steps):
            if next(step, True):
                steps.remove(step)
                ending.append(step)
    for step in ending:
        next(step, None)


GATHER_SEMS = [
    pltpu.SemaphoreType.DMA((4, 6)),
    pltpu.SemaphoreType.DMA((4, 5)),
    pltpu.SemaphoreType.DMA,
]


def gather(me, own, slot, part, sems):
    snd, rcv, loc = sems
    local = pltpu.make_async_copy(own, slot(me.z, me.q), loc)
    local.start()

    def line(z, k, src, to):
        return remote(src, slot(z, me.q), snd.at[z, k], rcv.at[z, 0], me.at(to, me.q))

    @pl.when(me.z < 3)
    def _():
        line(me.z, 0, own, me.z + 1).start()

    @pl.when(me.z > 0)
    def _():
        line(me.z, 1, own, me.z - 1).start()

    def arrive(j):
        z = me.order(j)
        line(z, 0, slot(z, me.q), me.z).wait_recv()

        @pl.when(me.inner == 1)
        def _():
            step = 3 - 2 * me.z if j == 1 else 2 * me.z - 3
            line(z, 0, slot(z, me.q), me.z + step).start()

    yield from in_plane(me, own, slot, part, snd, rcv, arrive)
    local.wait()

    @pl.when(me.z < 3)
    def _():
        line(me.z, 0, own, me.z + 1).wait_send()

    @pl.when(me.z > 0)
    def _():
        line(me.z, 1, own, me.z - 1).wait_send()

    @pl.when(me.inner == 1)
    def _():
        for j in range(1, 4):
            z = me.order(j)
            line(z, 0, slot(z, me.q), me.z).wait_send()


def in_plane(me, own, slot, part, snd, rcv, arrive):
    def across(z, k, src):
        q = (me.xq, me.yq)[k]
        return remote(src, slot(z, me.q), snd.at[z, 2 + k], rcv.at[z, 1 + k], me.at(me.z, q))

    def corner(z, k):
        src = part(z, (me.xq, me.yq)[k], k)
        if src is None:
            return None
        return remote(src, src, snd.at[z, 4 + k], rcv.at[z, 3 + k], me.at(me.z, (me.yq, me.xq)[k]))

    for k in range(2):
        across(me.z, k, own).start()
    yield
    for j in range(1, 5):
        if j < 4:
            arrive(j)
            z = me.order(j)
            for k in range(2):
                across(z, k, slot(z, me.q)).start()
        z = me.order(j - 1)
        for k in range(2):
            q = (me.xq, me.yq)[k]
            remote(
                slot(z, q), slot(z, q), snd.at[z, 2 + k], rcv.at[z, 1 + k], me.at(me.z, q)
            ).wait_recv()
            copy = corner(z, k)
            if copy is not None:
                copy.start()
        yield
    yield True
    for j in range(4):
        z = me.order(j)
        for k in range(2):
            src = part(z, me.dq, k)
            if src is not None:
                remote(src, src, snd.at[z, 4 + k], rcv.at[z, 3 + k], me.at(me.z, me.xq)).wait_recv()
    for j in range(4):
        z = me.order(j)
        for k in range(2):
            across(z, k, slot(z, me.q)).wait_send()
            copy = corner(z, k)
            if copy is not None:
                copy.wait_send()


PIECE_SEMS = [
    pltpu.SemaphoreType.DMA((4, 6)),
    pltpu.SemaphoreType.DMA((4, 5)),
    pltpu.SemaphoreType.DMA((4, 2)),
    pltpu.SemaphoreType.DMA((4, 2)),
]


def gather_pieces(me, sources, dst, sems):
    snd, rcv, piece_snd, piece_rcv = sems
    half = dst.shape[2] // 2

    def slot(z, q):
        return dst.at[:, 4 * z + q]

    def part(z, q, h):
        return dst.at[:, 4 * z + q, pl.ds(h * half, half)]

    def local(n):
        parts, piece = sources[n]
        return pltpu.make_async_copy(piece(me.z), dst.at[parts, me.r], piece_snd.at[me.z, n])

    def send(z, n):
        parts, piece = sources[n]
        return remote(
            piece(z), dst.at[parts, me.r], piece_snd.at[z, n], piece_rcv.at[me.z, n], me.at(z, me.q)
        )

    for n in range(len(sources)):
        local(n).start()
    for j in range(1, 3):
        for n in range(len(sources)):
            send(me.order(j), n).start()
    yield
    for n in range(len(sources)):
        send(me.order(3), n).start()
    yield

    def arrive(j):
        z = me.order(j)
        for n in range(len(sources)):
            view = dst.at[sources[n][0], 4 * z + me.q]
            remote(view, view, piece_snd.at[z, n], piece_rcv.at[z, n], me.at(z, me.q)).wait_recv()

    for n in range(len(sources)):
        local(n).wait()
    yield from in_plane(me, slot(me.z, me.q), slot, part, snd, rcv, arrive)
    for j in range(1, 4):
        for n in range(len(sources)):
            send(me.order(j), n).wait_send()


SPREAD_SEMS = [
    pltpu.SemaphoreType.DMA((4, 3)),
    pltpu.SemaphoreType.DMA((4, 2)),
    pltpu.SemaphoreType.DMA,
]


def spread(me, src, dst, sems):
    snd, rcv, loc = sems
    rows = src.shape[0] // 2
    mine = pl.ds(pl.multiple_of(me.t * rows, rows), rows)
    local = pltpu.make_async_copy(src, dst.at[me.z], loc)
    local.start()

    def slot(z):
        return dst.at[z, mine]

    def line(z, k, source, to):
        return remote(source, slot(z), snd.at[z, k], rcv.at[z, 0], me.at(to, me.q))

    def share(z):
        return remote(slot(z), slot(z), snd.at[z, 2], rcv.at[z, 1], me.other())

    @pl.when(me.z < 3)
    def _():
        line(me.z, 0, src.at[mine], me.z + 1).start()

    @pl.when(me.z > 0)
    def _():
        line(me.z, 1, src.at[mine], me.z - 1).start()

    yield
    for j in range(1, 4):
        z = me.order(j)
        line(z, 0, slot(z), me.z).wait_recv()

        @pl.when(me.inner == 1)
        def _():
            step = 3 - 2 * me.z if j == 1 else 2 * me.z - 3
            line(z, 0, slot(z), me.z + step).start()

        share(z).start()
        yield
    yield True
    other = pl.ds(pl.multiple_of((1 - me.t) * rows, rows), rows)
    for j in range(1, 4):
        z = me.order(j)
        remote(
            dst.at[z, other], dst.at[z, other], snd.at[z, 2], rcv.at[z, 1], me.other()
        ).wait_recv()
        share(z).wait_send()
    local.wait()

    @pl.when(me.z < 3)
    def _():
        line(me.z, 0, src.at[mine], me.z + 1).wait_send()

    @pl.when(me.z > 0)
    def _():
        line(me.z, 1, src.at[mine], me.z - 1).wait_send()

    @pl.when(me.inner == 1)
    def _():
        for j in range(1, 4):
            z = me.order(j)
            line(z, 0, slot(z), me.z).wait_send()


def swap(me, src, dst, sems):
    copy = remote(src, dst, sems[0], sems[1], me.other())
    copy.start()
    yield True
    copy.wait()


SWAP_SEMS = [pltpu.SemaphoreType.DMA, pltpu.SemaphoreType.DMA]


def add_rows(out, terms):
    rows = out.shape[0]
    step = 16

    @pl.loop(0, rows // step)
    def _(i):
        at = pl.ds(pl.multiple_of(i * step, step), step)
        total = terms[0][at].astype(f32)
        for term in terms[1:]:
            total += term[at].astype(f32)
        out[at] = total.astype(out.dtype)


def reduce_scratch(slots, rows, columns, dtype):
    return [
        pltpu.VMEM((slots, rows, columns), bf16),
        pltpu.VMEM((slots, rows, columns), bf16),
        pltpu.VMEM((slots, rows, columns), bf16),
        pltpu.VMEM((rows, columns), dtype),
        pltpu.SemaphoreType.DMA((slots, 3)),
        pltpu.SemaphoreType.DMA((slots, 2)),
        pltpu.SemaphoreType.DMA((3,)),
    ]


def line_sum_scratch(rows, columns):
    return [
        pltpu.VMEM((LINE, 2 * rows, columns), bf16),
        pltpu.VMEM((LINE, rows, columns), bf16),
        pltpu.VMEM((2, 3, rows, columns), bf16),
        pltpu.SemaphoreType.DMA((LINE,)),
        pltpu.SemaphoreType.DMA((LINE,)),
        pltpu.SemaphoreType.DMA((2, 3)),
        pltpu.SemaphoreType.DMA((2, 3)),
        pltpu.SemaphoreType.DMA((3,)),
    ]


class LineSum:
    def __init__(self, me, out, scratch):
        self.me = me
        self.src, self.there, self.landed, *self.sems = scratch
        rows = self.there.shape[1]
        self.mine = pl.ds(pl.multiple_of(me.t * rows, rows), rows)
        self.theirs = pl.ds(pl.multiple_of((1 - me.t) * rows, rows), rows)
        self.out = out

    def here(self, z):
        return self.src.at[z, self.mine]

    def cross(self, z):
        snd, rcv = self.sems[:2]
        source = self.src.at[z, self.theirs]
        return remote(source, self.there.at[z], snd.at[z], rcv.at[z], self.me.other())

    def send(self, way, k, source):
        me = self.me
        snd, rcv = self.sems[2:4]
        to = me.at(me.z + 1 - 2 * way, me.q)
        return remote(source, self.landed.at[way, k], snd.at[way, k], rcv.at[way, k], to)

    def ends(self):
        me = self.me
        end = self.sems[4]
        done = self.here(me.z)
        keep = pltpu.make_async_copy(done, self.out.at[self.mine], end.at[0])
        return keep, remote(done, self.out.at[self.mine], end.at[1], end.at[2], me.other())

    def fold(self, z):
        self.cross(z).wait_recv()
        add_rows(self.here(z), (self.here(z), self.there.at[z]))

    def step(self, k):
        for way in range(2):
            w = self.me.z if way == 0 else 3 - self.me.z
            block = 3 + w - k if way == 0 else k - w

            @pl.when(w <= k)
            def _():
                if k:

                    @pl.when(w < k)
                    def _():
                        self.send(way, k - 1, self.here(0)).wait_send()

                @pl.when(w == 0)
                def _():
                    self.send(way, k, self.here(block)).start()

                if k:

                    @pl.when(w > 0)
                    def _():
                        partial = self.landed.at[way, k - 1]
                        self.send(way, k - 1, partial).wait_recv()
                        add_rows(partial, (partial, self.here(block)))
                        self.send(way, k, partial).start()

    def finish(self):
        for way in range(2):
            w = self.me.z if way == 0 else 3 - self.me.z

            @pl.when(w > 0)
            def _():
                last = self.landed.at[way, 2]
                self.send(way, 2, last).wait_recv()
                here = self.here(self.me.z)
                add_rows(here, (here, last))

            @pl.when(w < 3)
            def _():
                self.send(way, 2, self.here(0)).wait_send()

        for copy in self.ends():
            copy.start()

    def close(self):
        for z in range(LINE):
            self.cross(z).wait_send()
        for copy in self.ends():
            copy.wait()


def reduce_window(me, reach, src, out, scratch):
    here, there, landed, total, snd, rcv, end = scratch
    rows = here.shape[1]
    slots = reach + 1
    mine = pl.ds(pl.multiple_of(me.t * rows, rows), rows)
    theirs = pl.ds(pl.multiple_of((1 - me.t) * rows, rows), rows)
    start = jnp.maximum(me.r - reach, 0)

    def cross(j):
        return remote(src.at[j, theirs], there.at[j], snd.at[j, 0], rcv.at[j, 0], me.other())

    def local(j):
        return pltpu.make_async_copy(src.at[j, mine], here.at[j], snd.at[j, 1])

    def back(k):
        j = me.r - k - start
        return remote(
            here.at[j], landed.at[k], snd.at[k, 2], rcv.at[k, 1], (me.base + me.r - k, me.t)
        )

    for j in range(slots):
        cross(j).start()
        local(j).start()
    yield
    for j in range(slots):
        local(j).wait()
        cross(j).wait_recv()
        add_rows(here.at[j], (here.at[j], there.at[j]))
    for k in range(reach, 0, -1):

        @pl.when(me.r >= k)
        def _():
            back(k).start()

    yield
    add_rows(total, [here.at[me.r - start]])
    for k in range(1, slots):

        @pl.when(me.r + k < RING)
        def _():
            remote(
                landed.at[k], landed.at[k], snd.at[k, 2], rcv.at[k, 1], me.at(me.z, me.q)
            ).wait_recv()
            add_rows(total, (total, landed.at[k]))

    keep = pltpu.make_async_copy(total, out.at[mine], end.at[0])
    give = remote(total, out.at[mine], end.at[1], end.at[2], me.other())
    keep.start()
    give.start()
    yield True
    for j in range(slots):
        cross(j).wait_send()
    for k in range(1, slots):

        @pl.when(me.r >= k)
        def _():
            back(k).wait_send()

    keep.wait()
    give.wait()


PLANE_SEMS = [pltpu.SemaphoreType.DMA((4,)), pltpu.SemaphoreType.DMA((4,))]


def add_blocks(out, more):
    blocks, rows, _ = out.shape
    steps = rows // 16

    @pl.loop(0, blocks * steps)
    def _(i):
        n = lax.div(i, steps)
        at = pl.ds(pl.multiple_of(lax.rem(i, steps) * 16, 16), 16)
        out[n, at] = (out[n, at].astype(f32) + more[n, at].astype(f32)).astype(out.dtype)


def scatter_buffers(rows, columns):
    half = (2, LINE, rows // 2, columns)
    return [((2,) + half, bf16)] + [(half, bf16)] * 3 + [((LINE, rows, columns), bf16)]


SCATTER_SEMS = [
    pltpu.SemaphoreType.DMA((6,)),
    pltpu.SemaphoreType.DMA((6,)),
    pltpu.SemaphoreType.DMA((8,)),
    pltpu.SemaphoreType.DMA((4,)),
    pltpu.SemaphoreType.DMA((4,)),
]


def scatter(me, src, done, buffers, here, there, sems):
    got, kept, passed, got_two, total = buffers
    snd, rcv, loc, line_snd, line_rcv = sems
    half = src.shape[2] // 2
    across = pl.ds(0, src.shape[3])
    first, second = [], []

    def held(ref, h, i):
        return ref.at[h, i, :, :, across]

    for h in range(2):
        q = (me.xq, me.yq)[h]
        rows = pl.ds(h * half, half)
        for i in range(2):
            n = 2 * h + i
            view = src.at[:, (q, me.dq)[i], rows]
            first.append(remote(view, got.at[h, i], snd.at[n], rcv.at[n], me.at(me.z, q)))
        q = (me.yq, me.xq)[h]
        second.append(
            remote(passed.at[h], got_two.at[h], snd.at[4 + h], rcv.at[4 + h], me.at(me.z, q))
        )
    yield
    for copy in first:
        copy.start()
    yield
    for copy in first:
        copy.wait_recv()
    loads, stores = [], []
    for h in range(2):
        for i in range(2):
            n = 2 * h + i
            view = src.at[:, (me.q, (me.yq, me.xq)[h])[i], pl.ds(h * half, half)]
            loads.append(pltpu.make_async_copy(view, held(here, h, i), loc.at[n]))
            loads.append(pltpu.make_async_copy(got.at[h, i], held(there, h, i), loc.at[4 + n]))
            stores.append(
                pltpu.make_async_copy(held(here, h, i), (kept, passed)[i].at[h], loc.at[n])
            )
    for copy in loads:
        copy.start()
    for copy in loads:
        copy.wait()
    for h in range(2):
        for i in range(2):
            add_blocks(held(here, h, i), held(there, h, i))
    for copy in stores:
        copy.start()
    for copy in stores:
        copy.wait()
    for copy in second:
        copy.start()
    yield
    for copy in second:
        copy.wait_recv()
    loads, stores = [], []
    for h in range(2):
        loads.append(pltpu.make_async_copy(kept.at[h], held(here, h, 0), loc.at[h]))
        loads.append(pltpu.make_async_copy(got_two.at[h], held(there, h, 0), loc.at[4 + h]))
        stores.append(
            pltpu.make_async_copy(held(here, h, 0), total.at[:, pl.ds(h * half, half)], loc.at[h])
        )
    for copy in loads:
        copy.start()
    for copy in loads:
        copy.wait()
    for h in range(2):
        add_blocks(held(here, h, 0), held(there, h, 0))
    for copy in stores:
        copy.start()
    for copy in stores:
        copy.wait()

    def send(j):
        z = me.order(j)
        return remote(total.at[z], done.at[me.z], line_snd.at[z], line_rcv.at[me.z], me.at(z, me.q))

    def local():
        return pltpu.make_async_copy(total.at[me.z], done.at[me.z], loc.at[7])

    local().start()
    for j in (3, 2, 1):
        send(j).start()
    yield True
    for j in range(1, 4):
        z = me.order(j)
        remote(done.at[z], done.at[z], line_snd.at[z], line_rcv.at[z], me.at(z, me.q)).wait_recv()
    local().wait()
    for copy in first + second:
        copy.wait_send()
    for j in range(1, 4):
        send(j).wait_send()


PLANE_SUM_SEMS = [
    pltpu.SemaphoreType.DMA((3, 6)),
    pltpu.SemaphoreType.DMA((3, 6)),
    pltpu.SemaphoreType.DMA((4,)),
]


class PlaneSum:
    def __init__(self, me, src, buffers, total, here, there, sems):
        self.me, self.src, self.total = me, src, total
        self.got, self.kept, self.passed, self.got_two = buffers
        self.here, self.there = here, there
        self.snd, self.rcv, self.loc = sems
        self.half = src.shape[3] // 2

    def view(self, part, place, h):
        return self.src.at[part, :, place, pl.ds(h * self.half, self.half)]

    def sends(self, part):
        me = self.me
        copies = []
        for h in range(2):
            q = (me.xq, me.yq)[h]
            for i in range(2):
                n = 2 * h + i
                copies.append(
                    remote(
                        self.view(part, (q, me.dq)[i], h),
                        self.got.at[part, h, i],
                        self.snd.at[part, n],
                        self.rcv.at[part, n],
                        me.at(me.z, q),
                    )
                )
        return copies

    def start(self, part):
        for copy in self.sends(part):
            copy.start()

    def fold(self, part):
        me = self.me
        for copy in self.sends(part):
            copy.wait_recv()
        for h in range(2):
            places = (me.q, (me.yq, me.xq)[h])
            loads, stores = [], []
            for i in range(2):
                a, b = self.here.at[i], self.there.at[i]
                loads.append(pltpu.make_async_copy(self.view(part, places[i], h), a, self.loc.at[i]))
                loads.append(
                    pltpu.make_async_copy(self.got.at[part, h, i], b, self.loc.at[2 + i])
                )
                stores.append(
                    pltpu.make_async_copy(
                        a, (self.kept, self.passed)[i].at[h, part], self.loc.at[i]
                    )
                )
            for copy in loads:
                copy.start()
            for copy in loads:
                copy.wait()
            for i in range(2):
                add_blocks(self.here.at[i], self.there.at[i])
            for copy in stores:
                copy.start()
            for copy in stores:
                copy.wait()

    def second(self, part):
        me = self.me
        return [
            remote(
                self.passed.at[h, part],
                self.got_two.at[h, part],
                self.snd.at[part, 4 + h],
                self.rcv.at[part, 4 + h],
                me.at(me.z, (me.yq, me.xq)[h]),
            )
            for h in range(2)
        ]

    def pass_on(self, part):
        for copy in self.second(part):
            copy.start()

    def fold_again(self, part):
        for copy in self.second(part):
            copy.wait_recv()
        loads, stores = [], []
        for h in range(2):
            a, b = self.here.at[h], self.there.at[h]
            target = self.total.at[part, :, pl.ds(h * self.half, self.half)]
            loads.append(pltpu.make_async_copy(self.kept.at[h, part], a, self.loc.at[h]))
            loads.append(pltpu.make_async_copy(self.got_two.at[h, part], b, self.loc.at[2 + h]))
            stores.append(pltpu.make_async_copy(a, target, self.loc.at[h]))
        for copy in loads:
            copy.start()
        for copy in loads:
            copy.wait()
        for h in range(2):
            add_blocks(self.here.at[h], self.there.at[h])
        for copy in stores:
            copy.start()
        for copy in stores:
            copy.wait()

    def close(self, part):
        for copy in self.sends(part) + self.second(part):
            copy.wait_send()


LINE_SEMS = [pltpu.SemaphoreType.DMA((4,)), pltpu.SemaphoreType.DMA((4,)), pltpu.SemaphoreType.DMA]


def line_exchange(me, src, done, sems):
    snd, rcv, loc = sems
    local = pltpu.make_async_copy(src.at[me.z], done.at[me.z], loc)
    local.start()

    def send(j):
        z = me.order(j)
        return remote(src.at[z], done.at[me.z], snd.at[z], rcv.at[me.z], me.at(z, me.q))

    for j in (3, 2, 1):
        send(j).start()
    yield True
    for j in range(1, 4):
        z = me.order(j)
        remote(done.at[z], done.at[z], snd.at[z], rcv.at[z], me.at(z, me.q)).wait_recv()
    for j in range(1, 4):
        send(j).wait_send()
    local.wait()


def transfer(number, inputs, outputs, scratch, steps, whole=False, near=()):
    flat = [item for group in scratch for item in group]
    sizes = [len(group) for group in scratch]

    def kernel(*refs):
        ins = refs[: len(inputs)]
        outs = refs[len(inputs) : len(inputs) + len(outputs)]
        rest = refs[len(inputs) + len(outputs) :]
        groups = []
        for size in sizes:
            groups.append(rest[:size])
            rest = rest[size:]
        me = Place()
        me.greet(whole)
        run(steps(me, ins, outs, groups))

    return pl.pallas_call(
        kernel,
        out_shape=[jax.ShapeDtypeStruct(shape, dtype) for shape, dtype in outputs],
        in_specs=[VMEM if i in near else ANY for i in range(len(inputs))],
        out_specs=[ANY] * len(outputs),
        scratch_shapes=flat,
        compiler_params=pltpu.CompilerParams(
            collective_id=number, has_side_effects=True, vmem_limit_bytes=62 * 2**20
        ),
    )(*inputs)


def gather_rows(me, src, dst, sems):
    rows = src.shape[0]
    cut = -(-rows // 32) * 16

    def part(z, q, h):
        if cut == rows and h:
            return None
        return dst.at[4 * z + q, pl.ds(h * cut, (rows - cut) if h else cut)]

    return gather(me, src, lambda z, q: dst.at[4 * z + q], part, sems)


def group_lists(groups):
    return [[r + RING * g for g in range(groups)] for r in range(RING)]


def grow(x, axis, groups):
    if groups == 1:
        return x
    return lax.all_gather(x, "seq", axis=axis, tiled=True, axis_index_groups=group_lists(groups))


def shrink(x, axis, groups):
    if groups == 1:
        return x
    return lax.psum_scatter(
        x, "seq", scatter_dimension=axis, tiled=True, axis_index_groups=group_lists(groups)
    )


def to_places(x, groups):
    if groups == 1:
        return x
    return x.reshape(x.shape[0], groups, RING, -1).swapaxes(1, 2).reshape(x.shape)


def from_places(x, groups):
    if groups == 1:
        return x
    return x.reshape(x.shape[0], RING, groups, -1).swapaxes(1, 2).reshape(x.shape)


def normalize(stream, scale_vec):
    return (
        stream * lax.rsqrt(jnp.mean(stream * stream, axis=-1, keepdims=True) + epsilon) * scale_vec
    )


def rotate(values, places, head_count, direction):
    head_size = values.shape[1] // head_count
    shaped = values.reshape(values.shape[0], head_count, head_size)
    quarter = head_size // 4
    first_part = shaped[..., :quarter]
    second = shaped[..., quarter : 2 * quarter]
    remainder = shaped[..., 2 * quarter :]
    frequency = 10000.0 ** (-jnp.arange(quarter, dtype=jnp.float32) / quarter)
    angles = places.astype(jnp.float32)[:, None] * frequency[None, :]
    cosine = jnp.cos(angles)[:, None, :]
    sine_part = direction * jnp.sin(angles)[:, None, :]
    turned = jnp.concatenate(
        [
            first_part * cosine - second * sine_part,
            second * cosine + first_part * sine_part,
            remainder,
        ],
        axis=-1,
    )
    return turned.reshape(values.shape)


def dot(a, b, ca=1, cb=0):
    return lax.dot_general(a, b, (((ca,), (cb,)), ((), ())), preferred_element_type=f32)


def body(
    inputs,
    segment_ids,
    cotangent,
    attn_gain,
    query_weight,
    key_value_weight,
    out_weight,
    out_bias,
    mlp_gain,
    gate_up_weight,
    gate_up_bias,
    down_weight,
    down_bias,
):
    seq_index = lax.axis_index("seq")
    t = lax.axis_index("tensor")
    r = seq_index % RING
    z = r // 4
    q = r % 4
    groups = lax.axis_size("seq") // RING
    tokens, width = inputs.shape
    inputs = to_places(inputs, groups)
    cotangent = to_places(cotangent, groups)
    heads = query_weight.shape[1] // HD
    hidden_half = gate_up_weight.shape[2]
    block = -(-hidden_half // (LINE * LANES)) * LANES
    block_start = jnp.minimum(z * block, hidden_half - block)
    block_skip = z * block - block_start
    reach = (W + tokens - 2) // tokens
    span = (reach + 1) * tokens
    first_block = jnp.maximum(r - reach, 0)
    scale_factor = HD ** (-0.5)
    assert tokens * RING == SEQ_LEN and lax.axis_size("tensor") == 2

    def own_features(x):
        if groups == 1:
            return x
        both = lax.all_gather(x, "tensor", axis=0)
        both = lax.all_gather(both, "seq", axis=0, axis_index_groups=group_lists(groups))
        both = both.reshape((2, -1) + x.shape[1:])
        return lax.dynamic_index_in_dim(both, t, 0, keepdims=False)

    kv_own = own_features(key_value_weight)
    kv_rows, columns = kv_own.shape
    vectors = [own_features(v) for v in (attn_gain, out_bias, mlp_gain, down_bias)]
    hidden_bias = grow(gate_up_bias, 1, groups)
    marks = jnp.stack([segment_ids // 256, segment_ids % 256]).astype(bf16)

    def pad_to(x, n):
        return jnp.pad(x, ((0, 0), (0, n - x.shape[1])))

    small = jnp.concatenate(
        [
            pad_to(jnp.stack(vectors), columns),
            pad_to(hidden_bias, columns),
            pad_to(marks, columns),
            jnp.zeros((8, columns), bf16),
        ]
    )
    query_own = grow(query_weight, 0, groups)
    out_own = grow(out_weight.T, 0, groups)
    gate_up_own = grow(gate_up_weight, 1, groups)
    down_own = grow(down_weight.T, 0, groups)
    rows = query_own.shape[0]
    places = r * tokens + jnp.arange(tokens, dtype=jnp.int32)
    frequency = 10000.0 ** (-jnp.arange(HD // 4, dtype=f32) / (HD // 4))
    angles = places.astype(f32)[:, None] * frequency[None, :]
    turn_cos = jnp.concatenate([jnp.cos(angles), jnp.cos(angles)], axis=1)
    turn_sin = jnp.concatenate([-jnp.sin(angles), jnp.sin(angles)], axis=1)
    own_marks = segment_ids.astype(f32)[:, None]
    feature = jnp.arange(width)[None, :]
    pick_device = (feature // kv_rows == jnp.arange(2 * RING)[:, None]).astype(bf16)
    pick_entry = (feature % kv_rows == jnp.arange(LANES)[:, None]).astype(bf16)

    def first_steps(me, ins, outs, groups_in):
        (
            own_query, own_kvw, own_small, own_out, own_gate_up, own_down, x_in, cot_in,
            marks_column, cos2, sin2, device_of, entry_of,
        ) = ins
        (
            query_all, kvw_all, small_all, kv_all, out_all, ffn_all, cot_out, mixed_out, log_out,
            middle_out, normed_two_out, queries_out, normed_out, vec_out, marks_out,
        ) = outs
        (
            query_sems, kvw_sems, small_sems, kv_sems, out_sems, ffn_sems, cot_sems, spread_sems,
            swap_sems, scratch,
        ) = groups_in
        (
            qs, win, weight, kvw, mask, mixed, part, theirs, x, middle, normed, normed_two, logs,
            small, small_wide, vec, marks_row, kv_low, loads,
        ) = scratch

        def load(n, src, dst):
            return pltpu.make_async_copy(src, dst, loads.at[n])

        def turn(v):
            first = v[:, : HD // 2]
            turned = first * cos2[...] + pltpu.roll(first, HD // 4, 1) * sin2[...]
            return jnp.concatenate([turned, v[:, HD // 2 :]], axis=1)

        def columns_of(source, lead):
            def piece(place):
                at = jnp.minimum(place * block, hidden_half - block)
                at = pl.ds(pl.multiple_of(at, LANES), block)
                return source.at[:, :, at] if lead else source.at[:, at]

            return piece

        def share(n, ref):
            mine = ref.at[:, me.t]
            return remote(mine, mine, swap_sems[0].at[n], swap_sems[1].at[n], me.other())

        smalls = gather_rows(me, own_small, small_all.at[:, me.t], small_sems)
        kvws = gather_rows(me, own_kvw, kvw_all.at[:, me.t], kvw_sems)
        queries = gather_rows(me, own_query, query_all, query_sems)
        keys = gather_rows(me, kv_low, kv_all, kv_sems)
        outw = gather_rows(me, own_out, out_all, out_sems)
        ffn = gather_pieces(
            me,
            [(pl.ds(0, 2), columns_of(own_gate_up, True)), (2, columns_of(own_down, False))],
            ffn_all,
            ffn_sems,
        )
        cot = spread(me, cot_in, cot_out, cot_sems)
        load(0, x_in, x).start()
        for n in range(5):
            next(smalls)
            next(kvws)
            next(queries)
            if n == 3:
                next(outw)
        next(ffn)
        for _ in smalls:
            pass
        share(0, small_all).start()
        for _ in kvws:
            pass
        share(1, kvw_all).start()
        share(0, small_all).wait()
        load(1, small_all, small).start()
        load(1, small_all, small).wait()
        small_wide[...] = small[...].reshape(small_wide.shape).astype(f32)
        vec[...] = jnp.zeros(vec.shape, f32)
        for i in range(4):
            piece = small_wide[:, i, :LANES].astype(bf16)
            spread_out = dot(piece, device_of[...], 0, 0) * entry_of[...].astype(f32)
            vec[i : i + 1] = jnp.sum(spread_out, axis=0, keepdims=True)
        start = jnp.maximum(me.r - reach, 0)
        row_places = me.r * tokens + lax.broadcasted_iota(jnp.int32, (tokens, 1), 0)

        @pl.loop(0, reach + 1)
        def _(i):
            at = pl.ds(pl.multiple_of(i * tokens, tokens), tokens)
            high = small_wide[2 * (start + i), 6:7, :tokens]
            low = small_wide[2 * (start + i), 7:8, :tokens]
            key_marks = high * 256.0 + low
            marks_row[:, at] = key_marks
            key_places = (start + i) * tokens + lax.broadcasted_iota(jnp.int32, (1, tokens), 1)
            gap = row_places - key_places
            seen = (gap >= 0) & (gap < W) & (marks_column[...] == key_marks)
            mask[:, at] = jnp.where(seen, 0.0, -1e30)

        load(1, vec, vec_out).start()
        load(2, marks_row, marks_out).start()
        load(0, x_in, x).wait()

        @pl.loop(0, tokens // 16)
        def _(i):
            at = pl.ds(pl.multiple_of(i * 16, 16), 16)
            value = x[at].astype(f32)
            scale = lax.rsqrt(jnp.mean(value * value, axis=1, keepdims=True) + epsilon)
            normed[at] = (value * scale * vec[0:1]).astype(bf16)

        load(0, normed, normed_out).start()
        share(1, kvw_all).wait()
        load(3, kvw_all, kvw).start()
        load(3, kvw_all, kvw).wait()
        both = dot(normed[...], kvw[...].reshape(width, 2 * HD))
        kv_low[:, :HD] = turn(both[:, :HD]).astype(bf16)
        kv_low[:, HD:] = both[:, HD:].astype(bf16)
        next(keys)
        for _ in queries:
            pass
        load(3, query_all, weight).start()
        load(3, query_all, weight).wait()

        @pl.loop(0, heads)
        def _(h):
            at = pl.ds(pl.multiple_of(h * HD, HD), HD)
            value = dot(normed[...], weight[:, :, at].reshape(width, HD))
            qs[:, at] = (turn(value) * scale_factor).astype(bf16)

        load(4, qs, queries_out).start()
        for _ in range(3):
            next(outw)
            next(keys)
        for _ in keys:
            pass
        next(ffn)
        next(ffn)
        load(3, kv_all.at[pl.ds(start, reach + 1)], win).start()
        load(3, kv_all.at[pl.ds(start, reach + 1)], win).wait()

        @pl.loop(0, heads)
        def _(h):
            at = pl.ds(pl.multiple_of(h * HD, HD), HD)
            window = win[...].reshape(span, 2 * HD)
            scores = dot(qs[:, at], window[:, :HD], 1, 1) + mask[...]
            top = jnp.max(scores, axis=1, keepdims=True)
            exponent = jnp.exp(scores - top)
            total = jnp.sum(exponent, axis=1, keepdims=True)
            blend = dot(exponent.astype(bf16), window[:, HD:])
            mixed[:, at] = (blend / total).astype(bf16)
            logs[h] = top + jnp.log(total)

        load(5, mixed, mixed_out).start()
        load(6, logs, log_out).start()
        next(outw)
        for _ in outw:
            pass
        next(ffn)
        load(3, out_all, weight).start()
        load(3, out_all, weight).wait()

        @pl.loop(0, LINE)
        def _(i):
            at = pl.ds(pl.multiple_of(i * 4 * rows, LANES), 4 * rows)
            piece = weight[pl.ds(4 * i, 4)].reshape(4 * rows, heads * HD)
            part[:, at] = dot(mixed[...], piece, 1, 1).astype(bf16)

        swapped = remote(part, theirs, swap_sems[0].at[2], swap_sems[1].at[2], me.other())
        swapped.start()
        swapped.wait()

        @pl.loop(0, tokens // 16)
        def _(i):
            at = pl.ds(pl.multiple_of(i * 16, 16), 16)
            total = x[at].astype(f32) + (part[at].astype(f32) + theirs[at].astype(f32)) + vec[1:2]
            middle[at] = total
            scale = lax.rsqrt(jnp.mean(total * total, axis=1, keepdims=True) + epsilon)
            normed_two[at] = (total * scale * vec[2:3]).astype(bf16)

        out = spread(me, normed_two, normed_two_out, spread_sems)
        next(out)
        load(7, middle, middle_out).start()
        next(out)
        next(ffn)
        next(out)
        next(ffn)
        next(out)
        next(cot)
        next(ffn)
        for _ in range(3):
            next(cot)
        for step in (ffn, out, cot):
            for _ in step:
                pass
        for n, src, dst in (
            (0, normed, normed_out),
            (1, vec, vec_out),
            (2, marks_row, marks_out),
            (4, qs, queries_out),
            (5, mixed, mixed_out),
            (6, logs, log_out),
            (7, middle, middle_out),
        ):
            load(n, src, dst).wait()
        return []

    query_shape = (tokens, heads * HD)
    (
        query_full, kv_full, smalls, kv_all, out_full, ffn_full, cot_all, mixed_low, log_total,
        middle, normed_all, queries, normed, vec, window_marks,
    ) = transfer(
        0,
        [
            query_own, kv_own, small, out_own, gate_up_own, down_own, inputs, cotangent,
            own_marks, turn_cos, turn_sin, pick_device, pick_entry,
        ],
        [
            ((RING,) + query_own.shape, bf16),
            ((RING, 2) + kv_own.shape, bf16),
            ((RING, 2) + small.shape, bf16),
            ((RING, tokens, 2 * HD), bf16),
            ((RING,) + out_own.shape, bf16),
            ((3, RING, rows, block), bf16),
            ((LINE,) + inputs.shape, bf16),
            (query_shape, bf16),
            ((heads, tokens, 1), f32),
            (inputs.shape, f32),
            ((LINE,) + inputs.shape, bf16),
            (query_shape, bf16),
            (inputs.shape, bf16),
            ((8, width), f32),
            ((1, span), f32),
        ],
        [
            GATHER_SEMS,
            GATHER_SEMS,
            GATHER_SEMS,
            GATHER_SEMS,
            GATHER_SEMS,
            PIECE_SEMS,
            SPREAD_SEMS,
            SPREAD_SEMS,
            [pltpu.SemaphoreType.DMA((3,)), pltpu.SemaphoreType.DMA((3,))],
            [
                pltpu.VMEM(query_shape, bf16),
                pltpu.VMEM((reach + 1, tokens, 2 * HD), bf16),
                pltpu.VMEM((RING,) + out_own.shape, bf16),
                pltpu.VMEM((RING, 2) + kv_own.shape, bf16),
                pltpu.VMEM((tokens, span), f32),
                pltpu.VMEM(query_shape, bf16),
                pltpu.VMEM(inputs.shape, bf16),
                pltpu.VMEM(inputs.shape, bf16),
                pltpu.VMEM(inputs.shape, bf16),
                pltpu.VMEM(inputs.shape, f32),
                pltpu.VMEM(inputs.shape, bf16),
                pltpu.VMEM(inputs.shape, bf16),
                pltpu.VMEM((heads, tokens, 1), f32),
                pltpu.VMEM((RING, 2) + small.shape, bf16),
                pltpu.VMEM((2 * RING,) + small.shape, f32),
                pltpu.VMEM((8, width), f32),
                pltpu.VMEM((1, span), f32),
                pltpu.VMEM((tokens, 2 * HD), bf16),
                pltpu.SemaphoreType.DMA((8,)),
            ],
        ],
        first_steps,
        near=(8, 9, 10, 11, 12),
    )
    query_full = query_full.reshape(width, heads * HD)
    kv_full = kv_full.reshape(width, columns)
    out_full = out_full.reshape(width, heads * HD)
    ffn_full = ffn_full.reshape(3, width, block)
    gain_one, _, gain_two, bias_down = (vec[i] for i in range(4))
    stream = inputs.astype(f32)

    def hidden_vector(row):
        piece = smalls[:, :, row, : hidden_bias.shape[1]].reshape(RING, 2, groups, -1)
        return jnp.transpose(piece, (2, 0, 1, 3)).reshape(-1).astype(f32)

    bias_gate_up = jnp.stack([hidden_vector(4 + i) for i in range(2)])
    bias_local = lax.dynamic_slice_in_dim(bias_gate_up, t * hidden_half + block_start, block, 1)

    ours = (jnp.arange(block) >= block_skip).astype(f32)[None, :]
    part_rows = 4 * rows
    pace = block // 2

    def third_steps(me, ins, outs, groups_in):
        normed_in, cot_in, weights_in, bias, valid = ins
        normed_grad_out, mlp_out, total, bias_own, bias_theirs, term, *buffers = outs
        one_scratch, two_scratch, plane_sems, swap_sems, scratch = groups_in
        (
            weights, normed_v, cot_v, chunks, hidden, gate_low, up_low, bias_sum, bias_low,
            stage, here, there, loads,
        ) = scratch
        one = LineSum(me, normed_grad_out, one_scratch)
        two = LineSum(me, mlp_out, two_scratch)
        plane = PlaneSum(me, term, buffers, total, here, there, plane_sems)

        def load(n, src, dst):
            return pltpu.make_async_copy(src, dst, loads.at[n])

        def part_columns(i):
            return pl.ds(pl.multiple_of(i * part_rows, LANES), part_rows)

        def rows_of(i):
            return pl.ds(pl.multiple_of(i * tokens, tokens), tokens)

        for n in range(3):
            load(n, weights_in.at[n], weights.at[n]).start()
        load(3, normed_in.at[0], normed_v).start()
        load(4, cot_in.at[0], cot_v).start()
        bias_sum[...] = jnp.zeros(bias_sum.shape, f32)
        for n in range(3):
            load(n, weights_in.at[n], weights.at[n]).wait()

        def both_ways(place):
            load(3, normed_in.at[place], normed_v).wait()
            load(4, cot_in.at[place], cot_v).wait()
            at = rows_of(place)

            @pl.loop(0, 2)
            def _(n):
                part = pl.ds(pl.multiple_of(n * pace, LANES), pace)
                gate = dot(normed_v[...], weights[0, :, part]) + bias[0:1, part]
                up = dot(normed_v[...], weights[1, :, part]) + bias[1:2, part]
                grad = dot(cot_v[...], weights[2, :, part]) * valid[:, part]
                square = gate * gate
                slope = 0.7978845608028654 * (1.0 + 3.0 * 0.044715 * square)
                turn = jnp.tanh(0.7978845608028654 * gate * (1.0 + 0.044715 * square))
                side = 0.5 * (1.0 + turn)
                unit = gate * side
                hidden[at, part] = (unit * up * valid[:, part]).astype(bf16)
                gate_grad = grad * up * (side + 0.5 * gate * (1.0 - turn * turn) * slope)
                gate_low[at, part] = gate_grad.astype(bf16)
                up_low[at, part] = (grad * unit).astype(bf16)
                for i, low in enumerate((gate_low, up_low)):
                    bias_sum[i : i + 1, part] += jnp.sum(
                        low[at, part].astype(f32), axis=0, keepdims=True
                    )

            @pl.when(place < LINE - 1)
            def _():
                load(3, normed_in.at[place + 1], normed_v).start()
                load(4, cot_in.at[place + 1], cot_v).start()

        pl.loop(0, LINE)(both_ways)

        def back(place):
            at = rows_of(place)

            @pl.loop(0, LINE)
            def _(i):
                lines = part_columns(i)
                value = dot(gate_low[at], weights[0, lines], 1, 1)
                value += dot(up_low[at], weights[1, lines], 1, 1)
                one.src[place, :, lines] = value.astype(bf16)

            one.cross(place).start()

        bias_low[...] = bias_sum[...].astype(bf16)
        bias_swap = remote(bias_low, bias_theirs, swap_sems[0], swap_sems[1], me.other())
        bias_swap.start()
        bias_keep = load(0, bias_low, bias_own)
        bias_keep.start()

        def chunk(source, i, slot):
            return load(3 + slot, source.at[:, :, part_columns(i)], chunks.at[slot])

        def stored(n, target):
            return load(1 + n, stage.at[n], target)

        def weight_term(slot, factor, n, target):
            left = chunks[slot].reshape(LINE * tokens, part_rows)
            stage[n] = dot(left, factor[...], 0, 0).astype(bf16).reshape(stage.shape[1:])
            stored(n, target).start()

        def outputs_of(place):
            @pl.loop(0, LINE)
            def _(i):
                lines = part_columns(i)
                value = dot(hidden[rows_of(place)], weights[2, lines], 1, 1)
                two.src[place, :, lines] = value.astype(bf16)

            two.cross(place).start()

        def down_terms(i):
            slot = lax.rem(i, 2)
            chunk(cot_in, i, slot).wait()

            @pl.when(i < LINE - 1)
            def _():
                chunk(cot_in, i + 1, 1 - slot).start()

            @pl.when(i > 1)
            def _():
                stored(slot, term.at[2, i]).wait()

            weight_term(slot, hidden, slot, term.at[2, i])

        def gate_up_terms(i):
            slot = lax.rem(i, 2)
            chunk(normed_in, i, slot).wait()

            @pl.when(i < LINE - 1)
            def _():
                chunk(normed_in, i + 1, 1 - slot).start()

            for n, factor in enumerate((gate_low, up_low)):

                @pl.when(i > 0)
                def _():
                    stored(n, term.at[n, i]).wait()

                weight_term(slot, factor, n, term.at[n, i])

        chunk(cot_in, 0, 0).start()

        @pl.loop(0, 2)
        def _(i):
            outputs_of(3 - 3 * i)

        two.fold(3)
        two.fold(0)
        two.step(0)
        pl.loop(0, LINE)(down_terms)
        chunk(normed_in, 0, 0).start()
        for n in range(2):
            stored(n, term.at[2, 0]).wait()
        plane.start(2)

        @pl.loop(0, 2)
        def _(i):
            outputs_of(2 - i)

        two.fold(2)
        two.fold(1)
        two.step(1)
        pl.loop(0, LINE)(gate_up_terms)
        for n in range(2):
            stored(n, term.at[n, 0]).wait()
        plane.start(0)
        two.step(2)

        @pl.loop(0, 2)
        def _(i):
            back(3 - 3 * i)

        one.fold(3)
        one.fold(0)
        one.step(0)

        @pl.loop(0, 2)
        def _(i):
            back(2 - i)

        one.fold(2)
        one.fold(1)
        two.finish()
        one.step(1)
        plane.fold(2)
        plane.pass_on(2)
        one.step(2)
        plane.fold(0)
        plane.pass_on(0)
        plane.fold_again(2)
        one.finish()
        plane.fold_again(0)
        one.close()
        two.close()
        for part in (0, 2):
            plane.close(part)
        bias_swap.wait()
        bias_keep.wait()
        return []

    half_shape = (2, 3, LINE, rows // 2, block)
    normed_two_grad, mlp_out, ffn_total, hidden_bias_part, bias_theirs, ffn_term = transfer(
        1,
        [normed_all, cot_all, ffn_full, bias_local, ours],
        [
            ((tokens, width), bf16),
            ((tokens, width), bf16),
            ((3, LINE, rows, block), bf16),
            ((16, block), bf16),
            ((16, block), bf16),
            ((3, LINE, 4, rows, block), bf16),
            ((3, 2, 2, LINE, rows // 2, block), bf16),
            (half_shape, bf16),
            (half_shape, bf16),
            (half_shape, bf16),
        ],
        [
            line_sum_scratch(tokens // 2, width),
            line_sum_scratch(tokens // 2, width),
            PLANE_SUM_SEMS,
            SWAP_SEMS,
            [
                pltpu.VMEM((3, width, block), bf16),
                pltpu.VMEM((tokens, width), bf16),
                pltpu.VMEM((tokens, width), bf16),
                pltpu.VMEM((2, LINE, tokens, part_rows), bf16),
                pltpu.VMEM((LINE * tokens, block), bf16),
                pltpu.VMEM((LINE * tokens, block), bf16),
                pltpu.VMEM((LINE * tokens, block), bf16),
                pltpu.VMEM((16, block), f32),
                pltpu.VMEM((16, block), bf16),
                pltpu.VMEM((2, 4, rows, block), bf16),
                pltpu.VMEM((2, LINE, rows // 2, block), bf16),
                pltpu.VMEM((2, LINE, rows // 2, block), bf16),
                pltpu.SemaphoreType.DMA((5,)),
            ],
        ],
        third_steps,
        near=(3, 4),
    )[:6]
    cot_full = cotangent.astype(f32)
    _, norm_two_pull = jax.vjp(normalize, middle, gain_two)
    middle_part, gain_two_grad = norm_two_pull(normed_two_grad.astype(f32))
    middle_grad = cot_full + middle_part
    middle_low = middle_grad.astype(bf16)

    def core_features(full):
        blocks = full.reshape(full.shape[0], RING, groups, 2, -1)
        blocks = lax.dynamic_index_in_dim(blocks, t, 3, keepdims=False)
        return jnp.moveaxis(blocks, 1, 0).reshape(RING, full.shape[0], -1)

    def core_hidden(full):
        blocks = full.reshape(full.shape[0], groups, RING, 2, -1)
        blocks = lax.dynamic_index_in_dim(blocks, t, 3, keepdims=False)
        return jnp.transpose(blocks, (2, 0, 1, 3)).reshape(RING, full.shape[0], -1)

    vector_terms = core_features(
        jnp.stack([jnp.sum(middle_grad, axis=0), gain_two_grad, jnp.sum(cot_full, axis=0)])
    )
    bias_pair = jnp.where(
        t == 0,
        jnp.stack([hidden_bias_part, bias_theirs]),
        jnp.stack([bias_theirs, hidden_bias_part]),
    )[:, :2].astype(f32)
    bias_terms = jnp.zeros((2, 2, hidden_half), f32)
    bias_terms = lax.dynamic_update_slice_in_dim(bias_terms, bias_pair, block_start, 2)
    bias_terms = core_hidden(jnp.swapaxes(bias_terms, 0, 1).reshape(2, -1))

    def widen(x):
        return jnp.pad(x, ((0, 0), (0, 0), (0, HD - x.shape[2])))

    small_terms = jnp.concatenate(
        [widen(vector_terms), widen(bias_terms), jnp.zeros((RING, 27, HD), f32)], axis=1
    ).astype(bf16)

    chunk = 3 if (reach + 1) % 3 == 0 else 1
    pieces = (reach + 1) // chunk
    kv_size = rows + small_terms.shape[1]
    vector_rows = -(-width // (LANES * 32)) * 32

    def fourth_steps(me, ins, outs, groups_in):
        (
            low_in, out_in, mixed_in, q_in, kv_in, logs_in, normed_in, query_in, kvw_in,
            ffn_in, total_in, small_in, grad_in, x_in,
            marks_row, marks_column, cos2, sin2, gain,
        ) = ins
        ffn_done, out_done, query_done, kv_done, input_out, gain_all = outs[:6]
        out_term, query_term, kv_term = outs[6:9]
        out_buffers, kv_buffers, ffn_buffers = outs[9:14], outs[14:19], outs[19:24]
        query_buffers = (outs[24:29], outs[29:34])
        (
            line_sems, line_sems_two, ffn_sems, out_sems, query_sems, more_sems, kv_sems, window_scratch, swap_sems, last_sems,
            vector_sems, scratch,
        ) = groups_in
        (
            low, weight, mixed, qs, win, normed_v, logs, mixed_grad, q_grad, window_sum, mask,
            kv_total, kv_low, kvw, stage, kv_stage, here, there, kv_here, kv_there, part, theirs,
            gain_sum, gain_rows, gain_low, loads,
        ) = scratch

        def load(n, src, dst):
            return pltpu.make_async_copy(src, dst, loads.at[n])

        def turn(v, direction):
            first = v[:, : HD // 2]
            turned = first * cos2[...] + direction * (pltpu.roll(first, HD // 4, 1) * sin2[...])
            return jnp.concatenate([turned, v[:, HD // 2 :]], axis=1)

        part_rows = 4 * rows

        def part_columns(i):
            return pl.ds(pl.multiple_of(i * part_rows, LANES), part_rows)

        lines = [
            line_exchange(me, total_in.at[2], ffn_done.at[2], line_sems),
            line_exchange(me, total_in.at[0], ffn_done.at[0], line_sems_two),
        ]
        ffn = scatter(me, ffn_in.at[1], ffn_done.at[1], ffn_buffers, here, there, ffn_sems)
        outw = scatter(me, out_term, out_done, out_buffers, here, there, out_sems)
        query, more = (
            scatter(me, query_term.at[n], query_done.at[n], query_buffers[n], here, there, sems)
            for n, sems in enumerate((query_sems, more_sems))
        )
        kvw_steps = scatter(
            me, kv_term, kv_done.at[me.t], kv_buffers, kv_here, kv_there, kv_sems
        )
        for step in [ffn, outw, query, more, kvw_steps] + lines + [ffn]:
            next(step)
        start = jnp.maximum(me.r - reach, 0)
        first_loads = [
            load(0, low_in, low),
            load(1, mixed_in, mixed),
            load(2, out_in, weight),
            load(3, q_in, qs),
            load(4, kv_in.at[pl.ds(start, reach + 1)], win),
            load(5, logs_in, logs),
            load(6, normed_in, normed_v),
            load(7, kvw_in, kvw),
        ]
        for copy in first_loads:
            copy.start()
        first_loads[0].wait()
        first_loads[1].wait()

        def weight_term(left, right, targets):
            width_of = heads * HD // len(targets)

            @pl.loop(0, LINE)
            def _(i):
                value = dot(left[:, part_columns(i)], right[...], 0, 0).astype(bf16)
                stage[...] = value.reshape(stage.shape)
                copies = [
                    load(8 + n, stage.at[:, :, pl.ds(n * width_of, width_of)], term.at[i])
                    for n, term in enumerate(targets)
                ]
                for copy in copies:
                    copy.start()
                for copy in copies:
                    copy.wait()

        weight_term(low, mixed, [out_term])
        first_loads[2].wait()

        @pl.loop(0, heads)
        def _(h):
            at = pl.ds(pl.multiple_of(h * HD, HD), HD)
            mixed_grad[:, at] = dot(low[...], weight[:, at]).astype(bf16)

        load(2, query_in, weight).start()
        load(0, x_in, low).start()
        row_places = me.r * tokens + lax.broadcasted_iota(jnp.int32, (tokens, 1), 0)

        @pl.loop(0, reach + 1)
        def _(i):
            at = pl.ds(pl.multiple_of(i * tokens, tokens), tokens)
            key_places = (start + i) * tokens + lax.broadcasted_iota(jnp.int32, (1, tokens), 1)
            gap = row_places - key_places
            seen = (gap >= 0) & (gap < W) & (marks_column[...] == marks_row[:, at])
            mask[:, at] = jnp.where(seen, 0.0, -1e30)
            window_sum[i] = jnp.zeros((tokens, 2 * HD), f32)

        for copy in first_loads[3:]:
            copy.wait()

        @pl.loop(0, heads)
        def _(h):
            at = pl.ds(pl.multiple_of(h * HD, HD), HD)
            q_head = qs[:, at]
            grad = mixed_grad[:, at]
            inner = jnp.sum(grad.astype(f32) * mixed[:, at].astype(f32), axis=1, keepdims=True)
            log = logs[h]
            q_sum = jnp.zeros((tokens, HD), f32)
            for c in range(pieces):
                blocks = pl.ds(c * chunk, chunk)
                both = win[blocks].reshape(chunk * tokens, 2 * HD)
                k, v = both[:, :HD], both[:, HD:]
                span_at = pl.ds(c * chunk * tokens, chunk * tokens)
                probs = jnp.exp(dot(q_head, k, 1, 1) + mask[:, span_at] - log)
                value_sum = dot(probs.astype(bf16), grad, 0, 0)
                score_grad = (probs * (dot(grad, v, 1, 1) - inner)).astype(bf16)
                q_sum += dot(score_grad, k)
                key_sum = dot(score_grad, q_head, 0, 0)
                window_sum[blocks, :, :HD] += key_sum.reshape(chunk, tokens, HD)
                window_sum[blocks, :, HD:] += value_sum.reshape(chunk, tokens, HD)
            q_grad[:, at] = (turn(q_sum, -1.0) * scale_factor).astype(bf16)

            @pl.when(h == heads - 1)
            def _():
                next(outw)


        @pl.loop(0, reach + 1)
        def _(i):
            win[i] = window_sum[i].astype(bf16)

        window_steps = reduce_window(me, reach, win, kv_total, window_scratch)
        next(window_steps)
        load(5, grad_in, mask).start()
        next(window_steps)
        weight_term(normed_v, q_grad, [query_term.at[0], query_term.at[1]])
        load(2, query_in, weight).wait()

        @pl.loop(0, LINE)
        def _(i):
            piece = weight[pl.ds(pl.multiple_of(i * part_rows, LANES), part_rows)]
            part[:, part_columns(i)] = dot(q_grad[...], piece, 1, 1).astype(bf16)

        swapped = remote(part, theirs, swap_sems[0], swap_sems[1], me.other())
        swapped.start()
        next(ffn)
        next(outw)
        next(query)
        next(ffn)
        next(window_steps)
        next(window_steps, None)

        kv_low[:, :HD] = turn(kv_total[:, :HD], -1.0).astype(bf16)
        kv_low[:, HD:] = kv_total[:, HD:].astype(bf16)
        ours_at = pl.ds(pl.multiple_of(me.t * HD, HD), HD)
        small_copy = load(0, x_in, low)
        small_copy.wait()

        @pl.loop(0, LINE)
        def _(i):
            value = dot(normed_v[:, part_columns(i)], kv_low[:, ours_at], 0, 0).astype(bf16)
            kv_stage[:, pl.ds(0, rows)] = value.reshape(4, rows, HD)
            copy = load(9, small_in.at[pl.ds(4 * i, 4)], kv_stage.at[:, pl.ds(rows, kv_size - rows)])
            copy.start()
            copy.wait()
            copy = load(9, kv_stage, kv_term.at[i])
            copy.start()
            copy.wait()

        next(more)
        next(kvw_steps)
        next(outw)
        next(query)

        swapped.wait()

        @pl.loop(0, width // (2 * HD))
        def _(i):
            at = pl.ds(pl.multiple_of(i * 2 * HD, 2 * HD), 2 * HD)
            more = dot(kv_low[...], kvw[at], 1, 1)
            window_sum[i] = part[:, at].astype(f32) + theirs[:, at].astype(f32) + more

        gain_sum[...] = jnp.zeros(gain_sum.shape, f32)
        load(5, grad_in, mask).wait()

        @pl.loop(0, tokens // 16)
        def _(i):
            at = pl.ds(pl.multiple_of(i * 16, 16), 16)
            grad = jnp.concatenate([window_sum[n, at] for n in range(width // (2 * HD))], axis=1)
            stream_rows = low[at].astype(f32)
            scale = lax.rsqrt(
                jnp.mean(stream_rows * stream_rows, axis=1, keepdims=True) + epsilon
            )
            unit = stream_rows * scale
            gain_sum[...] += grad * unit
            scaled = grad * gain[...]
            inner = jnp.mean(scaled * unit, axis=1, keepdims=True)
            mask[at] = mask[at] + scale * (scaled - unit * inner)

        load(5, mask, input_out).start()
        gain_rows[...] = jnp.zeros(gain_rows.shape, f32)
        gain_total = jnp.sum(gain_sum[...], axis=0, keepdims=True)
        for i in range(width // LANES):
            gain_rows[pl.ds(i, 1)] = gain_total[:, i * LANES : (i + 1) * LANES]
        gain_low[...] = gain_rows[...].astype(bf16)

        def gain_send(k):
            to = (me.base + lax.rem(me.r + k, RING), me.t)
            return remote(
                gain_low, gain_all.at[me.r], vector_sems[0].at[k], vector_sems[1].at[me.r], to
            )

        keep_gain = load(9, gain_low, gain_all.at[me.r])
        keep_gain.start()

        @pl.loop(1, RING)
        def _(k):
            gain_send(k).start()

        next(more)
        next(kvw_steps)
        next(query)
        next(more)
        next(kvw_steps)
        for step in lines + [ffn, outw, query, more, kvw_steps]:
            for _ in step:
                pass
        mine = kv_done.at[me.t]
        last = remote(mine, mine, last_sems[0], last_sems[1], me.other())
        last.start()

        @pl.loop(1, RING)
        def _(k):
            gain_send(k).wait_send()
            source = lax.rem(me.r + k, RING)
            landed = gain_all.at[source]
            remote(
                landed, landed, vector_sems[0].at[k], vector_sems[1].at[source], me.at(me.z, me.q)
            ).wait_recv()

        keep_gain.wait()
        load(5, mask, input_out).wait()
        last.wait()
        return []

    term_shape = (LINE, 4, rows, heads * HD)
    ffn_shape = (3, LINE, rows, block)
    half = (2, 2, LINE, rows // 2, heads * HD)
    kv_half = (2, 2, LINE, kv_size // 2, HD)
    ffn_done, out_done, query_done, kv_done, input_grad, gain_all = transfer(
        2,
        [
            middle_low, out_full, mixed_low, queries, kv_all, log_total, normed, query_full, kv_full,
            ffn_term, ffn_total, small_terms, middle_grad, inputs,
            window_marks, own_marks, turn_cos, turn_sin, gain_one[None],
        ],
        [
            (ffn_shape, bf16),
            ((LINE, rows, heads * HD), bf16),
            ((2, LINE, rows, heads * HD // 2), bf16),
            ((2, LINE, kv_size, HD), bf16),
            (inputs.shape, f32),
            ((RING, vector_rows, LANES), bf16),
            (term_shape, bf16),
            ((2,) + term_shape[:-1] + (heads * HD // 2,), bf16),
            ((LINE, 4, kv_size, HD), bf16),
        ]
        + scatter_buffers(rows, heads * HD)
        + scatter_buffers(kv_size, HD)
        + scatter_buffers(rows, block)
        + scatter_buffers(rows, heads * HD // 2) * 2,
        [
            LINE_SEMS,
            LINE_SEMS,
            SCATTER_SEMS,
            SCATTER_SEMS,
            SCATTER_SEMS,
            SCATTER_SEMS,
            SCATTER_SEMS,
            reduce_scratch(reach + 1, tokens // 2, 2 * HD, f32),
            SWAP_SEMS,
            SWAP_SEMS,
            [pltpu.SemaphoreType.DMA((RING,)), pltpu.SemaphoreType.DMA((RING,))],
            [
                pltpu.VMEM(inputs.shape, bf16),
                pltpu.VMEM(out_full.shape, bf16),
                pltpu.VMEM(queries.shape, bf16),
                pltpu.VMEM(queries.shape, bf16),
                pltpu.VMEM((reach + 1, tokens, 2 * HD), bf16),
                pltpu.VMEM(inputs.shape, bf16),
                pltpu.VMEM((heads, tokens, 1), f32),
                pltpu.VMEM(queries.shape, bf16),
                pltpu.VMEM(queries.shape, bf16),
                pltpu.VMEM((reach + 1, tokens, 2 * HD), f32),
                pltpu.VMEM(inputs.shape, f32),
                pltpu.VMEM((tokens, 2 * HD), f32),
                pltpu.VMEM((tokens, 2 * HD), bf16),
                pltpu.VMEM(kv_full.shape, bf16),
                pltpu.VMEM((4, rows, heads * HD), bf16),
                pltpu.VMEM((4, kv_size, HD), bf16),
                pltpu.VMEM(half, bf16),
                pltpu.VMEM(half, bf16),
                pltpu.VMEM(kv_half, bf16),
                pltpu.VMEM(kv_half, bf16),
                pltpu.VMEM(inputs.shape, bf16),
                pltpu.VMEM(inputs.shape, bf16),
                pltpu.VMEM((16, width), f32),
                pltpu.VMEM((vector_rows, LANES), f32),
                pltpu.VMEM((vector_rows, LANES), bf16),
                pltpu.SemaphoreType.DMA((10,)),
            ],
        ],
        fourth_steps,
        whole=True,
        near=(14, 15, 16, 17, 18),
    )[:6]
    output = (middle + mlp_out.astype(f32) + bias_down).astype(bf16)

    last_skip = LINE * block - hidden_half
    ffn_grad = jnp.concatenate(
        [ffn_done[:, i] for i in range(LINE - 1)] + [ffn_done[:, LINE - 1, :, last_skip:]], axis=2
    )
    ffn_grad = shrink(ffn_grad.astype(f32), 1, groups)
    out_grad = shrink(jnp.sum(out_done.astype(f32), axis=0), 0, groups).T
    query_sum = jnp.sum(query_done.astype(f32), axis=1)
    query_grad = shrink(jnp.concatenate([query_sum[0], query_sum[1]], axis=1), 0, groups)
    kv_sums = jnp.sum(kv_done.astype(f32), axis=1)
    small_sums = lax.dynamic_index_in_dim(kv_sums[:, rows:], t, 0, keepdims=False)
    kv_grad = jnp.concatenate([kv_sums[0, :rows], kv_sums[1, :rows]], axis=1)
    kv_grad = lax.dynamic_index_in_dim(kv_grad.reshape(groups, 2, -1, columns), t, 1, keepdims=False)
    key_value_grad = shrink(kv_grad.reshape(kv_rows, columns), 0, groups)
    gain_sum = jnp.sum(gain_all[:, : width // LANES].astype(f32), axis=0).reshape(
        RING, groups, 2, kv_rows // groups
    )
    gain_sum = lax.dynamic_index_in_dim(gain_sum, r, 0, keepdims=False)
    gain_sum = lax.dynamic_index_in_dim(gain_sum, t, 1, keepdims=False).reshape(kv_rows)
    small_grads = [shrink(v, 0, groups) for v in [gain_sum] + [small_sums[i, :kv_rows] for i in range(3)]]
    gate_up_bias_grad = shrink(small_sums[3:5, : hidden_bias.shape[1]], 1, groups)
    return (
        from_places(output, groups),
        from_places(input_grad, groups),
        small_grads[0],
        query_grad,
        key_value_grad,
        out_grad,
        small_grads[1],
        small_grads[2],
        ffn_grad[:2],
        gate_up_bias_grad,
        ffn_grad[2].T,
        small_grads[3],
    )


def solution(mesh):
    in_specs = (
        P("seq", None),
        P("seq"),
        P("seq", None),
        P(("seq", "tensor")),
        P("seq", "tensor"),
        P(("seq", "tensor"), None),
        P("tensor", "seq"),
        P(("seq", "tensor")),
        P(("seq", "tensor")),
        P(None, "seq", "tensor"),
        P(None, ("seq", "tensor")),
        P("tensor", "seq"),
        P(("seq", "tensor")),
    )
    out_specs = (
        P("seq", None),
        P("seq", None),
        P(("seq", "tensor")),
        P("seq", "tensor"),
        P(("seq", "tensor"), None),
        P("tensor", "seq"),
        P(("seq", "tensor")),
        P(("seq", "tensor")),
        P(None, "seq", "tensor"),
        P(None, ("seq", "tensor")),
        P("tensor", "seq"),
        P(("seq", "tensor")),
    )
    return jax.shard_map(body, mesh=mesh, in_specs=in_specs, out_specs=out_specs, check_vma=False)
```

```python
import functools

import jax
import jax.numpy as jnp
from jax import lax
from jax.experimental import pallas as pl
from jax.experimental.pallas import tpu as pltpu
from jax.sharding import PartitionSpec as P

HD = 256
W = 2048
SEQ_LEN = 4096
LINE = 4
RING = 16
LANES = 128

epsilon = 1e-06
bf16 = jnp.bfloat16
f32 = jnp.float32
MESH = pl.DeviceIdType.MESH
ANY = pl.BlockSpec(memory_space=pl.ANY)
VMEM = pl.BlockSpec(memory_space=pltpu.VMEM)


class Place:
    def __init__(self):
        seq = lax.axis_index("seq")
        self.t = lax.axis_index("tensor")
        self.r = lax.rem(seq, RING)
        self.base = seq - self.r
        self.z = lax.div(self.r, 4)
        self.q = lax.rem(self.r, 4)
        self.xq = self.q + 1 - 2 * lax.rem(self.q, 2)
        self.yq = self.q + 2 - 4 * lax.div(self.q, 2)
        self.dq = 3 - self.q
        self.half = lax.div(self.z, 2)
        self.inner = self.z + self.half * (3 - 2 * self.z)

    def at(self, z, q):
        return (self.base + 4 * z + q, self.t)

    def other(self):
        return (self.base + self.r, 1 - self.t)

    def order(self, j):
        v = j + self.inner * (1 - 2 * j if j < 2 else 0)
        return v + self.half * (3 - 2 * v)

    def greet(self, whole=False):
        barrier = pltpu.get_barrier_semaphore()
        if whole:
            peers = [
                (self.base + lax.rem(self.r + k, RING), self.t) for k in range(1, RING)
            ]
        else:
            peers = [self.at(lax.rem(self.z + k, 4), self.q) for k in range(1, 4)]
            peers += [self.at(self.z, self.xq), self.at(self.z, self.yq)]
        peers.append(self.other())
        for peer in peers:
            pl.semaphore_signal(barrier, inc=1, device_id=peer, device_id_type=MESH)
        pl.semaphore_wait(barrier, len(peers))


def remote(src, dst, send, recv, device):
    return pltpu.make_async_remote_copy(
        src_ref=src, dst_ref=dst, send_sem=send, recv_sem=recv, device_id=device, device_id_type=MESH
    )


def run(steps):
    steps, ending = list(steps), []
    while steps:
        for step in list(steps):
            if next(step, True):
                steps.remove(step)
                ending.append(step)
    for step in ending:
        next(step, None)


GATHER_SEMS = [
    pltpu.SemaphoreType.DMA((4, 6)),
    pltpu.SemaphoreType.DMA((4, 5)),
    pltpu.SemaphoreType.DMA,
]


def gather(me, own, slot, part, sems):
    snd, rcv, loc = sems
    local = pltpu.make_async_copy(own, slot(me.z, me.q), loc)
    local.start()

    def line(z, k, src, to):
        return remote(src, slot(z, me.q), snd.at[z, k], rcv.at[z, 0], me.at(to, me.q))

    @pl.when(me.z < 3)
    def _():
        line(me.z, 0, own, me.z + 1).start()

    @pl.when(me.z > 0)
    def _():
        line(me.z, 1, own, me.z - 1).start()

    def arrive(j):
        z = me.order(j)
        line(z, 0, slot(z, me.q), me.z).wait_recv()

        @pl.when(me.inner == 1)
        def _():
            step = 3 - 2 * me.z if j == 1 else 2 * me.z - 3
            line(z, 0, slot(z, me.q), me.z + step).start()

    yield from in_plane(me, own, slot, part, snd, rcv, arrive)
    local.wait()

    @pl.when(me.z < 3)
    def _():
        line(me.z, 0, own, me.z + 1).wait_send()

    @pl.when(me.z > 0)
    def _():
        line(me.z, 1, own, me.z - 1).wait_send()

    @pl.when(me.inner == 1)
    def _():
        for j in range(1, 4):
            z = me.order(j)
            line(z, 0, slot(z, me.q), me.z).wait_send()


def in_plane(me, own, slot, part, snd, rcv, arrive):
    def across(z, k, src):
        q = (me.xq, me.yq)[k]
        return remote(src, slot(z, me.q), snd.at[z, 2 + k], rcv.at[z, 1 + k], me.at(me.z, q))

    def corner(z, k):
        src = part(z, (me.xq, me.yq)[k], k)
        if src is None:
            return None
        return remote(src, src, snd.at[z, 4 + k], rcv.at[z, 3 + k], me.at(me.z, (me.yq, me.xq)[k]))

    for k in range(2):
        across(me.z, k, own).start()
    yield
    for j in range(1, 5):
        if j < 4:
            arrive(j)
            z = me.order(j)
            for k in range(2):
                across(z, k, slot(z, me.q)).start()
        z = me.order(j - 1)
        for k in range(2):
            q = (me.xq, me.yq)[k]
            remote(
                slot(z, q), slot(z, q), snd.at[z, 2 + k], rcv.at[z, 1 + k], me.at(me.z, q)
            ).wait_recv()
            copy = corner(z, k)
            if copy is not None:
                copy.start()
        yield
    yield True
    for j in range(4):
        z = me.order(j)
        for k in range(2):
            src = part(z, me.dq, k)
            if src is not None:
                remote(src, src, snd.at[z, 4 + k], rcv.at[z, 3 + k], me.at(me.z, me.xq)).wait_recv()
    for j in range(4):
        z = me.order(j)
        for k in range(2):
            across(z, k, slot(z, me.q)).wait_send()
            copy = corner(z, k)
            if copy is not None:
                copy.wait_send()


PIECE_SEMS = [
    pltpu.SemaphoreType.DMA((4, 6)),
    pltpu.SemaphoreType.DMA((4, 5)),
    pltpu.SemaphoreType.DMA((4, 2)),
    pltpu.SemaphoreType.DMA((4, 2)),
]


def gather_pieces(me, sources, dst, sems):
    snd, rcv, piece_snd, piece_rcv = sems
    half = dst.shape[2] // 2

    def slot(z, q):
        return dst.at[:, 4 * z + q]

    def part(z, q, h):
        return dst.at[:, 4 * z + q, pl.ds(h * half, half)]

    def local(n):
        parts, piece = sources[n]
        return pltpu.make_async_copy(piece(me.z), dst.at[parts, me.r], piece_snd.at[me.z, n])

    def send(z, n):
        parts, piece = sources[n]
        return remote(
            piece(z), dst.at[parts, me.r], piece_snd.at[z, n], piece_rcv.at[me.z, n], me.at(z, me.q)
        )

    for n in range(len(sources)):
        local(n).start()
    for j in range(1, 3):
        for n in range(len(sources)):
            send(me.order(j), n).start()
    yield
    for n in range(len(sources)):
        send(me.order(3), n).start()
    yield

    def arrive(j):
        z = me.order(j)
        for n in range(len(sources)):
            view = dst.at[sources[n][0], 4 * z + me.q]
            remote(view, view, piece_snd.at[z, n], piece_rcv.at[z, n], me.at(z, me.q)).wait_recv()

    for n in range(len(sources)):
        local(n).wait()
    yield from in_plane(me, slot(me.z, me.q), slot, part, snd, rcv, arrive)
    for j in range(1, 4):
        for n in range(len(sources)):
            send(me.order(j), n).wait_send()


SPREAD_SEMS = [
    pltpu.SemaphoreType.DMA((4, 3)),
    pltpu.SemaphoreType.DMA((4, 2)),
    pltpu.SemaphoreType.DMA,
]


def spread(me, src, dst, sems):
    snd, rcv, loc = sems
    rows = src.shape[0] // 2
    mine = pl.ds(pl.multiple_of(me.t * rows, rows), rows)
    local = pltpu.make_async_copy(src, dst.at[me.z], loc)
    local.start()

    def slot(z):
        return dst.at[z, mine]

    def line(z, k, source, to):
        return remote(source, slot(z), snd.at[z, k], rcv.at[z, 0], me.at(to, me.q))

    def share(z):
        return remote(slot(z), slot(z), snd.at[z, 2], rcv.at[z, 1], me.other())

    @pl.when(me.z < 3)
    def _():
        line(me.z, 0, src.at[mine], me.z + 1).start()

    @pl.when(me.z > 0)
    def _():
        line(me.z, 1, src.at[mine], me.z - 1).start()

    yield
    for j in range(1, 4):
        z = me.order(j)
        line(z, 0, slot(z), me.z).wait_recv()

        @pl.when(me.inner == 1)
        def _():
            step = 3 - 2 * me.z if j == 1 else 2 * me.z - 3
            line(z, 0, slot(z), me.z + step).start()

        share(z).start()
        yield
    yield True
    other = pl.ds(pl.multiple_of((1 - me.t) * rows, rows), rows)
    for j in range(1, 4):
        z = me.order(j)
        remote(
            dst.at[z, other], dst.at[z, other], snd.at[z, 2], rcv.at[z, 1], me.other()
        ).wait_recv()
        share(z).wait_send()
    local.wait()

    @pl.when(me.z < 3)
    def _():
        line(me.z, 0, src.at[mine], me.z + 1).wait_send()

    @pl.when(me.z > 0)
    def _():
        line(me.z, 1, src.at[mine], me.z - 1).wait_send()

    @pl.when(me.inner == 1)
    def _():
        for j in range(1, 4):
            z = me.order(j)
            line(z, 0, slot(z), me.z).wait_send()


def swap(me, src, dst, sems):
    copy = remote(src, dst, sems[0], sems[1], me.other())
    copy.start()
    yield True
    copy.wait()


SWAP_SEMS = [pltpu.SemaphoreType.DMA, pltpu.SemaphoreType.DMA]


def add_rows(out, terms):
    rows = out.shape[0]
    step = 16

    @pl.loop(0, rows // step)
    def _(i):
        at = pl.ds(pl.multiple_of(i * step, step), step)
        total = terms[0][at].astype(f32)
        for term in terms[1:]:
            total += term[at].astype(f32)
        out[at] = total.astype(out.dtype)


def reduce_scratch(slots, rows, columns, dtype):
    return [
        pltpu.VMEM((slots, rows, columns), bf16),
        pltpu.VMEM((slots, rows, columns), bf16),
        pltpu.VMEM((slots, rows, columns), bf16),
        pltpu.VMEM((rows, columns), dtype),
        pltpu.SemaphoreType.DMA((slots, 3)),
        pltpu.SemaphoreType.DMA((slots, 2)),
        pltpu.SemaphoreType.DMA((3,)),
    ]


def line_sum_scratch(rows, columns):
    return [
        pltpu.VMEM((LINE, 2 * rows, columns), bf16),
        pltpu.VMEM((LINE, rows, columns), bf16),
        pltpu.VMEM((2, 3, rows, columns), bf16),
        pltpu.SemaphoreType.DMA((LINE,)),
        pltpu.SemaphoreType.DMA((LINE,)),
        pltpu.SemaphoreType.DMA((2, 3)),
        pltpu.SemaphoreType.DMA((2, 3)),
        pltpu.SemaphoreType.DMA((3,)),
    ]


class LineSum:
    def __init__(self, me, out, scratch):
        self.me = me
        self.src, self.there, self.landed, *self.sems = scratch
        rows = self.there.shape[1]
        self.mine = pl.ds(pl.multiple_of(me.t * rows, rows), rows)
        self.theirs = pl.ds(pl.multiple_of((1 - me.t) * rows, rows), rows)
        self.out = out

    def here(self, z):
        return self.src.at[z, self.mine]

    def cross(self, z):
        snd, rcv = self.sems[:2]
        source = self.src.at[z, self.theirs]
        return remote(source, self.there.at[z], snd.at[z], rcv.at[z], self.me.other())

    def send(self, way, k, source):
        me = self.me
        snd, rcv = self.sems[2:4]
        to = me.at(me.z + 1 - 2 * way, me.q)
        return remote(source, self.landed.at[way, k], snd.at[way, k], rcv.at[way, k], to)

    def ends(self):
        me = self.me
        end = self.sems[4]
        done = self.here(me.z)
        keep = pltpu.make_async_copy(done, self.out.at[self.mine], end.at[0])
        return keep, remote(done, self.out.at[self.mine], end.at[1], end.at[2], me.other())

    def fold(self, z):
        self.cross(z).wait_recv()
        add_rows(self.here(z), (self.here(z), self.there.at[z]))

    def step(self, k):
        for way in range(2):
            w = self.me.z if way == 0 else 3 - self.me.z
            block = 3 + w - k if way == 0 else k - w

            @pl.when(w <= k)
            def _():
                if k:

                    @pl.when(w < k)
                    def _():
                        self.send(way, k - 1, self.here(0)).wait_send()

                @pl.when(w == 0)
                def _():
                    self.send(way, k, self.here(block)).start()

                if k:

                    @pl.when(w > 0)
                    def _():
                        partial = self.landed.at[way, k - 1]
                        self.send(way, k - 1, partial).wait_recv()
                        add_rows(partial, (partial, self.here(block)))
                        self.send(way, k, partial).start()

    def finish(self):
        for way in range(2):
            w = self.me.z if way == 0 else 3 - self.me.z

            @pl.when(w > 0)
            def _():
                last = self.landed.at[way, 2]
                self.send(way, 2, last).wait_recv()
                here = self.here(self.me.z)
                add_rows(here, (here, last))

            @pl.when(w < 3)
            def _():
                self.send(way, 2, self.here(0)).wait_send()

        for copy in self.ends():
            copy.start()

    def close(self):
        for z in range(LINE):
            self.cross(z).wait_send()
        for copy in self.ends():
            copy.wait()


def reduce_window(me, reach, src, out, scratch):
    here, there, landed, total, snd, rcv, end = scratch
    rows = here.shape[1]
    slots = reach + 1
    mine = pl.ds(pl.multiple_of(me.t * rows, rows), rows)
    theirs = pl.ds(pl.multiple_of((1 - me.t) * rows, rows), rows)
    start = jnp.maximum(me.r - reach, 0)

    def cross(j):
        return remote(src.at[j, theirs], there.at[j], snd.at[j, 0], rcv.at[j, 0], me.other())

    def local(j):
        return pltpu.make_async_copy(src.at[j, mine], here.at[j], snd.at[j, 1])

    def back(k):
        j = me.r - k - start
        return remote(
            here.at[j], landed.at[k], snd.at[k, 2], rcv.at[k, 1], (me.base + me.r - k, me.t)
        )

    for j in range(slots):
        cross(j).start()
        local(j).start()
    yield
    for j in range(slots):
        local(j).wait()
        cross(j).wait_recv()
        add_rows(here.at[j], (here.at[j], there.at[j]))
    for k in range(reach, 0, -1):

        @pl.when(me.r >= k)
        def _():
            back(k).start()

    yield
    add_rows(total, [here.at[me.r - start]])
    for k in range(1, slots):

        @pl.when(me.r + k < RING)
        def _():
            remote(
                landed.at[k], landed.at[k], snd.at[k, 2], rcv.at[k, 1], me.at(me.z, me.q)
            ).wait_recv()
            add_rows(total, (total, landed.at[k]))

    keep = pltpu.make_async_copy(total, out.at[mine], end.at[0])
    give = remote(total, out.at[mine], end.at[1], end.at[2], me.other())
    keep.start()
    give.start()
    yield True
    for j in range(slots):
        cross(j).wait_send()
    for k in range(1, slots):

        @pl.when(me.r >= k)
        def _():
            back(k).wait_send()

    keep.wait()
    give.wait()


PLANE_SEMS = [pltpu.SemaphoreType.DMA((4,)), pltpu.SemaphoreType.DMA((4,))]


def add_blocks(out, more):
    blocks, rows, _ = out.shape
    steps = rows // 16

    @pl.loop(0, blocks * steps)
    def _(i):
        n = lax.div(i, steps)
        at = pl.ds(pl.multiple_of(lax.rem(i, steps) * 16, 16), 16)
        out[n, at] = (out[n, at].astype(f32) + more[n, at].astype(f32)).astype(out.dtype)


def scatter_buffers(rows, columns):
    half = (2, LINE, rows // 2, columns)
    return [((2,) + half, bf16)] + [(half, bf16)] * 3 + [((LINE, rows, columns), bf16)]


SCATTER_SEMS = [
    pltpu.SemaphoreType.DMA((6,)),
    pltpu.SemaphoreType.DMA((6,)),
    pltpu.SemaphoreType.DMA((8,)),
    pltpu.SemaphoreType.DMA((4,)),
    pltpu.SemaphoreType.DMA((4,)),
]


def scatter(me, src, done, buffers, here, there, sems):
    got, kept, passed, got_two, total = buffers
    snd, rcv, loc, line_snd, line_rcv = sems
    half = src.shape[2] // 2
    across = pl.ds(0, src.shape[3])
    first, second = [], []

    def held(ref, h, i):
        return ref.at[h, i, :, :, across]

    for h in range(2):
        q = (me.xq, me.yq)[h]
        rows = pl.ds(h * half, half)
        for i in range(2):
            n = 2 * h + i
            view = src.at[:, (q, me.dq)[i], rows]
            first.append(remote(view, got.at[h, i], snd.at[n], rcv.at[n], me.at(me.z, q)))
        q = (me.yq, me.xq)[h]
        second.append(
            remote(passed.at[h], got_two.at[h], snd.at[4 + h], rcv.at[4 + h], me.at(me.z, q))
        )
    yield
    for copy in first:
        copy.start()
    yield
    for copy in first:
        copy.wait_recv()
    loads, stores = [], []
    for h in range(2):
        for i in range(2):
            n = 2 * h + i
            view = src.at[:, (me.q, (me.yq, me.xq)[h])[i], pl.ds(h * half, half)]
            loads.append(pltpu.make_async_copy(view, held(here, h, i), loc.at[n]))
            loads.append(pltpu.make_async_copy(got.at[h, i], held(there, h, i), loc.at[4 + n]))
            stores.append(
                pltpu.make_async_copy(held(here, h, i), (kept, passed)[i].at[h], loc.at[n])
            )
    for copy in loads:
        copy.start()
    for copy in loads:
        copy.wait()
    for h in range(2):
        for i in range(2):
            add_blocks(held(here, h, i), held(there, h, i))
    for copy in stores:
        copy.start()
    for copy in stores:
        copy.wait()
    for copy in second:
        copy.start()
    yield
    for copy in second:
        copy.wait_recv()
    loads, stores = [], []
    for h in range(2):
        loads.append(pltpu.make_async_copy(kept.at[h], held(here, h, 0), loc.at[h]))
        loads.append(pltpu.make_async_copy(got_two.at[h], held(there, h, 0), loc.at[4 + h]))
        stores.append(
            pltpu.make_async_copy(held(here, h, 0), total.at[:, pl.ds(h * half, half)], loc.at[h])
        )
    for copy in loads:
        copy.start()
    for copy in loads:
        copy.wait()
    for h in range(2):
        add_blocks(held(here, h, 0), held(there, h, 0))
    for copy in stores:
        copy.start()
    for copy in stores:
        copy.wait()

    def send(j):
        z = me.order(j)
        return remote(total.at[z], done.at[me.z], line_snd.at[z], line_rcv.at[me.z], me.at(z, me.q))

    def local():
        return pltpu.make_async_copy(total.at[me.z], done.at[me.z], loc.at[7])

    local().start()
    for j in (3, 2, 1):
        send(j).start()
    yield True
    for j in range(1, 4):
        z = me.order(j)
        remote(done.at[z], done.at[z], line_snd.at[z], line_rcv.at[z], me.at(z, me.q)).wait_recv()
    local().wait()
    for copy in first + second:
        copy.wait_send()
    for j in range(1, 4):
        send(j).wait_send()


PLANE_SUM_SEMS = [
    pltpu.SemaphoreType.DMA((3, 6)),
    pltpu.SemaphoreType.DMA((3, 6)),
    pltpu.SemaphoreType.DMA((4,)),
]


class PlaneSum:
    def __init__(self, me, src, buffers, total, here, there, sems):
        self.me, self.src, self.total = me, src, total
        self.got, self.kept, self.passed, self.got_two = buffers
        self.here, self.there = here, there
        self.snd, self.rcv, self.loc = sems
        self.half = src.shape[3] // 2

    def view(self, part, place, h):
        return self.src.at[part, :, place, pl.ds(h * self.half, self.half)]

    def sends(self, part):
        me = self.me
        copies = []
        for h in range(2):
            q = (me.xq, me.yq)[h]
            for i in range(2):
                n = 2 * h + i
                copies.append(
                    remote(
                        self.view(part, (q, me.dq)[i], h),
                        self.got.at[part, h, i],
                        self.snd.at[part, n],
                        self.rcv.at[part, n],
                        me.at(me.z, q),
                    )
                )
        return copies

    def start(self, part):
        for copy in self.sends(part):
            copy.start()

    def fold(self, part):
        me = self.me
        for copy in self.sends(part):
            copy.wait_recv()
        for h in range(2):
            places = (me.q, (me.yq, me.xq)[h])
            loads, stores = [], []
            for i in range(2):
                a, b = self.here.at[i], self.there.at[i]
                loads.append(pltpu.make_async_copy(self.view(part, places[i], h), a, self.loc.at[i]))
                loads.append(
                    pltpu.make_async_copy(self.got.at[part, h, i], b, self.loc.at[2 + i])
                )
                stores.append(
                    pltpu.make_async_copy(
                        a, (self.kept, self.passed)[i].at[h, part], self.loc.at[i]
                    )
                )
            for copy in loads:
                copy.start()
            for copy in loads:
                copy.wait()
            for i in range(2):
                add_blocks(self.here.at[i], self.there.at[i])
            for copy in stores:
                copy.start()
            for copy in stores:
                copy.wait()

    def second(self, part):
        me = self.me
        return [
            remote(
                self.passed.at[h, part],
                self.got_two.at[h, part],
                self.snd.at[part, 4 + h],
                self.rcv.at[part, 4 + h],
                me.at(me.z, (me.yq, me.xq)[h]),
            )
            for h in range(2)
        ]

    def pass_on(self, part):
        for copy in self.second(part):
            copy.start()

    def fold_again(self, part):
        for copy in self.second(part):
            copy.wait_recv()
        loads, stores = [], []
        for h in range(2):
            a, b = self.here.at[h], self.there.at[h]
            target = self.total.at[part, :, pl.ds(h * self.half, self.half)]
            loads.append(pltpu.make_async_copy(self.kept.at[h, part], a, self.loc.at[h]))
            loads.append(pltpu.make_async_copy(self.got_two.at[h, part], b, self.loc.at[2 + h]))
            stores.append(pltpu.make_async_copy(a, target, self.loc.at[h]))
        for copy in loads:
            copy.start()
        for copy in loads:
            copy.wait()
        for h in range(2):
            add_blocks(self.here.at[h], self.there.at[h])
        for copy in stores:
            copy.start()
        for copy in stores:
            copy.wait()

    def close(self, part):
        for copy in self.sends(part) + self.second(part):
            copy.wait_send()


LINE_SEMS = [pltpu.SemaphoreType.DMA((4,)), pltpu.SemaphoreType.DMA((4,)), pltpu.SemaphoreType.DMA]


def line_exchange(me, src, done, sems):
    snd, rcv, loc = sems
    local = pltpu.make_async_copy(src.at[me.z], done.at[me.z], loc)
    local.start()

    def send(j):
        z = me.order(j)
        return remote(src.at[z], done.at[me.z], snd.at[z], rcv.at[me.z], me.at(z, me.q))

    for j in (3, 2, 1):
        send(j).start()
    yield True
    for j in range(1, 4):
        z = me.order(j)
        remote(done.at[z], done.at[z], snd.at[z], rcv.at[z], me.at(z, me.q)).wait_recv()
    for j in range(1, 4):
        send(j).wait_send()
    local.wait()


def transfer(number, inputs, outputs, scratch, steps, whole=False, near=()):
    flat = [item for group in scratch for item in group]
    sizes = [len(group) for group in scratch]

    def kernel(*refs):
        ins = refs[: len(inputs)]
        outs = refs[len(inputs) : len(inputs) + len(outputs)]
        rest = refs[len(inputs) + len(outputs) :]
        groups = []
        for size in sizes:
            groups.append(rest[:size])
            rest = rest[size:]
        me = Place()
        me.greet(whole)
        run(steps(me, ins, outs, groups))

    return pl.pallas_call(
        kernel,
        out_shape=[jax.ShapeDtypeStruct(shape, dtype) for shape, dtype in outputs],
        in_specs=[VMEM if i in near else ANY for i in range(len(inputs))],
        out_specs=[ANY] * len(outputs),
        scratch_shapes=flat,
        compiler_params=pltpu.CompilerParams(
            collective_id=number, has_side_effects=True, vmem_limit_bytes=62 * 2**20
        ),
    )(*inputs)


def gather_rows(me, src, dst, sems):
    rows = src.shape[0]
    cut = -(-rows // 32) * 16

    def part(z, q, h):
        if cut == rows and h:
            return None
        return dst.at[4 * z + q, pl.ds(h * cut, (rows - cut) if h else cut)]

    return gather(me, src, lambda z, q: dst.at[4 * z + q], part, sems)


def group_lists(groups):
    return [[r + RING * g for g in range(groups)] for r in range(RING)]


def grow(x, axis, groups):
    if groups == 1:
        return x
    return lax.all_gather(x, "seq", axis=axis, tiled=True, axis_index_groups=group_lists(groups))


def shrink(x, axis, groups):
    if groups == 1:
        return x
    return lax.psum_scatter(
        x, "seq", scatter_dimension=axis, tiled=True, axis_index_groups=group_lists(groups)
    )


def to_places(x, groups):
    if groups == 1:
        return x
    return x.reshape(x.shape[0], groups, RING, -1).swapaxes(1, 2).reshape(x.shape)


def from_places(x, groups):
    if groups == 1:
        return x
    return x.reshape(x.shape[0], RING, groups, -1).swapaxes(1, 2).reshape(x.shape)


def normalize(stream, scale_vec):
    return (
        stream * lax.rsqrt(jnp.mean(stream * stream, axis=-1, keepdims=True) + epsilon) * scale_vec
    )


def rotate(values, places, head_count, direction):
    head_size = values.shape[1] // head_count
    shaped = values.reshape(values.shape[0], head_count, head_size)
    quarter = head_size // 4
    first_part = shaped[..., :quarter]
    second = shaped[..., quarter : 2 * quarter]
    remainder = shaped[..., 2 * quarter :]
    frequency = 10000.0 ** (-jnp.arange(quarter, dtype=jnp.float32) / quarter)
    angles = places.astype(jnp.float32)[:, None] * frequency[None, :]
    cosine = jnp.cos(angles)[:, None, :]
    sine_part = direction * jnp.sin(angles)[:, None, :]
    turned = jnp.concatenate(
        [
            first_part * cosine - second * sine_part,
            second * cosine + first_part * sine_part,
            remainder,
        ],
        axis=-1,
    )
    return turned.reshape(values.shape)


def dot(a, b, ca=1, cb=0):
    return lax.dot_general(a, b, (((ca,), (cb,)), ((), ())), preferred_element_type=f32)


def body(
    inputs,
    segment_ids,
    cotangent,
    attn_gain,
    query_weight,
    key_value_weight,
    out_weight,
    out_bias,
    mlp_gain,
    gate_up_weight,
    gate_up_bias,
    down_weight,
    down_bias,
):
    seq_index = lax.axis_index("seq")
    t = lax.axis_index("tensor")
    r = seq_index % RING
    z = r // 4
    q = r % 4
    groups = lax.axis_size("seq") // RING
    tokens, width = inputs.shape
    inputs = to_places(inputs, groups)
    cotangent = to_places(cotangent, groups)
    heads = query_weight.shape[1] // HD
    hidden_half = gate_up_weight.shape[2]
    block = -(-hidden_half // (LINE * LANES)) * LANES
    block_start = jnp.minimum(z * block, hidden_half - block)
    block_skip = z * block - block_start
    reach = (W + tokens - 2) // tokens
    span = (reach + 1) * tokens
    first_block = jnp.maximum(r - reach, 0)
    scale_factor = HD ** (-0.5)
    assert tokens * RING == SEQ_LEN and lax.axis_size("tensor") == 2

    def own_features(x):
        if groups == 1:
            return x
        both = lax.all_gather(x, "tensor", axis=0)
        both = lax.all_gather(both, "seq", axis=0, axis_index_groups=group_lists(groups))
        both = both.reshape((2, -1) + x.shape[1:])
        return lax.dynamic_index_in_dim(both, t, 0, keepdims=False)

    kv_own = own_features(key_value_weight)
    kv_rows, columns = kv_own.shape
    vectors = [own_features(v) for v in (attn_gain, out_bias, mlp_gain, down_bias)]
    hidden_bias = grow(gate_up_bias, 1, groups)
    marks = jnp.stack([segment_ids // 256, segment_ids % 256]).astype(bf16)

    def pad_to(x, n):
        return jnp.pad(x, ((0, 0), (0, n - x.shape[1])))

    small = jnp.concatenate(
        [
            pad_to(jnp.stack(vectors), columns),
            pad_to(hidden_bias, columns),
            pad_to(marks, columns),
            jnp.zeros((8, columns), bf16),
        ]
    )
    query_own = grow(query_weight, 0, groups)
    out_own = grow(out_weight.T, 0, groups)
    gate_up_own = grow(gate_up_weight, 1, groups)
    down_own = grow(down_weight.T, 0, groups)
    rows = query_own.shape[0]
    places = r * tokens + jnp.arange(tokens, dtype=jnp.int32)
    frequency = 10000.0 ** (-jnp.arange(HD // 4, dtype=f32) / (HD // 4))
    angles = places.astype(f32)[:, None] * frequency[None, :]
    turn_cos = jnp.concatenate([jnp.cos(angles), jnp.cos(angles)], axis=1)
    turn_sin = jnp.concatenate([-jnp.sin(angles), jnp.sin(angles)], axis=1)
    own_marks = segment_ids.astype(f32)[:, None]
    feature = jnp.arange(width)[None, :]
    pick_device = (feature // kv_rows == jnp.arange(2 * RING)[:, None]).astype(bf16)
    pick_entry = (feature % kv_rows == jnp.arange(LANES)[:, None]).astype(bf16)

    def first_steps(me, ins, outs, groups_in):
        (
            own_query, own_kvw, own_small, own_out, own_gate_up, own_down, x_in, cot_in,
            marks_column, cos2, sin2, device_of, entry_of,
        ) = ins
        (
            query_all, kvw_all, small_all, kv_all, out_all, ffn_all, cot_out, mixed_out, log_out,
            middle_out, normed_two_out, queries_out, normed_out, vec_out, marks_out,
        ) = outs
        (
            query_sems, kvw_sems, small_sems, kv_sems, out_sems, ffn_sems, cot_sems, spread_sems,
            swap_sems, scratch,
        ) = groups_in
        (
            qs, win, weight, kvw, mask, mixed, part, theirs, x, middle, normed, normed_two, logs,
            small, small_wide, vec, marks_row, kv_low, loads,
        ) = scratch

        def load(n, src, dst):
            return pltpu.make_async_copy(src, dst, loads.at[n])

        def turn(v):
            first = v[:, : HD // 2]
            turned = first * cos2[...] + pltpu.roll(first, HD // 4, 1) * sin2[...]
            return jnp.concatenate([turned, v[:, HD // 2 :]], axis=1)

        def columns_of(source, lead):
            def piece(place):
                at = jnp.minimum(place * block, hidden_half - block)
                at = pl.ds(pl.multiple_of(at, LANES), block)
                return source.at[:, :, at] if lead else source.at[:, at]

            return piece

        def share(n, ref):
            mine = ref.at[:, me.t]
            return remote(mine, mine, swap_sems[0].at[n], swap_sems[1].at[n], me.other())

        smalls = gather_rows(me, own_small, small_all.at[:, me.t], small_sems)
        kvws = gather_rows(me, own_kvw, kvw_all.at[:, me.t], kvw_sems)
        queries = gather_rows(me, own_query, query_all, query_sems)
        keys = gather_rows(me, kv_low, kv_all, kv_sems)
        outw = gather_rows(me, own_out, out_all, out_sems)
        ffn = gather_pieces(
            me,
            [(pl.ds(0, 2), columns_of(own_gate_up, True)), (2, columns_of(own_down, False))],
            ffn_all,
            ffn_sems,
        )
        cot = spread(me, cot_in, cot_out, cot_sems)
        load(0, x_in, x).start()
        for n in range(5):
            next(smalls)
            next(kvws)
            next(queries)
            if n == 3:
                next(outw)
                next(ffn)
        for _ in smalls:
            pass
        share(0, small_all).start()
        for _ in kvws:
            pass
        share(1, kvw_all).start()
        share(0, small_all).wait()
        load(1, small_all, small).start()
        load(1, small_all, small).wait()
        small_wide[...] = small[...].reshape(small_wide.shape).astype(f32)
        vec[...] = jnp.zeros(vec.shape, f32)
        for i in range(4):
            piece = small_wide[:, i, :LANES].astype(bf16)
            spread_out = dot(piece, device_of[...], 0, 0) * entry_of[...].astype(f32)
            vec[i : i + 1] = jnp.sum(spread_out, axis=0, keepdims=True)
        start = jnp.maximum(me.r - reach, 0)
        row_places = me.r * tokens + lax.broadcasted_iota(jnp.int32, (tokens, 1), 0)

        @pl.loop(0, reach + 1)
        def _(i):
            at = pl.ds(pl.multiple_of(i * tokens, tokens), tokens)
            high = small_wide[2 * (start + i), 6:7, :tokens]
            low = small_wide[2 * (start + i), 7:8, :tokens]
            key_marks = high * 256.0 + low
            marks_row[:, at] = key_marks
            key_places = (start + i) * tokens + lax.broadcasted_iota(jnp.int32, (1, tokens), 1)
            gap = row_places - key_places
            seen = (gap >= 0) & (gap < W) & (marks_column[...] == key_marks)
            mask[:, at] = jnp.where(seen, 0.0, -1e30)

        load(1, vec, vec_out).start()
        load(2, marks_row, marks_out).start()
        load(0, x_in, x).wait()

        @pl.loop(0, tokens // 16)
        def _(i):
            at = pl.ds(pl.multiple_of(i * 16, 16), 16)
            value = x[at].astype(f32)
            scale = lax.rsqrt(jnp.mean(value * value, axis=1, keepdims=True) + epsilon)
            normed[at] = (value * scale * vec[0:1]).astype(bf16)

        load(0, normed, normed_out).start()
        share(1, kvw_all).wait()
        load(3, kvw_all, kvw).start()
        load(3, kvw_all, kvw).wait()
        both = dot(normed[...], kvw[...].reshape(width, 2 * HD))
        kv_low[:, :HD] = turn(both[:, :HD]).astype(bf16)
        kv_low[:, HD:] = both[:, HD:].astype(bf16)
        next(keys)
        for _ in queries:
            pass
        load(3, query_all, weight).start()
        load(3, query_all, weight).wait()

        @pl.loop(0, heads)
        def _(h):
            at = pl.ds(pl.multiple_of(h * HD, HD), HD)
            value = dot(normed[...], weight[:, :, at].reshape(width, HD))
            qs[:, at] = (turn(value) * scale_factor).astype(bf16)

        load(4, qs, queries_out).start()
        for _ in range(3):
            next(outw)
            next(keys)
        for _ in keys:
            pass
        next(ffn)
        next(ffn)
        load(3, kv_all.at[pl.ds(start, reach + 1)], win).start()
        load(3, kv_all.at[pl.ds(start, reach + 1)], win).wait()

        @pl.loop(0, heads)
        def _(h):
            at = pl.ds(pl.multiple_of(h * HD, HD), HD)
            window = win[...].reshape(span, 2 * HD)
            scores = dot(qs[:, at], window[:, :HD], 1, 1) + mask[...]
            top = jnp.max(scores, axis=1, keepdims=True)
            exponent = jnp.exp(scores - top)
            total = jnp.sum(exponent, axis=1, keepdims=True)
            blend = dot(exponent.astype(bf16), window[:, HD:])
            mixed[:, at] = (blend / total).astype(bf16)
            logs[h] = top + jnp.log(total)

        load(5, mixed, mixed_out).start()
        load(6, logs, log_out).start()
        next(outw)
        for _ in outw:
            pass
        next(ffn)
        load(3, out_all, weight).start()
        load(3, out_all, weight).wait()

        @pl.loop(0, LINE)
        def _(i):
            at = pl.ds(pl.multiple_of(i * 4 * rows, LANES), 4 * rows)
            piece = weight[pl.ds(4 * i, 4)].reshape(4 * rows, heads * HD)
            part[:, at] = dot(mixed[...], piece, 1, 1).astype(bf16)

        swapped = remote(part, theirs, swap_sems[0].at[2], swap_sems[1].at[2], me.other())
        swapped.start()
        swapped.wait()

        @pl.loop(0, tokens // 16)
        def _(i):
            at = pl.ds(pl.multiple_of(i * 16, 16), 16)
            total = x[at].astype(f32) + (part[at].astype(f32) + theirs[at].astype(f32)) + vec[1:2]
            middle[at] = total
            scale = lax.rsqrt(jnp.mean(total * total, axis=1, keepdims=True) + epsilon)
            normed_two[at] = (total * scale * vec[2:3]).astype(bf16)

        out = spread(me, normed_two, normed_two_out, spread_sems)
        next(out)
        load(7, middle, middle_out).start()
        next(out)
        next(ffn)
        next(out)
        next(ffn)
        next(out)
        next(cot)
        next(ffn)
        for _ in range(3):
            next(cot)
        for step in (ffn, out, cot):
            for _ in step:
                pass
        for n, src, dst in (
            (0, normed, normed_out),
            (1, vec, vec_out),
            (2, marks_row, marks_out),
            (4, qs, queries_out),
            (5, mixed, mixed_out),
            (6, logs, log_out),
            (7, middle, middle_out),
        ):
            load(n, src, dst).wait()
        return []

    query_shape = (tokens, heads * HD)
    (
        query_full, kv_full, smalls, kv_all, out_full, ffn_full, cot_all, mixed_low, log_total,
        middle, normed_all, queries, normed, vec, window_marks,
    ) = transfer(
        0,
        [
            query_own, kv_own, small, out_own, gate_up_own, down_own, inputs, cotangent,
            own_marks, turn_cos, turn_sin, pick_device, pick_entry,
        ],
        [
            ((RING,) + query_own.shape, bf16),
            ((RING, 2) + kv_own.shape, bf16),
            ((RING, 2) + small.shape, bf16),
            ((RING, tokens, 2 * HD), bf16),
            ((RING,) + out_own.shape, bf16),
            ((3, RING, rows, block), bf16),
            ((LINE,) + inputs.shape, bf16),
            (query_shape, bf16),
            ((heads, tokens, 1), f32),
            (inputs.shape, f32),
            ((LINE,) + inputs.shape, bf16),
            (query_shape, bf16),
            (inputs.shape, bf16),
            ((8, width), f32),
            ((1, span), f32),
        ],
        [
            GATHER_SEMS,
            GATHER_SEMS,
            GATHER_SEMS,
            GATHER_SEMS,
            GATHER_SEMS,
            PIECE_SEMS,
            SPREAD_SEMS,
            SPREAD_SEMS,
            [pltpu.SemaphoreType.DMA((3,)), pltpu.SemaphoreType.DMA((3,))],
            [
                pltpu.VMEM(query_shape, bf16),
                pltpu.VMEM((reach + 1, tokens, 2 * HD), bf16),
                pltpu.VMEM((RING,) + out_own.shape, bf16),
                pltpu.VMEM((RING, 2) + kv_own.shape, bf16),
                pltpu.VMEM((tokens, span), f32),
                pltpu.VMEM(query_shape, bf16),
                pltpu.VMEM(inputs.shape, bf16),
                pltpu.VMEM(inputs.shape, bf16),
                pltpu.VMEM(inputs.shape, bf16),
                pltpu.VMEM(inputs.shape, f32),
                pltpu.VMEM(inputs.shape, bf16),
                pltpu.VMEM(inputs.shape, bf16),
                pltpu.VMEM((heads, tokens, 1), f32),
                pltpu.VMEM((RING, 2) + small.shape, bf16),
                pltpu.VMEM((2 * RING,) + small.shape, f32),
                pltpu.VMEM((8, width), f32),
                pltpu.VMEM((1, span), f32),
                pltpu.VMEM((tokens, 2 * HD), bf16),
                pltpu.SemaphoreType.DMA((8,)),
            ],
        ],
        first_steps,
        near=(8, 9, 10, 11, 12),
    )
    query_full = query_full.reshape(width, heads * HD)
    kv_full = kv_full.reshape(width, columns)
    out_full = out_full.reshape(width, heads * HD)
    ffn_full = ffn_full.reshape(3, width, block)
    gain_one, _, gain_two, bias_down = (vec[i] for i in range(4))
    stream = inputs.astype(f32)

    def hidden_vector(row):
        piece = smalls[:, :, row, : hidden_bias.shape[1]].reshape(RING, 2, groups, -1)
        return jnp.transpose(piece, (2, 0, 1, 3)).reshape(-1).astype(f32)

    bias_gate_up = jnp.stack([hidden_vector(4 + i) for i in range(2)])
    bias_local = lax.dynamic_slice_in_dim(bias_gate_up, t * hidden_half + block_start, block, 1)

    ours = (jnp.arange(block) >= block_skip).astype(f32)[None, :]
    part_rows = 4 * rows
    pace = block // 2

    def third_steps(me, ins, outs, groups_in):
        normed_in, cot_in, weights_in, bias, valid = ins
        normed_grad_out, mlp_out, total, bias_own, bias_theirs, term, *buffers = outs
        one_scratch, two_scratch, plane_sems, swap_sems, scratch = groups_in
        (
            weights, normed_v, cot_v, chunks, hidden, gate_low, up_low, bias_sum, bias_low,
            stage, here, there, loads,
        ) = scratch
        one = LineSum(me, normed_grad_out, one_scratch)
        two = LineSum(me, mlp_out, two_scratch)
        plane = PlaneSum(me, term, buffers, total, here, there, plane_sems)

        def load(n, src, dst):
            return pltpu.make_async_copy(src, dst, loads.at[n])

        def part_columns(i):
            return pl.ds(pl.multiple_of(i * part_rows, LANES), part_rows)

        def rows_of(i):
            return pl.ds(pl.multiple_of(i * tokens, tokens), tokens)

        for n in range(3):
            load(n, weights_in.at[n], weights.at[n]).start()
        load(3, normed_in.at[0], normed_v).start()
        load(4, cot_in.at[0], cot_v).start()
        bias_sum[...] = jnp.zeros(bias_sum.shape, f32)
        for n in range(3):
            load(n, weights_in.at[n], weights.at[n]).wait()

        def both_ways(place):
            load(3, normed_in.at[place], normed_v).wait()
            load(4, cot_in.at[place], cot_v).wait()
            at = rows_of(place)

            @pl.loop(0, 2)
            def _(n):
                part = pl.ds(pl.multiple_of(n * pace, LANES), pace)
                gate = dot(normed_v[...], weights[0, :, part]) + bias[0:1, part]
                up = dot(normed_v[...], weights[1, :, part]) + bias[1:2, part]
                grad = dot(cot_v[...], weights[2, :, part]) * valid[:, part]
                square = gate * gate
                slope = 0.7978845608028654 * (1.0 + 3.0 * 0.044715 * square)
                turn = jnp.tanh(0.7978845608028654 * gate * (1.0 + 0.044715 * square))
                side = 0.5 * (1.0 + turn)
                unit = gate * side
                hidden[at, part] = (unit * up * valid[:, part]).astype(bf16)
                gate_grad = grad * up * (side + 0.5 * gate * (1.0 - turn * turn) * slope)
                gate_low[at, part] = gate_grad.astype(bf16)
                up_low[at, part] = (grad * unit).astype(bf16)
                for i, low in enumerate((gate_low, up_low)):
                    bias_sum[i : i + 1, part] += jnp.sum(
                        low[at, part].astype(f32), axis=0, keepdims=True
                    )

            @pl.when(place < LINE - 1)
            def _():
                load(3, normed_in.at[place + 1], normed_v).start()
                load(4, cot_in.at[place + 1], cot_v).start()

        pl.loop(0, LINE)(both_ways)

        def back(place):
            at = rows_of(place)

            @pl.loop(0, LINE)
            def _(i):
                lines = part_columns(i)
                value = dot(gate_low[at], weights[0, lines], 1, 1)
                value += dot(up_low[at], weights[1, lines], 1, 1)
                one.src[place, :, lines] = value.astype(bf16)

            one.cross(place).start()

        bias_low[...] = bias_sum[...].astype(bf16)
        bias_swap = remote(bias_low, bias_theirs, swap_sems[0], swap_sems[1], me.other())
        bias_swap.start()
        bias_keep = load(0, bias_low, bias_own)
        bias_keep.start()

        def chunk(source, i, slot):
            return load(3 + slot, source.at[:, :, part_columns(i)], chunks.at[slot])

        def stored(n, target):
            return load(1 + n, stage.at[n], target)

        def weight_term(slot, factor, n, target):
            left = chunks[slot].reshape(LINE * tokens, part_rows)
            stage[n] = dot(left, factor[...], 0, 0).astype(bf16).reshape(stage.shape[1:])
            stored(n, target).start()

        def outputs_of(place):
            @pl.loop(0, LINE)
            def _(i):
                lines = part_columns(i)
                value = dot(hidden[rows_of(place)], weights[2, lines], 1, 1)
                two.src[place, :, lines] = value.astype(bf16)

            two.cross(place).start()

        def down_terms(i):
            slot = lax.rem(i, 2)
            chunk(cot_in, i, slot).wait()

            @pl.when(i < LINE - 1)
            def _():
                chunk(cot_in, i + 1, 1 - slot).start()

            @pl.when(i > 1)
            def _():
                stored(slot, term.at[2, i]).wait()

            weight_term(slot, hidden, slot, term.at[2, i])

        def gate_up_terms(i):
            slot = lax.rem(i, 2)
            chunk(normed_in, i, slot).wait()

            @pl.when(i < LINE - 1)
            def _():
                chunk(normed_in, i + 1, 1 - slot).start()

            for n, factor in enumerate((gate_low, up_low)):

                @pl.when(i > 0)
                def _():
                    stored(n, term.at[n, i]).wait()

                weight_term(slot, factor, n, term.at[n, i])

        chunk(cot_in, 0, 0).start()

        @pl.loop(0, 2)
        def _(i):
            outputs_of(3 - 3 * i)

        two.fold(3)
        two.fold(0)
        two.step(0)
        pl.loop(0, LINE)(down_terms)
        chunk(normed_in, 0, 0).start()
        for n in range(2):
            stored(n, term.at[2, 0]).wait()
        plane.start(2)

        @pl.loop(0, 2)
        def _(i):
            outputs_of(2 - i)

        two.fold(2)
        two.fold(1)
        two.step(1)
        pl.loop(0, LINE)(gate_up_terms)
        for n in range(2):
            stored(n, term.at[n, 0]).wait()
        plane.start(0)
        two.step(2)

        @pl.loop(0, 2)
        def _(i):
            back(3 - 3 * i)

        one.fold(3)
        one.fold(0)
        one.step(0)

        @pl.loop(0, 2)
        def _(i):
            back(2 - i)

        one.fold(2)
        one.fold(1)
        two.finish()
        one.step(1)
        plane.fold(2)
        plane.pass_on(2)
        one.step(2)
        plane.fold(0)
        plane.pass_on(0)
        plane.fold_again(2)
        one.finish()
        plane.fold_again(0)
        one.close()
        two.close()
        for part in (0, 2):
            plane.close(part)
        bias_swap.wait()
        bias_keep.wait()
        return []

    half_shape = (2, 3, LINE, rows // 2, block)
    normed_two_grad, mlp_out, ffn_total, hidden_bias_part, bias_theirs, ffn_term = transfer(
        1,
        [normed_all, cot_all, ffn_full, bias_local, ours],
        [
            ((tokens, width), bf16),
            ((tokens, width), bf16),
            ((3, LINE, rows, block), bf16),
            ((16, block), bf16),
            ((16, block), bf16),
            ((3, LINE, 4, rows, block), bf16),
            ((3, 2, 2, LINE, rows // 2, block), bf16),
            (half_shape, bf16),
            (half_shape, bf16),
            (half_shape, bf16),
        ],
        [
            line_sum_scratch(tokens // 2, width),
            line_sum_scratch(tokens // 2, width),
            PLANE_SUM_SEMS,
            SWAP_SEMS,
            [
                pltpu.VMEM((3, width, block), bf16),
                pltpu.VMEM((tokens, width), bf16),
                pltpu.VMEM((tokens, width), bf16),
                pltpu.VMEM((2, LINE, tokens, part_rows), bf16),
                pltpu.VMEM((LINE * tokens, block), bf16),
                pltpu.VMEM((LINE * tokens, block), bf16),
                pltpu.VMEM((LINE * tokens, block), bf16),
                pltpu.VMEM((16, block), f32),
                pltpu.VMEM((16, block), bf16),
                pltpu.VMEM((2, 4, rows, block), bf16),
                pltpu.VMEM((2, LINE, rows // 2, block), bf16),
                pltpu.VMEM((2, LINE, rows // 2, block), bf16),
                pltpu.SemaphoreType.DMA((5,)),
            ],
        ],
        third_steps,
        near=(3, 4),
    )[:6]
    cot_full = cotangent.astype(f32)
    _, norm_two_pull = jax.vjp(normalize, middle, gain_two)
    middle_part, gain_two_grad = norm_two_pull(normed_two_grad.astype(f32))
    middle_grad = cot_full + middle_part
    middle_low = middle_grad.astype(bf16)

    def core_features(full):
        blocks = full.reshape(full.shape[0], RING, groups, 2, -1)
        blocks = lax.dynamic_index_in_dim(blocks, t, 3, keepdims=False)
        return jnp.moveaxis(blocks, 1, 0).reshape(RING, full.shape[0], -1)

    def core_hidden(full):
        blocks = full.reshape(full.shape[0], groups, RING, 2, -1)
        blocks = lax.dynamic_index_in_dim(blocks, t, 3, keepdims=False)
        return jnp.transpose(blocks, (2, 0, 1, 3)).reshape(RING, full.shape[0], -1)

    vector_terms = core_features(
        jnp.stack([jnp.sum(middle_grad, axis=0), gain_two_grad, jnp.sum(cot_full, axis=0)])
    )
    bias_pair = jnp.where(
        t == 0,
        jnp.stack([hidden_bias_part, bias_theirs]),
        jnp.stack([bias_theirs, hidden_bias_part]),
    )[:, :2].astype(f32)
    bias_terms = jnp.zeros((2, 2, hidden_half), f32)
    bias_terms = lax.dynamic_update_slice_in_dim(bias_terms, bias_pair, block_start, 2)
    bias_terms = core_hidden(jnp.swapaxes(bias_terms, 0, 1).reshape(2, -1))

    def widen(x):
        return jnp.pad(x, ((0, 0), (0, 0), (0, HD - x.shape[2])))

    small_terms = jnp.concatenate(
        [widen(vector_terms), widen(bias_terms), jnp.zeros((RING, 27, HD), f32)], axis=1
    ).astype(bf16)

    chunk = 3 if (reach + 1) % 3 == 0 else 1
    pieces = (reach + 1) // chunk
    kv_size = rows + small_terms.shape[1]
    vector_rows = -(-width // (LANES * 32)) * 32

    def fourth_steps(me, ins, outs, groups_in):
        (
            low_in, out_in, mixed_in, q_in, kv_in, logs_in, normed_in, query_in, kvw_in,
            ffn_in, total_in, small_in, grad_in, x_in,
            marks_row, marks_column, cos2, sin2, gain,
        ) = ins
        ffn_done, out_done, query_done, kv_done, input_out, gain_all = outs[:6]
        out_term, query_term, kv_term = outs[6:9]
        out_buffers, kv_buffers, ffn_buffers = outs[9:14], outs[14:19], outs[19:24]
        query_buffers = (outs[24:29], outs[29:34])
        (
            line_sems, line_sems_two, ffn_sems, out_sems, query_sems, more_sems, kv_sems, window_scratch, swap_sems, last_sems,
            vector_sems, scratch,
        ) = groups_in
        (
            low, weight, mixed, qs, win, normed_v, logs, mixed_grad, q_grad, window_sum, mask,
            kv_total, kv_low, kvw, stage, kv_stage, here, there, kv_here, kv_there, part, theirs,
            gain_sum, gain_rows, gain_low, loads,
        ) = scratch

        def load(n, src, dst):
            return pltpu.make_async_copy(src, dst, loads.at[n])

        def turn(v, direction):
            first = v[:, : HD // 2]
            turned = first * cos2[...] + direction * (pltpu.roll(first, HD // 4, 1) * sin2[...])
            return jnp.concatenate([turned, v[:, HD // 2 :]], axis=1)

        part_rows = 4 * rows

        def part_columns(i):
            return pl.ds(pl.multiple_of(i * part_rows, LANES), part_rows)

        lines = [
            line_exchange(me, total_in.at[2], ffn_done.at[2], line_sems),
            line_exchange(me, total_in.at[0], ffn_done.at[0], line_sems_two),
        ]
        ffn = scatter(me, ffn_in.at[1], ffn_done.at[1], ffn_buffers, here, there, ffn_sems)
        outw = scatter(me, out_term, out_done, out_buffers, here, there, out_sems)
        query, more = (
            scatter(me, query_term.at[n], query_done.at[n], query_buffers[n], here, there, sems)
            for n, sems in enumerate((query_sems, more_sems))
        )
        kvw_steps = scatter(
            me, kv_term, kv_done.at[me.t], kv_buffers, kv_here, kv_there, kv_sems
        )
        for step in [ffn, outw, query, more, kvw_steps] + lines + [ffn]:
            next(step)
        start = jnp.maximum(me.r - reach, 0)
        first_loads = [
            load(0, low_in, low),
            load(1, mixed_in, mixed),
            load(2, out_in, weight),
            load(3, q_in, qs),
            load(4, kv_in.at[pl.ds(start, reach + 1)], win),
            load(5, logs_in, logs),
            load(6, normed_in, normed_v),
            load(7, kvw_in, kvw),
        ]
        for copy in first_loads:
            copy.start()
        first_loads[0].wait()
        first_loads[1].wait()

        def weight_term(left, right, targets):
            width_of = heads * HD // len(targets)

            @pl.loop(0, LINE)
            def _(i):
                value = dot(left[:, part_columns(i)], right[...], 0, 0).astype(bf16)
                stage[...] = value.reshape(stage.shape)
                copies = [
                    load(8 + n, stage.at[:, :, pl.ds(n * width_of, width_of)], term.at[i])
                    for n, term in enumerate(targets)
                ]
                for copy in copies:
                    copy.start()
                for copy in copies:
                    copy.wait()

        weight_term(low, mixed, [out_term])
        first_loads[2].wait()

        @pl.loop(0, heads)
        def _(h):
            at = pl.ds(pl.multiple_of(h * HD, HD), HD)
            mixed_grad[:, at] = dot(low[...], weight[:, at]).astype(bf16)

        load(2, query_in, weight).start()
        load(0, x_in, low).start()
        row_places = me.r * tokens + lax.broadcasted_iota(jnp.int32, (tokens, 1), 0)

        @pl.loop(0, reach + 1)
        def _(i):
            at = pl.ds(pl.multiple_of(i * tokens, tokens), tokens)
            key_places = (start + i) * tokens + lax.broadcasted_iota(jnp.int32, (1, tokens), 1)
            gap = row_places - key_places
            seen = (gap >= 0) & (gap < W) & (marks_column[...] == marks_row[:, at])
            mask[:, at] = jnp.where(seen, 0.0, -1e30)
            window_sum[i] = jnp.zeros((tokens, 2 * HD), f32)

        for copy in first_loads[3:]:
            copy.wait()

        @pl.loop(0, heads)
        def _(h):
            at = pl.ds(pl.multiple_of(h * HD, HD), HD)
            q_head = qs[:, at]
            grad = mixed_grad[:, at]
            inner = jnp.sum(grad.astype(f32) * mixed[:, at].astype(f32), axis=1, keepdims=True)
            log = logs[h]
            q_sum = jnp.zeros((tokens, HD), f32)
            for c in range(pieces):
                blocks = pl.ds(c * chunk, chunk)
                both = win[blocks].reshape(chunk * tokens, 2 * HD)
                k, v = both[:, :HD], both[:, HD:]
                span_at = pl.ds(c * chunk * tokens, chunk * tokens)
                probs = jnp.exp(dot(q_head, k, 1, 1) + mask[:, span_at] - log)
                value_sum = dot(probs.astype(bf16), grad, 0, 0)
                score_grad = (probs * (dot(grad, v, 1, 1) - inner)).astype(bf16)
                q_sum += dot(score_grad, k)
                key_sum = dot(score_grad, q_head, 0, 0)
                window_sum[blocks, :, :HD] += key_sum.reshape(chunk, tokens, HD)
                window_sum[blocks, :, HD:] += value_sum.reshape(chunk, tokens, HD)
            q_grad[:, at] = (turn(q_sum, -1.0) * scale_factor).astype(bf16)

            @pl.when(h == heads - 1)
            def _():
                next(outw)


        @pl.loop(0, reach + 1)
        def _(i):
            win[i] = window_sum[i].astype(bf16)

        window_steps = reduce_window(me, reach, win, kv_total, window_scratch)
        next(window_steps)
        load(5, grad_in, mask).start()
        next(window_steps)
        weight_term(normed_v, q_grad, [query_term.at[0], query_term.at[1]])
        load(2, query_in, weight).wait()

        @pl.loop(0, LINE)
        def _(i):
            piece = weight[pl.ds(pl.multiple_of(i * part_rows, LANES), part_rows)]
            part[:, part_columns(i)] = dot(q_grad[...], piece, 1, 1).astype(bf16)

        swapped = remote(part, theirs, swap_sems[0], swap_sems[1], me.other())
        swapped.start()
        next(ffn)
        next(outw)
        next(query)
        next(ffn)
        next(window_steps)
        next(window_steps, None)

        kv_low[:, :HD] = turn(kv_total[:, :HD], -1.0).astype(bf16)
        kv_low[:, HD:] = kv_total[:, HD:].astype(bf16)
        ours_at = pl.ds(pl.multiple_of(me.t * HD, HD), HD)
        small_copy = load(0, x_in, low)
        small_copy.wait()

        @pl.loop(0, LINE)
        def _(i):
            value = dot(normed_v[:, part_columns(i)], kv_low[:, ours_at], 0, 0).astype(bf16)
            kv_stage[:, pl.ds(0, rows)] = value.reshape(4, rows, HD)
            copy = load(9, small_in.at[pl.ds(4 * i, 4)], kv_stage.at[:, pl.ds(rows, kv_size - rows)])
            copy.start()
            copy.wait()
            copy = load(9, kv_stage, kv_term.at[i])
            copy.start()
            copy.wait()

        next(more)
        next(kvw_steps)
        next(outw)
        next(query)

        swapped.wait()

        @pl.loop(0, width // (2 * HD))
        def _(i):
            at = pl.ds(pl.multiple_of(i * 2 * HD, 2 * HD), 2 * HD)
            more = dot(kv_low[...], kvw[at], 1, 1)
            window_sum[i] = part[:, at].astype(f32) + theirs[:, at].astype(f32) + more

        gain_sum[...] = jnp.zeros(gain_sum.shape, f32)
        load(5, grad_in, mask).wait()

        @pl.loop(0, tokens // 16)
        def _(i):
            at = pl.ds(pl.multiple_of(i * 16, 16), 16)
            grad = jnp.concatenate([window_sum[n, at] for n in range(width // (2 * HD))], axis=1)
            stream_rows = low[at].astype(f32)
            scale = lax.rsqrt(
                jnp.mean(stream_rows * stream_rows, axis=1, keepdims=True) + epsilon
            )
            unit = stream_rows * scale
            gain_sum[...] += grad * unit
            scaled = grad * gain[...]
            inner = jnp.mean(scaled * unit, axis=1, keepdims=True)
            mask[at] = mask[at] + scale * (scaled - unit * inner)

        load(5, mask, input_out).start()
        gain_rows[...] = jnp.zeros(gain_rows.shape, f32)
        gain_total = jnp.sum(gain_sum[...], axis=0, keepdims=True)
        for i in range(width // LANES):
            gain_rows[pl.ds(i, 1)] = gain_total[:, i * LANES : (i + 1) * LANES]
        gain_low[...] = gain_rows[...].astype(bf16)

        def gain_send(k):
            to = (me.base + lax.rem(me.r + k, RING), me.t)
            return remote(
                gain_low, gain_all.at[me.r], vector_sems[0].at[k], vector_sems[1].at[me.r], to
            )

        keep_gain = load(9, gain_low, gain_all.at[me.r])
        keep_gain.start()

        @pl.loop(1, RING)
        def _(k):
            gain_send(k).start()

        next(more)
        next(kvw_steps)
        next(query)
        next(more)
        next(kvw_steps)
        for step in lines + [ffn, outw, query, more, kvw_steps]:
            for _ in step:
                pass
        mine = kv_done.at[me.t]
        last = remote(mine, mine, last_sems[0], last_sems[1], me.other())
        last.start()

        @pl.loop(1, RING)
        def _(k):
            gain_send(k).wait_send()
            source = lax.rem(me.r + k, RING)
            landed = gain_all.at[source]
            remote(
                landed, landed, vector_sems[0].at[k], vector_sems[1].at[source], me.at(me.z, me.q)
            ).wait_recv()

        keep_gain.wait()
        load(5, mask, input_out).wait()
        last.wait()
        return []

    term_shape = (LINE, 4, rows, heads * HD)
    ffn_shape = (3, LINE, rows, block)
    half = (2, 2, LINE, rows // 2, heads * HD)
    kv_half = (2, 2, LINE, kv_size // 2, HD)
    ffn_done, out_done, query_done, kv_done, input_grad, gain_all = transfer(
        2,
        [
            middle_low, out_full, mixed_low, queries, kv_all, log_total, normed, query_full, kv_full,
            ffn_term, ffn_total, small_terms, middle_grad, inputs,
            window_marks, own_marks, turn_cos, turn_sin, gain_one[None],
        ],
        [
            (ffn_shape, bf16),
            ((LINE, rows, heads * HD), bf16),
            ((2, LINE, rows, heads * HD // 2), bf16),
            ((2, LINE, kv_size, HD), bf16),
            (inputs.shape, f32),
            ((RING, vector_rows, LANES), bf16),
            (term_shape, bf16),
            ((2,) + term_shape[:-1] + (heads * HD // 2,), bf16),
            ((LINE, 4, kv_size, HD), bf16),
        ]
        + scatter_buffers(rows, heads * HD)
        + scatter_buffers(kv_size, HD)
        + scatter_buffers(rows, block)
        + scatter_buffers(rows, heads * HD // 2) * 2,
        [
            LINE_SEMS,
            LINE_SEMS,
            SCATTER_SEMS,
            SCATTER_SEMS,
            SCATTER_SEMS,
            SCATTER_SEMS,
            SCATTER_SEMS,
            reduce_scratch(reach + 1, tokens // 2, 2 * HD, f32),
            SWAP_SEMS,
            SWAP_SEMS,
            [pltpu.SemaphoreType.DMA((RING,)), pltpu.SemaphoreType.DMA((RING,))],
            [
                pltpu.VMEM(inputs.shape, bf16),
                pltpu.VMEM(out_full.shape, bf16),
                pltpu.VMEM(queries.shape, bf16),
                pltpu.VMEM(queries.shape, bf16),
                pltpu.VMEM((reach + 1, tokens, 2 * HD), bf16),
                pltpu.VMEM(inputs.shape, bf16),
                pltpu.VMEM((heads, tokens, 1), f32),
                pltpu.VMEM(queries.shape, bf16),
                pltpu.VMEM(queries.shape, bf16),
                pltpu.VMEM((reach + 1, tokens, 2 * HD), f32),
                pltpu.VMEM(inputs.shape, f32),
                pltpu.VMEM((tokens, 2 * HD), f32),
                pltpu.VMEM((tokens, 2 * HD), bf16),
                pltpu.VMEM(kv_full.shape, bf16),
                pltpu.VMEM((4, rows, heads * HD), bf16),
                pltpu.VMEM((4, kv_size, HD), bf16),
                pltpu.VMEM(half, bf16),
                pltpu.VMEM(half, bf16),
                pltpu.VMEM(kv_half, bf16),
                pltpu.VMEM(kv_half, bf16),
                pltpu.VMEM(inputs.shape, bf16),
                pltpu.VMEM(inputs.shape, bf16),
                pltpu.VMEM((16, width), f32),
                pltpu.VMEM((vector_rows, LANES), f32),
                pltpu.VMEM((vector_rows, LANES), bf16),
                pltpu.SemaphoreType.DMA((10,)),
            ],
        ],
        fourth_steps,
        whole=True,
        near=(14, 15, 16, 17, 18),
    )[:6]
    output = (middle + mlp_out.astype(f32) + bias_down).astype(bf16)

    last_skip = LINE * block - hidden_half
    ffn_grad = jnp.concatenate(
        [ffn_done[:, i] for i in range(LINE - 1)] + [ffn_done[:, LINE - 1, :, last_skip:]], axis=2
    )
    ffn_grad = shrink(ffn_grad.astype(f32), 1, groups)
    out_grad = shrink(jnp.sum(out_done.astype(f32), axis=0), 0, groups).T
    query_sum = jnp.sum(query_done.astype(f32), axis=1)
    query_grad = shrink(jnp.concatenate([query_sum[0], query_sum[1]], axis=1), 0, groups)
    kv_sums = jnp.sum(kv_done.astype(f32), axis=1)
    small_sums = lax.dynamic_index_in_dim(kv_sums[:, rows:], t, 0, keepdims=False)
    kv_grad = jnp.concatenate([kv_sums[0, :rows], kv_sums[1, :rows]], axis=1)
    kv_grad = lax.dynamic_index_in_dim(kv_grad.reshape(groups, 2, -1, columns), t, 1, keepdims=False)
    key_value_grad = shrink(kv_grad.reshape(kv_rows, columns), 0, groups)
    gain_sum = jnp.sum(gain_all[:, : width // LANES].astype(f32), axis=0).reshape(
        RING, groups, 2, kv_rows // groups
    )
    gain_sum = lax.dynamic_index_in_dim(gain_sum, r, 0, keepdims=False)
    gain_sum = lax.dynamic_index_in_dim(gain_sum, t, 1, keepdims=False).reshape(kv_rows)
    small_grads = [shrink(v, 0, groups) for v in [gain_sum] + [small_sums[i, :kv_rows] for i in range(3)]]
    gate_up_bias_grad = shrink(small_sums[3:5, : hidden_bias.shape[1]], 1, groups)
    return (
        from_places(output, groups),
        from_places(input_grad, groups),
        small_grads[0],
        query_grad,
        key_value_grad,
        out_grad,
        small_grads[1],
        small_grads[2],
        ffn_grad[:2],
        gate_up_bias_grad,
        ffn_grad[2].T,
        small_grads[3],
    )


def solution(mesh):
    in_specs = (
        P("seq", None),
        P("seq"),
        P("seq", None),
        P(("seq", "tensor")),
        P("seq", "tensor"),
        P(("seq", "tensor"), None),
        P("tensor", "seq"),
        P(("seq", "tensor")),
        P(("seq", "tensor")),
        P(None, "seq", "tensor"),
        P(None, ("seq", "tensor")),
        P("tensor", "seq"),
        P(("seq", "tensor")),
    )
    out_specs = (
        P("seq", None),
        P("seq", None),
        P(("seq", "tensor")),
        P("seq", "tensor"),
        P(("seq", "tensor"), None),
        P("tensor", "seq"),
        P(("seq", "tensor")),
        P(("seq", "tensor")),
        P(None, "seq", "tensor"),
        P(None, ("seq", "tensor")),
        P("tensor", "seq"),
        P(("seq", "tensor")),
    )
    return jax.shard_map(body, mesh=mesh, in_specs=in_specs, out_specs=out_specs, check_vma=False)
```
